32 devices in a mesh: space: 8 (over z, y), scene: 4 (over x, core).
Axes of the slice: x: 2, y: 2, z: 4, core: 2. Of those that a mesh axis runs over, the one named last changes fastest.
Arguments:
- feats: bfloat16 [256, 512, 128], P(('scene', 'space')), parts along dimension 0, may hold values from -6 to 6
- mask: int32 [256, 512], P(('scene', 'space')), parts along dimension 0, may hold values from 0 to 1, as said below
- neighbours: int32 [256, 8], P(('scene', 'space')), parts along dimension 0, may hold values from -1 to 63, as said below
- weight_one: bfloat16 [27, 128, 128], replicated, may hold values from -0.109375 to 0.109375
- weight_two: bfloat16 [27, 128, 128], replicated, may hold values from -0.109375 to 0.109375
- cotangent: bfloat16 [256, 512, 128], P(('scene', 'space')), parts along dimension 0, may hold values from -12 to 12
Outputs:
- output: bfloat16 [256, 512, 128], P(('scene', 'space')), parts along dimension 0
- grad_input: bfloat16 [256, 512, 128], P(('scene', 'space')), parts along dimension 0
- grad_w1: float32 [108, 128, 128], P('scene'), parts along dimension 0
- grad_w2: float32 [108, 128, 128], P('scene'), parts along dimension 0
The draws below stay inside these ranges and needn't reach their ends.
There are 4 independent parts, one for each index of `scene`. The reference program is written for one: setup_inputs(seed, part) draws one part's arguments, and reference() takes and returns one part's arrays. A program takes and returns all parts, laid end to end along the dimension named above; an argument that names none is the same for every part. Nothing has to cross between parts.
Inputs may be any that keep to these rules, and one draw needn't show every extreme that they name: `mask`: 1 where the voxel is occupied, else 0; an empty brick (see neighbours) is 0 throughout. `neighbours`: A brick number or -1. Brick g is held by index g // 8 of space, and the entries of brick g name only bricks held by that index or by the index one lower or one higher. If brick g names brick h in a direction, h names g in the opposite one (entry 7 - j for entry j). Empty bricks have only -1 entries and are named by no entry. Brick 64 - 1 is named in every draw.
All inputs are finite; a program needn't handle non-finite values.
Results may differ from the reference program's by a relative error of at most 0.02.
Values may be sent and summed in bfloat16 or wider, within the bound.
No kernel may reach another device: no remote copies, remote signals or barrier semaphores. Data moves between devices by JAX's collectives and lax.ppermute only.
A program may use at most 192 MiB of HBM per device.

```python
import math
import jax
import jax.numpy as jnp
from jax import lax

C = 128
EDGE = 8
VOX = 512
TILE = 1
WIDE = 8
BR_DEV = 8
BRICKS = 64
N_SPACE = 8


DIRECTIONS = ((-1, -1), (-1, 0), (-1, 1), (0, -1), (0, 1), (1, -1), (1, 0), (1, 1))


def geometry(key):
    base_key = jax.random.fold_in(key, 7)
    key_fill, key_density, key_voxel = jax.random.split(base_key, 3)
    width_x = N_SPACE * TILE
    width_y = WIDE
    coord_x = jnp.arange(width_x, dtype=jnp.int32)[:, None] * jnp.ones((1, width_y), jnp.int32)
    coord_y = jnp.ones((width_x, 1), jnp.int32) * jnp.arange(width_y, dtype=jnp.int32)[None, :]
    present = jax.random.randint(key_fill, (width_x, width_y), 0, 4) > 0
    corner_pair = (coord_x >= width_x - 2) & (coord_y == width_y - 1)
    present = present | corner_pair
    number = coord_x * width_y + coord_y
    padded_present = jnp.pad(present, 1)
    padded_number = jnp.pad(number, 1, constant_values=-1)
    columns = []
    for step_x, step_y in DIRECTIONS:
        beside = padded_present[1 + step_x:1 + step_x + width_x, 1 + step_y:1 + step_y + width_y]
        number_near = padded_number[1 + step_x:1 + step_x + width_x, 1 + step_y:1 + step_y + width_y]
        columns.append(jnp.where(beside & present, number_near, -1))
    neighbour_list = jnp.stack(columns, axis=-1).reshape(-1, 8).astype(jnp.int32)
    density = jax.random.randint(key_density, (width_x, width_y, 1), 2, 9)
    voxel_draw = jax.random.randint(key_voxel, (width_x, width_y, VOX), 0, 8)
    occupancy = ((voxel_draw < density) & present[:, :, None]).astype(jnp.int32).reshape(-1, VOX)
    return (neighbour_list, occupancy)


def draw_neighbours(key, part):
    return geometry(key)[0]


def draw_mask(key, part):
    return geometry(key)[1]


def steps_of(key, shape, shards, smallest, top_value):
    factor_of = 1.0
    for dim, shards_of in shards:
        steps = jax.random.uniform(jax.random.fold_in(jax.random.fold_in(key, 6), dim), (shards_of,), jnp.float32, smallest / len(shards), top_value / len(shards))
        factor_of = factor_of * jnp.repeat(jnp.exp(steps), shape[dim] // shards_of).reshape((-1,) + (1,) * (len(shape) - 1 - dim))
    return factor_of


def noise(own_key, extent, scale, reach, shards=(), kind=jnp.bfloat16):
    values = scale * jax.random.normal(own_key, extent, jnp.float32)
    if shards:
        values = values * steps_of(own_key, extent, shards, -0.22, 0.18)
    return jnp.clip(values, -reach, reach).astype(kind)


def setup_inputs(seed: int = 0, part: int = 0) -> dict:
    splits = jax.random.split(jax.random.key(seed), 7)
    own_keys = jax.random.split(jax.random.fold_in(splits[6], part), 7)
    return {
        "feats": noise(own_keys[0], (BRICKS, VOX, C), 1.0, 6.0, ((0, 8),)),
        "mask": draw_mask(jax.random.fold_in(jax.random.fold_in(splits[6], part), 71), part),
        "neighbours": draw_neighbours(jax.random.fold_in(jax.random.fold_in(splits[6], part), 71), part),
        "weight_one": noise(splits[3], (27, C, C), (27 * C) ** -0.5, 0.109375),
        "weight_two": noise(splits[4], (27, C, C), (27 * C) ** -0.5, 0.109375),
        "cotangent": noise(own_keys[5], (BRICKS, VOX, C), 2.0, 12.0, ((0, 8),)),
    }


DIRECTIONS = ((-1, -1), (-1, 0), (-1, 1), (0, -1), (0, 1), (1, -1), (1, 0), (1, 1))

def rim_slices(step_value, length):
    if step_value < 0:
        return (slice(length - 1, length), slice(0, 1))
    if step_value > 0:
        return (slice(0, 1), slice(length + 1, length + 2))
    return (slice(0, length), slice(1, length + 1))

def assemble(cube_view, sources, source_index):
    length = cube_view.shape[1]
    padded = jnp.pad(cube_view, ((0, 0), (1, 1), (1, 1), (1, 1), (0, 0)))
    for column, (step_x, step_y) in enumerate(DIRECTIONS):
        source_x, target_x = rim_slices(step_x, length)
        source_y, target_y = rim_slices(step_y, length)
        rim_cells = sources[:, source_x, source_y]
        fetched = jnp.take(rim_cells, source_index[:, column].astype(jnp.int32), axis=0)
        padded = padded.at[:, target_x, target_y, 1:length + 1].set(fetched)
    return padded

def window_stack(padded, shift_x, flipped):
    length = padded.shape[1] - 2
    channels = padded.shape[-1]
    pieces = []
    for shift_y in range(3):
        for shift_z in range(3):
            if flipped:
                corner_x, corner_y, corner_z = (2 - shift_x, 2 - shift_y, 2 - shift_z)
            else:
                corner_x, corner_y, corner_z = (shift_x, shift_y, shift_z)
            cells = padded[:, corner_x:corner_x + length, corner_y:corner_y + length, corner_z:corner_z + length]
            pieces.append(cells.reshape(-1, channels))
    return jnp.concatenate(pieces, axis=1)

def convolve(padded, weight, flipped):
    channels = padded.shape[-1]
    summed = None
    for shift_x in range(3):
        stacked = window_stack(padded, shift_x, flipped)
        weight_block = weight[9 * shift_x:9 * shift_x + 9]
        if flipped:
            weight_block = jnp.swapaxes(weight_block, 1, 2)
        partial_sum = jnp.dot(stacked, weight_block.reshape(9 * channels, channels), preferred_element_type=jnp.float32)
        summed = partial_sum if summed is None else summed + partial_sum
    return summed

def weight_grad(padded, grads):
    channels = padded.shape[-1]
    blocks = []
    for shift_x in range(3):
        stacked = window_stack(padded, shift_x, False)
        product = lax.dot_general(stacked, grads, (((0,), (0,)), ((), ())), preferred_element_type=jnp.float32)
        blocks.append(product.reshape(9, channels, channels))
    return jnp.concatenate(blocks, axis=0)

def silu_slope(values):
    sigmoid_value = jax.nn.sigmoid(values)
    return sigmoid_value * (1.0 + values * (1.0 - sigmoid_value))

def reference(feats, mask, neighbours, weight_one, weight_two, cotangent):
    bricks, voxels, channels = feats.shape
    occupied = mask.reshape(-1, 1).astype(jnp.float32)
    source_index = jnp.where(neighbours >= 0, neighbours, bricks).astype(jnp.int32)
    blank_brick = jnp.zeros((1, EDGE, EDGE, EDGE, channels), jnp.bfloat16)

    def extend(flat_field):
        cube_view = flat_field.reshape(bricks, EDGE, EDGE, EDGE, channels)
        return assemble(cube_view, jnp.concatenate([cube_view, blank_brick], axis=0), source_index)
    inputs = feats * mask[:, :, None].astype(jnp.bfloat16)
    padded_in = extend(inputs)
    first_pre = convolve(padded_in, weight_one, False)
    hidden = (occupied * jax.nn.silu(first_pre)).astype(jnp.bfloat16)
    padded_hidden = extend(hidden)
    second_pre = convolve(padded_hidden, weight_two, False)
    output = (occupied * jax.nn.silu(second_pre)).astype(jnp.bfloat16)
    grad_second = (cotangent.reshape(-1, channels).astype(jnp.float32) * occupied * silu_slope(second_pre)).astype(jnp.bfloat16)
    back_second = convolve(extend(grad_second), weight_two, True)
    grad_first = (occupied * silu_slope(first_pre) * back_second).astype(jnp.bfloat16)
    grad_input = (occupied * convolve(extend(grad_first), weight_one, True)).astype(jnp.bfloat16)
    grad_scale = 1.0 / math.sqrt(voxels * BR_DEV)
    grad_w2 = weight_grad(padded_hidden, grad_second) * grad_scale
    grad_w1 = weight_grad(padded_in, grad_first) * grad_scale
    return (output.reshape(bricks, voxels, channels), grad_input.reshape(bricks, voxels, channels), grad_w1, grad_w2)
```

```python
import functools
import math

import jax
import jax.numpy as jnp
from jax import lax
from jax.experimental import pallas as pl
from jax.experimental.pallas import tpu as pltpu
from jax.sharding import PartitionSpec as P

EDGE = 8
TILE = 1
WIDE = 8
SLAB = EDGE * EDGE
C = 128
TAPS = 9 * C
VMEM_LIMIT = 56 * 1024 * 1024

DIRECTIONS = ((-1, -1), (-1, 0), (-1, 1), (0, -1), (0, 1), (1, -1), (1, 0), (1, 1))


def picked(source, index, first, rows):
    found = source[jnp.maximum(index, 0), first : first + rows, :].astype(jnp.float32)
    return jnp.where(index >= 0, found, 0.0)


def slab_tiles(centre, top, bottom):
    cells = jnp.concatenate([top[8:16], centre, bottom[0:8]], axis=0).reshape(EDGE + 2, EDGE, C)
    place = lax.broadcasted_iota(jnp.int32, cells.shape, 1)
    below = jnp.where(place == 0, 0.0, pltpu.roll(cells, 1, 1))
    above = jnp.where(place == EDGE - 1, 0.0, pltpu.roll(cells, EDGE - 1, 1))
    even, odd = [], []
    for shifted in (below, cells, above):
        even.append(shifted.reshape((EDGE + 2) * EDGE, C).astype(jnp.bfloat16))
        odd.append(shifted[1 : EDGE + 1].reshape(SLAB, C).astype(jnp.bfloat16))
    return [e[0:SLAB] for e in even] + odd + [e[16 : 16 + SLAB] for e in even]


def build_stack(table, field, left, right, stack):
    bricks = field.shape[0]

    @pl.loop(0, bricks)
    def _(g):
        for a in range(EDGE + 2):
            if a == 0:
                source, first, near = left, 0, (table[g, 1], table[g, 0], table[g, 2])
            elif a == EDGE + 1:
                source, first, near = right, 0, (table[g, 6], table[g, 5], table[g, 7])
            else:
                source, first, near = field, (a - 1) * SLAB, (g, table[g, 3], table[g, 4])
            if source is field:
                centre = field[g, first : first + SLAB, :].astype(jnp.float32)
            else:
                centre = picked(source, near[0], first, SLAB)
            top = picked(source, near[1], first + SLAB - 16, 16)
            bottom = picked(source, near[2], first, 16)
            for t, tile in enumerate(slab_tiles(centre, top, bottom)):
                stack[g, a, :, t * C : (t + 1) * C] = tile


def pair_product(stack, weights, pair):
    bricks = stack.shape[0]
    rows = [stack[:, 2 * pair + j].reshape(bricks * SLAB, TAPS) for j in range(4)]
    return jnp.dot(
        jnp.concatenate(rows, axis=1), weights[...], preferred_element_type=jnp.float32
    )


def spread(values, bricks):
    return values.reshape(bricks, SLAB, C)


def slope_of(values):
    s = jax.nn.sigmoid(values)
    return s * (1.0 + values * (1.0 - s))


def put(result, low, high, half, values):
    result[:, half * SLAB : (half + 1) * SLAB, :] = values
    if half == 0 and low is not None:

        @pl.when(pl.program_id(0) == 0)
        def _():
            low[...] = values

    if half == 1 and high is not None:

        @pl.when(pl.program_id(0) == EDGE // 2 - 1)
        def _():
            high[...] = values


def first_kernel(table, field, left, right, weights, mask, pre, hidden, low, high, stack):
    pair = pl.program_id(0)
    bricks = field.shape[0]

    @pl.when(pair == 0)
    def _():
        build_stack(table, field, left, right, stack)

    both = pair_product(stack, weights, pair)
    pre[0] = both
    for half in range(2):
        values = both[:, half * C : (half + 1) * C]
        occupied = mask[:, half * SLAB : (half + 1) * SLAB, :].astype(jnp.float32)
        active = spread(values * jax.nn.sigmoid(values), bricks)
        put(hidden, low, high, half, (occupied * active).astype(jnp.bfloat16))


def second_kernel(
    table, field, left, right, weights, mask, cotangent, output, grad, low, high, stack
):
    pair = pl.program_id(0)
    bricks = field.shape[0]

    @pl.when(pair == 0)
    def _():
        build_stack(table, field, left, right, stack)

    both = pair_product(stack, weights, pair)
    for half in range(2):
        values = both[:, half * C : (half + 1) * C]
        rows = slice(half * SLAB, (half + 1) * SLAB)
        occupied = mask[:, rows, :].astype(jnp.float32)
        s = jax.nn.sigmoid(values)
        output[:, rows, :] = (occupied * spread(values * s, bricks)).astype(jnp.bfloat16)
        slope = spread(s * (1.0 + values * (1.0 - s)), bricks)
        received = cotangent[:, rows, :].astype(jnp.float32)
        put(grad, low, high, half, (received * occupied * slope).astype(jnp.bfloat16))


def third_kernel(table, field, left, right, weights, mask, pre, grad, low, high, stack):
    pair = pl.program_id(0)
    bricks = field.shape[0]

    @pl.when(pair == 0)
    def _():
        build_stack(table, field, left, right, stack)

    both = pair_product(stack, weights, pair)
    for half in range(2):
        columns = slice(half * C, (half + 1) * C)
        occupied = mask[:, half * SLAB : (half + 1) * SLAB, :].astype(jnp.float32)
        slope = slope_of(pre[0, :, columns])
        product = spread(slope * both[:, columns], bricks)
        put(grad, low, high, half, (occupied * product).astype(jnp.bfloat16))


def fourth_kernel(table, field, left, right, weights, mask, grad, stack):
    pair = pl.program_id(0)
    bricks = field.shape[0]

    @pl.when(pair == 0)
    def _():
        build_stack(table, field, left, right, stack)

    both = pair_product(stack, weights, pair)
    for half in range(2):
        occupied = mask[:, half * SLAB : (half + 1) * SLAB, :].astype(jnp.float32)
        values = spread(both[:, half * C : (half + 1) * C], bricks)
        put(grad, None, None, half, (occupied * values).astype(jnp.bfloat16))


def weight_kernel(scale, table, field, left, right, grads, result, stack, turned, total):
    bricks = field.shape[0]
    build_stack(table, field, left, right, stack)
    for a in range(EDGE):
        slab = grads[:, a * SLAB : (a + 1) * SLAB, :].reshape(bricks * SLAB, C)
        turned[a] = slab.astype(jnp.float32).T.astype(jnp.bfloat16)
    total[...] = jnp.zeros_like(total)

    def add(a, first, last):
        lhs = [turned[a - k1] for k1 in range(first, last)]
        lhs = lhs[0] if len(lhs) == 1 else jnp.concatenate(lhs, axis=0)
        product = jnp.dot(
            lhs,
            stack[:, a].reshape(bricks * SLAB, TAPS),
            preferred_element_type=jnp.float32,
        )
        total[first * C : last * C, :] += product

    add(0, 0, 1)
    add(1, 0, 2)

    @pl.loop(2, EDGE)
    def _(a):
        add(a, 0, 3)

    add(EDGE, 1, 3)
    add(EDGE + 1, 2, 3)
    for k1 in range(3):
        for t in range(9):
            block = total[k1 * C : (k1 + 1) * C, t * C : (t + 1) * C]
            result[9 * k1 + t] = (block.T * scale).astype(jnp.bfloat16)


def cost(flops, arrays):
    return pl.CostEstimate(
        flops=flops,
        bytes_accessed=sum(math.prod(a.shape) * a.dtype.itemsize for a in arrays),
        transcendentals=0,
    )


def whole(array):
    return pl.BlockSpec(array.shape, lambda i, n=len(array.shape): (0,) * n)


def run_conv(kernel, table, field, left, right, weights, by_rows, by_pair, outs):
    bricks, voxels, _ = field.shape
    pairs = EDGE // 2
    rows_spec = pl.BlockSpec((bricks, 2 * SLAB, C), lambda i: (0, i, 0))
    pair_spec = pl.BlockSpec((1, bricks * SLAB, 2 * C), lambda i: (i, 0, 0))
    edge_spec = pl.BlockSpec((bricks, SLAB, C), lambda i: (0, 0, 0))
    kinds = {
        "rows": (rows_spec, jax.ShapeDtypeStruct((bricks, voxels, C), jnp.bfloat16)),
        "pair": (pair_spec, jax.ShapeDtypeStruct((pairs, bricks * SLAB, 2 * C), jnp.float32)),
        "edge": (edge_spec, jax.ShapeDtypeStruct((bricks, SLAB, C), jnp.bfloat16)),
    }
    operands = [field, left, right, weights, *by_rows, *by_pair]
    return pl.pallas_call(
        kernel,
        grid=(pairs,),
        in_specs=[
            pl.BlockSpec(memory_space=pltpu.SMEM),
            *[whole(a) for a in (field, left, right, weights)],
            *[rows_spec for _ in by_rows],
            *[pair_spec for _ in by_pair],
        ],
        out_specs=[kinds[k][0] for k in outs],
        out_shape=[kinds[k][1] for k in outs],
        scratch_shapes=[pltpu.VMEM((bricks, EDGE + 2, SLAB, TAPS), jnp.bfloat16)],
        compiler_params=pltpu.CompilerParams(
            dimension_semantics=("arbitrary",), vmem_limit_bytes=VMEM_LIMIT
        ),
        cost_estimate=cost(
            2 * 36 * bricks * voxels * C * C, operands + [kinds[k][1] for k in outs]
        ),
    )(table, *operands)


def run_weight(table, field, left, right, grads, scale):
    bricks, voxels, _ = field.shape
    out = jax.ShapeDtypeStruct((27, C, C), jnp.bfloat16)
    return pl.pallas_call(
        functools.partial(weight_kernel, scale),
        in_specs=[
            pl.BlockSpec(memory_space=pltpu.SMEM),
            *[pl.BlockSpec(memory_space=pltpu.VMEM)] * 4,
        ],
        out_specs=pl.BlockSpec(memory_space=pltpu.VMEM),
        out_shape=out,
        scratch_shapes=[
            pltpu.VMEM((bricks, EDGE + 2, SLAB, TAPS), jnp.bfloat16),
            pltpu.VMEM((EDGE, C, bricks * SLAB), jnp.bfloat16),
            pltpu.VMEM((3 * C, TAPS), jnp.float32),
        ],
        compiler_params=pltpu.CompilerParams(vmem_limit_bytes=VMEM_LIMIT),
        cost_estimate=cost(2 * 27 * bricks * voxels * C * C, [field, left, right, grads, out]),
    )(table, field, left, right, grads)


def pair_weights(weight):
    flat = weight.reshape(3 * TAPS, C)
    blank = jnp.zeros((TAPS, C), weight.dtype)
    return jnp.concatenate(
        [jnp.concatenate([flat, blank], axis=0), jnp.concatenate([blank, flat], axis=0)], axis=1
    )


def turned_weights(weight):
    return pair_weights(jnp.swapaxes(weight[::-1], 1, 2))


def beside(low, high):
    count = lax.axis_size("space")
    left = lax.ppermute(high, "space", [(i, i + 1) for i in range(count - 1)])
    right = lax.ppermute(low, "space", [(i + 1, i) for i in range(count - 1)])
    return left, right


def column_body(feats, mask, neighbours, weight_one, weight_two, cotangent):
    bricks, voxels, channels = feats.shape
    my_index = lax.axis_index("space")
    steps = jnp.array([s for s, _ in DIRECTIONS], jnp.int32)
    local = neighbours - (my_index + steps)[None, :] * (TILE * WIDE)
    inside = (local >= 0) & (local < bricks) & (neighbours >= 0)
    strays = jnp.sum(((neighbours >= 0) & ~inside).astype(jnp.float32))
    strays = lax.psum(strays, ("scene", "space"))
    table = jnp.where(inside, local, -1)
    spread_mask = jnp.broadcast_to(mask.astype(jnp.bfloat16)[:, :, None], feats.shape)
    scale = 1.0 / math.sqrt(voxels * bricks)

    inputs = feats * spread_mask
    in_left, in_right = beside(inputs[:, :SLAB], inputs[:, voxels - SLAB :])
    pre, hidden, low, high = run_conv(
        first_kernel, table, inputs, in_left, in_right, pair_weights(weight_one),
        [spread_mask], [], ("pair", "rows", "edge", "edge"),
    )
    h_left, h_right = beside(low, high)
    output, grad_second, low, high = run_conv(
        second_kernel, table, hidden, h_left, h_right, pair_weights(weight_two),
        [spread_mask, cotangent], [], ("rows", "rows", "edge", "edge"),
    )
    s_left, s_right = beside(low, high)
    term_two = run_weight(table, hidden, h_left, h_right, grad_second, scale)
    grad_w2 = lax.psum(term_two, "space")
    grad_first, low, high = run_conv(
        third_kernel, table, grad_second, s_left, s_right, turned_weights(weight_two),
        [spread_mask], [pre], ("rows", "edge", "edge"),
    )
    f_left, f_right = beside(low, high)
    term_one = run_weight(table, inputs, in_left, in_right, grad_first, scale)
    grad_w1 = lax.psum(term_one, "space")
    (grad_input,) = run_conv(
        fourth_kernel, table, grad_first, f_left, f_right, turned_weights(weight_one),
        [spread_mask], [], ("rows",),
    )
    return strays, (
        output,
        grad_input,
        grad_w1.astype(jnp.float32),
        grad_w2.astype(jnp.float32),
    )


def body(*arguments):
    strays, results = column_body(*arguments)

    def again(state):
        return jnp.zeros_like(state[0]), general_body(*arguments)

    return lax.while_loop(lambda state: state[0] > 0.5, again, (strays, results))[1]


def padded_2(cells, sides, width):
    for axis, dim in sides:
        count = lax.axis_size(axis)
        ends = count - 1
        head = lax.slice_in_dim(cells, 0, width, axis=dim)
        tail = lax.slice_in_dim(cells, cells.shape[dim] - width, cells.shape[dim], axis=dim)
        cells = jnp.concatenate(
            [
                lax.ppermute(tail, axis, [(i, (i + 1) % count) for i in range(ends)]),
                cells,
                lax.ppermute(head, axis, [((i + 1) % count, i) for i in range(ends)]),
            ],
            axis=dim,
        )
    return cells


def rim_slices(step_value, length):
    if step_value < 0:
        return (slice(length - 1, length), slice(0, 1))
    if step_value > 0:
        return (slice(0, 1), slice(length + 1, length + 2))
    return (slice(0, length), slice(1, length + 1))


def assemble(cube_view, sources, source_index):
    length = cube_view.shape[1]
    padded = jnp.pad(cube_view, ((0, 0), (1, 1), (1, 1), (1, 1), (0, 0)))
    for column, (step_x, step_y) in enumerate(DIRECTIONS):
        source_x, target_x = rim_slices(step_x, length)
        source_y, target_y = rim_slices(step_y, length)
        rim_cells = sources[:, source_x, source_y]
        fetched = jnp.take(rim_cells, source_index[:, column], axis=0)
        padded = padded.at[:, target_x, target_y, 1 : length + 1].set(fetched)
    return padded


def window_stack(padded, shift_x, flipped):
    length = padded.shape[1] - 2
    channels = padded.shape[-1]
    pieces = []
    for shift_y in range(3):
        for shift_z in range(3):
            if flipped:
                corner_x, corner_y, corner_z = (2 - shift_x, 2 - shift_y, 2 - shift_z)
            else:
                corner_x, corner_y, corner_z = (shift_x, shift_y, shift_z)
            cells = padded[
                :,
                corner_x : corner_x + length,
                corner_y : corner_y + length,
                corner_z : corner_z + length,
            ]
            pieces.append(cells.reshape(-1, channels))
    return jnp.concatenate(pieces, axis=1)


def convolve(padded, weight, flipped):
    channels = padded.shape[-1]
    summed = None
    for shift_x in range(3):
        stacked = window_stack(padded, shift_x, flipped)
        weight_block = weight[9 * shift_x : 9 * shift_x + 9]
        if flipped:
            weight_block = jnp.swapaxes(weight_block, 1, 2)
        partial_sum = jnp.dot(
            stacked,
            weight_block.reshape(9 * channels, channels),
            preferred_element_type=jnp.float32,
        )
        summed = partial_sum if summed is None else summed + partial_sum
    return summed


def weight_grad(padded, grads):
    channels = padded.shape[-1]
    blocks = []
    for shift_x in range(3):
        stacked = window_stack(padded, shift_x, False)
        product = lax.dot_general(
            stacked, grads, (((0,), (0,)), ((), ())), preferred_element_type=jnp.float32
        )
        blocks.append(product.reshape(9, channels, channels))
    return jnp.concatenate(blocks, axis=0)


def silu_slope(values):
    sigmoid_value = jax.nn.sigmoid(values)
    return sigmoid_value * (1.0 + values * (1.0 - sigmoid_value))


def general_body(feats, mask, neighbours, weight_one, weight_two, cotangent):
    bricks, voxels, channels = feats.shape
    my_index = lax.axis_index("space")
    first_brick = (my_index * TILE - 1) * WIDE
    source_index = jnp.where(neighbours >= 0, neighbours - first_brick, (TILE + 2) * WIDE)
    occupied = mask.reshape(-1, 1).astype(jnp.float32)
    blank_brick = jnp.zeros((1, EDGE, EDGE, EDGE, channels), jnp.bfloat16)

    def join_sources(cube_view, left_side, right_side):
        sources = jnp.concatenate([left_side, cube_view, right_side, blank_brick], axis=0)
        return assemble(cube_view, sources, source_index)

    def extend_bricks(flat_field, received):
        cube_view = flat_field.reshape(bricks, EDGE, EDGE, EDGE, channels)
        left_side = received[0].reshape(WIDE, EDGE, EDGE, EDGE, channels)
        right_side = received[TILE + 1].reshape(WIDE, EDGE, EDGE, EDGE, channels)
        return join_sources(cube_view, left_side, right_side)

    def as_tiles(flat_field):
        return flat_field.reshape(TILE, WIDE, voxels, channels)

    inputs = feats * mask[:, :, None].astype(jnp.bfloat16)
    padded_in = extend_bricks(inputs, padded_2(as_tiles(inputs), (("space", 0),), 1))
    first_pre = convolve(padded_in, weight_one, False)
    hidden = (
        (occupied * jax.nn.silu(first_pre)).astype(jnp.bfloat16).reshape(bricks, voxels, channels)
    )
    padded_hidden = extend_bricks(hidden, padded_2(as_tiles(hidden), (("space", 0),), 1))
    second_pre = convolve(padded_hidden, weight_two, False)
    output = (occupied * jax.nn.silu(second_pre)).astype(jnp.bfloat16)
    grad_second = (
        cotangent.reshape(-1, channels).astype(jnp.float32) * occupied * silu_slope(second_pre)
    ).astype(jnp.bfloat16)
    grad_second_view = grad_second.reshape(bricks, voxels, channels)
    padded_second = extend_bricks(
        grad_second_view, padded_2(as_tiles(grad_second_view), (("space", 0),), 1)
    )
    back_second = convolve(padded_second, weight_two, True)
    grad_first = (occupied * silu_slope(first_pre) * back_second).astype(jnp.bfloat16)
    grad_scale = 1.0 / math.sqrt(voxels * bricks)
    grad_w2 = weight_grad(padded_hidden, grad_second) * grad_scale
    grad_w2 = lax.psum(grad_w2.astype(jnp.bfloat16), "space").astype(jnp.float32)
    grad_first_view = grad_first.reshape(bricks, voxels, channels)
    padded_first = extend_bricks(
        grad_first_view, padded_2(as_tiles(grad_first_view), (("space", 0),), 1)
    )
    grad_input = (occupied * convolve(padded_first, weight_one, True)).astype(jnp.bfloat16)
    grad_w1 = weight_grad(padded_in, grad_first) * grad_scale
    grad_w1 = lax.psum(grad_w1.astype(jnp.bfloat16), "space").astype(jnp.float32)
    return (
        output.reshape(bricks, voxels, channels),
        grad_input.reshape(bricks, voxels, channels),
        grad_w1,
        grad_w2,
    )


def solution(mesh):
    in_specs = (
        P(("scene", "space"), None, None),
        P(("scene", "space"), None),
        P(("scene", "space"), None),
        P(),
        P(),
        P(("scene", "space"), None, None),
    )
    out_specs = (
        P(("scene", "space"), None, None),
        P(("scene", "space"), None, None),
        P("scene", None, None),
        P("scene", None, None),
    )
    return jax.shard_map(body, mesh=mesh, in_specs=in_specs, out_specs=out_specs, check_vma=False)
```

```python
import functools
import math

import jax
import jax.numpy as jnp
from jax import lax
from jax.experimental import pallas as pl
from jax.experimental.pallas import tpu as pltpu
from jax.sharding import PartitionSpec as P

EDGE = 8
TILE = 1
WIDE = 8
SLAB = EDGE * EDGE
C = 128
TAPS = 9 * C
VMEM_LIMIT = 56 * 1024 * 1024

DIRECTIONS = ((-1, -1), (-1, 0), (-1, 1), (0, -1), (0, 1), (1, -1), (1, 0), (1, 1))


def picked(source, index, first, rows):
    found = source[jnp.maximum(index, 0), first : first + rows, :].astype(jnp.float32)
    return jnp.where(index >= 0, found, 0.0)


def slab_tiles(centre, top, bottom):
    cells = jnp.concatenate([top[8:16], centre, bottom[0:8]], axis=0).reshape(EDGE + 2, EDGE, C)
    place = lax.broadcasted_iota(jnp.int32, cells.shape, 1)
    below = jnp.where(place == 0, 0.0, pltpu.roll(cells, 1, 1))
    above = jnp.where(place == EDGE - 1, 0.0, pltpu.roll(cells, EDGE - 1, 1))
    even, odd = [], []
    for shifted in (below, cells, above):
        even.append(shifted.reshape((EDGE + 2) * EDGE, C).astype(jnp.bfloat16))
        odd.append(shifted[1 : EDGE + 1].reshape(SLAB, C).astype(jnp.bfloat16))
    return [e[0:SLAB] for e in even] + odd + [e[16 : 16 + SLAB] for e in even]


def build_stack(table, field, left, right, stack):
    bricks = field.shape[0]

    @pl.loop(0, bricks)
    def _(g):
        for a in range(EDGE + 2):
            if a == 0:
                source, first, near = left, 0, (table[g, 1], table[g, 0], table[g, 2])
            elif a == EDGE + 1:
                source, first, near = right, 0, (table[g, 6], table[g, 5], table[g, 7])
            else:
                source, first, near = field, (a - 1) * SLAB, (g, table[g, 3], table[g, 4])
            if source is field:
                centre = field[g, first : first + SLAB, :].astype(jnp.float32)
            else:
                centre = picked(source, near[0], first, SLAB)
            top = picked(source, near[1], first + SLAB - 16, 16)
            bottom = picked(source, near[2], first, 16)
            for t, tile in enumerate(slab_tiles(centre, top, bottom)):
                stack[g, a, :, t * C : (t + 1) * C] = tile


def fill_weights(weights, turned, filled):
    for half in range(2):
        columns = slice(half * C, (half + 1) * C)
        for j in range(4):
            k1 = j - half
            for t in range(9):
                first = j * TAPS + t * C
                if not 0 <= k1 <= 2:
                    block = jnp.zeros((C, C), jnp.bfloat16)
                elif turned:
                    block = weights[26 - 9 * k1 - t].astype(jnp.float32).T.astype(jnp.bfloat16)
                else:
                    block = weights[9 * k1 + t]
                filled[first : first + C, columns] = block


def prepare(turned, table, field, left, right, weights, stack, filled):
    @pl.when(pl.program_id(0) == 0)
    def _():
        fill_weights(weights, turned, filled)
        build_stack(table, field, left, right, stack)


def pair_product(stack, weights, pair):
    bricks = stack.shape[0]
    rows = [stack[:, 2 * pair + j].reshape(bricks * SLAB, TAPS) for j in range(4)]
    return jnp.dot(
        jnp.concatenate(rows, axis=1), weights[...], preferred_element_type=jnp.float32
    )


def spread(values, bricks):
    return values.reshape(bricks, SLAB, C)


def slope_of(values):
    s = jax.nn.sigmoid(values)
    return s * (1.0 + values * (1.0 - s))


def put(result, low, high, half, values):
    result[:, half * SLAB : (half + 1) * SLAB, :] = values
    if half == 0 and low is not None:

        @pl.when(pl.program_id(0) == 0)
        def _():
            low[...] = values

    if half == 1 and high is not None:

        @pl.when(pl.program_id(0) == EDGE // 2 - 1)
        def _():
            high[...] = values


def first_kernel(table, field, left, right, weights, mask, pre, hidden, low, high, stack, filled):
    pair = pl.program_id(0)
    bricks = field.shape[0]

    prepare(False, table, field, left, right, weights, stack, filled)
    both = pair_product(stack, filled, pair)
    pre[0] = both
    for half in range(2):
        values = both[:, half * C : (half + 1) * C]
        occupied = mask[:, half * SLAB : (half + 1) * SLAB, :].astype(jnp.float32)
        active = spread(values * jax.nn.sigmoid(values), bricks)
        put(hidden, low, high, half, (occupied * active).astype(jnp.bfloat16))


def second_kernel(
    table, field, left, right, weights, mask, cotangent, output, grad, low, high, stack, filled
):
    pair = pl.program_id(0)
    bricks = field.shape[0]

    prepare(False, table, field, left, right, weights, stack, filled)
    both = pair_product(stack, filled, pair)
    for half in range(2):
        values = both[:, half * C : (half + 1) * C]
        rows = slice(half * SLAB, (half + 1) * SLAB)
        occupied = mask[:, rows, :].astype(jnp.float32)
        s = jax.nn.sigmoid(values)
        output[:, rows, :] = (occupied * spread(values * s, bricks)).astype(jnp.bfloat16)
        slope = spread(s * (1.0 + values * (1.0 - s)), bricks)
        received = cotangent[:, rows, :].astype(jnp.float32)
        put(grad, low, high, half, (received * occupied * slope).astype(jnp.bfloat16))


def third_kernel(table, field, left, right, weights, mask, pre, grad, low, high, stack, filled):
    pair = pl.program_id(0)
    bricks = field.shape[0]

    prepare(True, table, field, left, right, weights, stack, filled)
    both = pair_product(stack, filled, pair)
    for half in range(2):
        columns = slice(half * C, (half + 1) * C)
        occupied = mask[:, half * SLAB : (half + 1) * SLAB, :].astype(jnp.float32)
        slope = slope_of(pre[0, :, columns])
        product = spread(slope * both[:, columns], bricks)
        put(grad, low, high, half, (occupied * product).astype(jnp.bfloat16))


def fourth_kernel(table, field, left, right, weights, mask, grad, stack, filled):
    pair = pl.program_id(0)
    bricks = field.shape[0]

    prepare(True, table, field, left, right, weights, stack, filled)
    both = pair_product(stack, filled, pair)
    for half in range(2):
        occupied = mask[:, half * SLAB : (half + 1) * SLAB, :].astype(jnp.float32)
        values = spread(both[:, half * C : (half + 1) * C], bricks)
        put(grad, None, None, half, (occupied * values).astype(jnp.bfloat16))


def weight_kernel(scale, table, mark, field, left, right, grads, result, stack, turned, total):
    bricks = field.shape[0]
    build_stack(table, field, left, right, stack)
    for a in range(EDGE):
        slab = grads[:, a * SLAB : (a + 1) * SLAB, :].reshape(bricks * SLAB, C)
        turned[a] = slab.astype(jnp.float32).T.astype(jnp.bfloat16)
    total[...] = jnp.zeros_like(total)

    def add(a, first, last):
        lhs = [turned[a - k1] for k1 in range(first, last)]
        lhs = lhs[0] if len(lhs) == 1 else jnp.concatenate(lhs, axis=0)
        product = jnp.dot(
            lhs,
            stack[:, a].reshape(bricks * SLAB, TAPS),
            preferred_element_type=jnp.float32,
        )
        total[first * C : last * C, :] += product

    add(0, 0, 1)
    add(1, 0, 2)

    @pl.loop(2, EDGE)
    def _(a):
        add(a, 0, 3)

    add(EDGE, 1, 3)
    add(EDGE + 1, 2, 3)
    for k1 in range(3):
        for t in range(9):
            block = total[k1 * C : (k1 + 1) * C, t * C : (t + 1) * C]
            result[9 * k1 + t] = (block.T * scale).astype(jnp.bfloat16)
    result[27] = jnp.full((C, C), mark[0], jnp.float32).astype(jnp.bfloat16)


def cost(flops, arrays):
    return pl.CostEstimate(
        flops=flops,
        bytes_accessed=sum(math.prod(a.shape) * a.dtype.itemsize for a in arrays),
        transcendentals=0,
    )


def whole(array):
    return pl.BlockSpec(array.shape, lambda i, n=len(array.shape): (0,) * n)


def run_conv(kernel, table, field, left, right, weights, by_rows, by_pair, outs):
    bricks, voxels, _ = field.shape
    pairs = EDGE // 2
    rows_spec = pl.BlockSpec((bricks, 2 * SLAB, C), lambda i: (0, i, 0))
    pair_spec = pl.BlockSpec((1, bricks * SLAB, 2 * C), lambda i: (i, 0, 0))
    edge_spec = pl.BlockSpec((bricks, SLAB, C), lambda i: (0, 0, 0))
    kinds = {
        "rows": (rows_spec, jax.ShapeDtypeStruct((bricks, voxels, C), jnp.bfloat16)),
        "pair": (pair_spec, jax.ShapeDtypeStruct((pairs, bricks * SLAB, 2 * C), jnp.float32)),
        "edge": (edge_spec, jax.ShapeDtypeStruct((bricks, SLAB, C), jnp.bfloat16)),
    }
    operands = [field, left, right, weights, *by_rows, *by_pair]
    return pl.pallas_call(
        kernel,
        grid=(pairs,),
        in_specs=[
            pl.BlockSpec(memory_space=pltpu.SMEM),
            *[whole(a) for a in (field, left, right, weights)],
            *[rows_spec for _ in by_rows],
            *[pair_spec for _ in by_pair],
        ],
        out_specs=[kinds[k][0] for k in outs],
        out_shape=[kinds[k][1] for k in outs],
        scratch_shapes=[
            pltpu.VMEM((bricks, EDGE + 2, SLAB, TAPS), jnp.bfloat16),
            pltpu.VMEM((4 * TAPS, 2 * C), jnp.bfloat16),
        ],
        compiler_params=pltpu.CompilerParams(
            dimension_semantics=("arbitrary",), vmem_limit_bytes=VMEM_LIMIT
        ),
        cost_estimate=cost(
            2 * 36 * bricks * voxels * C * C, operands + [kinds[k][1] for k in outs]
        ),
    )(table, *operands)


def run_weight(table, mark, field, left, right, grads, scale):
    bricks, voxels, _ = field.shape
    out = jax.ShapeDtypeStruct((28, C, C), jnp.bfloat16)
    return pl.pallas_call(
        functools.partial(weight_kernel, scale),
        in_specs=[
            *[pl.BlockSpec(memory_space=pltpu.SMEM)] * 2,
            *[pl.BlockSpec(memory_space=pltpu.VMEM)] * 4,
        ],
        out_specs=pl.BlockSpec(memory_space=pltpu.VMEM),
        out_shape=out,
        scratch_shapes=[
            pltpu.VMEM((bricks, EDGE + 2, SLAB, TAPS), jnp.bfloat16),
            pltpu.VMEM((EDGE, C, bricks * SLAB), jnp.bfloat16),
            pltpu.VMEM((3 * C, TAPS), jnp.float32),
        ],
        compiler_params=pltpu.CompilerParams(vmem_limit_bytes=VMEM_LIMIT),
        cost_estimate=cost(2 * 27 * bricks * voxels * C * C, [field, left, right, grads, out]),
    )(table, mark, field, left, right, grads)


def beside(low, high):
    count = lax.axis_size("space")
    left = lax.ppermute(high, "space", [(i, i + 1) for i in range(count - 1)])
    right = lax.ppermute(low, "space", [(i + 1, i) for i in range(count - 1)])
    return left, right


def summed(term, turn):
    count = lax.axis_size("space")
    order = [*range(0, count, 2), *range(count - 1, 0, -2)]
    order = order[turn:] + order[:turn]
    return lax.psum(term, "space", axis_index_groups=[order]).astype(jnp.float32)


def column_body(feats, mask, neighbours, weight_one, weight_two, cotangent):
    bricks, voxels, channels = feats.shape
    my_index = lax.axis_index("space")
    steps = jnp.array([s for s, _ in DIRECTIONS], jnp.int32)
    local = neighbours - (my_index + steps)[None, :] * (TILE * WIDE)
    inside = (local >= 0) & (local < bricks) & (neighbours >= 0)
    strays = jnp.any((neighbours >= 0) & ~inside).astype(jnp.float32).reshape(1)
    table = jnp.where(inside, local, -1)
    spread_mask = jnp.broadcast_to(mask.astype(jnp.bfloat16)[:, :, None], feats.shape)
    scale = 1.0 / math.sqrt(voxels * bricks)

    inputs = feats * spread_mask
    in_left, in_right = beside(inputs[:, :SLAB], inputs[:, voxels - SLAB :])
    pre, hidden, low, high = run_conv(
        first_kernel, table, inputs, in_left, in_right, weight_one,
        [spread_mask], [], ("pair", "rows", "edge", "edge"),
    )
    h_left, h_right = beside(low, high)
    output, grad_second, low, high = run_conv(
        second_kernel, table, hidden, h_left, h_right, weight_two,
        [spread_mask, cotangent], [], ("rows", "rows", "edge", "edge"),
    )
    s_left, s_right = beside(low, high)
    term_two = run_weight(table, strays, hidden, h_left, h_right, grad_second, scale)
    grad_w2 = summed(term_two, 0)
    grad_first, low, high = run_conv(
        third_kernel, table, grad_second, s_left, s_right, weight_two,
        [spread_mask], [pre], ("rows", "edge", "edge"),
    )
    term_one = run_weight(table, strays, inputs, in_left, in_right, grad_first, scale)
    term_one, low, high = lax.optimization_barrier((term_one, low, high))
    grad_w1 = summed(term_one, 1)
    f_left, f_right = beside(low, high)
    (grad_input,) = run_conv(
        fourth_kernel, table, grad_first, f_left, f_right, weight_one,
        [spread_mask], [], ("rows",),
    )
    return grad_w2[27, 0, 0], (output, grad_input, grad_w1[:27], grad_w2[:27])


def body(*arguments):
    strays, results = column_body(*arguments)

    def again(state):
        return jnp.zeros_like(state[0]), general_body(*arguments)

    return lax.while_loop(lambda state: state[0] > 0.5, again, (strays, results))[1]


def padded_2(cells, sides, width):
    for axis, dim in sides:
        count = lax.axis_size(axis)
        ends = count - 1
        head = lax.slice_in_dim(cells, 0, width, axis=dim)
        tail = lax.slice_in_dim(cells, cells.shape[dim] - width, cells.shape[dim], axis=dim)
        cells = jnp.concatenate(
            [
                lax.ppermute(tail, axis, [(i, (i + 1) % count) for i in range(ends)]),
                cells,
                lax.ppermute(head, axis, [((i + 1) % count, i) for i in range(ends)]),
            ],
            axis=dim,
        )
    return cells


def rim_slices(step_value, length):
    if step_value < 0:
        return (slice(length - 1, length), slice(0, 1))
    if step_value > 0:
        return (slice(0, 1), slice(length + 1, length + 2))
    return (slice(0, length), slice(1, length + 1))


def assemble(cube_view, sources, source_index):
    length = cube_view.shape[1]
    padded = jnp.pad(cube_view, ((0, 0), (1, 1), (1, 1), (1, 1), (0, 0)))
    for column, (step_x, step_y) in enumerate(DIRECTIONS):
        source_x, target_x = rim_slices(step_x, length)
        source_y, target_y = rim_slices(step_y, length)
        rim_cells = sources[:, source_x, source_y]
        fetched = jnp.take(rim_cells, source_index[:, column], axis=0)
        padded = padded.at[:, target_x, target_y, 1 : length + 1].set(fetched)
    return padded


def window_stack(padded, shift_x, flipped):
    length = padded.shape[1] - 2
    channels = padded.shape[-1]
    pieces = []
    for shift_y in range(3):
        for shift_z in range(3):
            if flipped:
                corner_x, corner_y, corner_z = (2 - shift_x, 2 - shift_y, 2 - shift_z)
            else:
                corner_x, corner_y, corner_z = (shift_x, shift_y, shift_z)
            cells = padded[
                :,
                corner_x : corner_x + length,
                corner_y : corner_y + length,
                corner_z : corner_z + length,
            ]
            pieces.append(cells.reshape(-1, channels))
    return jnp.concatenate(pieces, axis=1)


def convolve(padded, weight, flipped):
    channels = padded.shape[-1]
    summed = None
    for shift_x in range(3):
        stacked = window_stack(padded, shift_x, flipped)
        weight_block = weight[9 * shift_x : 9 * shift_x + 9]
        if flipped:
            weight_block = jnp.swapaxes(weight_block, 1, 2)
        partial_sum = jnp.dot(
            stacked,
            weight_block.reshape(9 * channels, channels),
            preferred_element_type=jnp.float32,
        )
        summed = partial_sum if summed is None else summed + partial_sum
    return summed


def weight_grad(padded, grads):
    channels = padded.shape[-1]
    blocks = []
    for shift_x in range(3):
        stacked = window_stack(padded, shift_x, False)
        product = lax.dot_general(
            stacked, grads, (((0,), (0,)), ((), ())), preferred_element_type=jnp.float32
        )
        blocks.append(product.reshape(9, channels, channels))
    return jnp.concatenate(blocks, axis=0)


def silu_slope(values):
    sigmoid_value = jax.nn.sigmoid(values)
    return sigmoid_value * (1.0 + values * (1.0 - sigmoid_value))


def general_body(feats, mask, neighbours, weight_one, weight_two, cotangent):
    bricks, voxels, channels = feats.shape
    my_index = lax.axis_index("space")
    first_brick = (my_index * TILE - 1) * WIDE
    source_index = jnp.where(neighbours >= 0, neighbours - first_brick, (TILE + 2) * WIDE)
    occupied = mask.reshape(-1, 1).astype(jnp.float32)
    blank_brick = jnp.zeros((1, EDGE, EDGE, EDGE, channels), jnp.bfloat16)

    def join_sources(cube_view, left_side, right_side):
        sources = jnp.concatenate([left_side, cube_view, right_side, blank_brick], axis=0)
        return assemble(cube_view, sources, source_index)

    def extend_bricks(flat_field, received):
        cube_view = flat_field.reshape(bricks, EDGE, EDGE, EDGE, channels)
        left_side = received[0].reshape(WIDE, EDGE, EDGE, EDGE, channels)
        right_side = received[TILE + 1].reshape(WIDE, EDGE, EDGE, EDGE, channels)
        return join_sources(cube_view, left_side, right_side)

    def as_tiles(flat_field):
        return flat_field.reshape(TILE, WIDE, voxels, channels)

    inputs = feats * mask[:, :, None].astype(jnp.bfloat16)
    padded_in = extend_bricks(inputs, padded_2(as_tiles(inputs), (("space", 0),), 1))
    first_pre = convolve(padded_in, weight_one, False)
    hidden = (
        (occupied * jax.nn.silu(first_pre)).astype(jnp.bfloat16).reshape(bricks, voxels, channels)
    )
    padded_hidden = extend_bricks(hidden, padded_2(as_tiles(hidden), (("space", 0),), 1))
    second_pre = convolve(padded_hidden, weight_two, False)
    output = (occupied * jax.nn.silu(second_pre)).astype(jnp.bfloat16)
    grad_second = (
        cotangent.reshape(-1, channels).astype(jnp.float32) * occupied * silu_slope(second_pre)
    ).astype(jnp.bfloat16)
    grad_second_view = grad_second.reshape(bricks, voxels, channels)
    padded_second = extend_bricks(
        grad_second_view, padded_2(as_tiles(grad_second_view), (("space", 0),), 1)
    )
    back_second = convolve(padded_second, weight_two, True)
    grad_first = (occupied * silu_slope(first_pre) * back_second).astype(jnp.bfloat16)
    grad_scale = 1.0 / math.sqrt(voxels * bricks)
    grad_w2 = weight_grad(padded_hidden, grad_second) * grad_scale
    grad_w2 = summed(grad_w2.astype(jnp.bfloat16), 0)
    grad_first_view = grad_first.reshape(bricks, voxels, channels)
    padded_first = extend_bricks(
        grad_first_view, padded_2(as_tiles(grad_first_view), (("space", 0),), 1)
    )
    grad_input = (occupied * convolve(padded_first, weight_one, True)).astype(jnp.bfloat16)
    grad_w1 = weight_grad(padded_in, grad_first) * grad_scale
    grad_w1 = summed(grad_w1.astype(jnp.bfloat16), 1)
    return (
        output.reshape(bricks, voxels, channels),
        grad_input.reshape(bricks, voxels, channels),
        grad_w1,
        grad_w2,
    )


def solution(mesh):
    in_specs = (
        P(("scene", "space"), None, None),
        P(("scene", "space"), None),
        P(("scene", "space"), None),
        P(),
        P(),
        P(("scene", "space"), None, None),
    )
    out_specs = (
        P(("scene", "space"), None, None),
        P(("scene", "space"), None, None),
        P("scene", None, None),
        P("scene", None, None),
    )
    return jax.shard_map(body, mesh=mesh, in_specs=in_specs, out_specs=out_specs, check_vma=False)
```

```python
import functools
import math

import jax
import jax.numpy as jnp
from jax import lax
from jax.experimental import pallas as pl
from jax.experimental.pallas import tpu as pltpu
from jax.sharding import PartitionSpec as P

EDGE = 8
TILE = 1
WIDE = 8
SLAB = EDGE * EDGE
C = 128
TAPS = 9 * C
VMEM_LIMIT = 56 * 1024 * 1024

DIRECTIONS = ((-1, -1), (-1, 0), (-1, 1), (0, -1), (0, 1), (1, -1), (1, 0), (1, 1))


def picked(source, index, first, rows):
    found = source[jnp.maximum(index, 0), first : first + rows, :].astype(jnp.float32)
    return jnp.where(index >= 0, found, 0.0)


def slab_tiles(centre, top, bottom):
    cells = jnp.concatenate([top[8:16], centre, bottom[0:8]], axis=0).reshape(EDGE + 2, EDGE, C)
    place = lax.broadcasted_iota(jnp.int32, cells.shape, 1)
    below = jnp.where(place == 0, 0.0, pltpu.roll(cells, 1, 1))
    above = jnp.where(place == EDGE - 1, 0.0, pltpu.roll(cells, EDGE - 1, 1))
    even, odd = [], []
    for shifted in (below, cells, above):
        even.append(shifted.reshape((EDGE + 2) * EDGE, C).astype(jnp.bfloat16))
        odd.append(shifted[1 : EDGE + 1].reshape(SLAB, C).astype(jnp.bfloat16))
    return [e[0:SLAB] for e in even] + odd + [e[16 : 16 + SLAB] for e in even]


def build_stack(table, field, left, right, stack):
    bricks = field.shape[0]

    @pl.loop(0, bricks)
    def _(g):
        for a in range(EDGE + 2):
            if a == 0:
                source, first, near = left, 0, (table[g, 1], table[g, 0], table[g, 2])
            elif a == EDGE + 1:
                source, first, near = right, 0, (table[g, 6], table[g, 5], table[g, 7])
            else:
                source, first, near = field, (a - 1) * SLAB, (g, table[g, 3], table[g, 4])
            if source is field:
                centre = field[g, first : first + SLAB, :].astype(jnp.float32)
            else:
                centre = picked(source, near[0], first, SLAB)
            top = picked(source, near[1], first + SLAB - 16, 16)
            bottom = picked(source, near[2], first, 16)
            for t, tile in enumerate(slab_tiles(centre, top, bottom)):
                stack[g, a, :, t * C : (t + 1) * C] = tile


def fill_weights(weights, turned, filled):
    for half in range(2):
        columns = slice(half * C, (half + 1) * C)
        for j in range(4):
            k1 = j - half
            for t in range(9):
                first = j * TAPS + t * C
                if not 0 <= k1 <= 2:
                    block = jnp.zeros((C, C), jnp.bfloat16)
                elif turned:
                    block = weights[26 - 9 * k1 - t].astype(jnp.float32).T.astype(jnp.bfloat16)
                else:
                    block = weights[9 * k1 + t]
                filled[first : first + C, columns] = block


def prepare(turned, table, field, left, right, weights, stack, filled):
    @pl.when(pl.program_id(0) == 0)
    def _():
        fill_weights(weights, turned, filled)
        build_stack(table, field, left, right, stack)


def pair_product(stack, weights, pair):
    bricks = stack.shape[0]
    rows = [stack[:, 2 * pair + j].reshape(bricks * SLAB, TAPS) for j in range(4)]
    return jnp.dot(
        jnp.concatenate(rows, axis=1), weights[...], preferred_element_type=jnp.float32
    )


def spread(values, bricks):
    return values.reshape(bricks, SLAB, C)


def slope_of(values):
    s = jax.nn.sigmoid(values)
    return s * (1.0 + values * (1.0 - s))


def put(result, low, high, half, values):
    result[:, half * SLAB : (half + 1) * SLAB, :] = values
    if half == 0 and low is not None:

        @pl.when(pl.program_id(0) == 0)
        def _():
            low[...] = values

    if half == 1 and high is not None:

        @pl.when(pl.program_id(0) == EDGE // 2 - 1)
        def _():
            high[...] = values


def first_kernel(table, field, left, right, weights, mask, pre, hidden, low, high, stack, filled):
    pair = pl.program_id(0)
    bricks = field.shape[0]

    prepare(False, table, field, left, right, weights, stack, filled)
    both = pair_product(stack, filled, pair)
    pre[0] = both
    for half in range(2):
        values = both[:, half * C : (half + 1) * C]
        occupied = mask[:, half * SLAB : (half + 1) * SLAB, :].astype(jnp.float32)
        active = spread(values * jax.nn.sigmoid(values), bricks)
        put(hidden, low, high, half, (occupied * active).astype(jnp.bfloat16))


def second_kernel(
    table, field, left, right, weights, mask, cotangent, output, grad, low, high, stack, filled
):
    pair = pl.program_id(0)
    bricks = field.shape[0]

    prepare(False, table, field, left, right, weights, stack, filled)
    both = pair_product(stack, filled, pair)
    for half in range(2):
        values = both[:, half * C : (half + 1) * C]
        rows = slice(half * SLAB, (half + 1) * SLAB)
        occupied = mask[:, rows, :].astype(jnp.float32)
        s = jax.nn.sigmoid(values)
        output[:, rows, :] = (occupied * spread(values * s, bricks)).astype(jnp.bfloat16)
        slope = spread(s * (1.0 + values * (1.0 - s)), bricks)
        received = cotangent[:, rows, :].astype(jnp.float32)
        put(grad, low, high, half, (received * occupied * slope).astype(jnp.bfloat16))


def third_kernel(table, field, left, right, weights, mask, pre, grad, low, high, stack, filled):
    pair = pl.program_id(0)
    bricks = field.shape[0]

    prepare(True, table, field, left, right, weights, stack, filled)
    both = pair_product(stack, filled, pair)
    for half in range(2):
        columns = slice(half * C, (half + 1) * C)
        occupied = mask[:, half * SLAB : (half + 1) * SLAB, :].astype(jnp.float32)
        slope = slope_of(pre[0, :, columns])
        product = spread(slope * both[:, columns], bricks)
        put(grad, low, high, half, (occupied * product).astype(jnp.bfloat16))


def fourth_kernel(table, field, left, right, weights, mask, grad, stack, filled):
    pair = pl.program_id(0)
    bricks = field.shape[0]

    prepare(True, table, field, left, right, weights, stack, filled)
    both = pair_product(stack, filled, pair)
    for half in range(2):
        occupied = mask[:, half * SLAB : (half + 1) * SLAB, :].astype(jnp.float32)
        values = spread(both[:, half * C : (half + 1) * C], bricks)
        put(grad, None, None, half, (occupied * values).astype(jnp.bfloat16))


def weight_kernel(scale, table, mark, field, left, right, grads, result, stack, turned, total):
    bricks = field.shape[0]
    build_stack(table, field, left, right, stack)
    for a in range(EDGE):
        slab = grads[:, a * SLAB : (a + 1) * SLAB, :].reshape(bricks * SLAB, C)
        turned[a] = slab.astype(jnp.float32).T.astype(jnp.bfloat16)
    total[...] = jnp.zeros_like(total)

    def add(a, first, last):
        lhs = [turned[a - k1] for k1 in range(first, last)]
        lhs = lhs[0] if len(lhs) == 1 else jnp.concatenate(lhs, axis=0)
        product = jnp.dot(
            lhs,
            stack[:, a].reshape(bricks * SLAB, TAPS),
            preferred_element_type=jnp.float32,
        )
        total[first * C : last * C, :] += product

    add(0, 0, 1)
    add(1, 0, 2)

    @pl.loop(2, EDGE)
    def _(a):
        add(a, 0, 3)

    add(EDGE, 1, 3)
    add(EDGE + 1, 2, 3)
    for k1 in range(3):
        for t in range(9):
            block = total[k1 * C : (k1 + 1) * C, t * C : (t + 1) * C]
            result[9 * k1 + t] = (block.T * scale).astype(jnp.bfloat16)
    result[27] = jnp.full((C, C), mark[0], jnp.float32).astype(jnp.bfloat16)


def cost(flops, arrays):
    return pl.CostEstimate(
        flops=flops,
        bytes_accessed=sum(math.prod(a.shape) * a.dtype.itemsize for a in arrays),
        transcendentals=0,
    )


def whole(array):
    return pl.BlockSpec(array.shape, lambda i, n=len(array.shape): (0,) * n)


def run_conv(kernel, table, field, left, right, weights, by_rows, by_pair, outs):
    bricks, voxels, _ = field.shape
    pairs = EDGE // 2
    rows_spec = pl.BlockSpec((bricks, 2 * SLAB, C), lambda i: (0, i, 0))
    pair_spec = pl.BlockSpec((1, bricks * SLAB, 2 * C), lambda i: (i, 0, 0))
    edge_spec = pl.BlockSpec((bricks, SLAB, C), lambda i: (0, 0, 0))
    kinds = {
        "rows": (rows_spec, jax.ShapeDtypeStruct((bricks, voxels, C), jnp.bfloat16)),
        "pair": (pair_spec, jax.ShapeDtypeStruct((pairs, bricks * SLAB, 2 * C), jnp.float32)),
        "edge": (edge_spec, jax.ShapeDtypeStruct((bricks, SLAB, C), jnp.bfloat16)),
    }
    operands = [field, left, right, weights, *by_rows, *by_pair]
    return pl.pallas_call(
        kernel,
        grid=(pairs,),
        in_specs=[
            pl.BlockSpec(memory_space=pltpu.SMEM),
            *[whole(a) for a in (field, left, right, weights)],
            *[rows_spec for _ in by_rows],
            *[pair_spec for _ in by_pair],
        ],
        out_specs=[kinds[k][0] for k in outs],
        out_shape=[kinds[k][1] for k in outs],
        scratch_shapes=[
            pltpu.VMEM((bricks, EDGE + 2, SLAB, TAPS), jnp.bfloat16),
            pltpu.VMEM((4 * TAPS, 2 * C), jnp.bfloat16),
        ],
        compiler_params=pltpu.CompilerParams(
            dimension_semantics=("arbitrary",), vmem_limit_bytes=VMEM_LIMIT
        ),
        cost_estimate=cost(
            2 * 36 * bricks * voxels * C * C, operands + [kinds[k][1] for k in outs]
        ),
    )(table, *operands)


def run_weight(table, mark, field, left, right, grads, scale):
    bricks, voxels, _ = field.shape
    out = jax.ShapeDtypeStruct((28, C, C), jnp.bfloat16)
    return pl.pallas_call(
        functools.partial(weight_kernel, scale),
        in_specs=[
            *[pl.BlockSpec(memory_space=pltpu.SMEM)] * 2,
            *[pl.BlockSpec(memory_space=pltpu.VMEM)] * 4,
        ],
        out_specs=pl.BlockSpec(memory_space=pltpu.VMEM),
        out_shape=out,
        scratch_shapes=[
            pltpu.VMEM((bricks, EDGE + 2, SLAB, TAPS), jnp.bfloat16),
            pltpu.VMEM((EDGE, C, bricks * SLAB), jnp.bfloat16),
            pltpu.VMEM((3 * C, TAPS), jnp.float32),
        ],
        compiler_params=pltpu.CompilerParams(vmem_limit_bytes=VMEM_LIMIT),
        cost_estimate=cost(2 * 27 * bricks * voxels * C * C, [field, left, right, grads, out]),
    )(table, mark, field, left, right, grads)


def beside(low, high):
    count = lax.axis_size("space")
    left = lax.ppermute(high, "space", [(i, i + 1) for i in range(count - 1)])
    right = lax.ppermute(low, "space", [(i + 1, i) for i in range(count - 1)])
    return left, right


def summed(term):
    count = lax.axis_size("space")
    parts = lax.all_to_all(term.reshape(count, -1, C), "space", 0, 0, tiled=True)
    part = jnp.sum(parts.astype(jnp.float32), axis=0).astype(jnp.bfloat16)
    parts = jnp.broadcast_to(part[None], (count,) + part.shape)
    parts = lax.all_to_all(parts, "space", 0, 0, tiled=True)
    return parts.reshape(28, C, C).astype(jnp.float32)


def column_body(feats, mask, neighbours, weight_one, weight_two, cotangent):
    bricks, voxels, channels = feats.shape
    my_index = lax.axis_index("space")
    steps = jnp.array([s for s, _ in DIRECTIONS], jnp.int32)
    local = neighbours - (my_index + steps)[None, :] * (TILE * WIDE)
    inside = (local >= 0) & (local < bricks) & (neighbours >= 0)
    strays = jnp.any((neighbours >= 0) & ~inside).astype(jnp.float32).reshape(1)
    table = jnp.where(inside, local, -1)
    spread_mask = jnp.broadcast_to(mask.astype(jnp.bfloat16)[:, :, None], feats.shape)
    scale = 1.0 / math.sqrt(voxels * bricks)

    inputs = feats * spread_mask
    in_left, in_right = beside(inputs[:, :SLAB], inputs[:, voxels - SLAB :])
    pre, hidden, low, high = run_conv(
        first_kernel, table, inputs, in_left, in_right, weight_one,
        [spread_mask], [], ("pair", "rows", "edge", "edge"),
    )
    h_left, h_right = beside(low, high)
    output, grad_second, low, high = run_conv(
        second_kernel, table, hidden, h_left, h_right, weight_two,
        [spread_mask, cotangent], [], ("rows", "rows", "edge", "edge"),
    )
    s_left, s_right = beside(low, high)
    term_two = run_weight(table, strays, hidden, h_left, h_right, grad_second, scale)
    grad_w2 = summed(term_two)
    grad_first, low, high = run_conv(
        third_kernel, table, grad_second, s_left, s_right, weight_two,
        [spread_mask], [pre], ("rows", "edge", "edge"),
    )
    term_one = run_weight(table, strays, inputs, in_left, in_right, grad_first, scale)
    term_one, low, high = lax.optimization_barrier((term_one, low, high))
    grad_w1 = summed(term_one)
    f_left, f_right = beside(low, high)
    (grad_input,) = run_conv(
        fourth_kernel, table, grad_first, f_left, f_right, weight_one,
        [spread_mask], [], ("rows",),
    )
    return grad_w2[27, 0, 0], (output, grad_input, grad_w1[:27], grad_w2[:27])


def body(*arguments):
    strays, results = column_body(*arguments)

    def again(state):
        return jnp.zeros_like(state[0]), general_body(*arguments)

    return lax.while_loop(lambda state: state[0] > 0.5, again, (strays, results))[1]


def padded_2(cells, sides, width):
    for axis, dim in sides:
        count = lax.axis_size(axis)
        ends = count - 1
        head = lax.slice_in_dim(cells, 0, width, axis=dim)
        tail = lax.slice_in_dim(cells, cells.shape[dim] - width, cells.shape[dim], axis=dim)
        cells = jnp.concatenate(
            [
                lax.ppermute(tail, axis, [(i, (i + 1) % count) for i in range(ends)]),
                cells,
                lax.ppermute(head, axis, [((i + 1) % count, i) for i in range(ends)]),
            ],
            axis=dim,
        )
    return cells


def rim_slices(step_value, length):
    if step_value < 0:
        return (slice(length - 1, length), slice(0, 1))
    if step_value > 0:
        return (slice(0, 1), slice(length + 1, length + 2))
    return (slice(0, length), slice(1, length + 1))


def assemble(cube_view, sources, source_index):
    length = cube_view.shape[1]
    padded = jnp.pad(cube_view, ((0, 0), (1, 1), (1, 1), (1, 1), (0, 0)))
    for column, (step_x, step_y) in enumerate(DIRECTIONS):
        source_x, target_x = rim_slices(step_x, length)
        source_y, target_y = rim_slices(step_y, length)
        rim_cells = sources[:, source_x, source_y]
        fetched = jnp.take(rim_cells, source_index[:, column], axis=0)
        padded = padded.at[:, target_x, target_y, 1 : length + 1].set(fetched)
    return padded


def window_stack(padded, shift_x, flipped):
    length = padded.shape[1] - 2
    channels = padded.shape[-1]
    pieces = []
    for shift_y in range(3):
        for shift_z in range(3):
            if flipped:
                corner_x, corner_y, corner_z = (2 - shift_x, 2 - shift_y, 2 - shift_z)
            else:
                corner_x, corner_y, corner_z = (shift_x, shift_y, shift_z)
            cells = padded[
                :,
                corner_x : corner_x + length,
                corner_y : corner_y + length,
                corner_z : corner_z + length,
            ]
            pieces.append(cells.reshape(-1, channels))
    return jnp.concatenate(pieces, axis=1)


def convolve(padded, weight, flipped):
    channels = padded.shape[-1]
    summed = None
    for shift_x in range(3):
        stacked = window_stack(padded, shift_x, flipped)
        weight_block = weight[9 * shift_x : 9 * shift_x + 9]
        if flipped:
            weight_block = jnp.swapaxes(weight_block, 1, 2)
        partial_sum = jnp.dot(
            stacked,
            weight_block.reshape(9 * channels, channels),
            preferred_element_type=jnp.float32,
        )
        summed = partial_sum if summed is None else summed + partial_sum
    return summed


def weight_grad(padded, grads):
    channels = padded.shape[-1]
    blocks = []
    for shift_x in range(3):
        stacked = window_stack(padded, shift_x, False)
        product = lax.dot_general(
            stacked, grads, (((0,), (0,)), ((), ())), preferred_element_type=jnp.float32
        )
        blocks.append(product.reshape(9, channels, channels))
    return jnp.concatenate(blocks, axis=0)


def silu_slope(values):
    sigmoid_value = jax.nn.sigmoid(values)
    return sigmoid_value * (1.0 + values * (1.0 - sigmoid_value))


def general_body(feats, mask, neighbours, weight_one, weight_two, cotangent):
    bricks, voxels, channels = feats.shape
    my_index = lax.axis_index("space")
    first_brick = (my_index * TILE - 1) * WIDE
    source_index = jnp.where(neighbours >= 0, neighbours - first_brick, (TILE + 2) * WIDE)
    occupied = mask.reshape(-1, 1).astype(jnp.float32)
    blank_brick = jnp.zeros((1, EDGE, EDGE, EDGE, channels), jnp.bfloat16)

    def join_sources(cube_view, left_side, right_side):
        sources = jnp.concatenate([left_side, cube_view, right_side, blank_brick], axis=0)
        return assemble(cube_view, sources, source_index)

    def extend_bricks(flat_field, received):
        cube_view = flat_field.reshape(bricks, EDGE, EDGE, EDGE, channels)
        left_side = received[0].reshape(WIDE, EDGE, EDGE, EDGE, channels)
        right_side = received[TILE + 1].reshape(WIDE, EDGE, EDGE, EDGE, channels)
        return join_sources(cube_view, left_side, right_side)

    def as_tiles(flat_field):
        return flat_field.reshape(TILE, WIDE, voxels, channels)

    inputs = feats * mask[:, :, None].astype(jnp.bfloat16)
    padded_in = extend_bricks(inputs, padded_2(as_tiles(inputs), (("space", 0),), 1))
    first_pre = convolve(padded_in, weight_one, False)
    hidden = (
        (occupied * jax.nn.silu(first_pre)).astype(jnp.bfloat16).reshape(bricks, voxels, channels)
    )
    padded_hidden = extend_bricks(hidden, padded_2(as_tiles(hidden), (("space", 0),), 1))
    second_pre = convolve(padded_hidden, weight_two, False)
    output = (occupied * jax.nn.silu(second_pre)).astype(jnp.bfloat16)
    grad_second = (
        cotangent.reshape(-1, channels).astype(jnp.float32) * occupied * silu_slope(second_pre)
    ).astype(jnp.bfloat16)
    grad_second_view = grad_second.reshape(bricks, voxels, channels)
    padded_second = extend_bricks(
        grad_second_view, padded_2(as_tiles(grad_second_view), (("space", 0),), 1)
    )
    back_second = convolve(padded_second, weight_two, True)
    grad_first = (occupied * silu_slope(first_pre) * back_second).astype(jnp.bfloat16)
    grad_scale = 1.0 / math.sqrt(voxels * bricks)
    grad_w2 = weight_grad(padded_hidden, grad_second) * grad_scale
    grad_w2 = jnp.pad(grad_w2.astype(jnp.bfloat16), ((0, 1), (0, 0), (0, 0)))
    grad_w2 = summed(grad_w2)[:27]
    grad_first_view = grad_first.reshape(bricks, voxels, channels)
    padded_first = extend_bricks(
        grad_first_view, padded_2(as_tiles(grad_first_view), (("space", 0),), 1)
    )
    grad_input = (occupied * convolve(padded_first, weight_one, True)).astype(jnp.bfloat16)
    grad_w1 = weight_grad(padded_in, grad_first) * grad_scale
    grad_w1 = jnp.pad(grad_w1.astype(jnp.bfloat16), ((0, 1), (0, 0), (0, 0)))
    grad_w1 = summed(grad_w1)[:27]
    return (
        output.reshape(bricks, voxels, channels),
        grad_input.reshape(bricks, voxels, channels),
        grad_w1,
        grad_w2,
    )


def solution(mesh):
    in_specs = (
        P(("scene", "space"), None, None),
        P(("scene", "space"), None),
        P(("scene", "space"), None),
        P(),
        P(),
        P(("scene", "space"), None, None),
    )
    out_specs = (
        P(("scene", "space"), None, None),
        P(("scene", "space"), None, None),
        P("scene", None, None),
        P("scene", None, None),
    )
    return jax.shard_map(body, mesh=mesh, in_specs=in_specs, out_specs=out_specs, check_vma=False)
```

```python
import functools
import math

import jax
import jax.numpy as jnp
from jax import lax
from jax.experimental import pallas as pl
from jax.experimental.pallas import tpu as pltpu
from jax.sharding import PartitionSpec as P

EDGE = 8
TILE = 1
WIDE = 8
SLAB = EDGE * EDGE
C = 128
TAPS = 9 * C
VMEM_LIMIT = 56 * 1024 * 1024

DIRECTIONS = ((-1, -1), (-1, 0), (-1, 1), (0, -1), (0, 1), (1, -1), (1, 0), (1, 1))


def picked(source, index, first, rows):
    found = source[jnp.maximum(index, 0), first : first + rows, :].astype(jnp.float32)
    return jnp.where(index >= 0, found, 0.0)


def slab_tiles(centre, top, bottom):
    cells = jnp.concatenate([top[8:16], centre, bottom[0:8]], axis=0).reshape(EDGE + 2, EDGE, C)
    place = lax.broadcasted_iota(jnp.int32, cells.shape, 1)
    below = jnp.where(place == 0, 0.0, pltpu.roll(cells, 1, 1))
    above = jnp.where(place == EDGE - 1, 0.0, pltpu.roll(cells, EDGE - 1, 1))
    even, odd = [], []
    for shifted in (below, cells, above):
        even.append(shifted.reshape((EDGE + 2) * EDGE, C).astype(jnp.bfloat16))
        odd.append(shifted[1 : EDGE + 1].reshape(SLAB, C).astype(jnp.bfloat16))
    return [e[0:SLAB] for e in even] + odd + [e[16 : 16 + SLAB] for e in even]


def build_stack(table, field, left, right, stack):
    bricks = field.shape[0]

    @pl.loop(0, bricks)
    def _(g):
        for a in range(EDGE + 2):
            if a == 0:
                source, first, near = left, 0, (table[g, 1], table[g, 0], table[g, 2])
            elif a == EDGE + 1:
                source, first, near = right, 0, (table[g, 6], table[g, 5], table[g, 7])
            else:
                source, first, near = field, (a - 1) * SLAB, (g, table[g, 3], table[g, 4])
            if source is field:
                centre = field[g, first : first + SLAB, :].astype(jnp.float32)
            else:
                centre = picked(source, near[0], first, SLAB)
            top = picked(source, near[1], first + SLAB - 16, 16)
            bottom = picked(source, near[2], first, 16)
            for t, tile in enumerate(slab_tiles(centre, top, bottom)):
                stack[g, a, :, t * C : (t + 1) * C] = tile


def fill_weights(weights, turned, filled):
    for half in range(2):
        columns = slice(half * C, (half + 1) * C)
        for j in range(4):
            k1 = j - half
            for t in range(9):
                first = j * TAPS + t * C
                if not 0 <= k1 <= 2:
                    block = jnp.zeros((C, C), jnp.bfloat16)
                elif turned:
                    block = weights[26 - 9 * k1 - t].astype(jnp.float32).T.astype(jnp.bfloat16)
                else:
                    block = weights[9 * k1 + t]
                filled[first : first + C, columns] = block


def prepare(turned, table, field, left, right, weights, stack, filled, kept=None, arrived=None):
    @pl.when(pl.program_id(0) == 0)
    def _():
        build_stack(table, field, left, right, stack)
        if kept is not None:
            pltpu.make_async_copy(stack, kept, arrived).start()
        fill_weights(weights, turned, filled)

    if kept is not None:

        @pl.when(pl.program_id(0) == pl.num_programs(0) - 1)
        def _():
            pltpu.make_async_copy(stack, kept, arrived).wait()


def pair_product(stack, weights, pair):
    bricks = stack.shape[0]
    rows = [stack[:, 2 * pair + j].reshape(bricks * SLAB, TAPS) for j in range(4)]
    return jnp.dot(
        jnp.concatenate(rows, axis=1), weights[...], preferred_element_type=jnp.float32
    )


def spread(values, bricks):
    return values.reshape(bricks, SLAB, C)


def slope_of(values):
    s = jax.nn.sigmoid(values)
    return s * (1.0 + values * (1.0 - s))


def put(result, low, high, half, values):
    result[:, half * SLAB : (half + 1) * SLAB, :] = values
    if half == 0 and low is not None:

        @pl.when(pl.program_id(0) == 0)
        def _():
            low[...] = values

    if half == 1 and high is not None:

        @pl.when(pl.program_id(0) == EDGE // 2 - 1)
        def _():
            high[...] = values


def first_kernel(
    table, field, left, right, weights, mask, pre, hidden, low, high, kept, stack, filled, arrived
):
    pair = pl.program_id(0)
    bricks = field.shape[0]

    prepare(False, table, field, left, right, weights, stack, filled, kept, arrived)
    both = pair_product(stack, filled, pair)
    pre[0] = both
    for half in range(2):
        values = both[:, half * C : (half + 1) * C]
        occupied = mask[:, half * SLAB : (half + 1) * SLAB, :].astype(jnp.float32)
        active = spread(values * jax.nn.sigmoid(values), bricks)
        put(hidden, low, high, half, (occupied * active).astype(jnp.bfloat16))


def second_kernel(
    table, field, left, right, weights, mask, cotangent, output, grad, low, high, kept, stack, filled, arrived
):
    pair = pl.program_id(0)
    bricks = field.shape[0]

    prepare(False, table, field, left, right, weights, stack, filled, kept, arrived)
    both = pair_product(stack, filled, pair)
    for half in range(2):
        values = both[:, half * C : (half + 1) * C]
        rows = slice(half * SLAB, (half + 1) * SLAB)
        occupied = mask[:, rows, :].astype(jnp.float32)
        s = jax.nn.sigmoid(values)
        output[:, rows, :] = (occupied * spread(values * s, bricks)).astype(jnp.bfloat16)
        slope = spread(s * (1.0 + values * (1.0 - s)), bricks)
        received = cotangent[:, rows, :].astype(jnp.float32)
        put(grad, low, high, half, (received * occupied * slope).astype(jnp.bfloat16))


def third_kernel(table, field, left, right, weights, mask, pre, grad, low, high, stack, filled):
    pair = pl.program_id(0)
    bricks = field.shape[0]

    prepare(True, table, field, left, right, weights, stack, filled)
    both = pair_product(stack, filled, pair)
    for half in range(2):
        columns = slice(half * C, (half + 1) * C)
        occupied = mask[:, half * SLAB : (half + 1) * SLAB, :].astype(jnp.float32)
        slope = slope_of(pre[0, :, columns])
        product = spread(slope * both[:, columns], bricks)
        put(grad, low, high, half, (occupied * product).astype(jnp.bfloat16))


def fourth_kernel(table, field, left, right, weights, mask, grad, stack, filled):
    pair = pl.program_id(0)
    bricks = field.shape[0]

    prepare(True, table, field, left, right, weights, stack, filled)
    both = pair_product(stack, filled, pair)
    for half in range(2):
        occupied = mask[:, half * SLAB : (half + 1) * SLAB, :].astype(jnp.float32)
        values = spread(both[:, half * C : (half + 1) * C], bricks)
        put(grad, None, None, half, (occupied * values).astype(jnp.bfloat16))


def weight_kernel(scale, facts, stack, grads, result, turned, total):
    a = pl.program_id(0)
    bricks = grads.shape[0]

    @pl.when(a == 0)
    def _():
        for edge in (0, 1, EDGE + 2, EDGE + 3):
            turned[edge] = jnp.zeros_like(turned[edge])
        for slab in range(EDGE):
            rows = grads[:, slab * SLAB : (slab + 1) * SLAB, :].reshape(bricks * SLAB, C)
            turned[slab + 2] = rows.astype(jnp.float32).T.astype(jnp.bfloat16)

    def product(slabs):
        lhs = [turned[slab] for slab in slabs]
        return jnp.dot(
            lhs[0] if len(lhs) == 1 else jnp.concatenate(lhs, axis=0),
            stack[:, 0].reshape(bricks * SLAB, TAPS),
            preferred_element_type=jnp.float32,
        )

    @pl.when(a == 0)
    def _():
        total[0:C, :] = product([2])
        total[C:, :] = jnp.zeros_like(total[C:, :])

    @pl.when((a > 0) & (a <= EDGE))
    def _():
        total[...] += product([a + 2, a + 1, a])

    @pl.when(a == EDGE + 1)
    def _():
        total[2 * C :, :] += product([EDGE + 1])
        turn = 1 - facts[1]
        for n in range(28):
            half = n // 14
            place = half * (1 - turn) + (1 - half) * turn
            if n == 27:
                block = jnp.full((C, C), facts[0], jnp.int32).astype(jnp.float32)
            else:
                k1, t = n // 9, n % 9
                block = total[k1 * C : (k1 + 1) * C, t * C : (t + 1) * C].T * scale
            result[place, n % 14] = block.astype(jnp.bfloat16)


def cost(flops, arrays):
    return pl.CostEstimate(
        flops=flops,
        bytes_accessed=sum(math.prod(a.shape) * a.dtype.itemsize for a in arrays),
        transcendentals=0,
    )


def whole(array):
    return pl.BlockSpec(array.shape, lambda i, n=len(array.shape): (0,) * n)


def run_conv(kernel, table, field, left, right, weights, by_rows, by_pair, outs):
    bricks, voxels, _ = field.shape
    pairs = EDGE // 2
    rows_spec = pl.BlockSpec((bricks, 2 * SLAB, C), lambda i: (0, i, 0))
    pair_spec = pl.BlockSpec((1, bricks * SLAB, 2 * C), lambda i: (i, 0, 0))
    edge_spec = pl.BlockSpec((bricks, SLAB, C), lambda i: (0, 0, 0))
    kinds = {
        "rows": (rows_spec, jax.ShapeDtypeStruct((bricks, voxels, C), jnp.bfloat16)),
        "pair": (pair_spec, jax.ShapeDtypeStruct((pairs, bricks * SLAB, 2 * C), jnp.float32)),
        "stack": (
            pl.BlockSpec(memory_space=pl.ANY),
            jax.ShapeDtypeStruct((bricks, EDGE + 2, SLAB, TAPS), jnp.bfloat16),
        ),
        "edge": (edge_spec, jax.ShapeDtypeStruct((bricks, SLAB, C), jnp.bfloat16)),
    }
    operands = [field, left, right, weights, *by_rows, *by_pair]
    return pl.pallas_call(
        kernel,
        grid=(pairs,),
        in_specs=[
            pl.BlockSpec(memory_space=pltpu.SMEM),
            *[whole(a) for a in (field, left, right, weights)],
            *[rows_spec for _ in by_rows],
            *[pair_spec for _ in by_pair],
        ],
        out_specs=[kinds[k][0] for k in outs],
        out_shape=[kinds[k][1] for k in outs],
        scratch_shapes=[
            pltpu.VMEM((bricks, EDGE + 2, SLAB, TAPS), jnp.bfloat16),
            pltpu.VMEM((4 * TAPS, 2 * C), jnp.bfloat16),
            *([pltpu.SemaphoreType.DMA] if "stack" in outs else []),
        ],
        compiler_params=pltpu.CompilerParams(
            dimension_semantics=("arbitrary",), vmem_limit_bytes=VMEM_LIMIT
        ),
        cost_estimate=cost(
            2 * 36 * bricks * voxels * C * C, operands + [kinds[k][1] for k in outs]
        ),
    )(table, *operands)


def run_weight(facts, stack, grads, scale):
    bricks, voxels, _ = grads.shape
    out = jax.ShapeDtypeStruct((2, 14, C, C), jnp.bfloat16)
    return pl.pallas_call(
        functools.partial(weight_kernel, scale),
        grid=(EDGE + 2,),
        in_specs=[
            pl.BlockSpec(memory_space=pltpu.SMEM),
            pl.BlockSpec((bricks, 1, SLAB, TAPS), lambda a: (0, a, 0, 0)),
            whole(grads),
        ],
        out_specs=whole(out),
        out_shape=out,
        scratch_shapes=[
            pltpu.VMEM((EDGE + 4, C, bricks * SLAB), jnp.bfloat16),
            pltpu.VMEM((3 * C, TAPS), jnp.float32),
        ],
        compiler_params=pltpu.CompilerParams(
            dimension_semantics=("arbitrary",), vmem_limit_bytes=VMEM_LIMIT
        ),
        cost_estimate=cost(2 * 27 * bricks * voxels * C * C, [stack, grads, out]),
    )(facts, stack, grads)


def beside(low, high):
    count = lax.axis_size("space")
    left = lax.ppermute(high, "space", [(i, i + 1) for i in range(count - 1)])
    right = lax.ppermute(low, "space", [(i + 1, i) for i in range(count - 1)])
    return left, right


def summed(halves):
    count = lax.axis_size("space")
    members = count // 2
    swap = [(i, i ^ 1) for i in range(count)]
    groups = [[i for i in range(count) if i % 2 == b] for b in range(2)]
    received = lax.ppermute(halves[0], "space", swap)
    half = (halves[1].astype(jnp.float32) + received.astype(jnp.float32)).astype(jnp.bfloat16)
    parts = half.reshape(members, -1, C)
    parts = lax.all_to_all(parts, "space", 0, 0, axis_index_groups=groups, tiled=True)
    part = jnp.sum(parts.astype(jnp.float32), axis=0).astype(jnp.bfloat16)
    parts = jnp.broadcast_to(part[None], (members,) + part.shape)
    parts = lax.all_to_all(parts, "space", 0, 0, axis_index_groups=groups, tiled=True)
    half = parts.reshape(14, C, C)
    other = lax.ppermute(half, "space", swap)
    even = lax.axis_index("space") % 2 == 0
    first = jnp.where(even, half, other).astype(jnp.float32)
    second = jnp.where(even, other, half).astype(jnp.float32)
    return jnp.concatenate([first, second[:13]], axis=0), second[13, 0, 0]


def column_body(feats, mask, neighbours, weight_one, weight_two, cotangent):
    bricks, voxels, channels = feats.shape
    my_index = lax.axis_index("space")
    steps = jnp.array([s for s, _ in DIRECTIONS], jnp.int32)
    local = neighbours - (my_index + steps)[None, :] * (TILE * WIDE)
    inside = (local >= 0) & (local < bricks) & (neighbours >= 0)
    strays = jnp.any((neighbours >= 0) & ~inside).astype(jnp.int32)
    facts = jnp.stack([strays, my_index % 2])
    table = jnp.where(inside, local, -1)
    spread_mask = jnp.broadcast_to(mask.astype(jnp.bfloat16)[:, :, None], feats.shape)
    scale = 1.0 / math.sqrt(voxels * bricks)

    inputs = feats * spread_mask
    in_left, in_right = beside(inputs[:, :SLAB], inputs[:, voxels - SLAB :])
    pre, hidden, low, high, in_stack = run_conv(
        first_kernel, table, inputs, in_left, in_right, weight_one,
        [spread_mask], [], ("pair", "rows", "edge", "edge", "stack"),
    )
    h_left, h_right = beside(low, high)
    output, grad_second, low, high, h_stack = run_conv(
        second_kernel, table, hidden, h_left, h_right, weight_two,
        [spread_mask, cotangent], [], ("rows", "rows", "edge", "edge", "stack"),
    )
    s_left, s_right = beside(low, high)
    term_two = run_weight(facts, h_stack, grad_second, scale)
    term_two, s_left, s_right = lax.optimization_barrier((term_two, s_left, s_right))
    grad_w2, strays = summed(term_two)
    grad_first, low, high = run_conv(
        third_kernel, table, grad_second, s_left, s_right, weight_two,
        [spread_mask], [pre], ("rows", "edge", "edge"),
    )
    term_one = run_weight(facts, in_stack, grad_first, scale)
    term_one, low, high = lax.optimization_barrier((term_one, low, high))
    grad_w1, _ = summed(term_one)
    f_left, f_right = beside(low, high)
    (grad_input,) = run_conv(
        fourth_kernel, table, grad_first, f_left, f_right, weight_one,
        [spread_mask], [], ("rows",),
    )
    return strays, (output, grad_input, grad_w1, grad_w2)


def body(*arguments):
    strays, results = column_body(*arguments)

    def again(state):
        return jnp.zeros_like(state[0]), general_body(*arguments)

    return lax.while_loop(lambda state: state[0] > 0.5, again, (strays, results))[1]


def padded_2(cells, sides, width):
    for axis, dim in sides:
        count = lax.axis_size(axis)
        ends = count - 1
        head = lax.slice_in_dim(cells, 0, width, axis=dim)
        tail = lax.slice_in_dim(cells, cells.shape[dim] - width, cells.shape[dim], axis=dim)
        cells = jnp.concatenate(
            [
                lax.ppermute(tail, axis, [(i, (i + 1) % count) for i in range(ends)]),
                cells,
                lax.ppermute(head, axis, [((i + 1) % count, i) for i in range(ends)]),
            ],
            axis=dim,
        )
    return cells


def rim_slices(step_value, length):
    if step_value < 0:
        return (slice(length - 1, length), slice(0, 1))
    if step_value > 0:
        return (slice(0, 1), slice(length + 1, length + 2))
    return (slice(0, length), slice(1, length + 1))


def assemble(cube_view, sources, source_index):
    length = cube_view.shape[1]
    padded = jnp.pad(cube_view, ((0, 0), (1, 1), (1, 1), (1, 1), (0, 0)))
    for column, (step_x, step_y) in enumerate(DIRECTIONS):
        source_x, target_x = rim_slices(step_x, length)
        source_y, target_y = rim_slices(step_y, length)
        rim_cells = sources[:, source_x, source_y]
        fetched = jnp.take(rim_cells, source_index[:, column], axis=0)
        padded = padded.at[:, target_x, target_y, 1 : length + 1].set(fetched)
    return padded


def window_stack(padded, shift_x, flipped):
    length = padded.shape[1] - 2
    channels = padded.shape[-1]
    pieces = []
    for shift_y in range(3):
        for shift_z in range(3):
            if flipped:
                corner_x, corner_y, corner_z = (2 - shift_x, 2 - shift_y, 2 - shift_z)
            else:
                corner_x, corner_y, corner_z = (shift_x, shift_y, shift_z)
            cells = padded[
                :,
                corner_x : corner_x + length,
                corner_y : corner_y + length,
                corner_z : corner_z + length,
            ]
            pieces.append(cells.reshape(-1, channels))
    return jnp.concatenate(pieces, axis=1)


def convolve(padded, weight, flipped):
    channels = padded.shape[-1]
    summed = None
    for shift_x in range(3):
        stacked = window_stack(padded, shift_x, flipped)
        weight_block = weight[9 * shift_x : 9 * shift_x + 9]
        if flipped:
            weight_block = jnp.swapaxes(weight_block, 1, 2)
        partial_sum = jnp.dot(
            stacked,
            weight_block.reshape(9 * channels, channels),
            preferred_element_type=jnp.float32,
        )
        summed = partial_sum if summed is None else summed + partial_sum
    return summed


def weight_grad(padded, grads):
    channels = padded.shape[-1]
    blocks = []
    for shift_x in range(3):
        stacked = window_stack(padded, shift_x, False)
        product = lax.dot_general(
            stacked, grads, (((0,), (0,)), ((), ())), preferred_element_type=jnp.float32
        )
        blocks.append(product.reshape(9, channels, channels))
    return jnp.concatenate(blocks, axis=0)


def silu_slope(values):
    sigmoid_value = jax.nn.sigmoid(values)
    return sigmoid_value * (1.0 + values * (1.0 - sigmoid_value))


def in_halves(term):
    halves = jnp.pad(term.astype(jnp.bfloat16), ((0, 1), (0, 0), (0, 0))).reshape(2, 14, C, C)
    return jnp.where(lax.axis_index("space") % 2 == 0, halves[::-1], halves)


def general_body(feats, mask, neighbours, weight_one, weight_two, cotangent):
    bricks, voxels, channels = feats.shape
    my_index = lax.axis_index("space")
    first_brick = (my_index * TILE - 1) * WIDE
    source_index = jnp.where(neighbours >= 0, neighbours - first_brick, (TILE + 2) * WIDE)
    occupied = mask.reshape(-1, 1).astype(jnp.float32)
    blank_brick = jnp.zeros((1, EDGE, EDGE, EDGE, channels), jnp.bfloat16)

    def join_sources(cube_view, left_side, right_side):
        sources = jnp.concatenate([left_side, cube_view, right_side, blank_brick], axis=0)
        return assemble(cube_view, sources, source_index)

    def extend_bricks(flat_field, received):
        cube_view = flat_field.reshape(bricks, EDGE, EDGE, EDGE, channels)
        left_side = received[0].reshape(WIDE, EDGE, EDGE, EDGE, channels)
        right_side = received[TILE + 1].reshape(WIDE, EDGE, EDGE, EDGE, channels)
        return join_sources(cube_view, left_side, right_side)

    def as_tiles(flat_field):
        return flat_field.reshape(TILE, WIDE, voxels, channels)

    inputs = feats * mask[:, :, None].astype(jnp.bfloat16)
    padded_in = extend_bricks(inputs, padded_2(as_tiles(inputs), (("space", 0),), 1))
    first_pre = convolve(padded_in, weight_one, False)
    hidden = (
        (occupied * jax.nn.silu(first_pre)).astype(jnp.bfloat16).reshape(bricks, voxels, channels)
    )
    padded_hidden = extend_bricks(hidden, padded_2(as_tiles(hidden), (("space", 0),), 1))
    second_pre = convolve(padded_hidden, weight_two, False)
    output = (occupied * jax.nn.silu(second_pre)).astype(jnp.bfloat16)
    grad_second = (
        cotangent.reshape(-1, channels).astype(jnp.float32) * occupied * silu_slope(second_pre)
    ).astype(jnp.bfloat16)
    grad_second_view = grad_second.reshape(bricks, voxels, channels)
    padded_second = extend_bricks(
        grad_second_view, padded_2(as_tiles(grad_second_view), (("space", 0),), 1)
    )
    back_second = convolve(padded_second, weight_two, True)
    grad_first = (occupied * silu_slope(first_pre) * back_second).astype(jnp.bfloat16)
    grad_scale = 1.0 / math.sqrt(voxels * bricks)
    grad_w2 = weight_grad(padded_hidden, grad_second) * grad_scale
    grad_w2, _ = summed(in_halves(grad_w2))
    grad_first_view = grad_first.reshape(bricks, voxels, channels)
    padded_first = extend_bricks(
        grad_first_view, padded_2(as_tiles(grad_first_view), (("space", 0),), 1)
    )
    grad_input = (occupied * convolve(padded_first, weight_one, True)).astype(jnp.bfloat16)
    grad_w1 = weight_grad(padded_in, grad_first) * grad_scale
    grad_w1, _ = summed(in_halves(grad_w1))
    return (
        output.reshape(bricks, voxels, channels),
        grad_input.reshape(bricks, voxels, channels),
        grad_w1,
        grad_w2,
    )


def solution(mesh):
    in_specs = (
        P(("scene", "space"), None, None),
        P(("scene", "space"), None),
        P(("scene", "space"), None),
        P(),
        P(),
        P(("scene", "space"), None, None),
    )
    out_specs = (
        P(("scene", "space"), None, None),
        P(("scene", "space"), None, None),
        P("scene", None, None),
        P("scene", None, None),
    )
    return jax.shard_map(body, mesh=mesh, in_specs=in_specs, out_specs=out_specs, check_vma=False)
```

```python
import functools
import math

import jax
import jax.numpy as jnp
from jax import lax
from jax.experimental import pallas as pl
from jax.experimental.pallas import tpu as pltpu
from jax.sharding import PartitionSpec as P

EDGE = 8
TILE = 1
WIDE = 8
SLAB = EDGE * EDGE
C = 128
TAPS = 9 * C
VMEM_LIMIT = 56 * 1024 * 1024

DIRECTIONS = ((-1, -1), (-1, 0), (-1, 1), (0, -1), (0, 1), (1, -1), (1, 0), (1, 1))


def picked(source, index, first, rows):
    found = source[jnp.maximum(index, 0), first : first + rows, :].astype(jnp.float32)
    return jnp.where(index >= 0, found, 0.0)


def slab_tiles(centre, top, bottom):
    cells = jnp.concatenate([top[8:16], centre, bottom[0:8]], axis=0).reshape(EDGE + 2, EDGE, C)
    place = lax.broadcasted_iota(jnp.int32, cells.shape, 1)
    below = jnp.where(place == 0, 0.0, pltpu.roll(cells, 1, 1))
    above = jnp.where(place == EDGE - 1, 0.0, pltpu.roll(cells, EDGE - 1, 1))
    even, odd = [], []
    for shifted in (below, cells, above):
        even.append(shifted.reshape((EDGE + 2) * EDGE, C).astype(jnp.bfloat16))
        odd.append(shifted[1 : EDGE + 1].reshape(SLAB, C).astype(jnp.bfloat16))
    return [e[0:SLAB] for e in even] + odd + [e[16 : 16 + SLAB] for e in even]


def build_stack(table, field, left, right, stack):
    bricks = field.shape[0]

    @pl.loop(0, bricks)
    def _(g):
        for a in range(EDGE + 2):
            if a == 0:
                source, first, near = left, 0, (table[g, 1], table[g, 0], table[g, 2])
            elif a == EDGE + 1:
                source, first, near = right, 0, (table[g, 6], table[g, 5], table[g, 7])
            else:
                source, first, near = field, (a - 1) * SLAB, (g, table[g, 3], table[g, 4])
            if source is field:
                centre = field[g, first : first + SLAB, :].astype(jnp.float32)
            else:
                centre = picked(source, near[0], first, SLAB)
            top = picked(source, near[1], first + SLAB - 16, 16)
            bottom = picked(source, near[2], first, 16)
            for t, tile in enumerate(slab_tiles(centre, top, bottom)):
                stack[g, a, :, t * C : (t + 1) * C] = tile


def fill_weights(weights, turned, filled):
    for half in range(2):
        columns = slice(half * C, (half + 1) * C)
        for j in range(4):
            k1 = j - half
            for t in range(9):
                first = j * TAPS + t * C
                if not 0 <= k1 <= 2:
                    block = jnp.zeros((C, C), jnp.bfloat16)
                elif turned:
                    block = weights[26 - 9 * k1 - t].astype(jnp.float32).T.astype(jnp.bfloat16)
                else:
                    block = weights[9 * k1 + t]
                filled[first : first + C, columns] = block


def prepare(turned, table, field, left, right, weights, stack, filled):
    @pl.when(pl.program_id(0) == 0)
    def _():
        fill_weights(weights, turned, filled)
        build_stack(table, field, left, right, stack)


def pair_product(stack, weights, pair):
    bricks = stack.shape[0]
    rows = [stack[:, 2 * pair + j].reshape(bricks * SLAB, TAPS) for j in range(4)]
    return jnp.dot(
        jnp.concatenate(rows, axis=1), weights[...], preferred_element_type=jnp.float32
    )


def spread(values, bricks):
    return values.reshape(bricks, SLAB, C)


def slope_of(values):
    s = jax.nn.sigmoid(values)
    return s * (1.0 + values * (1.0 - s))


def put(result, low, high, half, values):
    result[:, half * SLAB : (half + 1) * SLAB, :] = values
    if half == 0 and low is not None:

        @pl.when(pl.program_id(0) == 0)
        def _():
            low[...] = values

    if half == 1 and high is not None:

        @pl.when(pl.program_id(0) == EDGE // 2 - 1)
        def _():
            high[...] = values


def first_kernel(
    table, field, left, right, weights, mask, pre, hidden, low, high, stack, filled
):
    pair = pl.program_id(0)
    bricks = field.shape[0]

    prepare(False, table, field, left, right, weights, stack, filled)
    both = pair_product(stack, filled, pair)
    pre[0] = both
    for half in range(2):
        values = both[:, half * C : (half + 1) * C]
        occupied = mask[:, half * SLAB : (half + 1) * SLAB, :].astype(jnp.float32)
        active = spread(values * jax.nn.sigmoid(values), bricks)
        put(hidden, low, high, half, (occupied * active).astype(jnp.bfloat16))


def second_kernel(
    table, field, left, right, weights, mask, cotangent, output, grad, low, high, stack, filled
):
    pair = pl.program_id(0)
    bricks = field.shape[0]

    prepare(False, table, field, left, right, weights, stack, filled)
    both = pair_product(stack, filled, pair)
    for half in range(2):
        values = both[:, half * C : (half + 1) * C]
        rows = slice(half * SLAB, (half + 1) * SLAB)
        occupied = mask[:, rows, :].astype(jnp.float32)
        s = jax.nn.sigmoid(values)
        output[:, rows, :] = (occupied * spread(values * s, bricks)).astype(jnp.bfloat16)
        slope = spread(s * (1.0 + values * (1.0 - s)), bricks)
        received = cotangent[:, rows, :].astype(jnp.float32)
        put(grad, low, high, half, (received * occupied * slope).astype(jnp.bfloat16))


def third_kernel(table, field, left, right, weights, mask, pre, grad, low, high, stack, filled):
    pair = pl.program_id(0)
    bricks = field.shape[0]

    prepare(True, table, field, left, right, weights, stack, filled)
    both = pair_product(stack, filled, pair)
    for half in range(2):
        columns = slice(half * C, (half + 1) * C)
        occupied = mask[:, half * SLAB : (half + 1) * SLAB, :].astype(jnp.float32)
        slope = slope_of(pre[0, :, columns])
        product = spread(slope * both[:, columns], bricks)
        put(grad, low, high, half, (occupied * product).astype(jnp.bfloat16))


def fourth_kernel(table, field, left, right, weights, mask, grad, stack, filled):
    pair = pl.program_id(0)
    bricks = field.shape[0]

    prepare(True, table, field, left, right, weights, stack, filled)
    both = pair_product(stack, filled, pair)
    for half in range(2):
        occupied = mask[:, half * SLAB : (half + 1) * SLAB, :].astype(jnp.float32)
        values = spread(both[:, half * C : (half + 1) * C], bricks)
        put(grad, None, None, half, (occupied * values).astype(jnp.bfloat16))


def weight_kernel(scale, table, facts, field, left, right, grads, sent, kept, stack, turned, total):
    bricks = grads.shape[0]
    build_stack(table, field, left, right, stack)
    for a in range(EDGE):
        slab = grads[:, a * SLAB : (a + 1) * SLAB, :].reshape(bricks * SLAB, C)
        turned[a] = slab.astype(jnp.float32).T.astype(jnp.bfloat16)
    total[...] = jnp.zeros_like(total)

    def add(a, first, last):
        lhs = [turned[a - k1] for k1 in range(first, last)]
        lhs = lhs[0] if len(lhs) == 1 else jnp.concatenate(lhs, axis=0)
        product = jnp.dot(
            lhs,
            stack[:, a].reshape(bricks * SLAB, TAPS),
            preferred_element_type=jnp.float32,
        )
        total[first * C : last * C, :] += product

    add(0, 0, 1)
    add(1, 0, 2)

    @pl.loop(2, EDGE)
    def _(a):
        add(a, 0, 3)

    add(EDGE, 1, 3)
    add(EDGE + 1, 2, 3)

    def put_halves(first, second):
        for n in range(28):
            if n == 27:
                block = jnp.full((C, C), facts[0], jnp.int32).astype(jnp.float32)
            else:
                k1, t = n // 9, n % 9
                block = total[k1 * C : (k1 + 1) * C, t * C : (t + 1) * C].T * scale
            half = first if n < 14 else second
            half[n % 14] = block.astype(jnp.bfloat16)

    @pl.when(facts[1] == 0)
    def _():
        put_halves(kept, sent)

    @pl.when(facts[1] == 1)
    def _():
        put_halves(sent, kept)


def cost(flops, arrays):
    return pl.CostEstimate(
        flops=flops,
        bytes_accessed=sum(math.prod(a.shape) * a.dtype.itemsize for a in arrays),
        transcendentals=0,
    )


def whole(array):
    return pl.BlockSpec(array.shape, lambda i, n=len(array.shape): (0,) * n)


def run_conv(kernel, table, field, left, right, weights, by_rows, by_pair, outs):
    bricks, voxels, _ = field.shape
    pairs = EDGE // 2
    rows_spec = pl.BlockSpec((bricks, 2 * SLAB, C), lambda i: (0, i, 0))
    pair_spec = pl.BlockSpec((1, bricks * SLAB, 2 * C), lambda i: (i, 0, 0))
    edge_spec = pl.BlockSpec((bricks, SLAB, C), lambda i: (0, 0, 0))
    kinds = {
        "rows": (rows_spec, jax.ShapeDtypeStruct((bricks, voxels, C), jnp.bfloat16)),
        "pair": (pair_spec, jax.ShapeDtypeStruct((pairs, bricks * SLAB, 2 * C), jnp.float32)),
        "edge": (edge_spec, jax.ShapeDtypeStruct((bricks, SLAB, C), jnp.bfloat16)),
    }
    operands = [field, left, right, weights, *by_rows, *by_pair]
    return pl.pallas_call(
        kernel,
        grid=(pairs,),
        in_specs=[
            pl.BlockSpec(memory_space=pltpu.SMEM),
            *[whole(a) for a in (field, left, right, weights)],
            *[rows_spec for _ in by_rows],
            *[pair_spec for _ in by_pair],
        ],
        out_specs=[kinds[k][0] for k in outs],
        out_shape=[kinds[k][1] for k in outs],
        scratch_shapes=[
            pltpu.VMEM((bricks, EDGE + 2, SLAB, TAPS), jnp.bfloat16),
            pltpu.VMEM((4 * TAPS, 2 * C), jnp.bfloat16),
        ],
        compiler_params=pltpu.CompilerParams(
            dimension_semantics=("arbitrary",), vmem_limit_bytes=VMEM_LIMIT
        ),
        cost_estimate=cost(
            2 * 36 * bricks * voxels * C * C, operands + [kinds[k][1] for k in outs]
        ),
    )(table, *operands)


def run_weight(table, facts, field, left, right, grads, scale):
    bricks, voxels, _ = field.shape
    half = jax.ShapeDtypeStruct((14, C, C), jnp.bfloat16)
    return pl.pallas_call(
        functools.partial(weight_kernel, scale),
        in_specs=[
            *[pl.BlockSpec(memory_space=pltpu.SMEM)] * 2,
            *[pl.BlockSpec(memory_space=pltpu.VMEM)] * 4,
        ],
        out_specs=[pl.BlockSpec(memory_space=pltpu.VMEM)] * 2,
        out_shape=[half, half],
        scratch_shapes=[
            pltpu.VMEM((bricks, EDGE + 2, SLAB, TAPS), jnp.bfloat16),
            pltpu.VMEM((EDGE, C, bricks * SLAB), jnp.bfloat16),
            pltpu.VMEM((3 * C, TAPS), jnp.float32),
        ],
        compiler_params=pltpu.CompilerParams(vmem_limit_bytes=VMEM_LIMIT),
        cost_estimate=cost(2 * 27 * bricks * voxels * C * C, [field, left, right, grads, half, half]),
    )(table, facts, field, left, right, grads)


def beside(low, high):
    count = lax.axis_size("space")
    left = lax.ppermute(high, "space", [(i, i + 1) for i in range(count - 1)])
    right = lax.ppermute(low, "space", [(i + 1, i) for i in range(count - 1)])
    return left, right


def swapped(half):
    count = lax.axis_size("space")
    return lax.ppermute(half, "space", [(i, i ^ 1) for i in range(count)])


def among(parts):
    count = lax.axis_size("space")
    groups = [[i for i in range(count) if i % 2 == b] for b in range(2)]
    return lax.all_to_all(parts, "space", 0, 0, axis_index_groups=groups, tiled=True)


def pair_sum(sent, kept):
    total = kept.astype(jnp.float32) + swapped(sent).astype(jnp.float32)
    return total.astype(jnp.bfloat16)


def part_sum(half):
    parts = among(half.reshape(lax.axis_size("space") // 2, -1, C))
    return jnp.sum(parts.astype(jnp.float32), axis=0).astype(jnp.bfloat16)


def gathered(part):
    members = lax.axis_size("space") // 2
    return among(jnp.broadcast_to(part[None], (members,) + part.shape)).reshape(14, C, C)


def joined(half):
    other = swapped(half)
    even = lax.axis_index("space") % 2 == 0
    first = jnp.where(even, half, other)
    second = jnp.where(even, other, half)
    blocks = jnp.concatenate([first, second[:13]], axis=0).astype(jnp.float32)
    return blocks, second[13, 0, 0].astype(jnp.float32)


def column_body(feats, mask, neighbours, weight_one, weight_two, cotangent):
    bricks, voxels, channels = feats.shape
    my_index = lax.axis_index("space")
    steps = jnp.array([s for s, _ in DIRECTIONS], jnp.int32)
    local = neighbours - (my_index + steps)[None, :] * (TILE * WIDE)
    inside = (local >= 0) & (local < bricks) & (neighbours >= 0)
    strays = jnp.any((neighbours >= 0) & ~inside).astype(jnp.int32)
    facts = jnp.stack([strays, my_index % 2])
    table = jnp.where(inside, local, -1)
    spread_mask = jnp.broadcast_to(mask.astype(jnp.bfloat16)[:, :, None], feats.shape)
    scale = 1.0 / math.sqrt(voxels * bricks)

    inputs = feats * spread_mask
    in_left, in_right = beside(inputs[:, :SLAB], inputs[:, voxels - SLAB :])
    together = lax.optimization_barrier
    pre, hidden, low, high = run_conv(
        first_kernel, table, inputs, in_left, in_right, weight_one,
        [spread_mask], [], ("pair", "rows", "edge", "edge"),
    )
    h_left, h_right = beside(low, high)
    output, grad_second, low, high = run_conv(
        second_kernel, table, hidden, h_left, h_right, weight_two,
        [spread_mask, cotangent], [], ("rows", "rows", "edge", "edge"),
    )
    s_left, s_right = beside(low, high)
    sent, kept = run_weight(table, facts, hidden, h_left, h_right, grad_second, scale)
    sent, s_left, s_right = together((sent, s_left, s_right))
    half_two = pair_sum(sent, kept)
    grad_first, low, high = run_conv(
        third_kernel, table, grad_second, s_left, s_right, weight_two,
        [spread_mask], [pre], ("rows", "edge", "edge"),
    )
    half_two, grad_first = together((half_two, grad_first))
    part_two = part_sum(half_two)
    sent, kept = run_weight(table, facts, inputs, in_left, in_right, grad_first, scale)
    sent, low, high = together((sent, low, high))
    half_one = pair_sum(sent, kept)
    half_two = gathered(part_two)
    f_left, f_right = beside(low, high)
    half_one, half_two = together((half_one, half_two))
    part_one = part_sum(half_one)
    (grad_input,) = run_conv(
        fourth_kernel, table, grad_first, f_left, f_right, weight_one,
        [spread_mask], [], ("rows",),
    )
    part_one, grad_input = together((part_one, grad_input))
    grad_w1, _ = joined(gathered(part_one))
    grad_w2, strays = joined(half_two)
    return strays, (output, grad_input, grad_w1, grad_w2)


def body(*arguments):
    strays, results = column_body(*arguments)

    def again(state):
        return jnp.zeros_like(state[0]), general_body(*arguments)

    return lax.while_loop(lambda state: state[0] > 0.5, again, (strays, results))[1]


def padded_2(cells, sides, width):
    for axis, dim in sides:
        count = lax.axis_size(axis)
        ends = count - 1
        head = lax.slice_in_dim(cells, 0, width, axis=dim)
        tail = lax.slice_in_dim(cells, cells.shape[dim] - width, cells.shape[dim], axis=dim)
        cells = jnp.concatenate(
            [
                lax.ppermute(tail, axis, [(i, (i + 1) % count) for i in range(ends)]),
                cells,
                lax.ppermute(head, axis, [((i + 1) % count, i) for i in range(ends)]),
            ],
            axis=dim,
        )
    return cells


def rim_slices(step_value, length):
    if step_value < 0:
        return (slice(length - 1, length), slice(0, 1))
    if step_value > 0:
        return (slice(0, 1), slice(length + 1, length + 2))
    return (slice(0, length), slice(1, length + 1))


def assemble(cube_view, sources, source_index):
    length = cube_view.shape[1]
    padded = jnp.pad(cube_view, ((0, 0), (1, 1), (1, 1), (1, 1), (0, 0)))
    for column, (step_x, step_y) in enumerate(DIRECTIONS):
        source_x, target_x = rim_slices(step_x, length)
        source_y, target_y = rim_slices(step_y, length)
        rim_cells = sources[:, source_x, source_y]
        fetched = jnp.take(rim_cells, source_index[:, column], axis=0)
        padded = padded.at[:, target_x, target_y, 1 : length + 1].set(fetched)
    return padded


def window_stack(padded, shift_x, flipped):
    length = padded.shape[1] - 2
    channels = padded.shape[-1]
    pieces = []
    for shift_y in range(3):
        for shift_z in range(3):
            if flipped:
                corner_x, corner_y, corner_z = (2 - shift_x, 2 - shift_y, 2 - shift_z)
            else:
                corner_x, corner_y, corner_z = (shift_x, shift_y, shift_z)
            cells = padded[
                :,
                corner_x : corner_x + length,
                corner_y : corner_y + length,
                corner_z : corner_z + length,
            ]
            pieces.append(cells.reshape(-1, channels))
    return jnp.concatenate(pieces, axis=1)


def convolve(padded, weight, flipped):
    channels = padded.shape[-1]
    summed = None
    for shift_x in range(3):
        stacked = window_stack(padded, shift_x, flipped)
        weight_block = weight[9 * shift_x : 9 * shift_x + 9]
        if flipped:
            weight_block = jnp.swapaxes(weight_block, 1, 2)
        partial_sum = jnp.dot(
            stacked,
            weight_block.reshape(9 * channels, channels),
            preferred_element_type=jnp.float32,
        )
        summed = partial_sum if summed is None else summed + partial_sum
    return summed


def weight_grad(padded, grads):
    channels = padded.shape[-1]
    blocks = []
    for shift_x in range(3):
        stacked = window_stack(padded, shift_x, False)
        product = lax.dot_general(
            stacked, grads, (((0,), (0,)), ((), ())), preferred_element_type=jnp.float32
        )
        blocks.append(product.reshape(9, channels, channels))
    return jnp.concatenate(blocks, axis=0)


def silu_slope(values):
    sigmoid_value = jax.nn.sigmoid(values)
    return sigmoid_value * (1.0 + values * (1.0 - sigmoid_value))


def general_sum(term):
    halves = jnp.pad(term.astype(jnp.bfloat16), ((0, 1), (0, 0), (0, 0))).reshape(2, 14, C, C)
    even = lax.axis_index("space") % 2 == 0
    sent = jnp.where(even, halves[1], halves[0])
    kept = jnp.where(even, halves[0], halves[1])
    return joined(gathered(part_sum(pair_sum(sent, kept))))[0]


def general_body(feats, mask, neighbours, weight_one, weight_two, cotangent):
    bricks, voxels, channels = feats.shape
    my_index = lax.axis_index("space")
    first_brick = (my_index * TILE - 1) * WIDE
    source_index = jnp.where(neighbours >= 0, neighbours - first_brick, (TILE + 2) * WIDE)
    occupied = mask.reshape(-1, 1).astype(jnp.float32)
    blank_brick = jnp.zeros((1, EDGE, EDGE, EDGE, channels), jnp.bfloat16)

    def join_sources(cube_view, left_side, right_side):
        sources = jnp.concatenate([left_side, cube_view, right_side, blank_brick], axis=0)
        return assemble(cube_view, sources, source_index)

    def extend_bricks(flat_field, received):
        cube_view = flat_field.reshape(bricks, EDGE, EDGE, EDGE, channels)
        left_side = received[0].reshape(WIDE, EDGE, EDGE, EDGE, channels)
        right_side = received[TILE + 1].reshape(WIDE, EDGE, EDGE, EDGE, channels)
        return join_sources(cube_view, left_side, right_side)

    def as_tiles(flat_field):
        return flat_field.reshape(TILE, WIDE, voxels, channels)

    inputs = feats * mask[:, :, None].astype(jnp.bfloat16)
    padded_in = extend_bricks(inputs, padded_2(as_tiles(inputs), (("space", 0),), 1))
    first_pre = convolve(padded_in, weight_one, False)
    hidden = (
        (occupied * jax.nn.silu(first_pre)).astype(jnp.bfloat16).reshape(bricks, voxels, channels)
    )
    padded_hidden = extend_bricks(hidden, padded_2(as_tiles(hidden), (("space", 0),), 1))
    second_pre = convolve(padded_hidden, weight_two, False)
    output = (occupied * jax.nn.silu(second_pre)).astype(jnp.bfloat16)
    grad_second = (
        cotangent.reshape(-1, channels).astype(jnp.float32) * occupied * silu_slope(second_pre)
    ).astype(jnp.bfloat16)
    grad_second_view = grad_second.reshape(bricks, voxels, channels)
    padded_second = extend_bricks(
        grad_second_view, padded_2(as_tiles(grad_second_view), (("space", 0),), 1)
    )
    back_second = convolve(padded_second, weight_two, True)
    grad_first = (occupied * silu_slope(first_pre) * back_second).astype(jnp.bfloat16)
    grad_scale = 1.0 / math.sqrt(voxels * bricks)
    grad_w2 = weight_grad(padded_hidden, grad_second) * grad_scale
    grad_w2 = general_sum(grad_w2)
    grad_first_view = grad_first.reshape(bricks, voxels, channels)
    padded_first = extend_bricks(
        grad_first_view, padded_2(as_tiles(grad_first_view), (("space", 0),), 1)
    )
    grad_input = (occupied * convolve(padded_first, weight_one, True)).astype(jnp.bfloat16)
    grad_w1 = weight_grad(padded_in, grad_first) * grad_scale
    grad_w1 = general_sum(grad_w1)
    return (
        output.reshape(bricks, voxels, channels),
        grad_input.reshape(bricks, voxels, channels),
        grad_w1,
        grad_w2,
    )


def solution(mesh):
    in_specs = (
        P(("scene", "space"), None, None),
        P(("scene", "space"), None),
        P(("scene", "space"), None),
        P(),
        P(),
        P(("scene", "space"), None, None),
    )
    out_specs = (
        P(("scene", "space"), None, None),
        P(("scene", "space"), None, None),
        P("scene", None, None),
        P("scene", None, None),
    )
    return jax.shard_map(body, mesh=mesh, in_specs=in_specs, out_specs=out_specs, check_vma=False)
```

```python
import functools
import math

import jax
import jax.numpy as jnp
from jax import lax
from jax.experimental import pallas as pl
from jax.experimental.pallas import tpu as pltpu
from jax.sharding import PartitionSpec as P

EDGE = 8
TILE = 1
WIDE = 8
SLAB = EDGE * EDGE
C = 128
TAPS = 9 * C
VMEM_LIMIT = 56 * 1024 * 1024

DIRECTIONS = ((-1, -1), (-1, 0), (-1, 1), (0, -1), (0, 1), (1, -1), (1, 0), (1, 1))


def picked(source, index, first, rows):
    found = source[jnp.maximum(index, 0), first : first + rows, :].astype(jnp.float32)
    return jnp.where(index >= 0, found, 0.0)


def slab_tiles(centre, top, bottom):
    cells = jnp.concatenate([top[8:16], centre, bottom[0:8]], axis=0).reshape(EDGE + 2, EDGE, C)
    place = lax.broadcasted_iota(jnp.int32, cells.shape, 1)
    below = jnp.where(place == 0, 0.0, pltpu.roll(cells, 1, 1))
    above = jnp.where(place == EDGE - 1, 0.0, pltpu.roll(cells, EDGE - 1, 1))
    even, odd = [], []
    for shifted in (below, cells, above):
        even.append(shifted.reshape((EDGE + 2) * EDGE, C).astype(jnp.bfloat16))
        odd.append(shifted[1 : EDGE + 1].reshape(SLAB, C).astype(jnp.bfloat16))
    return [e[0:SLAB] for e in even] + odd + [e[16 : 16 + SLAB] for e in even]


def build_stack(table, field, left, right, stack):
    bricks = field.shape[0]

    @pl.loop(0, bricks)
    def _(g):
        for a in range(EDGE + 2):
            if a == 0:
                source, first, near = left, 0, (table[g, 1], table[g, 0], table[g, 2])
            elif a == EDGE + 1:
                source, first, near = right, 0, (table[g, 6], table[g, 5], table[g, 7])
            else:
                source, first, near = field, (a - 1) * SLAB, (g, table[g, 3], table[g, 4])
            if source is field:
                centre = field[g, first : first + SLAB, :].astype(jnp.float32)
            else:
                centre = picked(source, near[0], first, SLAB)
            top = picked(source, near[1], first + SLAB - 16, 16)
            bottom = picked(source, near[2], first, 16)
            for t, tile in enumerate(slab_tiles(centre, top, bottom)):
                stack[g, a, :, t * C : (t + 1) * C] = tile


def fill_weights(weights, turned, filled):
    for half in range(2):
        columns = slice(half * C, (half + 1) * C)
        for j in range(4):
            k1 = j - half
            for t in range(9):
                first = j * TAPS + t * C
                if not 0 <= k1 <= 2:
                    block = jnp.zeros((C, C), jnp.bfloat16)
                elif turned:
                    block = weights[26 - 9 * k1 - t].astype(jnp.float32).T.astype(jnp.bfloat16)
                else:
                    block = weights[9 * k1 + t]
                filled[first : first + C, columns] = block


def prepare(turned, table, field, left, right, weights, stack, filled):
    @pl.when(pl.program_id(0) == 0)
    def _():
        fill_weights(weights, turned, filled)
        build_stack(table, field, left, right, stack)


def pair_product(stack, weights, pair):
    bricks = stack.shape[0]
    rows = [stack[:, 2 * pair + j].reshape(bricks * SLAB, TAPS) for j in range(4)]
    return jnp.dot(
        jnp.concatenate(rows, axis=1), weights[...], preferred_element_type=jnp.float32
    )


def spread(values, bricks):
    return values.reshape(bricks, SLAB, C)


def slope_of(values):
    s = jax.nn.sigmoid(values)
    return s * (1.0 + values * (1.0 - s))


def put(result, low, high, half, values):
    result[:, half * SLAB : (half + 1) * SLAB, :] = values
    if half == 0 and low is not None:

        @pl.when(pl.program_id(0) == 0)
        def _():
            low[...] = values

    if half == 1 and high is not None:

        @pl.when(pl.program_id(0) == EDGE // 2 - 1)
        def _():
            high[...] = values


def first_kernel(
    table, field, left, right, weights, mask, pre, hidden, low, high, stack, filled
):
    pair = pl.program_id(0)
    bricks = field.shape[0]

    prepare(False, table, field, left, right, weights, stack, filled)
    both = pair_product(stack, filled, pair)
    pre[0] = both
    for half in range(2):
        values = both[:, half * C : (half + 1) * C]
        occupied = mask[:, half * SLAB : (half + 1) * SLAB, :].astype(jnp.float32)
        active = spread(values * jax.nn.sigmoid(values), bricks)
        put(hidden, low, high, half, (occupied * active).astype(jnp.bfloat16))


def second_kernel(
    table, field, left, right, weights, mask, cotangent, output, grad, low, high, stack, filled
):
    pair = pl.program_id(0)
    bricks = field.shape[0]

    prepare(False, table, field, left, right, weights, stack, filled)
    both = pair_product(stack, filled, pair)
    for half in range(2):
        values = both[:, half * C : (half + 1) * C]
        rows = slice(half * SLAB, (half + 1) * SLAB)
        occupied = mask[:, rows, :].astype(jnp.float32)
        s = jax.nn.sigmoid(values)
        output[:, rows, :] = (occupied * spread(values * s, bricks)).astype(jnp.bfloat16)
        slope = spread(s * (1.0 + values * (1.0 - s)), bricks)
        received = cotangent[:, rows, :].astype(jnp.float32)
        put(grad, low, high, half, (received * occupied * slope).astype(jnp.bfloat16))


def third_kernel(table, field, left, right, weights, mask, pre, grad, low, high, stack, filled):
    pair = pl.program_id(0)
    bricks = field.shape[0]

    prepare(True, table, field, left, right, weights, stack, filled)
    both = pair_product(stack, filled, pair)
    for half in range(2):
        columns = slice(half * C, (half + 1) * C)
        occupied = mask[:, half * SLAB : (half + 1) * SLAB, :].astype(jnp.float32)
        slope = slope_of(pre[0, :, columns])
        product = spread(slope * both[:, columns], bricks)
        put(grad, low, high, half, (occupied * product).astype(jnp.bfloat16))


def fourth_kernel(table, field, left, right, weights, mask, grad, stack, filled):
    pair = pl.program_id(0)
    bricks = field.shape[0]

    prepare(True, table, field, left, right, weights, stack, filled)
    both = pair_product(stack, filled, pair)
    for half in range(2):
        occupied = mask[:, half * SLAB : (half + 1) * SLAB, :].astype(jnp.float32)
        values = spread(both[:, half * C : (half + 1) * C], bricks)
        put(grad, None, None, half, (occupied * values).astype(jnp.bfloat16))


def weight_kernel(scale, table, facts, field, left, right, grads, *rest):
    *outs, stack, turned, total, blocks = rest
    bricks = grads.shape[0]
    build_stack(table, field, left, right, stack)
    for a in range(EDGE):
        slab = grads[:, a * SLAB : (a + 1) * SLAB, :].reshape(bricks * SLAB, C)
        turned[a] = slab.astype(jnp.float32).T.astype(jnp.bfloat16)
    total[...] = jnp.zeros_like(total)

    def add(a, first, last):
        lhs = [turned[a - k1] for k1 in range(first, last)]
        lhs = lhs[0] if len(lhs) == 1 else jnp.concatenate(lhs, axis=0)
        product = jnp.dot(
            lhs,
            stack[:, a].reshape(bricks * SLAB, TAPS),
            preferred_element_type=jnp.float32,
        )
        total[first * C : last * C, :] += product

    add(0, 0, 1)
    add(1, 0, 2)

    @pl.loop(2, EDGE)
    def _(a):
        add(a, 0, 3)

    add(EDGE, 1, 3)
    add(EDGE + 1, 2, 3)
    for n in range(27):
        k1, t = n // 9, n % 9
        block = total[k1 * C : (k1 + 1) * C, t * C : (t + 1) * C].T * scale
        blocks[n * C : (n + 1) * C, :] = block.astype(jnp.bfloat16)
    blocks[27 * C :, :] = jnp.full((C, C), facts[0], jnp.int32).astype(jnp.float32).astype(jnp.bfloat16)
    n = 1
    for out in outs:
        for piece in range(out.shape[0]):
            first = pl.multiple_of(facts[n], 16)
            out[piece] = blocks[pl.ds(first, out.shape[1]), :]
            n += 1


def join_kernel(places, *rest):
    *pieces, result, blocks, arrived = rest
    for n, piece in enumerate(pieces):
        first = pl.multiple_of(places[n], 16)
        blocks[pl.ds(first, piece.shape[0]), :] = piece[...].astype(jnp.float32)
    copy = pltpu.make_async_copy(blocks.at[pl.ds(0, 27 * C)], result, arrived)
    copy.start()
    copy.wait()


def cost(flops, arrays):
    return pl.CostEstimate(
        flops=flops,
        bytes_accessed=sum(math.prod(a.shape) * a.dtype.itemsize for a in arrays),
        transcendentals=0,
    )


def whole(array):
    return pl.BlockSpec(array.shape, lambda i, n=len(array.shape): (0,) * n)


def run_conv(kernel, table, field, left, right, weights, by_rows, by_pair, outs):
    bricks, voxels, _ = field.shape
    pairs = EDGE // 2
    rows_spec = pl.BlockSpec((bricks, 2 * SLAB, C), lambda i: (0, i, 0))
    pair_spec = pl.BlockSpec((1, bricks * SLAB, 2 * C), lambda i: (i, 0, 0))
    edge_spec = pl.BlockSpec((bricks, SLAB, C), lambda i: (0, 0, 0))
    kinds = {
        "rows": (rows_spec, jax.ShapeDtypeStruct((bricks, voxels, C), jnp.bfloat16)),
        "pair": (pair_spec, jax.ShapeDtypeStruct((pairs, bricks * SLAB, 2 * C), jnp.float32)),
        "edge": (edge_spec, jax.ShapeDtypeStruct((bricks, SLAB, C), jnp.bfloat16)),
    }
    operands = [field, left, right, weights, *by_rows, *by_pair]
    return pl.pallas_call(
        kernel,
        grid=(pairs,),
        in_specs=[
            pl.BlockSpec(memory_space=pltpu.SMEM),
            *[whole(a) for a in (field, left, right, weights)],
            *[rows_spec for _ in by_rows],
            *[pair_spec for _ in by_pair],
        ],
        out_specs=[kinds[k][0] for k in outs],
        out_shape=[kinds[k][1] for k in outs],
        scratch_shapes=[
            pltpu.VMEM((bricks, EDGE + 2, SLAB, TAPS), jnp.bfloat16),
            pltpu.VMEM((4 * TAPS, 2 * C), jnp.bfloat16),
        ],
        compiler_params=pltpu.CompilerParams(
            dimension_semantics=("arbitrary",), vmem_limit_bytes=VMEM_LIMIT
        ),
        cost_estimate=cost(
            2 * 36 * bricks * voxels * C * C, operands + [kinds[k][1] for k in outs]
        ),
    )(table, *operands)


def run_weight(table, facts, field, left, right, grads, scale, shapes):
    bricks, voxels, _ = field.shape
    outs = [jax.ShapeDtypeStruct((*shape, C), jnp.bfloat16) for shape in shapes]
    return pl.pallas_call(
        functools.partial(weight_kernel, scale),
        in_specs=[
            *[pl.BlockSpec(memory_space=pltpu.SMEM)] * 2,
            *[pl.BlockSpec(memory_space=pltpu.VMEM)] * 4,
        ],
        out_specs=[pl.BlockSpec(memory_space=pltpu.VMEM) for _ in outs],
        out_shape=outs,
        scratch_shapes=[
            pltpu.VMEM((bricks, EDGE + 2, SLAB, TAPS), jnp.bfloat16),
            pltpu.VMEM((EDGE, C, bricks * SLAB), jnp.bfloat16),
            pltpu.VMEM((3 * C, TAPS), jnp.float32),
            pltpu.VMEM((28 * C, C), jnp.bfloat16),
        ],
        compiler_params=pltpu.CompilerParams(vmem_limit_bytes=VMEM_LIMIT),
        cost_estimate=cost(2 * 27 * bricks * voxels * C * C, [field, left, right, grads, *outs]),
    )(table, facts, field, left, right, grads)


def run_join(places, pieces):
    out = jax.ShapeDtypeStruct((27 * C, C), jnp.float32)
    return pl.pallas_call(
        join_kernel,
        in_specs=[
            pl.BlockSpec(memory_space=pltpu.SMEM),
            *[pl.BlockSpec(memory_space=pltpu.VMEM) for _ in pieces],
        ],
        out_specs=pl.BlockSpec(memory_space=pl.ANY),
        out_shape=out,
        scratch_shapes=[pltpu.VMEM((28 * C, C), jnp.float32), pltpu.SemaphoreType.DMA],
        compiler_params=pltpu.CompilerParams(vmem_limit_bytes=VMEM_LIMIT),
        cost_estimate=cost(0, [out, *pieces]),
    )(places, *pieces).reshape(27, C, C)


def beside(low, high):
    count = lax.axis_size("space")
    left = lax.ppermute(high, "space", [(i, i + 1) for i in range(count - 1)])
    right = lax.ppermute(low, "space", [(i + 1, i) for i in range(count - 1)])
    return left, right


def across(values, mask):
    count = lax.axis_size("space")
    return lax.ppermute(values, "space", [(i, i ^ mask) for i in range(count)])


def swapped(half):
    return across(half, 1)


def among(parts):
    count = lax.axis_size("space")
    groups = [[i for i in range(count) if i % 2 == b] for b in range(2)]
    return lax.all_to_all(parts, "space", 0, 0, axis_index_groups=groups, tiled=True)


def pair_sum(sent, kept):
    total = kept.astype(jnp.float32) + swapped(sent).astype(jnp.float32)
    return total.astype(jnp.bfloat16)


def part_sum(half):
    parts = among(half.reshape(lax.axis_size("space") // 2, -1, C))
    return jnp.sum(parts.astype(jnp.float32), axis=0).astype(jnp.bfloat16)


def gathered(part):
    members = lax.axis_size("space") // 2
    return among(jnp.broadcast_to(part[None], (members,) + part.shape)).reshape(14, C, C)


def joined(half):
    other = swapped(half)
    even = lax.axis_index("space") % 2 == 0
    first = jnp.where(even, half, other)
    second = jnp.where(even, other, half)
    blocks = jnp.concatenate([first, second[:13]], axis=0).astype(jnp.float32)
    return blocks, second[13, 0, 0].astype(jnp.float32)


def column_body(feats, mask, neighbours, weight_one, weight_two, cotangent):
    bricks, voxels, channels = feats.shape
    my_index = lax.axis_index("space")
    low, high = (
        feats[:, rows] * mask[:, rows, None].astype(jnp.bfloat16)
        for rows in (slice(0, SLAB), slice(voxels - SLAB, voxels))
    )
    in_left, in_right = beside(low, high)
    steps = jnp.array([s for s, _ in DIRECTIONS], jnp.int32)
    local = neighbours - (my_index + steps)[None, :] * (TILE * WIDE)
    inside = (local >= 0) & (local < bricks) & (neighbours >= 0)
    table = jnp.where(inside, local, -1)
    strays = jnp.any((neighbours >= 0) & ~inside).astype(jnp.int32)
    spread_mask = jnp.broadcast_to(mask.astype(jnp.bfloat16)[:, :, None], feats.shape)
    inputs = feats * spread_mask
    scale = 1.0 / math.sqrt(voxels * bricks)

    members = lax.axis_size("space") // 2
    bit, row = my_index % 2, my_index // 2
    rows = 28 * C // (2 * members)
    order = [*range(members // 2, members), *range(members // 2)]
    own = [(bit * members + (row ^ m)) * rows for m in range(members)]
    others = [((1 - bit) * members + (row ^ m)) * rows for m in range(members)]
    half_facts = jnp.stack([strays, (1 - bit) * 14 * C, bit * 14 * C])
    part_facts = jnp.stack([strays, *[others[m] for m in order], *[own[m] for m in order]])
    places = jnp.stack([*own, *others])
    together = lax.optimization_barrier
    in_left, in_right, inputs, spread_mask, table, half_facts, part_facts, places = together(
        (in_left, in_right, inputs, spread_mask, table, half_facts, part_facts, places)
    )

    pre, hidden, low, high = run_conv(
        first_kernel, table, inputs, in_left, in_right, weight_one,
        [spread_mask], [], ("pair", "rows", "edge", "edge"),
    )
    h_left, h_right = beside(low, high)
    output, grad_second, low, high = run_conv(
        second_kernel, table, hidden, h_left, h_right, weight_two,
        [spread_mask, cotangent], [], ("rows", "rows", "edge", "edge"),
    )
    s_left, s_right = beside(low, high)
    sent, kept = run_weight(
        table, half_facts, hidden, h_left, h_right, grad_second, scale, [(1, 14 * C)] * 2
    )
    sent, s_left, s_right = together((sent, s_left, s_right))
    half_two = pair_sum(sent, kept)
    grad_first, low, high = run_conv(
        third_kernel, table, grad_second, s_left, s_right, weight_two,
        [spread_mask], [pre], ("rows", "edge", "edge"),
    )
    half_two, grad_first = together((half_two, grad_first))
    part_two = part_sum(half_two)
    far = members - members // 2
    sent_far, sent_near, kept = run_weight(
        table, part_facts, inputs, in_left, in_right, grad_first, scale,
        [(far, rows), (members // 2, rows), (members, rows)],
    )
    sent_far, sent_near, low, high = together((sent_far, sent_near, low, high))
    received = {
        m: piece[n]
        for piece, masks in ((swapped(sent_far), order[:far]), (swapped(sent_near), order[far:]))
        for n, m in enumerate(masks)
    }
    f_left, f_right = beside(low, high)
    half_two = gathered(part_two)

    def summed(m):
        return kept[order.index(m)].astype(jnp.float32) + received[m].astype(jnp.float32)

    halves = [summed(m).astype(jnp.bfloat16) for m in order if m]
    *halves, f_left, f_right = together((*halves, f_left, f_right))
    arrived = [across(half, 2 * m) for half, m in zip(halves, [m for m in order if m])]
    (grad_input,) = run_conv(
        fourth_kernel, table, grad_first, f_left, f_right, weight_one,
        [spread_mask], [], ("rows",),
    )
    *arrived, grad_input = together((*arrived, grad_input))
    part = summed(0)
    for half in arrived:
        part = part + half.astype(jnp.float32)
    part = part.astype(jnp.bfloat16)
    same = {0: part} | {m: across(part, 2 * m) for m in order if m}
    other = {m: swapped(same[m]) for m in range(members)}
    grad_w1 = run_join(places, [parts[m] for parts in (same, other) for m in range(members)])
    grad_w2, strays = joined(half_two)
    return strays, (output, grad_input, grad_w1, grad_w2)


def body(*arguments):
    strays, results = column_body(*arguments)

    def again(state):
        return jnp.zeros_like(state[0]), general_body(*arguments)

    return lax.while_loop(lambda state: state[0] > 0.5, again, (strays, results))[1]


def padded_2(cells, sides, width):
    for axis, dim in sides:
        count = lax.axis_size(axis)
        ends = count - 1
        head = lax.slice_in_dim(cells, 0, width, axis=dim)
        tail = lax.slice_in_dim(cells, cells.shape[dim] - width, cells.shape[dim], axis=dim)
        cells = jnp.concatenate(
            [
                lax.ppermute(tail, axis, [(i, (i + 1) % count) for i in range(ends)]),
                cells,
                lax.ppermute(head, axis, [((i + 1) % count, i) for i in range(ends)]),
            ],
            axis=dim,
        )
    return cells


def rim_slices(step_value, length):
    if step_value < 0:
        return (slice(length - 1, length), slice(0, 1))
    if step_value > 0:
        return (slice(0, 1), slice(length + 1, length + 2))
    return (slice(0, length), slice(1, length + 1))


def assemble(cube_view, sources, source_index):
    length = cube_view.shape[1]
    padded = jnp.pad(cube_view, ((0, 0), (1, 1), (1, 1), (1, 1), (0, 0)))
    for column, (step_x, step_y) in enumerate(DIRECTIONS):
        source_x, target_x = rim_slices(step_x, length)
        source_y, target_y = rim_slices(step_y, length)
        rim_cells = sources[:, source_x, source_y]
        fetched = jnp.take(rim_cells, source_index[:, column], axis=0)
        padded = padded.at[:, target_x, target_y, 1 : length + 1].set(fetched)
    return padded


def window_stack(padded, shift_x, flipped):
    length = padded.shape[1] - 2
    channels = padded.shape[-1]
    pieces = []
    for shift_y in range(3):
        for shift_z in range(3):
            if flipped:
                corner_x, corner_y, corner_z = (2 - shift_x, 2 - shift_y, 2 - shift_z)
            else:
                corner_x, corner_y, corner_z = (shift_x, shift_y, shift_z)
            cells = padded[
                :,
                corner_x : corner_x + length,
                corner_y : corner_y + length,
                corner_z : corner_z + length,
            ]
            pieces.append(cells.reshape(-1, channels))
    return jnp.concatenate(pieces, axis=1)


def convolve(padded, weight, flipped):
    channels = padded.shape[-1]
    summed = None
    for shift_x in range(3):
        stacked = window_stack(padded, shift_x, flipped)
        weight_block = weight[9 * shift_x : 9 * shift_x + 9]
        if flipped:
            weight_block = jnp.swapaxes(weight_block, 1, 2)
        partial_sum = jnp.dot(
            stacked,
            weight_block.reshape(9 * channels, channels),
            preferred_element_type=jnp.float32,
        )
        summed = partial_sum if summed is None else summed + partial_sum
    return summed


def weight_grad(padded, grads):
    channels = padded.shape[-1]
    blocks = []
    for shift_x in range(3):
        stacked = window_stack(padded, shift_x, False)
        product = lax.dot_general(
            stacked, grads, (((0,), (0,)), ((), ())), preferred_element_type=jnp.float32
        )
        blocks.append(product.reshape(9, channels, channels))
    return jnp.concatenate(blocks, axis=0)


def silu_slope(values):
    sigmoid_value = jax.nn.sigmoid(values)
    return sigmoid_value * (1.0 + values * (1.0 - sigmoid_value))


def general_sum(term):
    halves = jnp.pad(term.astype(jnp.bfloat16), ((0, 1), (0, 0), (0, 0))).reshape(2, 14, C, C)
    even = lax.axis_index("space") % 2 == 0
    sent = jnp.where(even, halves[1], halves[0])
    kept = jnp.where(even, halves[0], halves[1])
    return joined(gathered(part_sum(pair_sum(sent, kept))))[0]


def general_body(feats, mask, neighbours, weight_one, weight_two, cotangent):
    bricks, voxels, channels = feats.shape
    my_index = lax.axis_index("space")
    first_brick = (my_index * TILE - 1) * WIDE
    source_index = jnp.where(neighbours >= 0, neighbours - first_brick, (TILE + 2) * WIDE)
    occupied = mask.reshape(-1, 1).astype(jnp.float32)
    blank_brick = jnp.zeros((1, EDGE, EDGE, EDGE, channels), jnp.bfloat16)

    def join_sources(cube_view, left_side, right_side):
        sources = jnp.concatenate([left_side, cube_view, right_side, blank_brick], axis=0)
        return assemble(cube_view, sources, source_index)

    def extend_bricks(flat_field, received):
        cube_view = flat_field.reshape(bricks, EDGE, EDGE, EDGE, channels)
        left_side = received[0].reshape(WIDE, EDGE, EDGE, EDGE, channels)
        right_side = received[TILE + 1].reshape(WIDE, EDGE, EDGE, EDGE, channels)
        return join_sources(cube_view, left_side, right_side)

    def as_tiles(flat_field):
        return flat_field.reshape(TILE, WIDE, voxels, channels)

    inputs = feats * mask[:, :, None].astype(jnp.bfloat16)
    padded_in = extend_bricks(inputs, padded_2(as_tiles(inputs), (("space", 0),), 1))
    first_pre = convolve(padded_in, weight_one, False)
    hidden = (
        (occupied * jax.nn.silu(first_pre)).astype(jnp.bfloat16).reshape(bricks, voxels, channels)
    )
    padded_hidden = extend_bricks(hidden, padded_2(as_tiles(hidden), (("space", 0),), 1))
    second_pre = convolve(padded_hidden, weight_two, False)
    output = (occupied * jax.nn.silu(second_pre)).astype(jnp.bfloat16)
    grad_second = (
        cotangent.reshape(-1, channels).astype(jnp.float32) * occupied * silu_slope(second_pre)
    ).astype(jnp.bfloat16)
    grad_second_view = grad_second.reshape(bricks, voxels, channels)
    padded_second = extend_bricks(
        grad_second_view, padded_2(as_tiles(grad_second_view), (("space", 0),), 1)
    )
    back_second = convolve(padded_second, weight_two, True)
    grad_first = (occupied * silu_slope(first_pre) * back_second).astype(jnp.bfloat16)
    grad_scale = 1.0 / math.sqrt(voxels * bricks)
    grad_w2 = weight_grad(padded_hidden, grad_second) * grad_scale
    grad_w2 = general_sum(grad_w2)
    grad_first_view = grad_first.reshape(bricks, voxels, channels)
    padded_first = extend_bricks(
        grad_first_view, padded_2(as_tiles(grad_first_view), (("space", 0),), 1)
    )
    grad_input = (occupied * convolve(padded_first, weight_one, True)).astype(jnp.bfloat16)
    grad_w1 = weight_grad(padded_in, grad_first) * grad_scale
    grad_w1 = general_sum(grad_w1)
    return (
        output.reshape(bricks, voxels, channels),
        grad_input.reshape(bricks, voxels, channels),
        grad_w1,
        grad_w2,
    )


def solution(mesh):
    in_specs = (
        P(("scene", "space"), None, None),
        P(("scene", "space"), None),
        P(("scene", "space"), None),
        P(),
        P(),
        P(("scene", "space"), None, None),
    )
    out_specs = (
        P(("scene", "space"), None, None),
        P(("scene", "space"), None, None),
        P("scene", None, None),
        P("scene", None, None),
    )
    return jax.shard_map(body, mesh=mesh, in_specs=in_specs, out_specs=out_specs, check_vma=False)
```

```python
import functools
import math

import jax
import jax.numpy as jnp
from jax import lax
from jax.experimental import pallas as pl
from jax.experimental.pallas import tpu as pltpu
from jax.sharding import PartitionSpec as P

EDGE = 8
TILE = 1
WIDE = 8
SLAB = EDGE * EDGE
C = 128
TAPS = 9 * C
VMEM_LIMIT = 56 * 1024 * 1024

DIRECTIONS = ((-1, -1), (-1, 0), (-1, 1), (0, -1), (0, 1), (1, -1), (1, 0), (1, 1))


def entry(facts, neighbours, brick, column):
    named = neighbours[brick, column]
    local = named - (facts[0] + DIRECTIONS[column][0]) * (TILE * WIDE)
    inside = (named >= 0) & (local >= 0) & (local < neighbours.shape[0])
    return jnp.where(inside, local, -1)


def picked(source, index, first, rows):
    found = source[jnp.maximum(index, 0), first : first + rows, :].astype(jnp.float32)
    return jnp.where(index >= 0, found, 0.0)


def slab_tiles(centre, top, bottom):
    cells = jnp.concatenate([top[8:16], centre, bottom[0:8]], axis=0).reshape(EDGE + 2, EDGE, C)
    place = lax.broadcasted_iota(jnp.int32, cells.shape, 1)
    below = jnp.where(place == 0, 0.0, pltpu.roll(cells, 1, 1))
    above = jnp.where(place == EDGE - 1, 0.0, pltpu.roll(cells, EDGE - 1, 1))
    even, odd = [], []
    for shifted in (below, cells, above):
        even.append(shifted.reshape((EDGE + 2) * EDGE, C).astype(jnp.bfloat16))
        odd.append(shifted[1 : EDGE + 1].reshape(SLAB, C).astype(jnp.bfloat16))
    return [e[0:SLAB] for e in even] + odd + [e[16 : 16 + SLAB] for e in even]


def build_slab(facts, neighbours, field, left, right, a, stack):
    for g in range(field.shape[0]):
        near = functools.partial(entry, facts, neighbours, g)
        if a == 0:
            source, first, names = left, 0, (near(1), near(0), near(2))
        elif a == EDGE + 1:
            source, first, names = right, 0, (near(6), near(5), near(7))
        else:
            source, first, names = field, (a - 1) * SLAB, (g, near(3), near(4))
        if source is field:
            centre = field[g, first : first + SLAB, :].astype(jnp.float32)
        else:
            centre = picked(source, names[0], first, SLAB)
        top = picked(source, names[1], first + SLAB - 16, 16)
        bottom = picked(source, names[2], first, 16)
        for t, tile in enumerate(slab_tiles(centre, top, bottom)):
            stack[g, :, t * C : (t + 1) * C] = tile


def fill_weights(weights, turned, filled):
    blank = jnp.zeros((C, C), jnp.bfloat16)
    for k1 in range(3):
        for t in range(9):
            block = weights[26 - 9 * k1 - t if turned else 9 * k1 + t]
            if turned:
                block = block.astype(jnp.float32).T.astype(jnp.bfloat16)
            for half in range(2):
                first = (k1 + half) * TAPS + t * C
                filled[first : first + C, half * C : (half + 1) * C] = block
    for t in range(9):
        filled[t * C : (t + 1) * C, C:] = blank
        filled[3 * TAPS + t * C : 3 * TAPS + (t + 1) * C, 0:C] = blank


def spread(values, bricks):
    return values.reshape(bricks, SLAB, C)


def conv_kernel(finish, turned, n_in, n_out, n_edge, facts, neighbours, *rest):
    n_ops, n_res = 4 + n_in, n_out + n_edge
    operands, rest = rest[:n_ops], rest[n_ops:]
    results, rest = rest[:n_res], rest[n_res:]
    local, rest = rest[:n_ops], rest[n_ops:]
    made, rest = rest[:n_res], rest[n_res:]
    stack, filled, came, gone = rest[: EDGE + 2], rest[-3], rest[-2], rest[-1]
    field, left, right, weights = local[:4]
    bricks = field.shape[0]
    copies = [
        pltpu.make_async_copy(there, here, came.at[n])
        for n, (there, here) in enumerate(zip(operands, local))
    ]
    for copy in copies:
        copy.start()
    for copy in copies[:3]:
        copy.wait()
    for a in range(4):
        build_slab(facts, neighbours, field, left, right, a, stack[a])
    copies[3].wait()
    fill_weights(weights, turned, filled)
    for copy in copies[4:]:
        copy.wait()
    leaving = []
    for pair in range(EDGE // 2):
        for a in (2 * pair + 4, 2 * pair + 5):
            if a < EDGE + 2:
                build_slab(facts, neighbours, field, left, right, a, stack[a])
        lhs = [stack[2 * pair + n][...].reshape(bricks * SLAB, TAPS) for n in range(4)]
        both = jnp.dot(
            jnp.concatenate(lhs, axis=1), filled[...], preferred_element_type=jnp.float32
        )
        for half in range(2):
            rows = slice((2 * pair + half) * SLAB, (2 * pair + half + 1) * SLAB)
            values = spread(both[:, half * C : (half + 1) * C], bricks)
            values = finish(values, *[array[:, rows, :].astype(jnp.float32) for array in local[4:]])
            for array, value in zip(made, values):
                array[:, rows, :] = value.astype(jnp.bfloat16)
            if n_edge and pair == 0 and half == 0:
                made[n_out][...] = values[-1].astype(jnp.bfloat16)
            if n_edge and pair == EDGE // 2 - 1 and half == 1:
                made[n_out + 1][...] = values[-1].astype(jnp.bfloat16)
        ready = [(n, pl.ds(2 * pair * SLAB, 2 * SLAB)) for n in range(n_out)]
        if n_edge and pair in (0, EDGE // 2 - 1):
            ready.append((n_out + (pair > 0), pl.ds(0, SLAB)))
        for n, rows in ready:
            copy = pltpu.make_async_copy(
                made[n].at[:, rows, :], results[n].at[:, rows, :], gone.at[len(leaving)]
            )
            copy.start()
            leaving.append(copy)
    for copy in leaving:
        copy.wait()


def finish_first(values, mask):
    s = jax.nn.sigmoid(values)
    return mask * (s * (1.0 + values * (1.0 - s))), mask * (values * s)


def finish_second(values, mask, cotangent):
    s = jax.nn.sigmoid(values)
    return mask * (values * s), cotangent * mask * (s * (1.0 + values * (1.0 - s)))


def finish_product(values, factor):
    return (factor * values,)


def weight_kernel(scale, counted, facts, neighbours, field, left, right, grads, *rest):
    outs, rest = rest[: -(EDGE + 5)], rest[-(EDGE + 5) :]
    stack, turned, total, blocks = rest[: EDGE + 2], rest[-3], rest[-2], rest[-1]
    bricks = grads.shape[0]

    def turn(a):
        slab = grads[:, a * SLAB : (a + 1) * SLAB, :].reshape(bricks * SLAB, C)
        turned[a] = slab.astype(jnp.float32).T.astype(jnp.bfloat16)

    build_slab(facts, neighbours, field, left, right, 0, stack[0])
    turn(0)
    for a in range(EDGE + 2):
        if a < EDGE + 1:
            build_slab(facts, neighbours, field, left, right, a + 1, stack[a + 1])
        if a < EDGE - 1:
            turn(a + 1)
        first, last = max(0, a - EDGE + 1), min(3, a + 1)
        lhs = [turned[a - k1] for k1 in range(first, last)]
        product = jnp.dot(
            lhs[0] if len(lhs) == 1 else jnp.concatenate(lhs, axis=0),
            stack[a][...].reshape(bricks * SLAB, TAPS),
            preferred_element_type=jnp.float32,
        )
        for n, k1 in enumerate(range(first, last)):
            rows, part = slice(k1 * C, (k1 + 1) * C), product[n * C : (n + 1) * C]
            total[rows, :] = part if a == k1 else total[rows, :] + part
    for n in range(27):
        k1, t = n // 9, n % 9
        block = total[k1 * C : (k1 + 1) * C, t * C : (t + 1) * C].T * scale
        blocks[n * C : (n + 1) * C, :] = block.astype(jnp.bfloat16)
    strays = 0
    for g in range(bricks if counted else 0):
        for column in range(len(DIRECTIONS)):
            lost = (neighbours[g, column] >= 0) & (entry(facts, neighbours, g, column) < 0)
            strays = strays + jnp.where(lost, 1, 0)
    strays = jnp.full((C, C), jnp.minimum(strays, 1), jnp.int32)
    blocks[27 * C :, :] = strays.astype(jnp.float32).astype(jnp.bfloat16)
    n = 1
    for out in outs:
        for piece in range(out.shape[0]):
            first = pl.multiple_of(facts[n], 16)
            out[piece] = blocks[pl.ds(first, out.shape[1]), :]
            n += 1


def join_kernel(places, *rest):
    *pieces, result, blocks, arrived = rest
    for n, piece in enumerate(pieces):
        first = pl.multiple_of(places[n], 16)
        blocks[pl.ds(first, piece.shape[0]), :] = piece[...].astype(jnp.float32)
    copy = pltpu.make_async_copy(blocks.at[pl.ds(0, 27 * C)], result, arrived)
    copy.start()
    copy.wait()


def cost(flops, arrays):
    return pl.CostEstimate(
        flops=flops,
        bytes_accessed=sum(math.prod(a.shape) * a.dtype.itemsize for a in arrays),
        transcendentals=0,
    )


def run_conv(finish, turned, facts, neighbours, field, left, right, weights, by_rows, n_out, n_edge):
    bricks, voxels, _ = field.shape
    rows = jax.ShapeDtypeStruct((bricks, voxels, C), jnp.bfloat16)
    edge = jax.ShapeDtypeStruct((bricks, SLAB, C), jnp.bfloat16)
    operands = [field, left, right, weights, *by_rows]
    outs = [rows] * n_out + [edge] * n_edge
    stack = pltpu.VMEM((bricks, SLAB, TAPS), jnp.bfloat16)
    return pl.pallas_call(
        functools.partial(conv_kernel, finish, turned, len(by_rows), n_out, n_edge),
        in_specs=[
            *[pl.BlockSpec(memory_space=pltpu.SMEM)] * 2,
            *[pl.BlockSpec(memory_space=pl.ANY) for _ in operands],
        ],
        out_specs=[pl.BlockSpec(memory_space=pl.ANY) for _ in outs],
        out_shape=outs,
        scratch_shapes=[
            *[pltpu.VMEM(a.shape, a.dtype) for a in operands + outs],
            *[stack] * (EDGE + 2),
            pltpu.VMEM((4 * TAPS, 2 * C), jnp.bfloat16),
            pltpu.SemaphoreType.DMA((len(operands),)),
            pltpu.SemaphoreType.DMA((n_out * EDGE // 2 + n_edge,)),
        ],
        compiler_params=pltpu.CompilerParams(vmem_limit_bytes=VMEM_LIMIT),
        cost_estimate=cost(2 * 36 * bricks * voxels * C * C, operands + outs),
    )(facts, neighbours, *operands)


def run_weight(facts, neighbours, field, left, right, grads, scale, shapes, counted):
    bricks, voxels, _ = field.shape
    outs = [jax.ShapeDtypeStruct((*shape, C), jnp.bfloat16) for shape in shapes]
    return pl.pallas_call(
        functools.partial(weight_kernel, scale, counted),
        in_specs=[
            *[pl.BlockSpec(memory_space=pltpu.SMEM)] * 2,
            *[pl.BlockSpec(memory_space=pltpu.VMEM)] * 4,
        ],
        out_specs=[pl.BlockSpec(memory_space=pltpu.VMEM) for _ in outs],
        out_shape=outs,
        scratch_shapes=[
            *[pltpu.VMEM((bricks, SLAB, TAPS), jnp.bfloat16)] * (EDGE + 2),
            pltpu.VMEM((EDGE, C, bricks * SLAB), jnp.bfloat16),
            pltpu.VMEM((3 * C, TAPS), jnp.float32),
            pltpu.VMEM((28 * C, C), jnp.bfloat16),
        ],
        compiler_params=pltpu.CompilerParams(vmem_limit_bytes=VMEM_LIMIT),
        cost_estimate=cost(2 * 27 * bricks * voxels * C * C, [field, left, right, grads, *outs]),
    )(facts, neighbours, field, left, right, grads)


def run_join(places, pieces):
    out = jax.ShapeDtypeStruct((27 * C, C), jnp.float32)
    return pl.pallas_call(
        join_kernel,
        in_specs=[
            pl.BlockSpec(memory_space=pltpu.SMEM),
            *[pl.BlockSpec(memory_space=pltpu.VMEM) for _ in pieces],
        ],
        out_specs=pl.BlockSpec(memory_space=pl.ANY),
        out_shape=out,
        scratch_shapes=[pltpu.VMEM((28 * C, C), jnp.float32), pltpu.SemaphoreType.DMA],
        compiler_params=pltpu.CompilerParams(vmem_limit_bytes=VMEM_LIMIT),
        cost_estimate=cost(0, [out, *pieces]),
    )(places, *pieces).reshape(27, C, C)


def beside(low, high):
    count = lax.axis_size("space")
    left = lax.ppermute(high, "space", [(i, i + 1) for i in range(count - 1)])
    right = lax.ppermute(low, "space", [(i + 1, i) for i in range(count - 1)])
    return left, right


def across(values, mask):
    count = lax.axis_size("space")
    return lax.ppermute(values, "space", [(i, i ^ mask) for i in range(count)])


def swapped(half):
    return across(half, 1)


def among(parts):
    count = lax.axis_size("space")
    groups = [[i for i in range(count) if i % 2 == b] for b in range(2)]
    return lax.all_to_all(parts, "space", 0, 0, axis_index_groups=groups, tiled=True)


def pair_sum(sent, kept):
    total = kept.astype(jnp.float32) + swapped(sent).astype(jnp.float32)
    return total.astype(jnp.bfloat16)


def part_sum(half):
    parts = among(half.reshape(lax.axis_size("space") // 2, -1, C))
    return jnp.sum(parts.astype(jnp.float32), axis=0).astype(jnp.bfloat16)


def gathered(part):
    members = lax.axis_size("space") // 2
    return among(jnp.broadcast_to(part[None], (members,) + part.shape)).reshape(14, C, C)


def joined(half):
    other = swapped(half)
    even = lax.axis_index("space") % 2 == 0
    first = jnp.where(even, half, other)
    second = jnp.where(even, other, half)
    blocks = jnp.concatenate([first, second[:13]], axis=0).astype(jnp.float32)
    return blocks, second[13, 0, 0].astype(jnp.float32)


def column_body(feats, mask, neighbours, weight_one, weight_two, cotangent):
    bricks, voxels, channels = feats.shape
    my_index = lax.axis_index("space")
    low, high = (
        feats[:, rows] * mask[:, rows, None].astype(jnp.bfloat16)
        for rows in (slice(0, SLAB), slice(voxels - SLAB, voxels))
    )
    in_left, in_right = beside(low, high)
    spread_mask = jnp.broadcast_to(mask.astype(jnp.bfloat16)[:, :, None], feats.shape)
    inputs = feats * spread_mask
    scale = 1.0 / math.sqrt(voxels * bricks)

    members = lax.axis_size("space") // 2
    bit, row = my_index % 2, my_index // 2
    rows = 28 * C // (2 * members)
    order = [*range(members // 2, members), *range(members // 2)]
    own = [(bit * members + (row ^ m)) * rows for m in range(members)]
    others = [((1 - bit) * members + (row ^ m)) * rows for m in range(members)]
    half_facts = jnp.stack([my_index, (1 - bit) * 14 * C, bit * 14 * C])
    part_facts = jnp.stack([my_index, *[others[m] for m in order], *[own[m] for m in order]])
    places = jnp.stack([*own, *others])
    together = lax.optimization_barrier
    in_left, in_right, inputs, spread_mask, half_facts = together(
        (in_left, in_right, inputs, spread_mask, half_facts)
    )

    slope, hidden, low, high = run_conv(
        finish_first, False, half_facts, neighbours, inputs, in_left, in_right, weight_one,
        [spread_mask], 2, 2,
    )
    h_left, h_right = beside(low, high)
    output, grad_second, low, high = run_conv(
        finish_second, False, half_facts, neighbours, hidden, h_left, h_right, weight_two,
        [spread_mask, cotangent], 2, 2,
    )
    s_left, s_right = beside(low, high)
    sent, kept = run_weight(
        half_facts, neighbours, hidden, h_left, h_right, grad_second, scale,
        [(1, 14 * C)] * 2, True,
    )
    sent, s_left, s_right = together((sent, s_left, s_right))
    half_two = pair_sum(sent, kept)
    grad_first, low, high = run_conv(
        finish_product, True, half_facts, neighbours, grad_second, s_left, s_right, weight_two,
        [slope], 1, 2,
    )
    half_two, grad_first = together((half_two, grad_first))
    part_two = part_sum(half_two)
    far = members - members // 2
    sent_far, sent_near, kept = run_weight(
        part_facts, neighbours, inputs, in_left, in_right, grad_first, scale,
        [(far, rows), (members // 2, rows), (members, rows)], False,
    )
    sent_far, sent_near, low, high = together((sent_far, sent_near, low, high))
    received = {
        m: piece[n]
        for piece, masks in ((swapped(sent_far), order[:far]), (swapped(sent_near), order[far:]))
        for n, m in enumerate(masks)
    }
    f_left, f_right = beside(low, high)
    half_two = gathered(part_two)

    def summed(m):
        return kept[order.index(m)].astype(jnp.float32) + received[m].astype(jnp.float32)

    halves = [summed(m).astype(jnp.bfloat16) for m in order if m]
    *halves, f_left, f_right = together((*halves, f_left, f_right))
    arrived = [across(half, 2 * m) for half, m in zip(halves, [m for m in order if m])]
    (grad_input,) = run_conv(
        finish_product, True, half_facts, neighbours, grad_first, f_left, f_right, weight_one,
        [spread_mask], 1, 0,
    )
    *arrived, grad_input = together((*arrived, grad_input))
    part = summed(0)
    for half in arrived:
        part = part + half.astype(jnp.float32)
    part = part.astype(jnp.bfloat16)
    same = {0: part} | {m: across(part, 2 * m) for m in order if m}
    other = {m: swapped(same[m]) for m in range(members)}
    grad_w1 = run_join(places, [parts[m] for parts in (same, other) for m in range(members)])
    grad_w2, strays = joined(half_two)
    return strays, (output, grad_input, grad_w1, grad_w2)


def body(*arguments):
    strays, results = column_body(*arguments)

    def again(state):
        return jnp.zeros_like(state[0]), general_body(*arguments)

    return lax.while_loop(lambda state: state[0] > 0.5, again, (strays, results))[1]


def padded_2(cells, sides, width):
    for axis, dim in sides:
        count = lax.axis_size(axis)
        ends = count - 1
        head = lax.slice_in_dim(cells, 0, width, axis=dim)
        tail = lax.slice_in_dim(cells, cells.shape[dim] - width, cells.shape[dim], axis=dim)
        cells = jnp.concatenate(
            [
                lax.ppermute(tail, axis, [(i, (i + 1) % count) for i in range(ends)]),
                cells,
                lax.ppermute(head, axis, [((i + 1) % count, i) for i in range(ends)]),
            ],
            axis=dim,
        )
    return cells


def rim_slices(step_value, length):
    if step_value < 0:
        return (slice(length - 1, length), slice(0, 1))
    if step_value > 0:
        return (slice(0, 1), slice(length + 1, length + 2))
    return (slice(0, length), slice(1, length + 1))


def assemble(cube_view, sources, source_index):
    length = cube_view.shape[1]
    padded = jnp.pad(cube_view, ((0, 0), (1, 1), (1, 1), (1, 1), (0, 0)))
    for column, (step_x, step_y) in enumerate(DIRECTIONS):
        source_x, target_x = rim_slices(step_x, length)
        source_y, target_y = rim_slices(step_y, length)
        rim_cells = sources[:, source_x, source_y]
        fetched = jnp.take(rim_cells, source_index[:, column], axis=0)
        padded = padded.at[:, target_x, target_y, 1 : length + 1].set(fetched)
    return padded


def window_stack(padded, shift_x, flipped):
    length = padded.shape[1] - 2
    channels = padded.shape[-1]
    pieces = []
    for shift_y in range(3):
        for shift_z in range(3):
            if flipped:
                corner_x, corner_y, corner_z = (2 - shift_x, 2 - shift_y, 2 - shift_z)
            else:
                corner_x, corner_y, corner_z = (shift_x, shift_y, shift_z)
            cells = padded[
                :,
                corner_x : corner_x + length,
                corner_y : corner_y + length,
                corner_z : corner_z + length,
            ]
            pieces.append(cells.reshape(-1, channels))
    return jnp.concatenate(pieces, axis=1)


def convolve(padded, weight, flipped):
    channels = padded.shape[-1]
    summed = None
    for shift_x in range(3):
        stacked = window_stack(padded, shift_x, flipped)
        weight_block = weight[9 * shift_x : 9 * shift_x + 9]
        if flipped:
            weight_block = jnp.swapaxes(weight_block, 1, 2)
        partial_sum = jnp.dot(
            stacked,
            weight_block.reshape(9 * channels, channels),
            preferred_element_type=jnp.float32,
        )
        summed = partial_sum if summed is None else summed + partial_sum
    return summed


def weight_grad(padded, grads):
    channels = padded.shape[-1]
    blocks = []
    for shift_x in range(3):
        stacked = window_stack(padded, shift_x, False)
        product = lax.dot_general(
            stacked, grads, (((0,), (0,)), ((), ())), preferred_element_type=jnp.float32
        )
        blocks.append(product.reshape(9, channels, channels))
    return jnp.concatenate(blocks, axis=0)


def silu_slope(values):
    sigmoid_value = jax.nn.sigmoid(values)
    return sigmoid_value * (1.0 + values * (1.0 - sigmoid_value))


def general_sum(term):
    halves = jnp.pad(term.astype(jnp.bfloat16), ((0, 1), (0, 0), (0, 0))).reshape(2, 14, C, C)
    even = lax.axis_index("space") % 2 == 0
    sent = jnp.where(even, halves[1], halves[0])
    kept = jnp.where(even, halves[0], halves[1])
    return joined(gathered(part_sum(pair_sum(sent, kept))))[0]


def general_body(feats, mask, neighbours, weight_one, weight_two, cotangent):
    bricks, voxels, channels = feats.shape
    my_index = lax.axis_index("space")
    first_brick = (my_index * TILE - 1) * WIDE
    source_index = jnp.where(neighbours >= 0, neighbours - first_brick, (TILE + 2) * WIDE)
    occupied = mask.reshape(-1, 1).astype(jnp.float32)
    blank_brick = jnp.zeros((1, EDGE, EDGE, EDGE, channels), jnp.bfloat16)

    def join_sources(cube_view, left_side, right_side):
        sources = jnp.concatenate([left_side, cube_view, right_side, blank_brick], axis=0)
        return assemble(cube_view, sources, source_index)

    def extend_bricks(flat_field, received):
        cube_view = flat_field.reshape(bricks, EDGE, EDGE, EDGE, channels)
        left_side = received[0].reshape(WIDE, EDGE, EDGE, EDGE, channels)
        right_side = received[TILE + 1].reshape(WIDE, EDGE, EDGE, EDGE, channels)
        return join_sources(cube_view, left_side, right_side)

    def as_tiles(flat_field):
        return flat_field.reshape(TILE, WIDE, voxels, channels)

    inputs = feats * mask[:, :, None].astype(jnp.bfloat16)
    padded_in = extend_bricks(inputs, padded_2(as_tiles(inputs), (("space", 0),), 1))
    first_pre = convolve(padded_in, weight_one, False)
    hidden = (
        (occupied * jax.nn.silu(first_pre)).astype(jnp.bfloat16).reshape(bricks, voxels, channels)
    )
    padded_hidden = extend_bricks(hidden, padded_2(as_tiles(hidden), (("space", 0),), 1))
    second_pre = convolve(padded_hidden, weight_two, False)
    output = (occupied * jax.nn.silu(second_pre)).astype(jnp.bfloat16)
    grad_second = (
        cotangent.reshape(-1, channels).astype(jnp.float32) * occupied * silu_slope(second_pre)
    ).astype(jnp.bfloat16)
    grad_second_view = grad_second.reshape(bricks, voxels, channels)
    padded_second = extend_bricks(
        grad_second_view, padded_2(as_tiles(grad_second_view), (("space", 0),), 1)
    )
    back_second = convolve(padded_second, weight_two, True)
    grad_first = (occupied * silu_slope(first_pre) * back_second).astype(jnp.bfloat16)
    grad_scale = 1.0 / math.sqrt(voxels * bricks)
    grad_w2 = weight_grad(padded_hidden, grad_second) * grad_scale
    grad_w2 = general_sum(grad_w2)
    grad_first_view = grad_first.reshape(bricks, voxels, channels)
    padded_first = extend_bricks(
        grad_first_view, padded_2(as_tiles(grad_first_view), (("space", 0),), 1)
    )
    grad_input = (occupied * convolve(padded_first, weight_one, True)).astype(jnp.bfloat16)
    grad_w1 = weight_grad(padded_in, grad_first) * grad_scale
    grad_w1 = general_sum(grad_w1)
    return (
        output.reshape(bricks, voxels, channels),
        grad_input.reshape(bricks, voxels, channels),
        grad_w1,
        grad_w2,
    )


def solution(mesh):
    in_specs = (
        P(("scene", "space"), None, None),
        P(("scene", "space"), None),
        P(("scene", "space"), None),
        P(),
        P(),
        P(("scene", "space"), None, None),
    )
    out_specs = (
        P(("scene", "space"), None, None),
        P(("scene", "space"), None, None),
        P("scene", None, None),
        P("scene", None, None),
    )
    return jax.shard_map(body, mesh=mesh, in_specs=in_specs, out_specs=out_specs, check_vma=False)
```

```python
import functools
import math

import jax
import jax.numpy as jnp
from jax import lax
from jax.experimental import pallas as pl
from jax.experimental.pallas import tpu as pltpu
from jax.sharding import PartitionSpec as P

EDGE = 8
TILE = 1
WIDE = 8
SLAB = EDGE * EDGE
C = 128
TAPS = 9 * C
VMEM_LIMIT = 36 * 1024 * 1024

DIRECTIONS = ((-1, -1), (-1, 0), (-1, 1), (0, -1), (0, 1), (1, -1), (1, 0), (1, 1))


def entry(facts, neighbours, brick, column):
    named = neighbours[brick, column]
    local = named - (facts[0] + DIRECTIONS[column][0]) * (TILE * WIDE)
    inside = (named >= 0) & (local >= 0) & (local < neighbours.shape[0])
    return jnp.where(inside, local, -1)


def picked(source, index, first, rows):
    found = source[jnp.maximum(index, 0), first : first + rows, :].astype(jnp.float32)
    return jnp.where(index >= 0, found, 0.0)


def slab_tiles(centre, top, bottom):
    cells = jnp.concatenate([top[8:16], centre, bottom[0:8]], axis=0).reshape(EDGE + 2, EDGE, C)
    place = lax.broadcasted_iota(jnp.int32, cells.shape, 1)
    below = jnp.where(place == 0, 0.0, pltpu.roll(cells, 1, 1))
    above = jnp.where(place == EDGE - 1, 0.0, pltpu.roll(cells, EDGE - 1, 1))
    even, odd = [], []
    for shifted in (below, cells, above):
        even.append(shifted.reshape((EDGE + 2) * EDGE, C).astype(jnp.bfloat16))
        odd.append(shifted[1 : EDGE + 1].reshape(SLAB, C).astype(jnp.bfloat16))
    return [e[0:SLAB] for e in even] + odd + [e[16 : 16 + SLAB] for e in even]


def build_slab(facts, neighbours, field, left, right, a, stack):
    for g in range(field.shape[0]):
        near = functools.partial(entry, facts, neighbours, g)
        if a == 0:
            source, first, names = left, 0, (near(1), near(0), near(2))
        elif a == EDGE + 1:
            source, first, names = right, 0, (near(6), near(5), near(7))
        else:
            source, first, names = field, (a - 1) * SLAB, (g, near(3), near(4))
        if source is field:
            centre = field[g, first : first + SLAB, :].astype(jnp.float32)
        else:
            centre = picked(source, names[0], first, SLAB)
        top = picked(source, names[1], first + SLAB - 16, 16)
        bottom = picked(source, names[2], first, 16)
        for t, tile in enumerate(slab_tiles(centre, top, bottom)):
            stack[g, :, t * C : (t + 1) * C] = tile


def fill_weights(weights, turned, filled):
    blank = jnp.zeros((C, C), jnp.bfloat16)
    for k1 in range(3):
        for t in range(9):
            block = weights[26 - 9 * k1 - t if turned else 9 * k1 + t]
            if turned:
                block = block.astype(jnp.float32).T.astype(jnp.bfloat16)
            for half in range(2):
                first = (k1 + half) * TAPS + t * C
                filled[first : first + C, half * C : (half + 1) * C] = block
    for t in range(9):
        filled[t * C : (t + 1) * C, C:] = blank
        filled[3 * TAPS + t * C : 3 * TAPS + (t + 1) * C, 0:C] = blank


def spread(values, bricks):
    return values.reshape(bricks, SLAB, C)


def conv_kernel(finish, turned, masked, n_in, n_out, n_edge, facts, neighbours, *rest):
    n_ops, n_res = 4 + n_in, n_out + n_edge
    operands, rest = rest[:n_ops], rest[n_ops:]
    results, rest = rest[:n_res], rest[n_res:]
    kept, rest = (rest[0], rest[1:]) if masked else (None, rest)
    local, rest = rest[:n_ops], rest[n_ops:]
    made, rest = rest[:n_res], rest[n_res:]
    stack, filled, came, gone = rest[: EDGE + 2], rest[-3], rest[-2], rest[-1]
    field, left, right, weights = local[:4]
    bricks = field.shape[0]
    copies = [
        pltpu.make_async_copy(there, here, came.at[n])
        for n, (there, here) in enumerate(zip(operands, local))
    ]
    for copy in copies:
        copy.start()
    for copy in copies[:3]:
        copy.wait()
    leaving = []
    if masked:
        copies[4].wait()
        field[...] = field[...] * local[4][...]
        leaving.append(pltpu.make_async_copy(field, kept, gone.at[0]))
        leaving[0].start()
    for a in range(4):
        build_slab(facts, neighbours, field, left, right, a, stack[a])
    copies[3].wait()
    fill_weights(weights, turned, filled)
    for copy in copies[5 if masked else 4 :]:
        copy.wait()
    for pair in range(EDGE // 2):
        for a in (2 * pair + 4, 2 * pair + 5):
            if a < EDGE + 2:
                build_slab(facts, neighbours, field, left, right, a, stack[a])
        lhs = [stack[2 * pair + n][...].reshape(bricks * SLAB, TAPS) for n in range(4)]
        both = jnp.dot(
            jnp.concatenate(lhs, axis=1), filled[...], preferred_element_type=jnp.float32
        )
        for half in range(2):
            rows = slice((2 * pair + half) * SLAB, (2 * pair + half + 1) * SLAB)
            values = spread(both[:, half * C : (half + 1) * C], bricks)
            values = finish(values, *[array[:, rows, :].astype(jnp.float32) for array in local[4:]])
            for array, value in zip(made, values):
                array[:, rows, :] = value.astype(jnp.bfloat16)
            if n_edge and pair == 0 and half == 0:
                made[n_out][...] = values[-1].astype(jnp.bfloat16)
            if n_edge and pair == EDGE // 2 - 1 and half == 1:
                made[n_out + 1][...] = values[-1].astype(jnp.bfloat16)
        ready = [(n, pl.ds(2 * pair * SLAB, 2 * SLAB)) for n in range(n_out)]
        if n_edge and pair in (0, EDGE // 2 - 1):
            ready.append((n_out + (pair > 0), pl.ds(0, SLAB)))
        for n, rows in ready:
            copy = pltpu.make_async_copy(
                made[n].at[:, rows, :], results[n].at[:, rows, :], gone.at[len(leaving)]
            )
            copy.start()
            leaving.append(copy)
    for copy in leaving:
        copy.wait()


def finish_first(values, mask):
    s = jax.nn.sigmoid(values)
    return mask * (s * (1.0 + values * (1.0 - s))), mask * (values * s)


def finish_second(values, mask, cotangent):
    s = jax.nn.sigmoid(values)
    return mask * (values * s), cotangent * mask * (s * (1.0 + values * (1.0 - s)))


def finish_product(values, factor):
    return (factor * values,)


def weight_kernel(scale, counted, facts, neighbours, field, left, right, grads, *rest):
    outs, rest = rest[: -(EDGE + 5)], rest[-(EDGE + 5) :]
    stack, turned, total, blocks = rest[: EDGE + 2], rest[-3], rest[-2], rest[-1]
    bricks = grads.shape[0]

    def turn(a):
        slab = grads[:, a * SLAB : (a + 1) * SLAB, :].reshape(bricks * SLAB, C)
        turned[a] = slab.astype(jnp.float32).T.astype(jnp.bfloat16)

    build_slab(facts, neighbours, field, left, right, 0, stack[0])
    turn(0)
    for a in range(EDGE + 2):
        if a < EDGE + 1:
            build_slab(facts, neighbours, field, left, right, a + 1, stack[a + 1])
        if a < EDGE - 1:
            turn(a + 1)
        first, last = max(0, a - EDGE + 1), min(3, a + 1)
        lhs = [turned[a - k1] for k1 in range(first, last)]
        product = jnp.dot(
            lhs[0] if len(lhs) == 1 else jnp.concatenate(lhs, axis=0),
            stack[a][...].reshape(bricks * SLAB, TAPS),
            preferred_element_type=jnp.float32,
        )
        for n, k1 in enumerate(range(first, last)):
            rows, part = slice(k1 * C, (k1 + 1) * C), product[n * C : (n + 1) * C]
            total[rows, :] = part if a == k1 else total[rows, :] + part
    for n in range(27):
        k1, t = n // 9, n % 9
        block = total[k1 * C : (k1 + 1) * C, t * C : (t + 1) * C].T * scale
        blocks[n * C : (n + 1) * C, :] = block.astype(jnp.bfloat16)
    strays = 0
    for g in range(bricks if counted else 0):
        for column in range(len(DIRECTIONS)):
            lost = (neighbours[g, column] >= 0) & (entry(facts, neighbours, g, column) < 0)
            strays = strays + jnp.where(lost, 1, 0)
    strays = jnp.full((C, C), jnp.minimum(strays, 1), jnp.int32)
    blocks[27 * C :, :] = strays.astype(jnp.float32).astype(jnp.bfloat16)
    n = 1
    for out in outs:
        for piece in range(out.shape[0]):
            first = pl.multiple_of(facts[n], 16)
            out[piece] = blocks[pl.ds(first, out.shape[1]), :]
            n += 1


def join_kernel(places, *rest):
    *pieces, result, corner, blocks, arrived = rest
    n = 0
    for piece in pieces:
        for part in [piece] if len(piece.shape) == 2 else [piece.at[m] for m in range(piece.shape[0])]:
            first = pl.multiple_of(places[n], 16)
            blocks[pl.ds(first, part.shape[0]), :] = part[...].astype(jnp.float32)
            n += 1
    corner[...] = blocks[27 * C : 27 * C + 8, :]
    copy = pltpu.make_async_copy(blocks.at[pl.ds(0, 27 * C)], result, arrived)
    copy.start()
    copy.wait()


def cost(flops, arrays):
    return pl.CostEstimate(
        flops=flops,
        bytes_accessed=sum(math.prod(a.shape) * a.dtype.itemsize for a in arrays),
        transcendentals=0,
    )


def run_conv(
    finish, turned, masked, facts, neighbours, field, left, right, weights, by_rows, n_out, n_edge
):
    bricks, voxels, _ = field.shape
    rows = jax.ShapeDtypeStruct((bricks, voxels, C), jnp.bfloat16)
    edge = jax.ShapeDtypeStruct((bricks, SLAB, C), jnp.bfloat16)
    operands = [field, left, right, weights, *by_rows]
    made = [rows] * n_out + [edge] * n_edge
    outs = made + [rows] * masked
    stack = pltpu.VMEM((bricks, SLAB, TAPS), jnp.bfloat16)
    return pl.pallas_call(
        functools.partial(conv_kernel, finish, turned, masked, len(by_rows), n_out, n_edge),
        in_specs=[
            *[pl.BlockSpec(memory_space=pltpu.SMEM)] * 2,
            *[pl.BlockSpec(memory_space=pl.ANY) for _ in operands],
        ],
        out_specs=[pl.BlockSpec(memory_space=pl.ANY) for _ in outs],
        out_shape=outs,
        scratch_shapes=[
            *[pltpu.VMEM(a.shape, a.dtype) for a in operands + made],
            *[stack] * (EDGE + 2),
            pltpu.VMEM((4 * TAPS, 2 * C), jnp.bfloat16),
            pltpu.SemaphoreType.DMA((len(operands),)),
            pltpu.SemaphoreType.DMA((n_out * EDGE // 2 + n_edge + masked,)),
        ],
        compiler_params=pltpu.CompilerParams(vmem_limit_bytes=VMEM_LIMIT),
        cost_estimate=cost(2 * 36 * bricks * voxels * C * C, operands + outs),
    )(facts, neighbours, *operands)


def run_weight(facts, neighbours, field, left, right, grads, scale, shapes, counted):
    bricks, voxels, _ = field.shape
    outs = [jax.ShapeDtypeStruct((*shape, C), jnp.bfloat16) for shape in shapes]
    return pl.pallas_call(
        functools.partial(weight_kernel, scale, counted),
        in_specs=[
            *[pl.BlockSpec(memory_space=pltpu.SMEM)] * 2,
            *[pl.BlockSpec(memory_space=pltpu.VMEM)] * 4,
        ],
        out_specs=[pl.BlockSpec(memory_space=pltpu.VMEM) for _ in outs],
        out_shape=outs,
        scratch_shapes=[
            *[pltpu.VMEM((bricks, SLAB, TAPS), jnp.bfloat16)] * (EDGE + 2),
            pltpu.VMEM((EDGE, C, bricks * SLAB), jnp.bfloat16),
            pltpu.VMEM((3 * C, TAPS), jnp.float32),
            pltpu.VMEM((28 * C, C), jnp.bfloat16),
        ],
        compiler_params=pltpu.CompilerParams(vmem_limit_bytes=VMEM_LIMIT),
        cost_estimate=cost(2 * 27 * bricks * voxels * C * C, [field, left, right, grads, *outs]),
    )(facts, neighbours, field, left, right, grads)


def run_join(places, pieces):
    out = jax.ShapeDtypeStruct((27 * C, C), jnp.float32)
    joined_blocks, corner = pl.pallas_call(
        join_kernel,
        in_specs=[
            pl.BlockSpec(memory_space=pltpu.SMEM),
            *[pl.BlockSpec(memory_space=pltpu.VMEM) for _ in pieces],
        ],
        out_specs=[pl.BlockSpec(memory_space=pl.ANY), pl.BlockSpec(memory_space=pltpu.VMEM)],
        out_shape=[out, jax.ShapeDtypeStruct((8, C), jnp.float32)],
        scratch_shapes=[pltpu.VMEM((28 * C, C), jnp.float32), pltpu.SemaphoreType.DMA],
        cost_estimate=cost(0, [out, *pieces]),
    )(places, *pieces)
    return joined_blocks.reshape(27, C, C), corner


def beside(low, high):
    count = lax.axis_size("space")
    left = lax.ppermute(high, "space", [(i, i + 1) for i in range(count - 1)])
    right = lax.ppermute(low, "space", [(i + 1, i) for i in range(count - 1)])
    return left, right


def across(values, mask):
    count = lax.axis_size("space")
    return lax.ppermute(values, "space", [(i, i ^ mask) for i in range(count)])


def swapped(half):
    return across(half, 1)


def among(parts):
    count = lax.axis_size("space")
    groups = [[i for i in range(count) if i % 2 == b] for b in range(2)]
    return lax.all_to_all(parts, "space", 0, 0, axis_index_groups=groups, tiled=True)


def handed(part):
    members = lax.axis_size("space") // 2
    masks = [*range(members // 2, members), *range(1, members // 2)]
    came = {m: across(part, 2 * m) for m in masks}
    return [part, *[came[m] for m in range(1, members)]]


def pair_sum(sent, kept):
    total = kept.astype(jnp.float32) + swapped(sent).astype(jnp.float32)
    return total.astype(jnp.bfloat16)


def part_sum(half):
    parts = among(half.reshape(lax.axis_size("space") // 2, -1, C))
    return jnp.sum(parts.astype(jnp.float32), axis=0).astype(jnp.bfloat16)


def gathered(part):
    members = lax.axis_size("space") // 2
    return among(jnp.broadcast_to(part[None], (members,) + part.shape)).reshape(14, C, C)


def joined(half):
    other = swapped(half)
    even = lax.axis_index("space") % 2 == 0
    first = jnp.where(even, half, other)
    second = jnp.where(even, other, half)
    return jnp.concatenate([first, second[:13]], axis=0).astype(jnp.float32)


def column_body(feats, mask, neighbours, weight_one, weight_two, cotangent):
    bricks, voxels, channels = feats.shape
    my_index = lax.axis_index("space")
    low, high = (
        feats[:, rows] * mask[:, rows, None].astype(jnp.bfloat16)
        for rows in (slice(0, SLAB), slice(voxels - SLAB, voxels))
    )
    in_left, in_right = beside(low, high)
    spread_mask = jnp.broadcast_to(mask.astype(jnp.bfloat16)[:, :, None], feats.shape)
    scale = 1.0 / math.sqrt(voxels * bricks)

    members = lax.axis_size("space") // 2
    bit, row = my_index % 2, my_index // 2
    rows = 28 * C // (2 * members)
    order = [*range(members // 2, members), *range(members // 2)]
    own = [(bit * members + (row ^ m)) * rows for m in range(members)]
    others = [((1 - bit) * members + (row ^ m)) * rows for m in range(members)]
    half_facts = jnp.stack([my_index, (1 - bit) * 14 * C, bit * 14 * C])
    part_facts = jnp.stack([my_index, *[others[m] for m in order], *[own[m] for m in order]])
    places = jnp.stack([*own, *others])
    together = lax.optimization_barrier
    in_left, in_right, spread_mask, half_facts = together(
        (in_left, in_right, spread_mask, half_facts)
    )

    slope, hidden, low, high, inputs = run_conv(
        finish_first, False, True, half_facts, neighbours, feats, in_left, in_right, weight_one,
        [spread_mask], 2, 2,
    )
    h_left, h_right = beside(low, high)
    output, grad_second, low, high = run_conv(
        finish_second, False, False, half_facts, neighbours, hidden, h_left, h_right, weight_two,
        [spread_mask, cotangent], 2, 2,
    )
    s_left, s_right = beside(low, high)
    sent, kept = run_weight(
        half_facts, neighbours, hidden, h_left, h_right, grad_second, scale,
        [(1, 14 * C)] * 2, True,
    )
    sent, s_left, s_right = together((sent, s_left, s_right))
    half_two = pair_sum(sent, kept)
    grad_first, low, high = run_conv(
        finish_product, True, False, half_facts, neighbours, grad_second, s_left, s_right, weight_two,
        [slope], 1, 2,
    )
    half_two, grad_first = together((half_two, grad_first))
    part_two = part_sum(half_two)
    far = members - members // 2
    sent_far, sent_near, kept = run_weight(
        part_facts, neighbours, inputs, in_left, in_right, grad_first, scale,
        [(far, rows), (members // 2, rows), (members, rows)], False,
    )
    sent_far, sent_near, low, high = together((sent_far, sent_near, low, high))
    received = {
        m: piece[n]
        for piece, masks in ((swapped(sent_far), order[:far]), (swapped(sent_near), order[far:]))
        for n, m in enumerate(masks)
    }
    same_two = handed(part_two)
    f_left, f_right = beside(low, high)

    def summed(m):
        return kept[order.index(m)].astype(jnp.float32) + received[m].astype(jnp.float32)

    halves = [summed(m).astype(jnp.bfloat16) for m in order if m]
    *halves, f_left, f_right = together((*halves, f_left, f_right))
    arrived = [across(half, 2 * m) for half, m in zip(halves, [m for m in order if m])]
    (grad_input,) = run_conv(
        finish_product, True, False, half_facts, neighbours, grad_first, f_left, f_right,
        weight_one, [spread_mask], 1, 0,
    )
    *arrived, grad_input, same_two = together((*arrived, grad_input, jnp.stack(same_two)))
    part = summed(0)
    for half in arrived:
        part = part + half.astype(jnp.float32)
    part = part.astype(jnp.bfloat16)
    same = handed(part)
    other_two = swapped(same_two)
    other = [swapped(piece) for piece in same]
    grad_w1, _ = run_join(places, [*same, *other])
    grad_w2, strays = run_join(places, [same_two, other_two])
    return strays[0, 0], (output, grad_input, grad_w1, grad_w2)


def body(*arguments):
    strays, results = column_body(*arguments)

    def again(state):
        return jnp.zeros_like(state[0]), general_body(*arguments)

    return lax.while_loop(lambda state: state[0] > 0.5, again, (strays, results))[1]


def extended(field, source_index):
    bricks = field.shape[0]
    left, right = beside(field, field)
    blank = jnp.zeros((1, *field.shape[1:]), field.dtype)
    sources = jnp.concatenate([left, field, right, blank], axis=0).reshape(-1, EDGE * C)
    cell = jnp.arange(EDGE + 2)
    side = jnp.where(cell == 0, 0, jnp.where(cell == EDGE + 1, 2, 1))
    direction = 3 * side[:, None] + side[None, :]
    own = bricks + jnp.arange(bricks)[:, None]
    named = jnp.concatenate([source_index[:, :4], own, source_index[:, 4:]], axis=1)
    place = (cell - 1) % EDGE
    columns = named[:, direction] * SLAB + place[:, None] * EDGE + place[None, :]
    padded = jnp.take(sources, columns, axis=0).reshape(bricks, EDGE + 2, EDGE + 2, EDGE, C)
    return jnp.pad(padded, ((0, 0), (0, 0), (0, 0), (1, 1), (0, 0)))


def shifted(padded, k):
    bricks = padded.shape[0]
    corner = (0, k // 9, k // 3 % 3, k % 3, 0)
    return lax.dynamic_slice(padded, corner, (bricks, EDGE, EDGE, EDGE, C)).reshape(-1, C)


def general_conv(padded, weight, turned):
    def add(k, total):
        block = lax.dynamic_index_in_dim(weight, k, keepdims=False)
        cells = shifted(padded, 26 - k if turned else k)
        return total + jnp.dot(
            cells, block.T if turned else block, preferred_element_type=jnp.float32
        )

    rows = padded.shape[0] * EDGE**3
    return lax.fori_loop(0, 27, add, jnp.zeros((rows, C), jnp.float32))


def general_grad(padded, grads, scale):
    def one(k):
        contract = (((0,), (0,)), ((), ()))
        return lax.dot_general(
            shifted(padded, k), grads, contract, preferred_element_type=jnp.float32
        )

    term = (lax.map(one, jnp.arange(27)) * scale).astype(jnp.bfloat16)
    halves = jnp.pad(term, ((0, 1), (0, 0), (0, 0))).reshape(2, 14, C, C)
    even = lax.axis_index("space") % 2 == 0
    sent = jnp.where(even, halves[1], halves[0])
    kept = jnp.where(even, halves[0], halves[1])
    return joined(gathered(part_sum(pair_sum(sent, kept))))


def silu_slope(values):
    s = jax.nn.sigmoid(values)
    return s * (1.0 + values * (1.0 - s))


def general_body(feats, mask, neighbours, weight_one, weight_two, cotangent):
    bricks, voxels, _ = feats.shape
    first_brick = (lax.axis_index("space") - 1) * bricks
    source_index = jnp.where(neighbours >= 0, neighbours - first_brick, 3 * bricks)
    occupied = mask.reshape(-1, 1).astype(jnp.float32)
    scale = 1.0 / math.sqrt(voxels * bricks)

    def rounded(values):
        return values.astype(jnp.bfloat16)

    def extend(values):
        return extended(values.reshape(bricks, voxels, C), source_index)

    padded_in = extend(feats * mask[:, :, None].astype(jnp.bfloat16))
    first_pre = general_conv(padded_in, weight_one, False)
    padded_hidden = extend(rounded(occupied * jax.nn.silu(first_pre)))
    second_pre = general_conv(padded_hidden, weight_two, False)
    output = rounded(occupied * jax.nn.silu(second_pre))
    received = cotangent.reshape(-1, C).astype(jnp.float32)
    grad_second = rounded(received * occupied * silu_slope(second_pre))
    back_second = general_conv(extend(grad_second), weight_two, True)
    grad_first = rounded(occupied * silu_slope(first_pre) * back_second)
    grad_input = rounded(occupied * general_conv(extend(grad_first), weight_one, True))
    return (
        output.reshape(feats.shape),
        grad_input.reshape(feats.shape),
        general_grad(padded_in, grad_first, scale),
        general_grad(padded_hidden, grad_second, scale),
    )


def solution(mesh):
    in_specs = (
        P(("scene", "space"), None, None),
        P(("scene", "space"), None),
        P(("scene", "space"), None),
        P(),
        P(),
        P(("scene", "space"), None, None),
    )
    out_specs = (
        P(("scene", "space"), None, None),
        P(("scene", "space"), None, None),
        P("scene", None, None),
        P("scene", None, None),
    )
    return jax.shard_map(body, mesh=mesh, in_specs=in_specs, out_specs=out_specs, check_vma=False)
```

```python
import functools
import math

import jax
import jax.numpy as jnp
from jax import lax
from jax.experimental import pallas as pl
from jax.experimental.pallas import tpu as pltpu
from jax.sharding import PartitionSpec as P

EDGE = 8
TILE = 1
WIDE = 8
SLAB = EDGE * EDGE
C = 128
TAPS = 9 * C
VMEM_LIMIT = 36 * 1024 * 1024

DIRECTIONS = ((-1, -1), (-1, 0), (-1, 1), (0, -1), (0, 1), (1, -1), (1, 0), (1, 1))


def entry(facts, neighbours, brick, column):
    named = neighbours[brick, column]
    local = named - (facts[0] + DIRECTIONS[column][0]) * (TILE * WIDE)
    inside = (named >= 0) & (local >= 0) & (local < neighbours.shape[0])
    return jnp.where(inside, local, -1)


def picked(source, index, first, rows):
    found = source[jnp.maximum(index, 0), first : first + rows, :].astype(jnp.float32)
    return jnp.where(index >= 0, found, 0.0)


def slab_tiles(centre, top, bottom):
    cells = jnp.concatenate([top[8:16], centre, bottom[0:8]], axis=0).reshape(EDGE + 2, EDGE, C)
    place = lax.broadcasted_iota(jnp.int32, cells.shape, 1)
    below = jnp.where(place == 0, 0.0, pltpu.roll(cells, 1, 1))
    above = jnp.where(place == EDGE - 1, 0.0, pltpu.roll(cells, EDGE - 1, 1))
    even, odd = [], []
    for shifted in (below, cells, above):
        even.append(shifted.reshape((EDGE + 2) * EDGE, C).astype(jnp.bfloat16))
        odd.append(shifted[1 : EDGE + 1].reshape(SLAB, C).astype(jnp.bfloat16))
    return [e[0:SLAB] for e in even] + odd + [e[16 : 16 + SLAB] for e in even]


def build_cells(facts, neighbours, field, left, right, g, a):
    near = functools.partial(entry, facts, neighbours, g)
    if a == 0:
        source, first, names = left, 0, (near(1), near(0), near(2))
    elif a == EDGE + 1:
        source, first, names = right, 0, (near(6), near(5), near(7))
    else:
        source, first, names = field, (a - 1) * SLAB, (g, near(3), near(4))
    if source is field:
        centre = field[g, first : first + SLAB, :].astype(jnp.float32)
    else:
        centre = picked(source, names[0], first, SLAB)
    top = picked(source, names[1], first + SLAB - 16, 16)
    bottom = picked(source, names[2], first, 16)
    return slab_tiles(centre, top, bottom)


def build_slab(facts, neighbours, field, left, right, a, stack):
    for g in range(field.shape[0]):
        for t, tile in enumerate(build_cells(facts, neighbours, field, left, right, g, a)):
            stack[g, :, t * C : (t + 1) * C] = tile


def build_stack(facts, neighbours, field, left, right, stack):
    @pl.loop(0, field.shape[0])
    def _(g):
        for a in range(EDGE + 2):
            for t, tile in enumerate(build_cells(facts, neighbours, field, left, right, g, a)):
                stack[g, a, :, t * C : (t + 1) * C] = tile


def fill_weights(weights, turned, filled):
    blank = jnp.zeros((C, C), jnp.bfloat16)
    for k1 in range(3):
        for t in range(9):
            block = weights[26 - 9 * k1 - t if turned else 9 * k1 + t]
            if turned:
                block = block.astype(jnp.float32).T.astype(jnp.bfloat16)
            for half in range(2):
                first = (k1 + half) * TAPS + t * C
                filled[first : first + C, half * C : (half + 1) * C] = block
    for t in range(9):
        filled[t * C : (t + 1) * C, C:] = blank
        filled[3 * TAPS + t * C : 3 * TAPS + (t + 1) * C, 0:C] = blank


def conv_kernel(finish, turned, masked, n_near, n_far, kinds, facts, neighbours, *rest):
    field, left, right, *rest = rest
    near, rest = rest[:n_near], rest[n_near:]
    operands, rest = rest[: 1 + n_far], rest[1 + n_far :]
    results, rest = rest[: len(kinds)], rest[len(kinds) :]
    edges, rest = (rest[:2], rest[2:]) if kinds[-1] == "vmem" else ((), rest)
    kept, rest = (rest[0], rest[1:]) if masked else (None, rest)
    local, rest = rest[: 1 + n_far], rest[1 + n_far :]
    *staged, stack, filled, came, gone = rest
    made, leaving = [], []
    for kind, result in zip(kinds, results):
        made.append(result if kind == "vmem" else staged.pop(0))
        if kind == "hbm":
            leaving.append((made[-1], result))
    copies = [
        pltpu.make_async_copy(there, here, came.at[n])
        for n, (there, here) in enumerate(zip(operands, local))
    ]
    for copy in copies:
        copy.start()
    if masked:
        kept[...] = field[...] * near[0][...]
        field = kept
    build_stack(facts, neighbours, field, left, right, stack)
    copies[0].wait()
    fill_weights(local[0], turned, filled)
    for copy in copies[1:]:
        copy.wait()
    bricks = field.shape[0] // 2
    factors = [*near, *local[1:]]

    def outgoing(pair):
        rows = pl.ds(pl.multiple_of(pair * 2 * SLAB, 2 * SLAB), 2 * SLAB)
        return [
            pltpu.make_async_copy(here.at[:, rows, :], there.at[:, rows, :], gone.at[n, pair])
            for n, (here, there) in enumerate(leaving)
        ]

    @pl.loop(0, EDGE // 2)
    def _(pair):
        for part in range(2):
            some = slice(part * bricks, (part + 1) * bricks)
            lhs = [stack[some, 2 * pair + n].reshape(bricks * SLAB, TAPS) for n in range(4)]
            both = jnp.dot(
                jnp.concatenate(lhs, axis=1), filled[...], preferred_element_type=jnp.float32
            )
            for half in range(2):
                rows = pl.ds(pl.multiple_of((2 * pair + half) * SLAB, SLAB), SLAB)
                values = both[:, half * C : (half + 1) * C].reshape(bricks, SLAB, C)
                values = finish(
                    values, *[array[some, rows, :].astype(jnp.float32) for array in factors]
                )
                for array, value in zip(made, values):
                    array[some, rows, :] = value.astype(jnp.bfloat16)
        for copy in outgoing(pair):
            copy.start()

    if edges:
        edges[0][...] = made[-1][:, :SLAB, :]
        edges[1][...] = made[-1][:, (EDGE - 1) * SLAB :, :]
    for pair in range(EDGE // 2):
        for copy in outgoing(pair):
            copy.wait()


def finish_first(values, mask):
    s = jax.nn.sigmoid(values)
    return mask * (s * (1.0 + values * (1.0 - s))), mask * (values * s)


def finish_second(values, mask, cotangent):
    s = jax.nn.sigmoid(values)
    return mask * (values * s), cotangent * mask * (s * (1.0 + values * (1.0 - s)))


def finish_product(values, factor):
    return (factor * values,)


def weight_kernel(scale, counted, facts, neighbours, field, left, right, grads, *rest):
    outs, rest = rest[: -(EDGE + 5)], rest[-(EDGE + 5) :]
    stack, turned, total, blocks = rest[: EDGE + 2], rest[-3], rest[-2], rest[-1]
    bricks = grads.shape[0]

    def turn(a):
        slab = grads[:, a * SLAB : (a + 1) * SLAB, :].reshape(bricks * SLAB, C)
        turned[a] = slab.astype(jnp.float32).T.astype(jnp.bfloat16)

    build_slab(facts, neighbours, field, left, right, 0, stack[0])
    turn(0)
    for a in range(EDGE + 2):
        if a < EDGE + 1:
            build_slab(facts, neighbours, field, left, right, a + 1, stack[a + 1])
        if a < EDGE - 1:
            turn(a + 1)
        first, last = max(0, a - EDGE + 1), min(3, a + 1)
        lhs = [turned[a - k1] for k1 in range(first, last)]
        product = jnp.dot(
            lhs[0] if len(lhs) == 1 else jnp.concatenate(lhs, axis=0),
            stack[a][...].reshape(bricks * SLAB, TAPS),
            preferred_element_type=jnp.float32,
        )
        for n, k1 in enumerate(range(first, last)):
            rows, part = slice(k1 * C, (k1 + 1) * C), product[n * C : (n + 1) * C]
            total[rows, :] = part if a == k1 else total[rows, :] + part
    for n in range(27):
        k1, t = n // 9, n % 9
        block = total[k1 * C : (k1 + 1) * C, t * C : (t + 1) * C].T * scale
        blocks[n * C : (n + 1) * C, :] = block.astype(jnp.bfloat16)
    strays = 0
    for g in range(bricks if counted else 0):
        for column in range(len(DIRECTIONS)):
            lost = (neighbours[g, column] >= 0) & (entry(facts, neighbours, g, column) < 0)
            strays = strays + jnp.where(lost, 1, 0)
    strays = jnp.full((C, C), jnp.minimum(strays, 1), jnp.int32)
    blocks[27 * C :, :] = strays.astype(jnp.float32).astype(jnp.bfloat16)
    n = 1
    for out in outs:
        for piece in range(out.shape[0]):
            first = pl.multiple_of(facts[n], 16)
            out[piece] = blocks[pl.ds(first, out.shape[1]), :]
            n += 1


def join_kernel(places, *rest):
    *pieces, result, blocks, arrived = rest
    for n, piece in enumerate(pieces):
        first = pl.multiple_of(places[n], 16)
        blocks[pl.ds(first, piece.shape[0]), :] = piece[...].astype(jnp.float32)
    copy = pltpu.make_async_copy(blocks.at[pl.ds(0, 27 * C)], result, arrived)
    copy.start()
    copy.wait()


def cost(flops, arrays):
    return pl.CostEstimate(
        flops=flops,
        bytes_accessed=sum(math.prod(a.shape) * a.dtype.itemsize for a in arrays),
        transcendentals=0,
    )


def run_conv(
    finish, turned, masked, facts, neighbours, field, left, right, weights, near, far, kinds
):
    bricks, voxels, _ = field.shape
    rows = jax.ShapeDtypeStruct((bricks, voxels, C), jnp.bfloat16)
    edge = jax.ShapeDtypeStruct((bricks, SLAB, C), jnp.bfloat16)
    operands = [weights, *far]
    spaces = {"vmem": pltpu.VMEM, "hbm": pltpu.HBM}
    outs = [(rows, spaces[kind]) for kind in kinds]
    outs += [(edge, pltpu.VMEM)] * (2 * (kinds[-1] == "vmem")) + [(rows, pltpu.VMEM)] * masked
    n_hbm = kinds.count("hbm")
    return pl.pallas_call(
        functools.partial(conv_kernel, finish, turned, masked, len(near), len(far), kinds),
        in_specs=[
            *[pl.BlockSpec(memory_space=pltpu.SMEM)] * 2,
            *[pl.BlockSpec(memory_space=pltpu.VMEM)] * (3 + len(near)),
            *[pl.BlockSpec(memory_space=pltpu.HBM) for _ in operands],
        ],
        out_specs=[pl.BlockSpec(memory_space=space) for _, space in outs],
        out_shape=[shape for shape, _ in outs],
        scratch_shapes=[
            *[pltpu.VMEM(a.shape, a.dtype) for a in operands],
            *[pltpu.VMEM(rows.shape, rows.dtype)] * n_hbm,
            pltpu.VMEM((bricks, EDGE + 2, SLAB, TAPS), jnp.bfloat16),
            pltpu.VMEM((4 * TAPS, 2 * C), jnp.bfloat16),
            pltpu.SemaphoreType.DMA((len(operands),)),
            pltpu.SemaphoreType.DMA((max(n_hbm, 1), EDGE // 2)),
        ],
        compiler_params=pltpu.CompilerParams(vmem_limit_bytes=VMEM_LIMIT),
        cost_estimate=cost(
            2 * 36 * bricks * voxels * C * C, [field, *near, *operands] + [shape for shape, _ in outs]
        ),
    )(facts, neighbours, field, left, right, *near, *operands)


def run_weight(facts, neighbours, field, left, right, grads, scale, shapes, counted):
    bricks, voxels, _ = field.shape
    outs = [jax.ShapeDtypeStruct((*shape, C), jnp.bfloat16) for shape in shapes]
    return pl.pallas_call(
        functools.partial(weight_kernel, scale, counted),
        in_specs=[
            *[pl.BlockSpec(memory_space=pltpu.SMEM)] * 2,
            *[pl.BlockSpec(memory_space=pltpu.VMEM)] * 4,
        ],
        out_specs=[pl.BlockSpec(memory_space=pltpu.VMEM) for _ in outs],
        out_shape=outs,
        scratch_shapes=[
            *[pltpu.VMEM((bricks, SLAB, TAPS), jnp.bfloat16)] * (EDGE + 2),
            pltpu.VMEM((EDGE, C, bricks * SLAB), jnp.bfloat16),
            pltpu.VMEM((3 * C, TAPS), jnp.float32),
            pltpu.VMEM((28 * C, C), jnp.bfloat16),
        ],
        compiler_params=pltpu.CompilerParams(vmem_limit_bytes=VMEM_LIMIT),
        cost_estimate=cost(2 * 27 * bricks * voxels * C * C, [field, left, right, grads, *outs]),
    )(facts, neighbours, field, left, right, grads)


def run_join(places, pieces):
    out = jax.ShapeDtypeStruct((27 * C, C), jnp.float32)
    return pl.pallas_call(
        join_kernel,
        in_specs=[
            pl.BlockSpec(memory_space=pltpu.SMEM),
            *[pl.BlockSpec(memory_space=pltpu.VMEM) for _ in pieces],
        ],
        out_specs=pl.BlockSpec(memory_space=pltpu.HBM),
        out_shape=out,
        scratch_shapes=[pltpu.VMEM((28 * C, C), jnp.float32), pltpu.SemaphoreType.DMA],
        cost_estimate=cost(0, [out, *pieces]),
    )(places, *pieces).reshape(27, C, C)


def beside(low, high):
    count = lax.axis_size("space")
    left = lax.ppermute(high, "space", [(i, i + 1) for i in range(count - 1)])
    right = lax.ppermute(low, "space", [(i + 1, i) for i in range(count - 1)])
    return left, right


def across(values, mask):
    count = lax.axis_size("space")
    return lax.ppermute(values, "space", [(i, i ^ mask) for i in range(count)])


def swapped(half):
    return across(half, 1)


def among(parts):
    count = lax.axis_size("space")
    groups = [[i for i in range(count) if i % 2 == b] for b in range(2)]
    return lax.all_to_all(parts, "space", 0, 0, axis_index_groups=groups, tiled=True)


def handed(part):
    members = lax.axis_size("space") // 2
    masks = [*range(members // 2, members), *range(1, members // 2)]
    came = {m: across(part, 2 * m) for m in masks}
    return [part, *[came[m] for m in range(1, members)]]


def pair_sum(sent, kept):
    total = kept.astype(jnp.float32) + swapped(sent).astype(jnp.float32)
    return total.astype(jnp.bfloat16)


def part_sum(half):
    parts = among(half.reshape(lax.axis_size("space") // 2, -1, C))
    return jnp.sum(parts.astype(jnp.float32), axis=0).astype(jnp.bfloat16)


def gathered(part):
    members = lax.axis_size("space") // 2
    return among(jnp.broadcast_to(part[None], (members,) + part.shape)).reshape(14, C, C)


def joined(half):
    other = swapped(half)
    even = lax.axis_index("space") % 2 == 0
    first = jnp.where(even, half, other)
    second = jnp.where(even, other, half)
    blocks = jnp.concatenate([first, second[:13]], axis=0).astype(jnp.float32)
    return blocks, second[13, 0, 0].astype(jnp.float32)


def column_body(feats, mask, neighbours, weight_one, weight_two, cotangent):
    bricks, voxels, channels = feats.shape
    my_index = lax.axis_index("space")
    low, high = (
        feats[:, rows] * mask[:, rows, None].astype(jnp.bfloat16)
        for rows in (slice(0, SLAB), slice(voxels - SLAB, voxels))
    )
    in_left, in_right = beside(low, high)
    spread_mask = jnp.broadcast_to(mask.astype(jnp.bfloat16)[:, :, None], feats.shape)
    scale = 1.0 / math.sqrt(voxels * bricks)

    members = lax.axis_size("space") // 2
    bit, row = my_index % 2, my_index // 2
    rows = 28 * C // (2 * members)
    order = [*range(members // 2, members), *range(members // 2)]
    own = [(bit * members + (row ^ m)) * rows for m in range(members)]
    others = [((1 - bit) * members + (row ^ m)) * rows for m in range(members)]
    half_facts = jnp.stack([my_index, (1 - bit) * 14 * C, bit * 14 * C])
    part_facts = jnp.stack([my_index, *[others[m] for m in order], *[own[m] for m in order]])
    places = jnp.stack([*own, *others])
    together = lax.optimization_barrier
    in_left, in_right, spread_mask, half_facts = together(
        (in_left, in_right, spread_mask, half_facts)
    )

    slope, hidden, low, high, inputs = run_conv(
        finish_first, False, True, half_facts, neighbours, feats, in_left, in_right, weight_one,
        [spread_mask], [], ("vmem", "vmem"),
    )
    h_left, h_right = beside(low, high)
    output, grad_second, low, high = run_conv(
        finish_second, False, False, half_facts, neighbours, hidden, h_left, h_right, weight_two,
        [spread_mask], [cotangent], ("hbm", "vmem"),
    )
    s_left, s_right = beside(low, high)
    sent, kept = run_weight(
        half_facts, neighbours, hidden, h_left, h_right, grad_second, scale,
        [(1, 14 * C)] * 2, True,
    )
    sent, s_left, s_right = together((sent, s_left, s_right))
    half_two = pair_sum(sent, kept)
    grad_first, low, high = run_conv(
        finish_product, True, False, half_facts, neighbours, grad_second, s_left, s_right, weight_two,
        [slope], [], ("vmem",),
    )
    half_two, grad_first = together((half_two, grad_first))
    part_two = part_sum(half_two)
    far = members - members // 2
    sent_far, sent_near, kept = run_weight(
        part_facts, neighbours, inputs, in_left, in_right, grad_first, scale,
        [(far, rows), (members // 2, rows), (members, rows)], False,
    )
    sent_far, sent_near, low, high = together((sent_far, sent_near, low, high))
    received = {
        m: piece[n]
        for piece, masks in ((swapped(sent_far), order[:far]), (swapped(sent_near), order[far:]))
        for n, m in enumerate(masks)
    }
    half_two = gathered(part_two)
    f_left, f_right = beside(low, high)

    def summed(m):
        return kept[order.index(m)].astype(jnp.float32) + received[m].astype(jnp.float32)

    halves = [summed(m).astype(jnp.bfloat16) for m in order if m]
    *halves, f_left, f_right = together((*halves, f_left, f_right))
    arrived = [across(half, 2 * m) for half, m in zip(halves, [m for m in order if m])]
    (grad_input,) = run_conv(
        finish_product, True, False, half_facts, neighbours, grad_first, f_left, f_right,
        weight_one, [spread_mask], [], ("hbm",),
    )
    *arrived, grad_input = together((*arrived, grad_input))
    part = summed(0)
    for half in arrived:
        part = part + half.astype(jnp.float32)
    part = part.astype(jnp.bfloat16)
    same = handed(part)
    other = [swapped(piece) for piece in same]
    grad_w2, strays = joined(half_two)
    *other, grad_w2, strays = together((*other, grad_w2, strays))
    grad_w1 = run_join(places, [*same, *other])
    return strays, (output, grad_input, grad_w1, grad_w2)


def body(*arguments):
    strays, results = column_body(*arguments)

    def again(state):
        return jnp.zeros_like(state[0]), general_body(*arguments)

    return lax.while_loop(lambda state: state[0] > 0.5, again, (strays, results))[1]


def extended(field, source_index):
    bricks = field.shape[0]
    left, right = beside(field, field)
    blank = jnp.zeros((1, *field.shape[1:]), field.dtype)
    sources = jnp.concatenate([left, field, right, blank], axis=0).reshape(-1, EDGE * C)
    cell = jnp.arange(EDGE + 2)
    side = jnp.where(cell == 0, 0, jnp.where(cell == EDGE + 1, 2, 1))
    direction = 3 * side[:, None] + side[None, :]
    own = bricks + jnp.arange(bricks)[:, None]
    named = jnp.concatenate([source_index[:, :4], own, source_index[:, 4:]], axis=1)
    place = (cell - 1) % EDGE
    columns = named[:, direction] * SLAB + place[:, None] * EDGE + place[None, :]
    padded = jnp.take(sources, columns, axis=0).reshape(bricks, EDGE + 2, EDGE + 2, EDGE, C)
    return jnp.pad(padded, ((0, 0), (0, 0), (0, 0), (1, 1), (0, 0)))


def shifted(padded, k):
    bricks = padded.shape[0]
    corner = (0, k // 9, k // 3 % 3, k % 3, 0)
    return lax.dynamic_slice(padded, corner, (bricks, EDGE, EDGE, EDGE, C)).reshape(-1, C)


def general_conv(padded, weight, turned):
    def add(k, total):
        block = lax.dynamic_index_in_dim(weight, k, keepdims=False)
        cells = shifted(padded, 26 - k if turned else k)
        return total + jnp.dot(
            cells, block.T if turned else block, preferred_element_type=jnp.float32
        )

    rows = padded.shape[0] * EDGE**3
    return lax.fori_loop(0, 27, add, jnp.zeros((rows, C), jnp.float32))


def general_grad(padded, grads, scale):
    def one(k):
        contract = (((0,), (0,)), ((), ()))
        return lax.dot_general(
            shifted(padded, k), grads, contract, preferred_element_type=jnp.float32
        )

    term = (lax.map(one, jnp.arange(27)) * scale).astype(jnp.bfloat16)
    halves = jnp.pad(term, ((0, 1), (0, 0), (0, 0))).reshape(2, 14, C, C)
    even = lax.axis_index("space") % 2 == 0
    sent = jnp.where(even, halves[1], halves[0])
    kept = jnp.where(even, halves[0], halves[1])
    return joined(gathered(part_sum(pair_sum(sent, kept))))[0]


def silu_slope(values):
    s = jax.nn.sigmoid(values)
    return s * (1.0 + values * (1.0 - s))


def general_body(feats, mask, neighbours, weight_one, weight_two, cotangent):
    bricks, voxels, _ = feats.shape
    first_brick = (lax.axis_index("space") - 1) * bricks
    source_index = jnp.where(neighbours >= 0, neighbours - first_brick, 3 * bricks)
    occupied = mask.reshape(-1, 1).astype(jnp.float32)
    scale = 1.0 / math.sqrt(voxels * bricks)

    def rounded(values):
        return values.astype(jnp.bfloat16)

    def extend(values):
        return extended(values.reshape(bricks, voxels, C), source_index)

    padded_in = extend(feats * mask[:, :, None].astype(jnp.bfloat16))
    first_pre = general_conv(padded_in, weight_one, False)
    padded_hidden = extend(rounded(occupied * jax.nn.silu(first_pre)))
    second_pre = general_conv(padded_hidden, weight_two, False)
    output = rounded(occupied * jax.nn.silu(second_pre))
    received = cotangent.reshape(-1, C).astype(jnp.float32)
    grad_second = rounded(received * occupied * silu_slope(second_pre))
    back_second = general_conv(extend(grad_second), weight_two, True)
    grad_first = rounded(occupied * silu_slope(first_pre) * back_second)
    grad_input = rounded(occupied * general_conv(extend(grad_first), weight_one, True))
    return (
        output.reshape(feats.shape),
        grad_input.reshape(feats.shape),
        general_grad(padded_in, grad_first, scale),
        general_grad(padded_hidden, grad_second, scale),
    )


def solution(mesh):
    in_specs = (
        P(("scene", "space"), None, None),
        P(("scene", "space"), None),
        P(("scene", "space"), None),
        P(),
        P(),
        P(("scene", "space"), None, None),
    )
    out_specs = (
        P(("scene", "space"), None, None),
        P(("scene", "space"), None, None),
        P("scene", None, None),
        P("scene", None, None),
    )
    return jax.shard_map(body, mesh=mesh, in_specs=in_specs, out_specs=out_specs, check_vma=False)
```

```python
import functools
import math

import jax
import jax.numpy as jnp
from jax import lax
from jax.experimental import pallas as pl
from jax.experimental.pallas import tpu as pltpu
from jax.sharding import PartitionSpec as P

EDGE = 8
TILE = 1
WIDE = 8
SLAB = EDGE * EDGE
C = 128
TAPS = 9 * C
VMEM_LIMIT = 36 * 1024 * 1024

DIRECTIONS = ((-1, -1), (-1, 0), (-1, 1), (0, -1), (0, 1), (1, -1), (1, 0), (1, 1))


def entry(facts, neighbours, brick, column):
    named = neighbours[brick, column]
    local = named - (facts[0] + DIRECTIONS[column][0]) * (TILE * WIDE)
    inside = (named >= 0) & (local >= 0) & (local < neighbours.shape[0])
    return jnp.where(inside, local, -1)


def picked(source, index, first, rows):
    found = source[jnp.maximum(index, 0), first : first + rows, :].astype(jnp.float32)
    return jnp.where(index >= 0, found, 0.0)


def padded_cells(facts, neighbours, field, left, right, g, a):
    near = functools.partial(entry, facts, neighbours, g)
    if a == 0:
        source, first, names = left, 0, (near(1), near(0), near(2))
    elif a == EDGE + 1:
        source, first, names = right, 0, (near(6), near(5), near(7))
    else:
        source, first, names = field, (a - 1) * SLAB, (g, near(3), near(4))
    if source is field:
        centre = field[g, first : first + SLAB, :].astype(jnp.float32)
    else:
        centre = picked(source, names[0], first, SLAB)
    top = picked(source, names[1], first + SLAB - 16, 16)
    bottom = picked(source, names[2], first, 16)
    return centre, jnp.concatenate([top[8:16], centre, bottom[0:8]], axis=0)


def before_and_behind(cells):
    place = lax.broadcasted_iota(jnp.int32, cells.shape, 1)
    before = jnp.where(place == 0, 0.0, pltpu.roll(cells, 1, 1))
    return before, jnp.where(place == EDGE - 1, 0.0, pltpu.roll(cells, EDGE - 1, 1))


def slab_tiles(cells):
    cells = cells.reshape(EDGE + 2, EDGE, C)
    before, behind = before_and_behind(cells)
    even, odd = [], []
    for shifted in (before, cells, behind):
        even.append(shifted.reshape((EDGE + 2) * EDGE, C).astype(jnp.bfloat16))
        odd.append(shifted[1 : EDGE + 1].reshape(SLAB, C).astype(jnp.bfloat16))
    return [e[0:SLAB] for e in even] + odd + [e[16 : 16 + SLAB] for e in even]


def build_slab(facts, neighbours, field, left, right, a, stack):
    for g in range(field.shape[0]):
        _, cells = padded_cells(facts, neighbours, field, left, right, g, a)
        for t, tile in enumerate(slab_tiles(cells)):
            stack[g, :, t * C : (t + 1) * C] = tile


def build_rows(facts, neighbours, field, left, right, stack):
    @pl.loop(0, field.shape[0])
    def _(g):
        for a in range(EDGE + 2):
            centre, cells = padded_cells(facts, neighbours, field, left, right, g, a)
            cells = cells.astype(jnp.bfloat16)
            stack[g, a, :, 0:C] = cells[0:SLAB]
            stack[g, a, :, C : 2 * C] = centre.astype(jnp.bfloat16)
            stack[g, a, :, 2 * C :] = cells[16 : 16 + SLAB]


def fill_weights(weights, turned, filled):
    for k1 in range(3):
        for k2 in range(3):
            for k3 in range(3):
                n = 9 * k1 + 3 * k2 + k3
                block = weights[26 - n if turned else n]
                if turned:
                    block = block.astype(jnp.float32).T.astype(jnp.bfloat16)
                for half in range(2):
                    row, column = 3 * (k1 + half) + k2, 2 * k3 + half
                    filled[row * C : (row + 1) * C, column * C : (column + 1) * C] = block
    blank = jnp.zeros((3 * C, C), jnp.bfloat16)
    for k3 in range(3):
        filled[9 * C :, 2 * k3 * C : (2 * k3 + 1) * C] = blank
        filled[: 3 * C, (2 * k3 + 1) * C : (2 * k3 + 2) * C] = blank


def conv_kernel(finish, turned, masked, n_near, n_far, kinds, facts, neighbours, *rest):
    field, left, right, *rest = rest
    near, rest = rest[:n_near], rest[n_near:]
    operands, rest = rest[: 1 + n_far], rest[1 + n_far :]
    results, rest = rest[: len(kinds)], rest[len(kinds) :]
    edges, rest = (rest[:2], rest[2:]) if kinds[-1] == "vmem" else ((), rest)
    kept, rest = (rest[0], rest[1:]) if masked else (None, rest)
    local, rest = rest[: 1 + n_far], rest[1 + n_far :]
    *staged, stack, filled, came, gone = rest
    made, leaving = [], []
    for kind, result in zip(kinds, results):
        made.append(result if kind == "vmem" else staged.pop(0))
        if kind == "hbm":
            leaving.append((made[-1], result))
    copies = [
        pltpu.make_async_copy(there, here, came.at[n])
        for n, (there, here) in enumerate(zip(operands, local))
    ]
    for copy in copies:
        copy.start()
    if masked:
        kept[...] = field[...] * near[0][...]
        field = kept
    build_rows(facts, neighbours, field, left, right, stack)
    copies[0].wait()
    fill_weights(local[0], turned, filled)
    for copy in copies[1:]:
        copy.wait()
    bricks = field.shape[0] // 2
    factors = [*near, *local[1:]]

    def outgoing(pair):
        rows = pl.ds(pl.multiple_of(pair * 2 * SLAB, 2 * SLAB), 2 * SLAB)
        return [
            pltpu.make_async_copy(here.at[:, rows, :], there.at[:, rows, :], gone.at[n, pair])
            for n, (here, there) in enumerate(leaving)
        ]

    @pl.loop(0, EDGE // 2)
    def _(pair):
        for part in range(2):
            some = slice(part * bricks, (part + 1) * bricks)
            lhs = [stack[some, 2 * pair + n].reshape(bricks * SLAB, 3 * C) for n in range(4)]
            shares = jnp.dot(
                jnp.concatenate(lhs, axis=1), filled[...], preferred_element_type=jnp.float32
            ).reshape(bricks * EDGE, EDGE, 6 * C)
            before, _ = before_and_behind(shares[:, :, : 2 * C])
            _, behind = before_and_behind(shares[:, :, 4 * C :])
            both = (before + shares[:, :, 2 * C : 4 * C] + behind).reshape(bricks * SLAB, 2 * C)
            for half in range(2):
                rows = pl.ds(pl.multiple_of((2 * pair + half) * SLAB, SLAB), SLAB)
                values = both[:, half * C : (half + 1) * C].reshape(bricks, SLAB, C)
                values = finish(
                    values, *[array[some, rows, :].astype(jnp.float32) for array in factors]
                )
                for array, value in zip(made, values):
                    array[some, rows, :] = value.astype(jnp.bfloat16)
        for copy in outgoing(pair):
            copy.start()

    if edges:
        edges[0][...] = made[-1][:, :SLAB, :]
        edges[1][...] = made[-1][:, (EDGE - 1) * SLAB :, :]
    for pair in range(EDGE // 2):
        for copy in outgoing(pair):
            copy.wait()


def finish_first(values, mask):
    s = jax.nn.sigmoid(values)
    return mask * (s * (1.0 + values * (1.0 - s))), mask * (values * s)


def finish_second(values, mask, cotangent):
    s = jax.nn.sigmoid(values)
    return mask * (values * s), cotangent * mask * (s * (1.0 + values * (1.0 - s)))


def finish_product(values, factor):
    return (factor * values,)


def weight_kernel(scale, counted, facts, neighbours, field, left, right, grads, *rest):
    outs, rest = rest[: -(EDGE + 5)], rest[-(EDGE + 5) :]
    stack, turned, total, blocks = rest[: EDGE + 2], rest[-3], rest[-2], rest[-1]
    bricks = grads.shape[0]

    def turn(a):
        slab = grads[:, a * SLAB : (a + 1) * SLAB, :].reshape(bricks * SLAB, C)
        turned[a] = slab.astype(jnp.float32).T.astype(jnp.bfloat16)

    build_slab(facts, neighbours, field, left, right, 0, stack[0])
    turn(0)
    for a in range(EDGE + 2):
        if a < EDGE + 1:
            build_slab(facts, neighbours, field, left, right, a + 1, stack[a + 1])
        if a < EDGE - 1:
            turn(a + 1)
        first, last = max(0, a - EDGE + 1), min(3, a + 1)
        lhs = [turned[a - k1] for k1 in range(first, last)]
        product = jnp.dot(
            lhs[0] if len(lhs) == 1 else jnp.concatenate(lhs, axis=0),
            stack[a][...].reshape(bricks * SLAB, TAPS),
            preferred_element_type=jnp.float32,
        )
        for n, k1 in enumerate(range(first, last)):
            rows, part = slice(k1 * C, (k1 + 1) * C), product[n * C : (n + 1) * C]
            total[rows, :] = part if a == k1 else total[rows, :] + part
    for n in range(27):
        k1, t = n // 9, n % 9
        block = total[k1 * C : (k1 + 1) * C, t * C : (t + 1) * C].T * scale
        blocks[n * C : (n + 1) * C, :] = block.astype(jnp.bfloat16)
    strays = 0
    for g in range(bricks if counted else 0):
        for column in range(len(DIRECTIONS)):
            lost = (neighbours[g, column] >= 0) & (entry(facts, neighbours, g, column) < 0)
            strays = strays + jnp.where(lost, 1, 0)
    strays = jnp.full((C, C), jnp.minimum(strays, 1), jnp.int32)
    blocks[27 * C :, :] = strays.astype(jnp.float32).astype(jnp.bfloat16)
    n = 1
    for out in outs:
        for piece in range(out.shape[0]):
            first = pl.multiple_of(facts[n], 16)
            out[piece] = blocks[pl.ds(first, out.shape[1]), :]
            n += 1


def join_kernel(places, *rest):
    *pieces, result, blocks, arrived = rest
    for n, piece in enumerate(pieces):
        first = pl.multiple_of(places[n], 16)
        blocks[pl.ds(first, piece.shape[0]), :] = piece[...].astype(jnp.float32)
    copy = pltpu.make_async_copy(blocks.at[pl.ds(0, 27 * C)], result, arrived)
    copy.start()
    copy.wait()


def cost(flops, arrays):
    return pl.CostEstimate(
        flops=flops,
        bytes_accessed=sum(math.prod(a.shape) * a.dtype.itemsize for a in arrays),
        transcendentals=0,
    )


def run_conv(
    finish, turned, masked, facts, neighbours, field, left, right, weights, near, far, kinds
):
    bricks, voxels, _ = field.shape
    rows = jax.ShapeDtypeStruct((bricks, voxels, C), jnp.bfloat16)
    edge = jax.ShapeDtypeStruct((bricks, SLAB, C), jnp.bfloat16)
    operands = [weights, *far]
    spaces = {"vmem": pltpu.VMEM, "hbm": pltpu.HBM}
    outs = [(rows, spaces[kind]) for kind in kinds]
    outs += [(edge, pltpu.VMEM)] * (2 * (kinds[-1] == "vmem")) + [(rows, pltpu.VMEM)] * masked
    n_hbm = kinds.count("hbm")
    return pl.pallas_call(
        functools.partial(conv_kernel, finish, turned, masked, len(near), len(far), kinds),
        in_specs=[
            *[pl.BlockSpec(memory_space=pltpu.SMEM)] * 2,
            *[pl.BlockSpec(memory_space=pltpu.VMEM)] * (3 + len(near)),
            *[pl.BlockSpec(memory_space=pltpu.HBM) for _ in operands],
        ],
        out_specs=[pl.BlockSpec(memory_space=space) for _, space in outs],
        out_shape=[shape for shape, _ in outs],
        scratch_shapes=[
            *[pltpu.VMEM(a.shape, a.dtype) for a in operands],
            *[pltpu.VMEM(rows.shape, rows.dtype)] * n_hbm,
            pltpu.VMEM((bricks, EDGE + 2, SLAB, 3 * C), jnp.bfloat16),
            pltpu.VMEM((12 * C, 6 * C), jnp.bfloat16),
            pltpu.SemaphoreType.DMA((len(operands),)),
            pltpu.SemaphoreType.DMA((max(n_hbm, 1), EDGE // 2)),
        ],
        compiler_params=pltpu.CompilerParams(vmem_limit_bytes=VMEM_LIMIT),
        cost_estimate=cost(
            2 * 36 * bricks * voxels * C * C, [field, *near, *operands] + [shape for shape, _ in outs]
        ),
    )(facts, neighbours, field, left, right, *near, *operands)


def run_weight(facts, neighbours, field, left, right, grads, scale, shapes, counted):
    bricks, voxels, _ = field.shape
    outs = [jax.ShapeDtypeStruct((*shape, C), jnp.bfloat16) for shape in shapes]
    return pl.pallas_call(
        functools.partial(weight_kernel, scale, counted),
        in_specs=[
            *[pl.BlockSpec(memory_space=pltpu.SMEM)] * 2,
            *[pl.BlockSpec(memory_space=pltpu.VMEM)] * 4,
        ],
        out_specs=[pl.BlockSpec(memory_space=pltpu.VMEM) for _ in outs],
        out_shape=outs,
        scratch_shapes=[
            *[pltpu.VMEM((bricks, SLAB, TAPS), jnp.bfloat16)] * (EDGE + 2),
            pltpu.VMEM((EDGE, C, bricks * SLAB), jnp.bfloat16),
            pltpu.VMEM((3 * C, TAPS), jnp.float32),
            pltpu.VMEM((28 * C, C), jnp.bfloat16),
        ],
        compiler_params=pltpu.CompilerParams(vmem_limit_bytes=VMEM_LIMIT),
        cost_estimate=cost(2 * 27 * bricks * voxels * C * C, [field, left, right, grads, *outs]),
    )(facts, neighbours, field, left, right, grads)


def run_join(places, pieces):
    out = jax.ShapeDtypeStruct((27 * C, C), jnp.float32)
    return pl.pallas_call(
        join_kernel,
        in_specs=[
            pl.BlockSpec(memory_space=pltpu.SMEM),
            *[pl.BlockSpec(memory_space=pltpu.VMEM) for _ in pieces],
        ],
        out_specs=pl.BlockSpec(memory_space=pltpu.HBM),
        out_shape=out,
        scratch_shapes=[pltpu.VMEM((28 * C, C), jnp.float32), pltpu.SemaphoreType.DMA],
        cost_estimate=cost(0, [out, *pieces]),
    )(places, *pieces).reshape(27, C, C)


def beside(low, high):
    count = lax.axis_size("space")
    left = lax.ppermute(high, "space", [(i, i + 1) for i in range(count - 1)])
    right = lax.ppermute(low, "space", [(i + 1, i) for i in range(count - 1)])
    return left, right


def across(values, mask):
    count = lax.axis_size("space")
    return lax.ppermute(values, "space", [(i, i ^ mask) for i in range(count)])


def swapped(half):
    return across(half, 1)


def among(parts):
    count = lax.axis_size("space")
    groups = [[i for i in range(count) if i % 2 == b] for b in range(2)]
    return lax.all_to_all(parts, "space", 0, 0, axis_index_groups=groups, tiled=True)


def handed(part):
    members = lax.axis_size("space") // 2
    masks = [*range(members // 2, members), *range(1, members // 2)]
    came = {m: across(part, 2 * m) for m in masks}
    return [part, *[came[m] for m in range(1, members)]]


def pair_sum(sent, kept):
    total = kept.astype(jnp.float32) + swapped(sent).astype(jnp.float32)
    return total.astype(jnp.bfloat16)


def in_parts(half):
    return half.reshape(lax.axis_size("space") // 2, -1, C)


def part_total(parts):
    return jnp.sum(parts.astype(jnp.float32), axis=0).astype(jnp.bfloat16)


def gathered(part):
    members = lax.axis_size("space") // 2
    return among(jnp.broadcast_to(part[None], (members,) + part.shape)).reshape(14, C, C)


def joined(half):
    other = swapped(half)
    even = lax.axis_index("space") % 2 == 0
    first = jnp.where(even, half, other)
    second = jnp.where(even, other, half)
    blocks = jnp.concatenate([first, second[:13]], axis=0).astype(jnp.float32)
    return blocks, second[13, 0, 0].astype(jnp.float32)


def column_body(feats, mask, neighbours, weight_one, weight_two, cotangent):
    bricks, voxels, channels = feats.shape
    my_index = lax.axis_index("space")
    low, high = (
        feats[:, rows] * mask[:, rows, None].astype(jnp.bfloat16)
        for rows in (slice(0, SLAB), slice(voxels - SLAB, voxels))
    )
    in_left, in_right = beside(low, high)
    spread_mask = jnp.broadcast_to(mask.astype(jnp.bfloat16)[:, :, None], feats.shape)
    scale = 1.0 / math.sqrt(voxels * bricks)

    members = lax.axis_size("space") // 2
    bit, row = my_index % 2, my_index // 2
    rows = 28 * C // (2 * members)
    order = [*range(members // 2, members), *range(members // 2)]
    own = [(bit * members + (row ^ m)) * rows for m in range(members)]
    others = [((1 - bit) * members + (row ^ m)) * rows for m in range(members)]
    half_facts = jnp.stack([my_index, (1 - bit) * 14 * C, bit * 14 * C])
    part_facts = jnp.stack([my_index, *[others[m] for m in order], *[own[m] for m in order]])
    places = jnp.stack([*own, *others])
    together = lax.optimization_barrier
    in_left, in_right, spread_mask, half_facts = together(
        (in_left, in_right, spread_mask, half_facts)
    )

    slope, hidden, low, high, inputs = run_conv(
        finish_first, False, True, half_facts, neighbours, feats, in_left, in_right, weight_one,
        [spread_mask], [], ("vmem", "vmem"),
    )
    h_left, h_right = beside(low, high)
    output, grad_second, low, high = run_conv(
        finish_second, False, False, half_facts, neighbours, hidden, h_left, h_right, weight_two,
        [spread_mask], [cotangent], ("hbm", "vmem"),
    )
    s_left, s_right = beside(low, high)
    sent, kept = run_weight(
        half_facts, neighbours, hidden, h_left, h_right, grad_second, scale,
        [(1, 14 * C)] * 2, True,
    )
    sent, s_left, s_right = together((sent, s_left, s_right))
    half_two = pair_sum(sent, kept)
    grad_first, low, high = run_conv(
        finish_product, True, False, half_facts, neighbours, grad_second, s_left, s_right, weight_two,
        [slope], [], ("vmem",),
    )
    half_two, grad_first = together((half_two, grad_first))
    parts_two = among(in_parts(half_two))
    far = members - members // 2
    sent_far, sent_near, kept = run_weight(
        part_facts, neighbours, inputs, in_left, in_right, grad_first, scale,
        [(far, rows), (members // 2, rows), (members, rows)], False,
    )
    sent_far, sent_near, low, high, parts_two = together(
        (sent_far, sent_near, low, high, parts_two)
    )
    part_two = part_total(parts_two)
    received = {
        m: piece[n]
        for piece, masks in ((swapped(sent_far), order[:far]), (swapped(sent_near), order[far:]))
        for n, m in enumerate(masks)
    }
    half_two = gathered(part_two)
    f_left, f_right = beside(low, high)

    def summed(m):
        return kept[order.index(m)].astype(jnp.float32) + received[m].astype(jnp.float32)

    halves = [summed(m).astype(jnp.bfloat16) for m in order if m]
    *halves, f_left, f_right = together((*halves, f_left, f_right))
    arrived = [across(half, 2 * m) for half, m in zip(halves, [m for m in order if m])]
    (grad_input,) = run_conv(
        finish_product, True, False, half_facts, neighbours, grad_first, f_left, f_right,
        weight_one, [spread_mask], [], ("hbm",),
    )
    *arrived, grad_input = together((*arrived, grad_input))
    part = summed(0)
    for half in arrived:
        part = part + half.astype(jnp.float32)
    part = part.astype(jnp.bfloat16)
    same = handed(part)
    other = [swapped(piece) for piece in same]
    grad_w2, strays = joined(half_two)
    *other, grad_w2, strays = together((*other, grad_w2, strays))
    grad_w1 = run_join(places, [*same, *other])
    return strays, (output, grad_input, grad_w1, grad_w2)


def body(*arguments):
    strays, results = column_body(*arguments)

    def again(state):
        return jnp.zeros_like(state[0]), general_body(*arguments)

    return lax.while_loop(lambda state: state[0] > 0.5, again, (strays, results))[1]


def extended(field, source_index):
    bricks = field.shape[0]
    left, right = beside(field, field)
    blank = jnp.zeros((1, *field.shape[1:]), field.dtype)
    sources = jnp.concatenate([left, field, right, blank], axis=0).reshape(-1, EDGE * C)
    cell = jnp.arange(EDGE + 2)
    side = jnp.where(cell == 0, 0, jnp.where(cell == EDGE + 1, 2, 1))
    direction = 3 * side[:, None] + side[None, :]
    own = bricks + jnp.arange(bricks)[:, None]
    named = jnp.concatenate([source_index[:, :4], own, source_index[:, 4:]], axis=1)
    place = (cell - 1) % EDGE
    columns = named[:, direction] * SLAB + place[:, None] * EDGE + place[None, :]
    padded = jnp.take(sources, columns, axis=0).reshape(bricks, EDGE + 2, EDGE + 2, EDGE, C)
    return jnp.pad(padded, ((0, 0), (0, 0), (0, 0), (1, 1), (0, 0)))


def shifted(padded, k):
    bricks = padded.shape[0]
    corner = (0, k // 9, k // 3 % 3, k % 3, 0)
    return lax.dynamic_slice(padded, corner, (bricks, EDGE, EDGE, EDGE, C)).reshape(-1, C)


def general_conv(padded, weight, turned):
    def add(k, total):
        block = lax.dynamic_index_in_dim(weight, k, keepdims=False)
        cells = shifted(padded, 26 - k if turned else k)
        return total + jnp.dot(
            cells, block.T if turned else block, preferred_element_type=jnp.float32
        )

    rows = padded.shape[0] * EDGE**3
    return lax.fori_loop(0, 27, add, jnp.zeros((rows, C), jnp.float32))


def general_grad(padded, grads, scale):
    def one(k):
        contract = (((0,), (0,)), ((), ()))
        return lax.dot_general(
            shifted(padded, k), grads, contract, preferred_element_type=jnp.float32
        )

    term = (lax.map(one, jnp.arange(27)) * scale).astype(jnp.bfloat16)
    halves = jnp.pad(term, ((0, 1), (0, 0), (0, 0))).reshape(2, 14, C, C)
    even = lax.axis_index("space") % 2 == 0
    sent = jnp.where(even, halves[1], halves[0])
    kept = jnp.where(even, halves[0], halves[1])
    return joined(gathered(part_total(among(in_parts(pair_sum(sent, kept))))))[0]


def silu_slope(values):
    s = jax.nn.sigmoid(values)
    return s * (1.0 + values * (1.0 - s))


def general_body(feats, mask, neighbours, weight_one, weight_two, cotangent):
    bricks, voxels, _ = feats.shape
    first_brick = (lax.axis_index("space") - 1) * bricks
    source_index = jnp.where(neighbours >= 0, neighbours - first_brick, 3 * bricks)
    occupied = mask.reshape(-1, 1).astype(jnp.float32)
    scale = 1.0 / math.sqrt(voxels * bricks)

    def rounded(values):
        return values.astype(jnp.bfloat16)

    def extend(values):
        return extended(values.reshape(bricks, voxels, C), source_index)

    padded_in = extend(feats * mask[:, :, None].astype(jnp.bfloat16))
    first_pre = general_conv(padded_in, weight_one, False)
    padded_hidden = extend(rounded(occupied * jax.nn.silu(first_pre)))
    second_pre = general_conv(padded_hidden, weight_two, False)
    output = rounded(occupied * jax.nn.silu(second_pre))
    received = cotangent.reshape(-1, C).astype(jnp.float32)
    grad_second = rounded(received * occupied * silu_slope(second_pre))
    back_second = general_conv(extend(grad_second), weight_two, True)
    grad_first = rounded(occupied * silu_slope(first_pre) * back_second)
    grad_input = rounded(occupied * general_conv(extend(grad_first), weight_one, True))
    return (
        output.reshape(feats.shape),
        grad_input.reshape(feats.shape),
        general_grad(padded_in, grad_first, scale),
        general_grad(padded_hidden, grad_second, scale),
    )


def solution(mesh):
    in_specs = (
        P(("scene", "space"), None, None),
        P(("scene", "space"), None),
        P(("scene", "space"), None),
        P(),
        P(),
        P(("scene", "space"), None, None),
    )
    out_specs = (
        P(("scene", "space"), None, None),
        P(("scene", "space"), None, None),
        P("scene", None, None),
        P("scene", None, None),
    )
    return jax.shard_map(body, mesh=mesh, in_specs=in_specs, out_specs=out_specs, check_vma=False)
```

```python
import functools
import math

import jax
import jax.numpy as jnp
from jax import lax
from jax.experimental import pallas as pl
from jax.experimental.pallas import tpu as pltpu
from jax.sharding import PartitionSpec as P

EDGE = 8
TILE = 1
WIDE = 8
SLAB = EDGE * EDGE
C = 128
TAPS = 9 * C
VMEM_LIMIT = 36 * 1024 * 1024

DIRECTIONS = ((-1, -1), (-1, 0), (-1, 1), (0, -1), (0, 1), (1, -1), (1, 0), (1, 1))


def entry(facts, neighbours, brick, column):
    named = neighbours[brick, column]
    local = named - (facts[0] + DIRECTIONS[column][0]) * (TILE * WIDE)
    inside = (named >= 0) & (local >= 0) & (local < neighbours.shape[0])
    return jnp.where(inside, local, -1)


def picked(source, index, first, rows):
    found = source[jnp.maximum(index, 0), first : first + rows, :].astype(jnp.float32)
    return jnp.where(index >= 0, found, 0.0)


def padded_cells(facts, neighbours, field, left, right, g, a):
    near = functools.partial(entry, facts, neighbours, g)
    if a == 0:
        source, first, names = left, 0, (near(1), near(0), near(2))
    elif a == EDGE + 1:
        source, first, names = right, 0, (near(6), near(5), near(7))
    else:
        source, first, names = field, (a - 1) * SLAB, (g, near(3), near(4))
    if source is field:
        centre = field[g, first : first + SLAB, :].astype(jnp.float32)
    else:
        centre = picked(source, names[0], first, SLAB)
    top = picked(source, names[1], first + SLAB - 16, 16)
    bottom = picked(source, names[2], first, 16)
    return centre, jnp.concatenate([top[8:16], centre, bottom[0:8]], axis=0)


def before_and_behind(cells):
    place = lax.broadcasted_iota(jnp.int32, cells.shape, 1)
    before = jnp.where(place == 0, 0.0, pltpu.roll(cells, 1, 1))
    return before, jnp.where(place == EDGE - 1, 0.0, pltpu.roll(cells, EDGE - 1, 1))


def slab_tiles(cells):
    cells = cells.reshape(EDGE + 2, EDGE, C)
    before, behind = before_and_behind(cells)
    even, odd = [], []
    for shifted in (before, cells, behind):
        even.append(shifted.reshape((EDGE + 2) * EDGE, C).astype(jnp.bfloat16))
        odd.append(shifted[1 : EDGE + 1].reshape(SLAB, C).astype(jnp.bfloat16))
    return [e[0:SLAB] for e in even] + odd + [e[16 : 16 + SLAB] for e in even]


def build_slab(facts, neighbours, field, left, right, a, stack):
    for g in range(field.shape[0]):
        _, cells = padded_cells(facts, neighbours, field, left, right, g, a)
        for t, tile in enumerate(slab_tiles(cells)):
            stack[g, :, t * C : (t + 1) * C] = tile


def build_rows(facts, neighbours, field, left, right, stack):
    @pl.loop(0, field.shape[0])
    def _(g):
        for a in range(EDGE + 2):
            centre, cells = padded_cells(facts, neighbours, field, left, right, g, a)
            cells = cells.astype(jnp.bfloat16)
            stack[g, a, :, 0:C] = cells[0:SLAB]
            stack[g, a, :, C : 2 * C] = centre.astype(jnp.bfloat16)
            stack[g, a, :, 2 * C :] = cells[16 : 16 + SLAB]


def fill_weights(weights, turned, filled):
    for k1 in range(3):
        for k2 in range(3):
            for k3 in range(3):
                n = 9 * k1 + 3 * k2 + k3
                block = weights[26 - n if turned else n]
                if turned:
                    block = block.astype(jnp.float32).T.astype(jnp.bfloat16)
                for half in range(2):
                    row, column = 3 * (k1 + half) + k2, 2 * k3 + half
                    filled[row * C : (row + 1) * C, column * C : (column + 1) * C] = block
    blank = jnp.zeros((3 * C, C), jnp.bfloat16)
    for k3 in range(3):
        filled[9 * C :, 2 * k3 * C : (2 * k3 + 1) * C] = blank
        filled[: 3 * C, (2 * k3 + 1) * C : (2 * k3 + 2) * C] = blank


def conv_kernel(finish, turned, masked, n_near, n_far, kinds, facts, neighbours, *rest):
    field, left, right, *rest = rest
    near, rest = rest[:n_near], rest[n_near:]
    operands, rest = rest[: 1 + n_far], rest[1 + n_far :]
    results, rest = rest[: len(kinds)], rest[len(kinds) :]
    edges, rest = (rest[:2], rest[2:]) if kinds[-1] == "vmem" else ((), rest)
    kept, rest = (rest[0], rest[1:]) if masked else (None, rest)
    local, rest = rest[: 1 + n_far], rest[1 + n_far :]
    *staged, stack, filled, came, gone = rest
    made, leaving = [], []
    for kind, result in zip(kinds, results):
        made.append(result if kind == "vmem" else staged.pop(0))
        if kind == "hbm":
            leaving.append((made[-1], result))
    copies = [
        pltpu.make_async_copy(there, here, came.at[n])
        for n, (there, here) in enumerate(zip(operands, local))
    ]
    for copy in copies:
        copy.start()
    if masked:
        kept[...] = field[...] * near[0][...]
        field = kept
    build_rows(facts, neighbours, field, left, right, stack)
    copies[0].wait()
    fill_weights(local[0], turned, filled)
    for copy in copies[1:]:
        copy.wait()
    bricks = field.shape[0] // 2
    factors = [*near, *local[1:]]

    def outgoing(pair):
        rows = pl.ds(pl.multiple_of(pair * 2 * SLAB, 2 * SLAB), 2 * SLAB)
        return [
            pltpu.make_async_copy(here.at[:, rows, :], there.at[:, rows, :], gone.at[n, pair])
            for n, (here, there) in enumerate(leaving)
        ]

    def step(pair):
        for part in range(2):
            some = slice(part * bricks, (part + 1) * bricks)
            lhs = [stack[some, 2 * pair + n].reshape(bricks * SLAB, 3 * C) for n in range(4)]
            shares = jnp.dot(
                jnp.concatenate(lhs, axis=1), filled[...], preferred_element_type=jnp.float32
            ).reshape(bricks * EDGE, EDGE, 6 * C)
            before, _ = before_and_behind(shares[:, :, : 2 * C])
            _, behind = before_and_behind(shares[:, :, 4 * C :])
            both = (before + shares[:, :, 2 * C : 4 * C] + behind).reshape(bricks * SLAB, 2 * C)
            for half in range(2):
                rows = pl.ds(pl.multiple_of((2 * pair + half) * SLAB, SLAB), SLAB)
                values = both[:, half * C : (half + 1) * C].reshape(bricks, SLAB, C)
                values = finish(
                    values, *[array[some, rows, :].astype(jnp.float32) for array in factors]
                )
                for array, value in zip(made, values):
                    array[some, rows, :] = value.astype(jnp.bfloat16)
        for copy in outgoing(pair):
            copy.start()

    @pl.loop(0, EDGE // 4)
    def _(n):
        step(2 * n)
        step(2 * n + 1)

    if edges:
        edges[0][...] = made[-1][:, :SLAB, :]
        edges[1][...] = made[-1][:, (EDGE - 1) * SLAB :, :]
    for pair in range(EDGE // 2):
        for copy in outgoing(pair):
            copy.wait()


def finish_first(values, mask):
    s = jax.nn.sigmoid(values)
    return mask * (s * (1.0 + values * (1.0 - s))), mask * (values * s)


def finish_second(values, mask, cotangent):
    s = jax.nn.sigmoid(values)
    return mask * (values * s), cotangent * mask * (s * (1.0 + values * (1.0 - s)))


def finish_product(values, factor):
    return (factor * values,)


def weight_kernel(scale, counted, facts, neighbours, field, left, right, grads, *rest):
    outs, rest = rest[: -(EDGE + 5)], rest[-(EDGE + 5) :]
    stack, turned, total, blocks = rest[: EDGE + 2], rest[-3], rest[-2], rest[-1]
    bricks = grads.shape[0]

    def turn(a):
        slab = grads[:, a * SLAB : (a + 1) * SLAB, :].reshape(bricks * SLAB, C)
        turned[a] = slab.astype(jnp.float32).T.astype(jnp.bfloat16)

    build_slab(facts, neighbours, field, left, right, 0, stack[0])
    turn(0)
    for a in range(EDGE + 2):
        if a < EDGE + 1:
            build_slab(facts, neighbours, field, left, right, a + 1, stack[a + 1])
        if a < EDGE - 1:
            turn(a + 1)
        first, last = max(0, a - EDGE + 1), min(3, a + 1)
        lhs = [turned[a - k1] for k1 in range(first, last)]
        product = jnp.dot(
            lhs[0] if len(lhs) == 1 else jnp.concatenate(lhs, axis=0),
            stack[a][...].reshape(bricks * SLAB, TAPS),
            preferred_element_type=jnp.float32,
        )
        for n, k1 in enumerate(range(first, last)):
            rows, part = slice(k1 * C, (k1 + 1) * C), product[n * C : (n + 1) * C]
            total[rows, :] = part if a == k1 else total[rows, :] + part
    for n in range(27):
        k1, t = n // 9, n % 9
        block = total[k1 * C : (k1 + 1) * C, t * C : (t + 1) * C].T * scale
        blocks[n * C : (n + 1) * C, :] = block.astype(jnp.bfloat16)
    strays = 0
    for g in range(bricks if counted else 0):
        for column in range(len(DIRECTIONS)):
            lost = (neighbours[g, column] >= 0) & (entry(facts, neighbours, g, column) < 0)
            strays = strays + jnp.where(lost, 1, 0)
    strays = jnp.full((C, C), jnp.minimum(strays, 1), jnp.int32)
    blocks[27 * C :, :] = strays.astype(jnp.float32).astype(jnp.bfloat16)
    n = 1
    for out in outs:
        for piece in range(out.shape[0]):
            first = pl.multiple_of(facts[n], 16)
            out[piece] = blocks[pl.ds(first, out.shape[1]), :]
            n += 1


def join_kernel(places, *rest):
    *pieces, result, blocks, arrived = rest
    for n, piece in enumerate(pieces):
        first = pl.multiple_of(places[n], 16)
        blocks[pl.ds(first, piece.shape[0]), :] = piece[...].astype(jnp.float32)
    copy = pltpu.make_async_copy(blocks.at[pl.ds(0, 27 * C)], result, arrived)
    copy.start()
    copy.wait()


def cost(flops, arrays):
    return pl.CostEstimate(
        flops=flops,
        bytes_accessed=sum(math.prod(a.shape) * a.dtype.itemsize for a in arrays),
        transcendentals=0,
    )


def run_conv(
    finish, turned, masked, facts, neighbours, field, left, right, weights, near, far, kinds
):
    bricks, voxels, _ = field.shape
    rows = jax.ShapeDtypeStruct((bricks, voxels, C), jnp.bfloat16)
    edge = jax.ShapeDtypeStruct((bricks, SLAB, C), jnp.bfloat16)
    operands = [weights, *far]
    spaces = {"vmem": pltpu.VMEM, "hbm": pltpu.HBM}
    outs = [(rows, spaces[kind]) for kind in kinds]
    outs += [(edge, pltpu.VMEM)] * (2 * (kinds[-1] == "vmem")) + [(rows, pltpu.VMEM)] * masked
    n_hbm = kinds.count("hbm")
    return pl.pallas_call(
        functools.partial(conv_kernel, finish, turned, masked, len(near), len(far), kinds),
        in_specs=[
            *[pl.BlockSpec(memory_space=pltpu.SMEM)] * 2,
            *[pl.BlockSpec(memory_space=pltpu.VMEM)] * (3 + len(near)),
            *[pl.BlockSpec(memory_space=pltpu.HBM) for _ in operands],
        ],
        out_specs=[pl.BlockSpec(memory_space=space) for _, space in outs],
        out_shape=[shape for shape, _ in outs],
        scratch_shapes=[
            *[pltpu.VMEM(a.shape, a.dtype) for a in operands],
            *[pltpu.VMEM(rows.shape, rows.dtype)] * n_hbm,
            pltpu.VMEM((bricks, EDGE + 2, SLAB, 3 * C), jnp.bfloat16),
            pltpu.VMEM((12 * C, 6 * C), jnp.bfloat16),
            pltpu.SemaphoreType.DMA((len(operands),)),
            pltpu.SemaphoreType.DMA((max(n_hbm, 1), EDGE // 2)),
        ],
        compiler_params=pltpu.CompilerParams(vmem_limit_bytes=VMEM_LIMIT),
        cost_estimate=cost(
            2 * 36 * bricks * voxels * C * C, [field, *near, *operands] + [shape for shape, _ in outs]
        ),
    )(facts, neighbours, field, left, right, *near, *operands)


def run_weight(facts, neighbours, field, left, right, grads, scale, shapes, counted):
    bricks, voxels, _ = field.shape
    outs = [jax.ShapeDtypeStruct((*shape, C), jnp.bfloat16) for shape in shapes]
    return pl.pallas_call(
        functools.partial(weight_kernel, scale, counted),
        in_specs=[
            *[pl.BlockSpec(memory_space=pltpu.SMEM)] * 2,
            *[pl.BlockSpec(memory_space=pltpu.VMEM)] * 4,
        ],
        out_specs=[pl.BlockSpec(memory_space=pltpu.VMEM) for _ in outs],
        out_shape=outs,
        scratch_shapes=[
            *[pltpu.VMEM((bricks, SLAB, TAPS), jnp.bfloat16)] * (EDGE + 2),
            pltpu.VMEM((EDGE, C, bricks * SLAB), jnp.bfloat16),
            pltpu.VMEM((3 * C, TAPS), jnp.float32),
            pltpu.VMEM((28 * C, C), jnp.bfloat16),
        ],
        compiler_params=pltpu.CompilerParams(vmem_limit_bytes=VMEM_LIMIT),
        cost_estimate=cost(2 * 27 * bricks * voxels * C * C, [field, left, right, grads, *outs]),
    )(facts, neighbours, field, left, right, grads)


def run_join(places, pieces):
    out = jax.ShapeDtypeStruct((27 * C, C), jnp.float32)
    return pl.pallas_call(
        join_kernel,
        in_specs=[
            pl.BlockSpec(memory_space=pltpu.SMEM),
            *[pl.BlockSpec(memory_space=pltpu.VMEM) for _ in pieces],
        ],
        out_specs=pl.BlockSpec(memory_space=pltpu.HBM),
        out_shape=out,
        scratch_shapes=[pltpu.VMEM((28 * C, C), jnp.float32), pltpu.SemaphoreType.DMA],
        cost_estimate=cost(0, [out, *pieces]),
    )(places, *pieces).reshape(27, C, C)


def beside(low, high):
    count = lax.axis_size("space")
    left = lax.ppermute(high, "space", [(i, i + 1) for i in range(count - 1)])
    right = lax.ppermute(low, "space", [(i + 1, i) for i in range(count - 1)])
    return left, right


def across(values, mask):
    count = lax.axis_size("space")
    return lax.ppermute(values, "space", [(i, i ^ mask) for i in range(count)])


def swapped(half):
    return across(half, 1)


def among(parts):
    count = lax.axis_size("space")
    groups = [[i for i in range(count) if i % 2 == b] for b in range(2)]
    return lax.all_to_all(parts, "space", 0, 0, axis_index_groups=groups, tiled=True)


def handed(part):
    members = lax.axis_size("space") // 2
    masks = [*range(members // 2, members), *range(1, members // 2)]
    came = {m: across(part, 2 * m) for m in masks}
    return [part, *[came[m] for m in range(1, members)]]


def pair_sum(sent, kept):
    total = kept.astype(jnp.float32) + swapped(sent).astype(jnp.float32)
    return total.astype(jnp.bfloat16)


def in_parts(half):
    return half.reshape(lax.axis_size("space") // 2, -1, C)


def part_total(parts):
    return jnp.sum(parts.astype(jnp.float32), axis=0).astype(jnp.bfloat16)


def gathered(part):
    members = lax.axis_size("space") // 2
    return among(jnp.broadcast_to(part[None], (members,) + part.shape)).reshape(14, C, C)


def joined(half):
    other = swapped(half)
    even = lax.axis_index("space") % 2 == 0
    first = jnp.where(even, half, other)
    second = jnp.where(even, other, half)
    blocks = jnp.concatenate([first, second[:13]], axis=0).astype(jnp.float32)
    return blocks, second[13, 0, 0].astype(jnp.float32)


def column_body(feats, mask, neighbours, weight_one, weight_two, cotangent):
    bricks, voxels, channels = feats.shape
    my_index = lax.axis_index("space")
    low, high = (
        feats[:, rows] * mask[:, rows, None].astype(jnp.bfloat16)
        for rows in (slice(0, SLAB), slice(voxels - SLAB, voxels))
    )
    in_left, in_right = beside(low, high)
    spread_mask = jnp.broadcast_to(mask.astype(jnp.bfloat16)[:, :, None], feats.shape)
    scale = 1.0 / math.sqrt(voxels * bricks)

    members = lax.axis_size("space") // 2
    bit, row = my_index % 2, my_index // 2
    rows = 28 * C // (2 * members)
    order = [*range(members // 2, members), *range(members // 2)]
    own = [(bit * members + (row ^ m)) * rows for m in range(members)]
    others = [((1 - bit) * members + (row ^ m)) * rows for m in range(members)]
    starts = [(i % 2 * members + i // 2) * rows for i in range(2 * members)]
    all_facts = jnp.stack([my_index, *starts])
    part_facts = jnp.stack([my_index, *[others[m] for m in order], *[own[m] for m in order]])
    places = jnp.stack([*own, *others])
    together = lax.optimization_barrier
    in_left, in_right, spread_mask, all_facts = together(
        (in_left, in_right, spread_mask, all_facts)
    )

    slope, hidden, low, high, inputs = run_conv(
        finish_first, False, True, all_facts, neighbours, feats, in_left, in_right, weight_one,
        [spread_mask], [], ("vmem", "vmem"),
    )
    h_left, h_right = beside(low, high)
    output, grad_second, low, high = run_conv(
        finish_second, False, False, all_facts, neighbours, hidden, h_left, h_right, weight_two,
        [spread_mask], [cotangent], ("hbm", "vmem"),
    )
    s_left, s_right = beside(low, high)
    (pieces_two,) = run_weight(
        all_facts, neighbours, hidden, h_left, h_right, grad_second, scale,
        [(2 * members, rows)], True,
    )
    pieces_two, s_left, s_right = together((pieces_two, s_left, s_right))
    parts_two = lax.all_to_all(pieces_two, "space", 0, 0, tiled=True)
    grad_first, low, high = run_conv(
        finish_product, True, False, all_facts, neighbours, grad_second, s_left, s_right, weight_two,
        [slope], [], ("vmem",),
    )
    far = members - members // 2
    sent_far, sent_near, kept = run_weight(
        part_facts, neighbours, inputs, in_left, in_right, grad_first, scale,
        [(far, rows), (members // 2, rows), (members, rows)], False,
    )
    parts_two, _ = together((parts_two, kept))
    part_two = part_total(parts_two)
    sent_far, sent_near, low, high = together((sent_far, sent_near, low, high))
    received = {
        m: piece[n]
        for piece, masks in ((swapped(sent_far), order[:far]), (swapped(sent_near), order[far:]))
        for n, m in enumerate(masks)
    }
    half_two = gathered(part_two)
    f_left, f_right = beside(low, high)

    def summed(m):
        return kept[order.index(m)].astype(jnp.float32) + received[m].astype(jnp.float32)

    halves = [summed(m).astype(jnp.bfloat16) for m in order if m]
    *halves, f_left, f_right, late_weight = together((*halves, f_left, f_right, weight_one))
    arrived = [across(half, 2 * m) for half, m in zip(halves, [m for m in order if m])]
    (grad_input,) = run_conv(
        finish_product, True, False, all_facts, neighbours, grad_first, f_left, f_right,
        late_weight, [spread_mask], [], ("hbm",),
    )
    *arrived, grad_input = together((*arrived, grad_input))
    part = summed(0)
    for half in arrived:
        part = part + half.astype(jnp.float32)
    part = part.astype(jnp.bfloat16)
    same = handed(part)
    other = [swapped(piece) for piece in same]
    grad_w2, strays = joined(half_two)
    *other, grad_w2, strays = together((*other, grad_w2, strays))
    grad_w1 = run_join(places, [*same, *other])
    return strays, (output, grad_input, grad_w1, grad_w2)


def body(*arguments):
    strays, results = column_body(*arguments)

    def again(state):
        return jnp.zeros_like(state[0]), general_body(*arguments)

    return lax.while_loop(lambda state: state[0] > 0.5, again, (strays, results))[1]


def extended(field, source_index):
    bricks = field.shape[0]
    left, right = beside(field, field)
    blank = jnp.zeros((1, *field.shape[1:]), field.dtype)
    sources = jnp.concatenate([left, field, right, blank], axis=0).reshape(-1, EDGE * C)
    cell = jnp.arange(EDGE + 2)
    side = jnp.where(cell == 0, 0, jnp.where(cell == EDGE + 1, 2, 1))
    direction = 3 * side[:, None] + side[None, :]
    own = bricks + jnp.arange(bricks)[:, None]
    named = jnp.concatenate([source_index[:, :4], own, source_index[:, 4:]], axis=1)
    place = (cell - 1) % EDGE
    columns = named[:, direction] * SLAB + place[:, None] * EDGE + place[None, :]
    padded = jnp.take(sources, columns, axis=0).reshape(bricks, EDGE + 2, EDGE + 2, EDGE, C)
    return jnp.pad(padded, ((0, 0), (0, 0), (0, 0), (1, 1), (0, 0)))


def shifted(padded, k):
    bricks = padded.shape[0]
    corner = (0, k // 9, k // 3 % 3, k % 3, 0)
    return lax.dynamic_slice(padded, corner, (bricks, EDGE, EDGE, EDGE, C)).reshape(-1, C)


def general_conv(padded, weight, turned):
    def add(k, total):
        block = lax.dynamic_index_in_dim(weight, k, keepdims=False)
        cells = shifted(padded, 26 - k if turned else k)
        return total + jnp.dot(
            cells, block.T if turned else block, preferred_element_type=jnp.float32
        )

    rows = padded.shape[0] * EDGE**3
    return lax.fori_loop(0, 27, add, jnp.zeros((rows, C), jnp.float32))


def general_grad(padded, grads, scale):
    def one(k):
        contract = (((0,), (0,)), ((), ()))
        return lax.dot_general(
            shifted(padded, k), grads, contract, preferred_element_type=jnp.float32
        )

    term = (lax.map(one, jnp.arange(27)) * scale).astype(jnp.bfloat16)
    halves = jnp.pad(term, ((0, 1), (0, 0), (0, 0))).reshape(2, 14, C, C)
    even = lax.axis_index("space") % 2 == 0
    sent = jnp.where(even, halves[1], halves[0])
    kept = jnp.where(even, halves[0], halves[1])
    return joined(gathered(part_total(among(in_parts(pair_sum(sent, kept))))))[0]


def silu_slope(values):
    s = jax.nn.sigmoid(values)
    return s * (1.0 + values * (1.0 - s))


def general_body(feats, mask, neighbours, weight_one, weight_two, cotangent):
    bricks, voxels, _ = feats.shape
    first_brick = (lax.axis_index("space") - 1) * bricks
    source_index = jnp.where(neighbours >= 0, neighbours - first_brick, 3 * bricks)
    occupied = mask.reshape(-1, 1).astype(jnp.float32)
    scale = 1.0 / math.sqrt(voxels * bricks)

    def rounded(values):
        return values.astype(jnp.bfloat16)

    def extend(values):
        return extended(values.reshape(bricks, voxels, C), source_index)

    padded_in = extend(feats * mask[:, :, None].astype(jnp.bfloat16))
    first_pre = general_conv(padded_in, weight_one, False)
    padded_hidden = extend(rounded(occupied * jax.nn.silu(first_pre)))
    second_pre = general_conv(padded_hidden, weight_two, False)
    output = rounded(occupied * jax.nn.silu(second_pre))
    received = cotangent.reshape(-1, C).astype(jnp.float32)
    grad_second = rounded(received * occupied * silu_slope(second_pre))
    back_second = general_conv(extend(grad_second), weight_two, True)
    grad_first = rounded(occupied * silu_slope(first_pre) * back_second)
    grad_input = rounded(occupied * general_conv(extend(grad_first), weight_one, True))
    return (
        output.reshape(feats.shape),
        grad_input.reshape(feats.shape),
        general_grad(padded_in, grad_first, scale),
        general_grad(padded_hidden, grad_second, scale),
    )


def solution(mesh):
    in_specs = (
        P(("scene", "space"), None, None),
        P(("scene", "space"), None),
        P(("scene", "space"), None),
        P(),
        P(),
        P(("scene", "space"), None, None),
    )
    out_specs = (
        P(("scene", "space"), None, None),
        P(("scene", "space"), None, None),
        P("scene", None, None),
        P("scene", None, None),
    )
    return jax.shard_map(body, mesh=mesh, in_specs=in_specs, out_specs=out_specs, check_vma=False)
```

```python
import functools
import math

import jax
import jax.numpy as jnp
from jax import lax
from jax.experimental import pallas as pl
from jax.experimental.pallas import tpu as pltpu
from jax.sharding import PartitionSpec as P

EDGE = 8
TILE = 1
WIDE = 8
SLAB = EDGE * EDGE
C = 128
TAPS = 9 * C
VMEM_LIMIT = 36 * 1024 * 1024

DIRECTIONS = ((-1, -1), (-1, 0), (-1, 1), (0, -1), (0, 1), (1, -1), (1, 0), (1, 1))


def entry(facts, neighbours, brick, column):
    named = neighbours[brick, column]
    local = named - (facts[0] + DIRECTIONS[column][0]) * (TILE * WIDE)
    inside = (named >= 0) & (local >= 0) & (local < neighbours.shape[0])
    return jnp.where(inside, local, -1)


def picked(source, index, first, rows):
    found = source[jnp.maximum(index, 0), first : first + rows, :].astype(jnp.float32)
    return jnp.where(index >= 0, found, 0.0)


def padded_cells(facts, neighbours, field, left, right, g, a):
    near = functools.partial(entry, facts, neighbours, g)
    if a == 0:
        source, first, names = left, 0, (near(1), near(0), near(2))
    elif a == EDGE + 1:
        source, first, names = right, 0, (near(6), near(5), near(7))
    else:
        source, first, names = field, (a - 1) * SLAB, (g, near(3), near(4))
    if source is field:
        centre = field[g, first : first + SLAB, :].astype(jnp.float32)
    else:
        centre = picked(source, names[0], first, SLAB)
    top = picked(source, names[1], first + SLAB - 16, 16)
    bottom = picked(source, names[2], first, 16)
    return centre, jnp.concatenate([top[8:16], centre, bottom[0:8]], axis=0)


def before_and_behind(cells):
    place = lax.broadcasted_iota(jnp.int32, cells.shape, 1)
    before = jnp.where(place == 0, 0.0, pltpu.roll(cells, 1, 1))
    return before, jnp.where(place == EDGE - 1, 0.0, pltpu.roll(cells, EDGE - 1, 1))


def slab_tiles(cells):
    cells = cells.reshape(EDGE + 2, EDGE, C)
    before, behind = before_and_behind(cells)
    even, odd = [], []
    for shifted in (before, cells, behind):
        even.append(shifted.reshape((EDGE + 2) * EDGE, C).astype(jnp.bfloat16))
        odd.append(shifted[1 : EDGE + 1].reshape(SLAB, C).astype(jnp.bfloat16))
    return [e[0:SLAB] for e in even] + odd + [e[16 : 16 + SLAB] for e in even]


def build_slab(facts, neighbours, field, left, right, a, stack):
    for g in range(field.shape[0]):
        _, cells = padded_cells(facts, neighbours, field, left, right, g, a)
        for t, tile in enumerate(slab_tiles(cells)):
            stack[g, :, t * C : (t + 1) * C] = tile


def build_rows(facts, neighbours, field, left, right, stack):
    @pl.loop(0, field.shape[0])
    def _(g):
        for a in range(EDGE + 2):
            centre, cells = padded_cells(facts, neighbours, field, left, right, g, a)
            cells = cells.astype(jnp.bfloat16)
            stack[g, a, :, 0:C] = cells[0:SLAB]
            stack[g, a, :, C : 2 * C] = centre.astype(jnp.bfloat16)
            stack[g, a, :, 2 * C :] = cells[16 : 16 + SLAB]


def fill_weights(weights, turned, filled):
    for k1 in range(3):
        for k2 in range(3):
            for k3 in range(3):
                n = 9 * k1 + 3 * k2 + k3
                block = weights[26 - n if turned else n]
                if turned:
                    block = block.astype(jnp.float32).T.astype(jnp.bfloat16)
                for half in range(2):
                    row, column = 3 * (k1 + half) + k2, 2 * k3 + half
                    filled[row * C : (row + 1) * C, column * C : (column + 1) * C] = block
    blank = jnp.zeros((3 * C, C), jnp.bfloat16)
    for k3 in range(3):
        filled[9 * C :, 2 * k3 * C : (2 * k3 + 1) * C] = blank
        filled[: 3 * C, (2 * k3 + 1) * C : (2 * k3 + 2) * C] = blank


def conv_kernel(finish, turned, masked, n_near, n_far, kinds, facts, neighbours, *rest):
    field, left, right, *rest = rest
    near, rest = rest[:n_near], rest[n_near:]
    operands, rest = rest[: 1 + n_far], rest[1 + n_far :]
    results, rest = rest[: len(kinds)], rest[len(kinds) :]
    edges, rest = (rest[:2], rest[2:]) if kinds[-1] == "vmem" else ((), rest)
    kept, rest = (rest[0], rest[1:]) if masked else (None, rest)
    local, rest = rest[: 1 + n_far], rest[1 + n_far :]
    *staged, stack, filled, came, gone = rest
    made, leaving = [], []
    for kind, result in zip(kinds, results):
        made.append(result if kind == "vmem" else staged.pop(0))
        if kind == "hbm":
            leaving.append((made[-1], result))
    copies = [
        pltpu.make_async_copy(there, here, came.at[n])
        for n, (there, here) in enumerate(zip(operands, local))
    ]
    for copy in copies:
        copy.start()
    if masked:
        kept[...] = field[...] * near[0][...]
        field = kept
    build_rows(facts, neighbours, field, left, right, stack)
    copies[0].wait()
    fill_weights(local[0], turned, filled)
    for copy in copies[1:]:
        copy.wait()
    bricks = field.shape[0] // 2
    factors = [*near, *local[1:]]

    def outgoing(pair):
        rows = pl.ds(pl.multiple_of(pair * 2 * SLAB, 2 * SLAB), 2 * SLAB)
        return [
            pltpu.make_async_copy(here.at[:, rows, :], there.at[:, rows, :], gone.at[n, pair])
            for n, (here, there) in enumerate(leaving)
        ]

    def step(pair):
        for part in range(2):
            some = slice(part * bricks, (part + 1) * bricks)
            lhs = [stack[some, 2 * pair + n].reshape(bricks * SLAB, 3 * C) for n in range(4)]
            shares = jnp.dot(
                jnp.concatenate(lhs, axis=1), filled[...], preferred_element_type=jnp.float32
            ).reshape(bricks * EDGE, EDGE, 6 * C)
            before, _ = before_and_behind(shares[:, :, : 2 * C])
            _, behind = before_and_behind(shares[:, :, 4 * C :])
            both = (before + shares[:, :, 2 * C : 4 * C] + behind).reshape(bricks * SLAB, 2 * C)
            for half in range(2):
                rows = pl.ds(pl.multiple_of((2 * pair + half) * SLAB, SLAB), SLAB)
                values = both[:, half * C : (half + 1) * C].reshape(bricks, SLAB, C)
                values = finish(
                    values, *[array[some, rows, :].astype(jnp.float32) for array in factors]
                )
                for array, value in zip(made, values):
                    array[some, rows, :] = value.astype(jnp.bfloat16)
        for copy in outgoing(pair):
            copy.start()

    @pl.loop(0, EDGE // 4)
    def _(n):
        step(2 * n)
        step(2 * n + 1)

    if edges:
        edges[0][...] = made[-1][:, :SLAB, :]
        edges[1][...] = made[-1][:, (EDGE - 1) * SLAB :, :]
    for pair in range(EDGE // 2):
        for copy in outgoing(pair):
            copy.wait()


def finish_first(values, mask):
    s = jax.nn.sigmoid(values)
    return mask * (s * (1.0 + values * (1.0 - s))), mask * (values * s)


def finish_second(values, mask, cotangent):
    s = jax.nn.sigmoid(values)
    return mask * (values * s), cotangent * mask * (s * (1.0 + values * (1.0 - s)))


def finish_product(values, factor):
    return (factor * values,)


def weight_kernel(scale, counted, facts, neighbours, field, left, right, grads, *rest):
    outs, rest = rest[: -(EDGE + 5)], rest[-(EDGE + 5) :]
    stack, turned, total, blocks = rest[: EDGE + 2], rest[-3], rest[-2], rest[-1]
    bricks = grads.shape[0]

    def turn(a):
        slab = grads[:, a * SLAB : (a + 1) * SLAB, :].reshape(bricks * SLAB, C)
        turned[a] = slab.astype(jnp.float32).T.astype(jnp.bfloat16)

    build_slab(facts, neighbours, field, left, right, 0, stack[0])
    turn(0)
    for a in range(EDGE + 2):
        if a < EDGE + 1:
            build_slab(facts, neighbours, field, left, right, a + 1, stack[a + 1])
        if a < EDGE - 1:
            turn(a + 1)
        first, last = max(0, a - EDGE + 1), min(3, a + 1)
        lhs = [turned[a - k1] for k1 in range(first, last)]
        product = jnp.dot(
            lhs[0] if len(lhs) == 1 else jnp.concatenate(lhs, axis=0),
            stack[a][...].reshape(bricks * SLAB, TAPS),
            preferred_element_type=jnp.float32,
        )
        for n, k1 in enumerate(range(first, last)):
            rows, part = slice(k1 * C, (k1 + 1) * C), product[n * C : (n + 1) * C]
            total[rows, :] = part if a == k1 else total[rows, :] + part
    for n in range(27):
        k1, t = n // 9, n % 9
        block = total[k1 * C : (k1 + 1) * C, t * C : (t + 1) * C].T * scale
        blocks[n * C : (n + 1) * C, :] = block.astype(jnp.bfloat16)
    strays = 0
    for g in range(bricks if counted else 0):
        for column in range(len(DIRECTIONS)):
            lost = (neighbours[g, column] >= 0) & (entry(facts, neighbours, g, column) < 0)
            strays = strays + jnp.where(lost, 1, 0)
    strays = jnp.full((C, C), jnp.minimum(strays, 1), jnp.int32)
    blocks[27 * C :, :] = strays.astype(jnp.float32).astype(jnp.bfloat16)
    n = 1
    for out in outs:
        for piece in range(out.shape[0]):
            first = pl.multiple_of(facts[n], 16)
            out[piece] = blocks[pl.ds(first, out.shape[1]), :]
            n += 1


def join_kernel(places, *rest):
    *pieces, result, blocks, arrived = rest
    for n, piece in enumerate(pieces):
        first = pl.multiple_of(places[n], 16)
        blocks[pl.ds(first, piece.shape[0]), :] = piece[...].astype(jnp.float32)
    copy = pltpu.make_async_copy(blocks.at[pl.ds(0, 27 * C)], result, arrived)
    copy.start()
    copy.wait()


def cost(flops, arrays):
    return pl.CostEstimate(
        flops=flops,
        bytes_accessed=sum(math.prod(a.shape) * a.dtype.itemsize for a in arrays),
        transcendentals=0,
    )


def run_conv(
    finish, turned, masked, facts, neighbours, field, left, right, weights, near, far, kinds
):
    bricks, voxels, _ = field.shape
    rows = jax.ShapeDtypeStruct((bricks, voxels, C), jnp.bfloat16)
    edge = jax.ShapeDtypeStruct((bricks, SLAB, C), jnp.bfloat16)
    operands = [weights, *far]
    spaces = {"vmem": pltpu.VMEM, "hbm": pltpu.HBM}
    outs = [(rows, spaces[kind]) for kind in kinds]
    outs += [(edge, pltpu.VMEM)] * (2 * (kinds[-1] == "vmem")) + [(rows, pltpu.VMEM)] * masked
    n_hbm = kinds.count("hbm")
    return pl.pallas_call(
        functools.partial(conv_kernel, finish, turned, masked, len(near), len(far), kinds),
        in_specs=[
            *[pl.BlockSpec(memory_space=pltpu.SMEM)] * 2,
            *[pl.BlockSpec(memory_space=pltpu.VMEM)] * (3 + len(near)),
            *[pl.BlockSpec(memory_space=pltpu.HBM) for _ in operands],
        ],
        out_specs=[pl.BlockSpec(memory_space=space) for _, space in outs],
        out_shape=[shape for shape, _ in outs],
        scratch_shapes=[
            *[pltpu.VMEM(a.shape, a.dtype) for a in operands],
            *[pltpu.VMEM(rows.shape, rows.dtype)] * n_hbm,
            pltpu.VMEM((bricks, EDGE + 2, SLAB, 3 * C), jnp.bfloat16),
            pltpu.VMEM((12 * C, 6 * C), jnp.bfloat16),
            pltpu.SemaphoreType.DMA((len(operands),)),
            pltpu.SemaphoreType.DMA((max(n_hbm, 1), EDGE // 2)),
        ],
        compiler_params=pltpu.CompilerParams(vmem_limit_bytes=VMEM_LIMIT),
        cost_estimate=cost(
            2 * 36 * bricks * voxels * C * C, [field, *near, *operands] + [shape for shape, _ in outs]
        ),
    )(facts, neighbours, field, left, right, *near, *operands)


def run_weight(facts, neighbours, field, left, right, grads, scale, shapes, counted):
    bricks, voxels, _ = field.shape
    outs = [jax.ShapeDtypeStruct((*shape, C), jnp.bfloat16) for shape in shapes]
    return pl.pallas_call(
        functools.partial(weight_kernel, scale, counted),
        in_specs=[
            *[pl.BlockSpec(memory_space=pltpu.SMEM)] * 2,
            *[pl.BlockSpec(memory_space=pltpu.VMEM)] * 4,
        ],
        out_specs=[pl.BlockSpec(memory_space=pltpu.VMEM) for _ in outs],
        out_shape=outs,
        scratch_shapes=[
            *[pltpu.VMEM((bricks, SLAB, TAPS), jnp.bfloat16)] * (EDGE + 2),
            pltpu.VMEM((EDGE, C, bricks * SLAB), jnp.bfloat16),
            pltpu.VMEM((3 * C, TAPS), jnp.float32),
            pltpu.VMEM((28 * C, C), jnp.bfloat16),
        ],
        compiler_params=pltpu.CompilerParams(vmem_limit_bytes=VMEM_LIMIT),
        cost_estimate=cost(2 * 27 * bricks * voxels * C * C, [field, left, right, grads, *outs]),
    )(facts, neighbours, field, left, right, grads)


def run_join(places, pieces):
    out = jax.ShapeDtypeStruct((27 * C, C), jnp.float32)
    return pl.pallas_call(
        join_kernel,
        in_specs=[
            pl.BlockSpec(memory_space=pltpu.SMEM),
            *[pl.BlockSpec(memory_space=pltpu.VMEM) for _ in pieces],
        ],
        out_specs=pl.BlockSpec(memory_space=pltpu.HBM),
        out_shape=out,
        scratch_shapes=[pltpu.VMEM((28 * C, C), jnp.float32), pltpu.SemaphoreType.DMA],
        cost_estimate=cost(0, [out, *pieces]),
    )(places, *pieces).reshape(27, C, C)


def beside(low, high):
    count = lax.axis_size("space")
    left = lax.ppermute(high, "space", [(i, i + 1) for i in range(count - 1)])
    right = lax.ppermute(low, "space", [(i + 1, i) for i in range(count - 1)])
    return left, right


def across(values, mask):
    count = lax.axis_size("space")
    return lax.ppermute(values, "space", [(i, i ^ mask) for i in range(count)])


def swapped(half):
    return across(half, 1)


def among(parts):
    count = lax.axis_size("space")
    groups = [[i for i in range(count) if i % 2 == b] for b in range(2)]
    return lax.all_to_all(parts, "space", 0, 0, axis_index_groups=groups, tiled=True)


def handed(part):
    members = lax.axis_size("space") // 2
    masks = [*range(members // 2, members), *range(1, members // 2)]
    came = {m: across(part, 2 * m) for m in masks}
    return [part, *[came[m] for m in range(1, members)]]


def pair_sum(sent, kept):
    total = kept.astype(jnp.float32) + swapped(sent).astype(jnp.float32)
    return total.astype(jnp.bfloat16)


def in_parts(half):
    return half.reshape(lax.axis_size("space") // 2, -1, C)


def part_total(parts):
    return jnp.sum(parts.astype(jnp.float32), axis=0).astype(jnp.bfloat16)


def gathered(part):
    members = lax.axis_size("space") // 2
    return among(jnp.broadcast_to(part[None], (members,) + part.shape)).reshape(14, C, C)


def joined(half):
    other = swapped(half)
    even = lax.axis_index("space") % 2 == 0
    first = jnp.where(even, half, other)
    second = jnp.where(even, other, half)
    blocks = jnp.concatenate([first, second[:13]], axis=0).astype(jnp.float32)
    return blocks, second[13, 0, 0].astype(jnp.float32)


def column_body(feats, mask, neighbours, weight_one, weight_two, cotangent):
    bricks, voxels, channels = feats.shape
    my_index = lax.axis_index("space")
    low, high = (
        feats[:, rows] * mask[:, rows, None].astype(jnp.bfloat16)
        for rows in (slice(0, SLAB), slice(voxels - SLAB, voxels))
    )
    in_left, in_right = beside(low, high)
    spread_mask = jnp.broadcast_to(mask.astype(jnp.bfloat16)[:, :, None], feats.shape)
    scale = 1.0 / math.sqrt(voxels * bricks)

    members = lax.axis_size("space") // 2
    bit, row = my_index % 2, my_index // 2
    rows = 28 * C // (2 * members)
    order = [*range(members // 2, members), *range(members // 2)]
    own = [(bit * members + (row ^ m)) * rows for m in range(members)]
    others = [((1 - bit) * members + (row ^ m)) * rows for m in range(members)]
    starts = [(i % 2 * members + i // 2) * rows for i in range(2 * members)]
    all_facts = jnp.stack([my_index, *starts])
    part_facts = jnp.stack([my_index, *[others[m] for m in order], *[own[m] for m in order]])
    places = jnp.stack([*own, *others])
    together = lax.optimization_barrier
    in_left, in_right, spread_mask, all_facts = together(
        (in_left, in_right, spread_mask, all_facts)
    )

    slope, hidden, low, high, inputs = run_conv(
        finish_first, False, True, all_facts, neighbours, feats, in_left, in_right, weight_one,
        [spread_mask], [], ("vmem", "vmem"),
    )
    h_left, h_right = beside(low, high)
    output, grad_second, low, high = run_conv(
        finish_second, False, False, all_facts, neighbours, hidden, h_left, h_right, weight_two,
        [spread_mask], [cotangent], ("hbm", "vmem"),
    )
    s_left, s_right = beside(low, high)
    (pieces_two,) = run_weight(
        all_facts, neighbours, hidden, h_left, h_right, grad_second, scale,
        [(2 * members, rows)], True,
    )
    pieces_two, s_left, s_right = together((pieces_two, s_left, s_right))
    parts_two = lax.all_to_all(pieces_two, "space", 0, 0, tiled=True)
    grad_first, low, high = run_conv(
        finish_product, True, False, all_facts, neighbours, grad_second, s_left, s_right, weight_two,
        [slope], [], ("vmem",),
    )
    far = members - members // 2
    sent_far, sent_near, kept = run_weight(
        part_facts, neighbours, inputs, in_left, in_right, grad_first, scale,
        [(far, rows), (members // 2, rows), (members, rows)], False,
    )
    parts_two, _ = together((parts_two, kept))
    part_two = part_total(parts_two)
    sent_far, sent_near, low, high = together((sent_far, sent_near, low, high))
    received = {
        m: piece[n]
        for piece, masks in ((swapped(sent_far), order[:far]), (swapped(sent_near), order[far:]))
        for n, m in enumerate(masks)
    }
    f_left, f_right = beside(low, high)

    def summed(m):
        return kept[order.index(m)].astype(jnp.float32) + received[m].astype(jnp.float32)

    halves = {m: summed(m).astype(jnp.bfloat16) for m in order if m}
    near = [m for m in order[far:] if m]
    *nearer, f_left, f_right, late_weight, part_two = together(
        (*[halves[m] for m in near], f_left, f_right, weight_one, part_two)
    )
    halves |= dict(zip(near, nearer))
    arrived = [across(halves[m], 2 * m) for m in order if m]
    half_two = gathered(part_two)
    (grad_input,) = run_conv(
        finish_product, True, False, all_facts, neighbours, grad_first, f_left, f_right,
        late_weight, [spread_mask], [], ("hbm",),
    )
    *arrived, grad_input = together((*arrived, grad_input))
    part = summed(0)
    for half in arrived:
        part = part + half.astype(jnp.float32)
    part = part.astype(jnp.bfloat16)
    same = handed(part)
    other = [swapped(piece) for piece in same]
    grad_w2, strays = joined(half_two)
    *other, grad_w2, strays = together((*other, grad_w2, strays))
    grad_w1 = run_join(places, [*same, *other])
    return strays, (output, grad_input, grad_w1, grad_w2)


def body(*arguments):
    strays, results = column_body(*arguments)

    def again(state):
        return jnp.zeros_like(state[0]), general_body(*arguments)

    return lax.while_loop(lambda state: state[0] > 0.5, again, (strays, results))[1]


def extended(field, source_index):
    bricks = field.shape[0]
    left, right = beside(field, field)
    blank = jnp.zeros((1, *field.shape[1:]), field.dtype)
    sources = jnp.concatenate([left, field, right, blank], axis=0).reshape(-1, EDGE * C)
    cell = jnp.arange(EDGE + 2)
    side = jnp.where(cell == 0, 0, jnp.where(cell == EDGE + 1, 2, 1))
    direction = 3 * side[:, None] + side[None, :]
    own = bricks + jnp.arange(bricks)[:, None]
    named = jnp.concatenate([source_index[:, :4], own, source_index[:, 4:]], axis=1)
    place = (cell - 1) % EDGE
    columns = named[:, direction] * SLAB + place[:, None] * EDGE + place[None, :]
    padded = jnp.take(sources, columns, axis=0).reshape(bricks, EDGE + 2, EDGE + 2, EDGE, C)
    return jnp.pad(padded, ((0, 0), (0, 0), (0, 0), (1, 1), (0, 0)))


def shifted(padded, k):
    bricks = padded.shape[0]
    corner = (0, k // 9, k // 3 % 3, k % 3, 0)
    return lax.dynamic_slice(padded, corner, (bricks, EDGE, EDGE, EDGE, C)).reshape(-1, C)


def general_conv(padded, weight, turned):
    def add(k, total):
        block = lax.dynamic_index_in_dim(weight, k, keepdims=False)
        cells = shifted(padded, 26 - k if turned else k)
        return total + jnp.dot(
            cells, block.T if turned else block, preferred_element_type=jnp.float32
        )

    rows = padded.shape[0] * EDGE**3
    return lax.fori_loop(0, 27, add, jnp.zeros((rows, C), jnp.float32))


def general_grad(padded, grads, scale):
    def one(k):
        contract = (((0,), (0,)), ((), ()))
        return lax.dot_general(
            shifted(padded, k), grads, contract, preferred_element_type=jnp.float32
        )

    term = (lax.map(one, jnp.arange(27)) * scale).astype(jnp.bfloat16)
    halves = jnp.pad(term, ((0, 1), (0, 0), (0, 0))).reshape(2, 14, C, C)
    even = lax.axis_index("space") % 2 == 0
    sent = jnp.where(even, halves[1], halves[0])
    kept = jnp.where(even, halves[0], halves[1])
    return joined(gathered(part_total(among(in_parts(pair_sum(sent, kept))))))[0]


def silu_slope(values):
    s = jax.nn.sigmoid(values)
    return s * (1.0 + values * (1.0 - s))


def general_body(feats, mask, neighbours, weight_one, weight_two, cotangent):
    bricks, voxels, _ = feats.shape
    first_brick = (lax.axis_index("space") - 1) * bricks
    source_index = jnp.where(neighbours >= 0, neighbours - first_brick, 3 * bricks)
    occupied = mask.reshape(-1, 1).astype(jnp.float32)
    scale = 1.0 / math.sqrt(voxels * bricks)

    def rounded(values):
        return values.astype(jnp.bfloat16)

    def extend(values):
        return extended(values.reshape(bricks, voxels, C), source_index)

    padded_in = extend(feats * mask[:, :, None].astype(jnp.bfloat16))
    first_pre = general_conv(padded_in, weight_one, False)
    padded_hidden = extend(rounded(occupied * jax.nn.silu(first_pre)))
    second_pre = general_conv(padded_hidden, weight_two, False)
    output = rounded(occupied * jax.nn.silu(second_pre))
    received = cotangent.reshape(-1, C).astype(jnp.float32)
    grad_second = rounded(received * occupied * silu_slope(second_pre))
    back_second = general_conv(extend(grad_second), weight_two, True)
    grad_first = rounded(occupied * silu_slope(first_pre) * back_second)
    grad_input = rounded(occupied * general_conv(extend(grad_first), weight_one, True))
    return (
        output.reshape(feats.shape),
        grad_input.reshape(feats.shape),
        general_grad(padded_in, grad_first, scale),
        general_grad(padded_hidden, grad_second, scale),
    )


def solution(mesh):
    in_specs = (
        P(("scene", "space"), None, None),
        P(("scene", "space"), None),
        P(("scene", "space"), None),
        P(),
        P(),
        P(("scene", "space"), None, None),
    )
    out_specs = (
        P(("scene", "space"), None, None),
        P(("scene", "space"), None, None),
        P("scene", None, None),
        P("scene", None, None),
    )
    return jax.shard_map(body, mesh=mesh, in_specs=in_specs, out_specs=out_specs, check_vma=False)
```

```python
import functools
import math

import jax
import jax.numpy as jnp
from jax import lax
from jax.experimental import pallas as pl
from jax.experimental.pallas import tpu as pltpu
from jax.sharding import PartitionSpec as P

EDGE = 8
TILE = 1
WIDE = 8
SLAB = EDGE * EDGE
C = 128
TAPS = 9 * C
VMEM_LIMIT = 36 * 1024 * 1024

DIRECTIONS = ((-1, -1), (-1, 0), (-1, 1), (0, -1), (0, 1), (1, -1), (1, 0), (1, 1))


def entry(facts, neighbours, brick, column):
    named = neighbours[brick, column]
    local = named - (facts[0] + DIRECTIONS[column][0]) * (TILE * WIDE)
    inside = (named >= 0) & (local >= 0) & (local < neighbours.shape[0])
    return jnp.where(inside, local, -1)


def picked(source, index, first, rows):
    found = source[jnp.maximum(index, 0), first : first + rows, :].astype(jnp.float32)
    return jnp.where(index >= 0, found, 0.0)


def padded_cells(facts, neighbours, field, left, right, g, a):
    near = functools.partial(entry, facts, neighbours, g)
    if a == 0:
        source, first, names = left, 0, (near(1), near(0), near(2))
    elif a == EDGE + 1:
        source, first, names = right, 0, (near(6), near(5), near(7))
    else:
        source, first, names = field, (a - 1) * SLAB, (g, near(3), near(4))
    if source is field:
        centre = field[g, first : first + SLAB, :].astype(jnp.float32)
    else:
        centre = picked(source, names[0], first, SLAB)
    top = picked(source, names[1], first + SLAB - 16, 16)
    bottom = picked(source, names[2], first, 16)
    return centre, jnp.concatenate([top[8:16], centre, bottom[0:8]], axis=0)


def before_and_behind(cells):
    place = lax.broadcasted_iota(jnp.int32, cells.shape, 1)
    before = jnp.where(place == 0, 0.0, pltpu.roll(cells, 1, 1))
    return before, jnp.where(place == EDGE - 1, 0.0, pltpu.roll(cells, EDGE - 1, 1))


def slab_tiles(cells):
    cells = cells.reshape(EDGE + 2, EDGE, C)
    before, behind = before_and_behind(cells)
    even, odd = [], []
    for shifted in (before, cells, behind):
        even.append(shifted.reshape((EDGE + 2) * EDGE, C).astype(jnp.bfloat16))
        odd.append(shifted[1 : EDGE + 1].reshape(SLAB, C).astype(jnp.bfloat16))
    return [e[0:SLAB] for e in even] + odd + [e[16 : 16 + SLAB] for e in even]


def build_slab(facts, neighbours, field, left, right, a, stack):
    for g in range(field.shape[0]):
        _, cells = padded_cells(facts, neighbours, field, left, right, g, a)
        for t, tile in enumerate(slab_tiles(cells)):
            stack[g, :, t * C : (t + 1) * C] = tile


def build_rows(facts, neighbours, field, left, right, slabs, stack):
    @pl.loop(0, field.shape[0])
    def _(g):
        for a in slabs:
            centre, cells = padded_cells(facts, neighbours, field, left, right, g, a)
            cells = cells.astype(jnp.bfloat16)
            stack[g, a, :, 0:C] = cells[0:SLAB]
            stack[g, a, :, C : 2 * C] = centre.astype(jnp.bfloat16)
            stack[g, a, :, 2 * C :] = cells[16 : 16 + SLAB]


def fill_weights(weights, turned, filled):
    for k1 in range(3):
        for k2 in range(3):
            for k3 in range(3):
                n = 9 * k1 + 3 * k2 + k3
                block = weights[26 - n if turned else n]
                if turned:
                    block = block.astype(jnp.float32).T.astype(jnp.bfloat16)
                for half in range(2):
                    row, column = 3 * (k1 + half) + k2, 2 * k3 + half
                    filled[row * C : (row + 1) * C, column * C : (column + 1) * C] = block
    blank = jnp.zeros((3 * C, C), jnp.bfloat16)
    for k3 in range(3):
        filled[9 * C :, 2 * k3 * C : (2 * k3 + 1) * C] = blank
        filled[: 3 * C, (2 * k3 + 1) * C : (2 * k3 + 2) * C] = blank


def conv_kernel(finish, turned, masked, pairs, n_near, n_far, kinds, facts, neighbours, *rest):
    field, left, right, *rest = rest
    near, rest = rest[:n_near], rest[n_near:]
    done, near = (near[-len(kinds) :], near[: -len(kinds)]) if pairs and not masked else ((), near)
    operands, rest = rest[: 1 + n_far], rest[1 + n_far :]
    results, rest = rest[: len(kinds)], rest[len(kinds) :]
    edges, rest = (rest[:2], rest[2:]) if kinds[-1] == "vmem" and not done else ((), rest)
    kept, rest = (rest[0], rest[1:]) if masked else (None, rest)
    local, rest = rest[: 1 + n_far], rest[1 + n_far :]
    *staged, stack, filled, came, gone = rest
    made, leaving = [], []
    for kind, result in zip(kinds, results):
        made.append(result if kind == "vmem" else staged.pop(0))
        if kind == "hbm":
            leaving.append((made[-1], result))
    copies = [
        pltpu.make_async_copy(there, here, came.at[n])
        for n, (there, here) in enumerate(zip(operands, local))
    ]
    for copy in copies:
        copy.start()
    if masked:
        kept[...] = field[...] * near[0][...]
        field = kept
    computed = pairs or tuple(range(EDGE // 2))
    slabs = sorted({2 * pair + n for pair in computed for n in range(4)})
    build_rows(facts, neighbours, field, left, right, slabs, stack)
    copies[0].wait()
    fill_weights(local[0], turned, filled)
    for copy in copies[1:]:
        copy.wait()
    bricks = field.shape[0] // 2
    factors = [*near, *local[1:]]

    def outgoing(pair):
        rows = pl.ds(at(pair * 2 * SLAB), 2 * SLAB)
        return [
            pltpu.make_async_copy(here.at[:, rows, :], there.at[:, rows, :], gone.at[n, pair])
            for n, (here, there) in enumerate(leaving)
        ]

    def step(pair):
        for part in range(2):
            some = slice(part * bricks, (part + 1) * bricks)
            lhs = [stack[some, 2 * pair + n].reshape(bricks * SLAB, 3 * C) for n in range(4)]
            shares = jnp.dot(
                jnp.concatenate(lhs, axis=1), filled[...], preferred_element_type=jnp.float32
            ).reshape(bricks * EDGE, EDGE, 6 * C)
            before, _ = before_and_behind(shares[:, :, : 2 * C])
            _, behind = before_and_behind(shares[:, :, 4 * C :])
            both = (before + shares[:, :, 2 * C : 4 * C] + behind).reshape(bricks * SLAB, 2 * C)
            for half in range(2):
                rows = pl.ds(at((2 * pair + half) * SLAB), SLAB)
                values = both[:, half * C : (half + 1) * C].reshape(bricks, SLAB, C)
                values = finish(
                    values, *[array[some, rows, :].astype(jnp.float32) for array in factors]
                )
                for array, value in zip(made, values):
                    array[some, rows, :] = value.astype(jnp.bfloat16)
        for copy in outgoing(pair):
            copy.start()

    if pairs:
        for pair in pairs:
            step(pair)
        for array, other in zip(made, done):
            for pair in set(range(EDGE // 2)) - set(pairs):
                rows = slice(2 * pair * SLAB, (2 * pair + 2) * SLAB)
                array[:, rows, :] = other[:, rows, :]
    else:

        @pl.loop(0, EDGE // 4)
        def _(n):
            step(2 * n)
            step(2 * n + 1)

    if edges:
        edges[0][...] = made[-1][:, :SLAB, :]
        edges[1][...] = made[-1][:, (EDGE - 1) * SLAB :, :]
    for pair in range(EDGE // 2):
        for copy in outgoing(pair):
            copy.wait()


def at(row):
    return row if isinstance(row, int) else pl.multiple_of(row, SLAB)


def finish_first(values, mask):
    s = jax.nn.sigmoid(values)
    return mask * (s * (1.0 + values * (1.0 - s))), mask * (values * s)


def finish_second(values, mask, cotangent):
    s = jax.nn.sigmoid(values)
    return mask * (values * s), cotangent * mask * (s * (1.0 + values * (1.0 - s)))


def finish_product(values, factor):
    return (factor * values,)


def weight_kernel(scale, counted, facts, neighbours, field, left, right, grads, *rest):
    outs, rest = rest[: -(EDGE + 5)], rest[-(EDGE + 5) :]
    stack, turned, total, blocks = rest[: EDGE + 2], rest[-3], rest[-2], rest[-1]
    bricks = grads.shape[0]

    def turn(a):
        slab = grads[:, a * SLAB : (a + 1) * SLAB, :].reshape(bricks * SLAB, C)
        turned[a] = slab.astype(jnp.float32).T.astype(jnp.bfloat16)

    build_slab(facts, neighbours, field, left, right, 0, stack[0])
    turn(0)
    for a in range(EDGE + 2):
        if a < EDGE + 1:
            build_slab(facts, neighbours, field, left, right, a + 1, stack[a + 1])
        if a < EDGE - 1:
            turn(a + 1)
        first, last = max(0, a - EDGE + 1), min(3, a + 1)
        lhs = [turned[a - k1] for k1 in range(first, last)]
        product = jnp.dot(
            lhs[0] if len(lhs) == 1 else jnp.concatenate(lhs, axis=0),
            stack[a][...].reshape(bricks * SLAB, TAPS),
            preferred_element_type=jnp.float32,
        )
        for n, k1 in enumerate(range(first, last)):
            rows, part = slice(k1 * C, (k1 + 1) * C), product[n * C : (n + 1) * C]
            total[rows, :] = part if a == k1 else total[rows, :] + part
    for n in range(27):
        k1, t = n // 9, n % 9
        block = total[k1 * C : (k1 + 1) * C, t * C : (t + 1) * C].T * scale
        blocks[n * C : (n + 1) * C, :] = block.astype(jnp.bfloat16)
    strays = 0
    for g in range(bricks if counted else 0):
        for column in range(len(DIRECTIONS)):
            lost = (neighbours[g, column] >= 0) & (entry(facts, neighbours, g, column) < 0)
            strays = strays + jnp.where(lost, 1, 0)
    strays = jnp.full((C, C), jnp.minimum(strays, 1), jnp.int32)
    blocks[27 * C :, :] = strays.astype(jnp.float32).astype(jnp.bfloat16)
    n = 1
    for out in outs:
        for piece in range(out.shape[0]):
            first = pl.multiple_of(facts[n], 16)
            out[piece] = blocks[pl.ds(first, out.shape[1]), :]
            n += 1


def join_kernel(places, *rest):
    *pieces, result, blocks, arrived = rest
    for n, piece in enumerate(pieces):
        first = pl.multiple_of(places[n], 16)
        blocks[pl.ds(first, piece.shape[0]), :] = piece[...].astype(jnp.float32)
    copy = pltpu.make_async_copy(blocks.at[pl.ds(0, 27 * C)], result, arrived)
    copy.start()
    copy.wait()


def cost(flops, arrays):
    return pl.CostEstimate(
        flops=flops,
        bytes_accessed=sum(math.prod(a.shape) * a.dtype.itemsize for a in arrays),
        transcendentals=0,
    )


def run_conv(
    finish, turned, masked, facts, neighbours, field, left, right, weights, near, far, kinds, pairs=()
):
    bricks, voxels, _ = field.shape
    rows = jax.ShapeDtypeStruct((bricks, voxels, C), jnp.bfloat16)
    edge = jax.ShapeDtypeStruct((bricks, SLAB, C), jnp.bfloat16)
    operands = [weights, *far]
    spaces = {"vmem": pltpu.VMEM, "hbm": pltpu.HBM}
    outs = [(rows, spaces[kind]) for kind in kinds]
    ends = kinds[-1] == "vmem" and (masked or not pairs)
    outs += [(edge, pltpu.VMEM)] * (2 * ends) + [(rows, pltpu.VMEM)] * masked
    n_hbm = kinds.count("hbm")
    return pl.pallas_call(
        functools.partial(conv_kernel, finish, turned, masked, pairs, len(near), len(far), kinds),
        in_specs=[
            *[pl.BlockSpec(memory_space=pltpu.SMEM)] * 2,
            *[pl.BlockSpec(memory_space=pltpu.VMEM)] * (3 + len(near)),
            *[pl.BlockSpec(memory_space=pltpu.HBM) for _ in operands],
        ],
        out_specs=[pl.BlockSpec(memory_space=space) for _, space in outs],
        out_shape=[shape for shape, _ in outs],
        scratch_shapes=[
            *[pltpu.VMEM(a.shape, a.dtype) for a in operands],
            *[pltpu.VMEM(rows.shape, rows.dtype)] * n_hbm,
            pltpu.VMEM((bricks, EDGE + 2, SLAB, 3 * C), jnp.bfloat16),
            pltpu.VMEM((12 * C, 6 * C), jnp.bfloat16),
            pltpu.SemaphoreType.DMA((len(operands),)),
            pltpu.SemaphoreType.DMA((max(n_hbm, 1), EDGE // 2)),
        ],
        compiler_params=pltpu.CompilerParams(vmem_limit_bytes=VMEM_LIMIT),
        cost_estimate=cost(
            (9 * len(pairs) or 36) * 2 * bricks * voxels * C * C, [field, *near, *operands] + [shape for shape, _ in outs]
        ),
    )(facts, neighbours, field, left, right, *near, *operands)


def run_weight(facts, neighbours, field, left, right, grads, scale, shapes, counted):
    bricks, voxels, _ = field.shape
    outs = [jax.ShapeDtypeStruct((*shape, C), jnp.bfloat16) for shape in shapes]
    return pl.pallas_call(
        functools.partial(weight_kernel, scale, counted),
        in_specs=[
            *[pl.BlockSpec(memory_space=pltpu.SMEM)] * 2,
            *[pl.BlockSpec(memory_space=pltpu.VMEM)] * 4,
        ],
        out_specs=[pl.BlockSpec(memory_space=pltpu.VMEM) for _ in outs],
        out_shape=outs,
        scratch_shapes=[
            *[pltpu.VMEM((bricks, SLAB, TAPS), jnp.bfloat16)] * (EDGE + 2),
            pltpu.VMEM((EDGE, C, bricks * SLAB), jnp.bfloat16),
            pltpu.VMEM((3 * C, TAPS), jnp.float32),
            pltpu.VMEM((28 * C, C), jnp.bfloat16),
        ],
        compiler_params=pltpu.CompilerParams(vmem_limit_bytes=VMEM_LIMIT),
        cost_estimate=cost(2 * 27 * bricks * voxels * C * C, [field, left, right, grads, *outs]),
    )(facts, neighbours, field, left, right, grads)


def run_join(places, pieces):
    out = jax.ShapeDtypeStruct((27 * C, C), jnp.float32)
    return pl.pallas_call(
        join_kernel,
        in_specs=[
            pl.BlockSpec(memory_space=pltpu.SMEM),
            *[pl.BlockSpec(memory_space=pltpu.VMEM) for _ in pieces],
        ],
        out_specs=pl.BlockSpec(memory_space=pltpu.HBM),
        out_shape=out,
        scratch_shapes=[pltpu.VMEM((28 * C, C), jnp.float32), pltpu.SemaphoreType.DMA],
        cost_estimate=cost(0, [out, *pieces]),
    )(places, *pieces).reshape(27, C, C)


def beside(low, high):
    count = lax.axis_size("space")
    left = lax.ppermute(high, "space", [(i, i + 1) for i in range(count - 1)])
    right = lax.ppermute(low, "space", [(i + 1, i) for i in range(count - 1)])
    return left, right


def across(values, mask):
    count = lax.axis_size("space")
    return lax.ppermute(values, "space", [(i, i ^ mask) for i in range(count)])


def swapped(half):
    return across(half, 1)


def among(parts):
    count = lax.axis_size("space")
    groups = [[i for i in range(count) if i % 2 == b] for b in range(2)]
    return lax.all_to_all(parts, "space", 0, 0, axis_index_groups=groups, tiled=True)


def handed(part):
    members = lax.axis_size("space") // 2
    masks = [*range(members // 2, members), *range(1, members // 2)]
    came = {m: across(part, 2 * m) for m in masks}
    return [part, *[came[m] for m in range(1, members)]]


def pair_sum(sent, kept):
    total = kept.astype(jnp.float32) + swapped(sent).astype(jnp.float32)
    return total.astype(jnp.bfloat16)


def in_parts(half):
    return half.reshape(lax.axis_size("space") // 2, -1, C)


def part_total(parts):
    return jnp.sum(parts.astype(jnp.float32), axis=0).astype(jnp.bfloat16)


def gathered(part):
    members = lax.axis_size("space") // 2
    return among(jnp.broadcast_to(part[None], (members,) + part.shape)).reshape(14, C, C)


def joined(half):
    other = swapped(half)
    even = lax.axis_index("space") % 2 == 0
    first = jnp.where(even, half, other)
    second = jnp.where(even, other, half)
    blocks = jnp.concatenate([first, second[:13]], axis=0).astype(jnp.float32)
    return blocks, second[13, 0, 0].astype(jnp.float32)


def column_body(feats, mask, neighbours, weight_one, weight_two, cotangent):
    bricks, voxels, channels = feats.shape
    my_index = lax.axis_index("space")
    low, high = (
        feats[:, rows] * mask[:, rows, None].astype(jnp.bfloat16)
        for rows in (slice(0, SLAB), slice(voxels - SLAB, voxels))
    )
    in_left, in_right = beside(low, high)
    spread_mask = jnp.broadcast_to(mask.astype(jnp.bfloat16)[:, :, None], feats.shape)
    scale = 1.0 / math.sqrt(voxels * bricks)

    members = lax.axis_size("space") // 2
    bit, row = my_index % 2, my_index // 2
    rows = 28 * C // (2 * members)
    order = [*range(members // 2, members), *range(members // 2)]
    own = [(bit * members + (row ^ m)) * rows for m in range(members)]
    others = [((1 - bit) * members + (row ^ m)) * rows for m in range(members)]
    starts = [(i % 2 * members + i // 2) * rows for i in range(2 * members)]
    all_facts = jnp.stack([my_index, *starts])
    part_facts = jnp.stack([my_index, *[others[m] for m in order], *[own[m] for m in order]])
    places = jnp.stack([*own, *others])
    together = lax.optimization_barrier
    in_left, in_right, spread_mask, all_facts = together(
        (in_left, in_right, spread_mask, all_facts)
    )

    slope, hidden, low, high, inputs = run_conv(
        finish_first, False, True, all_facts, neighbours, feats, in_left, in_right, weight_one,
        [spread_mask], [], ("vmem", "vmem"), (0, EDGE // 2 - 1),
    )
    h_left, h_right = beside(low, high)
    slope, hidden = run_conv(
        finish_first, False, False, all_facts, neighbours, inputs, in_left, in_right, weight_one,
        [spread_mask, slope, hidden], [], ("vmem", "vmem"), tuple(range(1, EDGE // 2 - 1)),
    )
    output, grad_second, low, high = run_conv(
        finish_second, False, False, all_facts, neighbours, hidden, h_left, h_right, weight_two,
        [spread_mask], [cotangent], ("hbm", "vmem"),
    )
    s_left, s_right = beside(low, high)
    (pieces_two,) = run_weight(
        all_facts, neighbours, hidden, h_left, h_right, grad_second, scale,
        [(2 * members, rows)], True,
    )
    pieces_two, s_left, s_right = together((pieces_two, s_left, s_right))
    parts_two = lax.all_to_all(pieces_two, "space", 0, 0, tiled=True)
    grad_first, low, high = run_conv(
        finish_product, True, False, all_facts, neighbours, grad_second, s_left, s_right, weight_two,
        [slope], [], ("vmem",),
    )
    far = members - members // 2
    sent_far, sent_near, kept = run_weight(
        part_facts, neighbours, inputs, in_left, in_right, grad_first, scale,
        [(far, rows), (members // 2, rows), (members, rows)], False,
    )
    parts_two, _ = together((parts_two, kept))
    part_two = part_total(parts_two)
    sent_far, sent_near, low, high = together((sent_far, sent_near, low, high))
    received = {
        m: piece[n]
        for piece, masks in ((swapped(sent_far), order[:far]), (swapped(sent_near), order[far:]))
        for n, m in enumerate(masks)
    }
    f_left, f_right = beside(low, high)

    def summed(m):
        return kept[order.index(m)].astype(jnp.float32) + received[m].astype(jnp.float32)

    halves = {m: summed(m).astype(jnp.bfloat16) for m in order if m}
    *farther, part_two = together((*[halves[m] for m in order[:far]], part_two))
    halves |= dict(zip(order, farther))
    half_two = gathered(part_two)
    near = [m for m in order[far:] if m]
    *nearer, f_left, f_right, late_weight = together(
        (*[halves[m] for m in near], f_left, f_right, weight_one)
    )
    halves |= dict(zip(near, nearer))
    arrived = [across(halves[m], 2 * m) for m in order if m]
    (grad_input,) = run_conv(
        finish_product, True, False, all_facts, neighbours, grad_first, f_left, f_right,
        late_weight, [spread_mask], [], ("hbm",),
    )
    *arrived, grad_input, half_two = together((*arrived, grad_input, half_two))
    part = summed(0)
    for half in arrived:
        part = part + half.astype(jnp.float32)
    part = part.astype(jnp.bfloat16)
    same = handed(part)
    other = [swapped(piece) for piece in same]
    grad_w2, strays = joined(half_two)
    *other, grad_w2, strays = together((*other, grad_w2, strays))
    grad_w1 = run_join(places, [*same, *other])
    return strays, (output, grad_input, grad_w1, grad_w2)


def body(*arguments):
    strays, results = column_body(*arguments)

    def again(state):
        return jnp.zeros_like(state[0]), general_body(*arguments)

    return lax.while_loop(lambda state: state[0] > 0.5, again, (strays, results))[1]


def extended(field, source_index):
    bricks = field.shape[0]
    left, right = beside(field, field)
    blank = jnp.zeros((1, *field.shape[1:]), field.dtype)
    sources = jnp.concatenate([left, field, right, blank], axis=0).reshape(-1, EDGE * C)
    cell = jnp.arange(EDGE + 2)
    side = jnp.where(cell == 0, 0, jnp.where(cell == EDGE + 1, 2, 1))
    direction = 3 * side[:, None] + side[None, :]
    own = bricks + jnp.arange(bricks)[:, None]
    named = jnp.concatenate([source_index[:, :4], own, source_index[:, 4:]], axis=1)
    place = (cell - 1) % EDGE
    columns = named[:, direction] * SLAB + place[:, None] * EDGE + place[None, :]
    padded = jnp.take(sources, columns, axis=0).reshape(bricks, EDGE + 2, EDGE + 2, EDGE, C)
    return jnp.pad(padded, ((0, 0), (0, 0), (0, 0), (1, 1), (0, 0)))


def shifted(padded, k):
    bricks = padded.shape[0]
    corner = (0, k // 9, k // 3 % 3, k % 3, 0)
    return lax.dynamic_slice(padded, corner, (bricks, EDGE, EDGE, EDGE, C)).reshape(-1, C)


def general_conv(padded, weight, turned):
    def add(k, total):
        block = lax.dynamic_index_in_dim(weight, k, keepdims=False)
        cells = shifted(padded, 26 - k if turned else k)
        return total + jnp.dot(
            cells, block.T if turned else block, preferred_element_type=jnp.float32
        )

    rows = padded.shape[0] * EDGE**3
    return lax.fori_loop(0, 27, add, jnp.zeros((rows, C), jnp.float32))


def general_grad(padded, grads, scale):
    def one(k):
        contract = (((0,), (0,)), ((), ()))
        return lax.dot_general(
            shifted(padded, k), grads, contract, preferred_element_type=jnp.float32
        )

    term = (lax.map(one, jnp.arange(27)) * scale).astype(jnp.bfloat16)
    halves = jnp.pad(term, ((0, 1), (0, 0), (0, 0))).reshape(2, 14, C, C)
    even = lax.axis_index("space") % 2 == 0
    sent = jnp.where(even, halves[1], halves[0])
    kept = jnp.where(even, halves[0], halves[1])
    return joined(gathered(part_total(among(in_parts(pair_sum(sent, kept))))))[0]


def silu_slope(values):
    s = jax.nn.sigmoid(values)
    return s * (1.0 + values * (1.0 - s))


def general_body(feats, mask, neighbours, weight_one, weight_two, cotangent):
    bricks, voxels, _ = feats.shape
    first_brick = (lax.axis_index("space") - 1) * bricks
    source_index = jnp.where(neighbours >= 0, neighbours - first_brick, 3 * bricks)
    occupied = mask.reshape(-1, 1).astype(jnp.float32)
    scale = 1.0 / math.sqrt(voxels * bricks)

    def rounded(values):
        return values.astype(jnp.bfloat16)

    def extend(values):
        return extended(values.reshape(bricks, voxels, C), source_index)

    padded_in = extend(feats * mask[:, :, None].astype(jnp.bfloat16))
    first_pre = general_conv(padded_in, weight_one, False)
    padded_hidden = extend(rounded(occupied * jax.nn.silu(first_pre)))
    second_pre = general_conv(padded_hidden, weight_two, False)
    output = rounded(occupied * jax.nn.silu(second_pre))
    received = cotangent.reshape(-1, C).astype(jnp.float32)
    grad_second = rounded(received * occupied * silu_slope(second_pre))
    back_second = general_conv(extend(grad_second), weight_two, True)
    grad_first = rounded(occupied * silu_slope(first_pre) * back_second)
    grad_input = rounded(occupied * general_conv(extend(grad_first), weight_one, True))
    return (
        output.reshape(feats.shape),
        grad_input.reshape(feats.shape),
        general_grad(padded_in, grad_first, scale),
        general_grad(padded_hidden, grad_second, scale),
    )


def solution(mesh):
    in_specs = (
        P(("scene", "space"), None, None),
        P(("scene", "space"), None),
        P(("scene", "space"), None),
        P(),
        P(),
        P(("scene", "space"), None, None),
    )
    out_specs = (
        P(("scene", "space"), None, None),
        P(("scene", "space"), None, None),
        P("scene", None, None),
        P("scene", None, None),
    )
    return jax.shard_map(body, mesh=mesh, in_specs=in_specs, out_specs=out_specs, check_vma=False)
```

```python
import functools
import math

import jax
import jax.numpy as jnp
from jax import lax
from jax.experimental import pallas as pl
from jax.experimental.pallas import tpu as pltpu
from jax.sharding import PartitionSpec as P

EDGE = 8
TILE = 1
WIDE = 8
SLAB = EDGE * EDGE
C = 128
TAPS = 9 * C
VMEM_LIMIT = 36 * 1024 * 1024

DIRECTIONS = ((-1, -1), (-1, 0), (-1, 1), (0, -1), (0, 1), (1, -1), (1, 0), (1, 1))


def entry(facts, neighbours, brick, column):
    named = neighbours[brick, column]
    local = named - (facts[0] + DIRECTIONS[column][0]) * (TILE * WIDE)
    inside = (named >= 0) & (local >= 0) & (local < neighbours.shape[0])
    return jnp.where(inside, local, -1)


def picked(source, index, first, rows):
    found = source[jnp.maximum(index, 0), first : first + rows, :].astype(jnp.float32)
    return jnp.where(index >= 0, found, 0.0)


def padded_cells(facts, neighbours, field, left, right, g, a):
    near = functools.partial(entry, facts, neighbours, g)
    if a == 0:
        source, first, names = left, 0, (near(1), near(0), near(2))
    elif a == EDGE + 1:
        source, first, names = right, 0, (near(6), near(5), near(7))
    else:
        source, first, names = field, (a - 1) * SLAB, (g, near(3), near(4))
    if source is field:
        centre = field[g, first : first + SLAB, :].astype(jnp.float32)
    else:
        centre = picked(source, names[0], first, SLAB)
    top = picked(source, names[1], first + SLAB - 16, 16)
    bottom = picked(source, names[2], first, 16)
    return centre, jnp.concatenate([top[8:16], centre, bottom[0:8]], axis=0)


def before_and_behind(cells):
    place = lax.broadcasted_iota(jnp.int32, cells.shape, 1)
    before = jnp.where(place == 0, 0.0, pltpu.roll(cells, 1, 1))
    return before, jnp.where(place == EDGE - 1, 0.0, pltpu.roll(cells, EDGE - 1, 1))


def slab_tiles(cells):
    cells = cells.reshape(EDGE + 2, EDGE, C)
    before, behind = before_and_behind(cells)
    even, odd = [], []
    for shifted in (before, cells, behind):
        even.append(shifted.reshape((EDGE + 2) * EDGE, C).astype(jnp.bfloat16))
        odd.append(shifted[1 : EDGE + 1].reshape(SLAB, C).astype(jnp.bfloat16))
    return [e[0:SLAB] for e in even] + odd + [e[16 : 16 + SLAB] for e in even]


def build_slab(facts, neighbours, field, left, right, a, stack):
    for g in range(field.shape[0]):
        _, cells = padded_cells(facts, neighbours, field, left, right, g, a)
        for t, tile in enumerate(slab_tiles(cells)):
            stack[g, :, t * C : (t + 1) * C] = tile


def build_rows(facts, neighbours, field, left, right, slabs, stack):
    @pl.loop(0, field.shape[0])
    def _(g):
        for a in slabs:
            centre, cells = padded_cells(facts, neighbours, field, left, right, g, a)
            cells = cells.astype(jnp.bfloat16)
            stack[g, a, :, 0:C] = cells[0:SLAB]
            stack[g, a, :, C : 2 * C] = centre.astype(jnp.bfloat16)
            stack[g, a, :, 2 * C :] = cells[16 : 16 + SLAB]


def fill_weights(weights, turned, filled):
    for k1 in range(3):
        for k2 in range(3):
            for k3 in range(3):
                n = 9 * k1 + 3 * k2 + k3
                block = weights[26 - n if turned else n]
                if turned:
                    block = block.astype(jnp.float32).T.astype(jnp.bfloat16)
                for half in range(2):
                    row, column = 3 * (k1 + half) + k2, 2 * k3 + half
                    filled[row * C : (row + 1) * C, column * C : (column + 1) * C] = block
    blank = jnp.zeros((3 * C, C), jnp.bfloat16)
    for k3 in range(3):
        filled[9 * C :, 2 * k3 * C : (2 * k3 + 1) * C] = blank
        filled[: 3 * C, (2 * k3 + 1) * C : (2 * k3 + 2) * C] = blank


def conv_kernel(finish, turned, masked, pairs, n_near, n_far, kinds, facts, neighbours, *rest):
    field, left, right, *rest = rest
    near, rest = rest[:n_near], rest[n_near:]
    done, near = (near[-len(kinds) :], near[: -len(kinds)]) if pairs and not masked else ((), near)
    operands, rest = rest[: 1 + n_far], rest[1 + n_far :]
    results, rest = rest[: len(kinds)], rest[len(kinds) :]
    edges, rest = (rest[:2], rest[2:]) if kinds[-1] == "vmem" and not done else ((), rest)
    kept, rest = (rest[0], rest[1:]) if masked else (None, rest)
    local, rest = rest[: 1 + n_far], rest[1 + n_far :]
    *staged, stack, filled, came, gone = rest
    made, leaving = [], []
    for kind, result in zip(kinds, results):
        made.append(result if kind == "vmem" else staged.pop(0))
        if kind == "hbm":
            leaving.append((made[-1], result))
    copies = [
        pltpu.make_async_copy(there, here, came.at[n])
        for n, (there, here) in enumerate(zip(operands, local))
    ]
    for copy in copies:
        copy.start()
    if masked:
        kept[...] = field[...] * near[0][...]
        field = kept
    computed = pairs or tuple(range(EDGE // 2))
    slabs = sorted({2 * pair + n for pair in computed for n in range(4)})
    build_rows(facts, neighbours, field, left, right, slabs, stack)
    copies[0].wait()
    fill_weights(local[0], turned, filled)
    for copy in copies[1:]:
        copy.wait()
    bricks = field.shape[0] // 2
    factors = [*near, *local[1:]]

    def outgoing(pair):
        rows = pl.ds(at(pair * 2 * SLAB), 2 * SLAB)
        return [
            pltpu.make_async_copy(here.at[:, rows, :], there.at[:, rows, :], gone.at[n, pair])
            for n, (here, there) in enumerate(leaving)
        ]

    def step(pair):
        for part in range(2):
            some = slice(part * bricks, (part + 1) * bricks)
            lhs = [stack[some, 2 * pair + n].reshape(bricks * SLAB, 3 * C) for n in range(4)]
            shares = jnp.dot(
                jnp.concatenate(lhs, axis=1), filled[...], preferred_element_type=jnp.float32
            ).reshape(bricks * EDGE, EDGE, 6 * C)
            before, _ = before_and_behind(shares[:, :, : 2 * C])
            _, behind = before_and_behind(shares[:, :, 4 * C :])
            both = (before + shares[:, :, 2 * C : 4 * C] + behind).reshape(bricks * SLAB, 2 * C)
            for half in range(2):
                rows = pl.ds(at((2 * pair + half) * SLAB), SLAB)
                values = both[:, half * C : (half + 1) * C].reshape(bricks, SLAB, C)
                values = finish(
                    values, *[array[some, rows, :].astype(jnp.float32) for array in factors]
                )
                for array, value in zip(made, values):
                    array[some, rows, :] = value.astype(jnp.bfloat16)
        for copy in outgoing(pair):
            copy.start()

    if pairs:
        for pair in pairs:
            step(pair)
        for array, other in zip(made, done):
            for pair in set(range(EDGE // 2)) - set(pairs):
                rows = slice(2 * pair * SLAB, (2 * pair + 2) * SLAB)
                array[:, rows, :] = other[:, rows, :]
    else:

        @pl.loop(0, EDGE // 4)
        def _(n):
            step(2 * n)
            step(2 * n + 1)

    if edges:
        edges[0][...] = made[-1][:, :SLAB, :]
        edges[1][...] = made[-1][:, (EDGE - 1) * SLAB :, :]
    for pair in range(EDGE // 2):
        for copy in outgoing(pair):
            copy.wait()


def at(row):
    return row if isinstance(row, int) else pl.multiple_of(row, SLAB)


def finish_first(values, mask):
    s = jax.nn.sigmoid(values)
    return mask * (s * (1.0 + values * (1.0 - s))), mask * (values * s)


def finish_second(values, mask, cotangent):
    s = jax.nn.sigmoid(values)
    return mask * (values * s), cotangent * mask * (s * (1.0 + values * (1.0 - s)))


def finish_product(values, factor):
    return (factor * values,)


def weight_kernel(scale, counted, facts, neighbours, field, left, right, grads, *rest):
    outs, rest = rest[: -(EDGE + 5)], rest[-(EDGE + 5) :]
    stack, turned, total, blocks = rest[: EDGE + 2], rest[-3], rest[-2], rest[-1]
    bricks = grads.shape[0]

    def turn(a):
        slab = grads[:, a * SLAB : (a + 1) * SLAB, :].reshape(bricks * SLAB, C)
        turned[a] = slab.astype(jnp.float32).T.astype(jnp.bfloat16)

    build_slab(facts, neighbours, field, left, right, 0, stack[0])
    turn(0)
    for a in range(EDGE + 2):
        if a < EDGE + 1:
            build_slab(facts, neighbours, field, left, right, a + 1, stack[a + 1])
        if a < EDGE - 1:
            turn(a + 1)
        first, last = max(0, a - EDGE + 1), min(3, a + 1)
        lhs = [turned[a - k1] for k1 in range(first, last)]
        product = jnp.dot(
            lhs[0] if len(lhs) == 1 else jnp.concatenate(lhs, axis=0),
            stack[a][...].reshape(bricks * SLAB, TAPS),
            preferred_element_type=jnp.float32,
        )
        for n, k1 in enumerate(range(first, last)):
            rows, part = slice(k1 * C, (k1 + 1) * C), product[n * C : (n + 1) * C]
            total[rows, :] = part if a == k1 else total[rows, :] + part
    for n in range(27):
        k1, t = n // 9, n % 9
        block = total[k1 * C : (k1 + 1) * C, t * C : (t + 1) * C].T * scale
        blocks[n * C : (n + 1) * C, :] = block.astype(jnp.bfloat16)
    strays = 0
    for g in range(bricks if counted else 0):
        for column in range(len(DIRECTIONS)):
            lost = (neighbours[g, column] >= 0) & (entry(facts, neighbours, g, column) < 0)
            strays = strays + jnp.where(lost, 1, 0)
    strays = jnp.full((C, C), jnp.minimum(strays, 1), jnp.int32)
    blocks[27 * C :, :] = strays.astype(jnp.float32).astype(jnp.bfloat16)
    n = 1
    for out in outs:
        for piece in range(out.shape[0]):
            first = pl.multiple_of(facts[n], 16)
            out[piece] = blocks[pl.ds(first, out.shape[1]), :]
            n += 1


def join_kernel(places, *rest):
    *pieces, result, blocks, arrived = rest
    for n, piece in enumerate(pieces):
        first = pl.multiple_of(places[n], 16)
        blocks[pl.ds(first, piece.shape[0]), :] = piece[...].astype(jnp.float32)
    copy = pltpu.make_async_copy(blocks.at[pl.ds(0, 27 * C)], result, arrived)
    copy.start()
    copy.wait()


def cost(flops, arrays):
    return pl.CostEstimate(
        flops=flops,
        bytes_accessed=sum(math.prod(a.shape) * a.dtype.itemsize for a in arrays),
        transcendentals=0,
    )


def run_conv(
    finish, turned, masked, facts, neighbours, field, left, right, weights, near, far, kinds, pairs=()
):
    bricks, voxels, _ = field.shape
    rows = jax.ShapeDtypeStruct((bricks, voxels, C), jnp.bfloat16)
    edge = jax.ShapeDtypeStruct((bricks, SLAB, C), jnp.bfloat16)
    operands = [weights, *far]
    spaces = {"vmem": pltpu.VMEM, "hbm": pltpu.HBM}
    outs = [(rows, spaces[kind]) for kind in kinds]
    ends = kinds[-1] == "vmem" and (masked or not pairs)
    outs += [(edge, pltpu.VMEM)] * (2 * ends) + [(rows, pltpu.VMEM)] * masked
    n_hbm = kinds.count("hbm")
    return pl.pallas_call(
        functools.partial(conv_kernel, finish, turned, masked, pairs, len(near), len(far), kinds),
        in_specs=[
            *[pl.BlockSpec(memory_space=pltpu.SMEM)] * 2,
            *[pl.BlockSpec(memory_space=pltpu.VMEM)] * (3 + len(near)),
            *[pl.BlockSpec(memory_space=pltpu.HBM) for _ in operands],
        ],
        out_specs=[pl.BlockSpec(memory_space=space) for _, space in outs],
        out_shape=[shape for shape, _ in outs],
        scratch_shapes=[
            *[pltpu.VMEM(a.shape, a.dtype) for a in operands],
            *[pltpu.VMEM(rows.shape, rows.dtype)] * n_hbm,
            pltpu.VMEM((bricks, EDGE + 2, SLAB, 3 * C), jnp.bfloat16),
            pltpu.VMEM((12 * C, 6 * C), jnp.bfloat16),
            pltpu.SemaphoreType.DMA((len(operands),)),
            pltpu.SemaphoreType.DMA((max(n_hbm, 1), EDGE // 2)),
        ],
        compiler_params=pltpu.CompilerParams(vmem_limit_bytes=VMEM_LIMIT),
        cost_estimate=cost(
            (9 * len(pairs) or 36) * 2 * bricks * voxels * C * C, [field, *near, *operands] + [shape for shape, _ in outs]
        ),
    )(facts, neighbours, field, left, right, *near, *operands)


def run_weight(facts, neighbours, field, left, right, grads, scale, shapes, counted):
    bricks, voxels, _ = field.shape
    outs = [jax.ShapeDtypeStruct((*shape, C), jnp.bfloat16) for shape in shapes]
    return pl.pallas_call(
        functools.partial(weight_kernel, scale, counted),
        in_specs=[
            *[pl.BlockSpec(memory_space=pltpu.SMEM)] * 2,
            *[pl.BlockSpec(memory_space=pltpu.VMEM)] * 4,
        ],
        out_specs=[pl.BlockSpec(memory_space=pltpu.VMEM) for _ in outs],
        out_shape=outs,
        scratch_shapes=[
            *[pltpu.VMEM((bricks, SLAB, TAPS), jnp.bfloat16)] * (EDGE + 2),
            pltpu.VMEM((EDGE, C, bricks * SLAB), jnp.bfloat16),
            pltpu.VMEM((3 * C, TAPS), jnp.float32),
            pltpu.VMEM((28 * C, C), jnp.bfloat16),
        ],
        compiler_params=pltpu.CompilerParams(vmem_limit_bytes=VMEM_LIMIT),
        cost_estimate=cost(2 * 27 * bricks * voxels * C * C, [field, left, right, grads, *outs]),
    )(facts, neighbours, field, left, right, grads)


def run_join(places, pieces):
    out = jax.ShapeDtypeStruct((27 * C, C), jnp.float32)
    return pl.pallas_call(
        join_kernel,
        in_specs=[
            pl.BlockSpec(memory_space=pltpu.SMEM),
            *[pl.BlockSpec(memory_space=pltpu.VMEM) for _ in pieces],
        ],
        out_specs=pl.BlockSpec(memory_space=pltpu.HBM),
        out_shape=out,
        scratch_shapes=[pltpu.VMEM((28 * C, C), jnp.float32), pltpu.SemaphoreType.DMA],
        cost_estimate=cost(0, [out, *pieces]),
    )(places, *pieces).reshape(27, C, C)


def beside(low, high):
    count = lax.axis_size("space")
    left = lax.ppermute(high, "space", [(i, i + 1) for i in range(count - 1)])
    right = lax.ppermute(low, "space", [(i + 1, i) for i in range(count - 1)])
    return left, right


def across(values, mask):
    count = lax.axis_size("space")
    return lax.ppermute(values, "space", [(i, i ^ mask) for i in range(count)])


def swapped(half):
    return across(half, 1)


def among(parts):
    count = lax.axis_size("space")
    groups = [[i for i in range(count) if i % 2 == b] for b in range(2)]
    return lax.all_to_all(parts, "space", 0, 0, axis_index_groups=groups, tiled=True)


def handed(part):
    members = lax.axis_size("space") // 2
    masks = [*range(members // 2, members), *range(1, members // 2)]
    came = {m: across(part, 2 * m) for m in masks}
    return [part, *[came[m] for m in range(1, members)]]


def pair_sum(sent, kept):
    total = kept.astype(jnp.float32) + swapped(sent).astype(jnp.float32)
    return total.astype(jnp.bfloat16)


def in_parts(half):
    return half.reshape(lax.axis_size("space") // 2, -1, C)


def part_total(parts):
    return jnp.sum(parts.astype(jnp.float32), axis=0).astype(jnp.bfloat16)


def gathered(part):
    members = lax.axis_size("space") // 2
    return among(jnp.broadcast_to(part[None], (members,) + part.shape)).reshape(14, C, C)


def joined(half):
    other = swapped(half)
    even = lax.axis_index("space") % 2 == 0
    first = jnp.where(even, half, other)
    second = jnp.where(even, other, half)
    blocks = jnp.concatenate([first, second[:13]], axis=0).astype(jnp.float32)
    return blocks, second[13, 0, 0].astype(jnp.float32)


def column_body(feats, mask, neighbours, weight_one, weight_two, cotangent):
    bricks, voxels, channels = feats.shape
    my_index = lax.axis_index("space")
    low, high = (
        feats[:, rows] * mask[:, rows, None].astype(jnp.bfloat16)
        for rows in (slice(0, SLAB), slice(voxels - SLAB, voxels))
    )
    in_left, in_right = beside(low, high)
    spread_mask = jnp.broadcast_to(mask.astype(jnp.bfloat16)[:, :, None], feats.shape)
    scale = 1.0 / math.sqrt(voxels * bricks)

    members = lax.axis_size("space") // 2
    bit, row = my_index % 2, my_index // 2
    rows = 28 * C // (2 * members)
    order = [*range(members // 2, members), *range(members // 2)]
    own = [(bit * members + (row ^ m)) * rows for m in range(members)]
    others = [((1 - bit) * members + (row ^ m)) * rows for m in range(members)]
    starts = [(i % 2 * members + i // 2) * rows for i in range(2 * members)]
    all_facts = jnp.stack([my_index, *starts])
    part_facts = jnp.stack([my_index, *[others[m] for m in order], *[own[m] for m in order]])
    places = jnp.stack([*own, *others])
    together = lax.optimization_barrier
    in_left, in_right, spread_mask, all_facts = together(
        (in_left, in_right, spread_mask, all_facts)
    )

    slope, hidden, low, high, inputs = run_conv(
        finish_first, False, True, all_facts, neighbours, feats, in_left, in_right, weight_one,
        [spread_mask], [], ("vmem", "vmem"), (0, EDGE // 2 - 1),
    )
    h_left, h_right = beside(low, high)
    slope, hidden = run_conv(
        finish_first, False, False, all_facts, neighbours, inputs, in_left, in_right, weight_one,
        [spread_mask, slope, hidden], [], ("vmem", "vmem"), tuple(range(1, EDGE // 2 - 1)),
    )
    output, grad_second, low, high = run_conv(
        finish_second, False, False, all_facts, neighbours, hidden, h_left, h_right, weight_two,
        [spread_mask], [cotangent], ("hbm", "vmem"),
    )
    s_left, s_right = beside(low, high)
    (pieces_two,) = run_weight(
        all_facts, neighbours, hidden, h_left, h_right, grad_second, scale,
        [(2 * members, rows)], True,
    )
    pieces_two, s_left, s_right = together((pieces_two, s_left, s_right))
    parts_two = lax.all_to_all(pieces_two, "space", 0, 0, tiled=True)
    grad_first, low, high = run_conv(
        finish_product, True, False, all_facts, neighbours, grad_second, s_left, s_right, weight_two,
        [slope], [], ("vmem",),
    )
    far = members - members // 2
    sent_far, sent_near, kept = run_weight(
        part_facts, neighbours, inputs, in_left, in_right, grad_first, scale,
        [(far, rows), (members // 2, rows), (members, rows)], False,
    )
    f_left, f_right = beside(low, high)
    parts_two, late_weight, _ = together((parts_two, weight_one, kept))
    part_two = part_total(parts_two)
    received = {
        m: piece[n]
        for piece, masks in ((swapped(sent_far), order[:far]), (swapped(sent_near), order[far:]))
        for n, m in enumerate(masks)
    }
    (grad_input,) = run_conv(
        finish_product, True, False, all_facts, neighbours, grad_first, f_left, f_right,
        late_weight, [spread_mask], [], ("hbm",),
    )

    def summed(m):
        return kept[order.index(m)].astype(jnp.float32) + received[m].astype(jnp.float32)

    masks = [m for m in order if m]
    *halves, grad_input, part_two = together(
        (*[summed(m).astype(jnp.bfloat16) for m in masks], grad_input, part_two)
    )
    arrived = [across(half, 2 * m) for half, m in zip(halves, masks)]
    half_two = gathered(part_two)
    *arrived, half_two = together((*arrived, half_two))
    part = summed(0)
    for half in arrived:
        part = part + half.astype(jnp.float32)
    part = part.astype(jnp.bfloat16)
    same = handed(part)
    other = [swapped(piece) for piece in same]
    grad_w2, strays = joined(half_two)
    *other, grad_w2, strays = together((*other, grad_w2, strays))
    grad_w1 = run_join(places, [*same, *other])
    return strays, (output, grad_input, grad_w1, grad_w2)


def body(*arguments):
    strays, results = column_body(*arguments)

    def again(state):
        return jnp.zeros_like(state[0]), general_body(*arguments)

    return lax.while_loop(lambda state: state[0] > 0.5, again, (strays, results))[1]


def extended(field, source_index):
    bricks = field.shape[0]
    left, right = beside(field, field)
    blank = jnp.zeros((1, *field.shape[1:]), field.dtype)
    sources = jnp.concatenate([left, field, right, blank], axis=0).reshape(-1, EDGE * C)
    cell = jnp.arange(EDGE + 2)
    side = jnp.where(cell == 0, 0, jnp.where(cell == EDGE + 1, 2, 1))
    direction = 3 * side[:, None] + side[None, :]
    own = bricks + jnp.arange(bricks)[:, None]
    named = jnp.concatenate([source_index[:, :4], own, source_index[:, 4:]], axis=1)
    place = (cell - 1) % EDGE
    columns = named[:, direction] * SLAB + place[:, None] * EDGE + place[None, :]
    padded = jnp.take(sources, columns, axis=0).reshape(bricks, EDGE + 2, EDGE + 2, EDGE, C)
    return jnp.pad(padded, ((0, 0), (0, 0), (0, 0), (1, 1), (0, 0)))


def shifted(padded, k):
    bricks = padded.shape[0]
    corner = (0, k // 9, k // 3 % 3, k % 3, 0)
    return lax.dynamic_slice(padded, corner, (bricks, EDGE, EDGE, EDGE, C)).reshape(-1, C)


def general_conv(padded, weight, turned):
    def add(k, total):
        block = lax.dynamic_index_in_dim(weight, k, keepdims=False)
        cells = shifted(padded, 26 - k if turned else k)
        return total + jnp.dot(
            cells, block.T if turned else block, preferred_element_type=jnp.float32
        )

    rows = padded.shape[0] * EDGE**3
    return lax.fori_loop(0, 27, add, jnp.zeros((rows, C), jnp.float32))


def general_grad(padded, grads, scale):
    def one(k):
        contract = (((0,), (0,)), ((), ()))
        return lax.dot_general(
            shifted(padded, k), grads, contract, preferred_element_type=jnp.float32
        )

    term = (lax.map(one, jnp.arange(27)) * scale).astype(jnp.bfloat16)
    halves = jnp.pad(term, ((0, 1), (0, 0), (0, 0))).reshape(2, 14, C, C)
    even = lax.axis_index("space") % 2 == 0
    sent = jnp.where(even, halves[1], halves[0])
    kept = jnp.where(even, halves[0], halves[1])
    return joined(gathered(part_total(among(in_parts(pair_sum(sent, kept))))))[0]


def silu_slope(values):
    s = jax.nn.sigmoid(values)
    return s * (1.0 + values * (1.0 - s))


def general_body(feats, mask, neighbours, weight_one, weight_two, cotangent):
    bricks, voxels, _ = feats.shape
    first_brick = (lax.axis_index("space") - 1) * bricks
    source_index = jnp.where(neighbours >= 0, neighbours - first_brick, 3 * bricks)
    occupied = mask.reshape(-1, 1).astype(jnp.float32)
    scale = 1.0 / math.sqrt(voxels * bricks)

    def rounded(values):
        return values.astype(jnp.bfloat16)

    def extend(values):
        return extended(values.reshape(bricks, voxels, C), source_index)

    padded_in = extend(feats * mask[:, :, None].astype(jnp.bfloat16))
    first_pre = general_conv(padded_in, weight_one, False)
    padded_hidden = extend(rounded(occupied * jax.nn.silu(first_pre)))
    second_pre = general_conv(padded_hidden, weight_two, False)
    output = rounded(occupied * jax.nn.silu(second_pre))
    received = cotangent.reshape(-1, C).astype(jnp.float32)
    grad_second = rounded(received * occupied * silu_slope(second_pre))
    back_second = general_conv(extend(grad_second), weight_two, True)
    grad_first = rounded(occupied * silu_slope(first_pre) * back_second)
    grad_input = rounded(occupied * general_conv(extend(grad_first), weight_one, True))
    return (
        output.reshape(feats.shape),
        grad_input.reshape(feats.shape),
        general_grad(padded_in, grad_first, scale),
        general_grad(padded_hidden, grad_second, scale),
    )


def solution(mesh):
    in_specs = (
        P(("scene", "space"), None, None),
        P(("scene", "space"), None),
        P(("scene", "space"), None),
        P(),
        P(),
        P(("scene", "space"), None, None),
    )
    out_specs = (
        P(("scene", "space"), None, None),
        P(("scene", "space"), None, None),
        P("scene", None, None),
        P("scene", None, None),
    )
    return jax.shard_map(body, mesh=mesh, in_specs=in_specs, out_specs=out_specs, check_vma=False)
```

```python
import functools
import math

import jax
import jax.numpy as jnp
from jax import lax
from jax.experimental import pallas as pl
from jax.experimental.pallas import tpu as pltpu
from jax.sharding import PartitionSpec as P

EDGE = 8
TILE = 1
WIDE = 8
SLAB = EDGE * EDGE
C = 128
TAPS = 9 * C
VMEM_LIMIT = 36 * 1024 * 1024

DIRECTIONS = ((-1, -1), (-1, 0), (-1, 1), (0, -1), (0, 1), (1, -1), (1, 0), (1, 1))


def entry(facts, neighbours, brick, column):
    named = neighbours[brick, column]
    local = named - (facts[0] + DIRECTIONS[column][0]) * (TILE * WIDE)
    inside = (named >= 0) & (local >= 0) & (local < neighbours.shape[0])
    return jnp.where(inside, local, -1)


def picked(source, index, first, rows):
    found = source[jnp.maximum(index, 0), first : first + rows, :].astype(jnp.float32)
    return jnp.where(index >= 0, found, 0.0)


def padded_cells(facts, neighbours, field, left, right, g, a):
    near = functools.partial(entry, facts, neighbours, g)
    if a == 0:
        source, first, names = left, 0, (near(1), near(0), near(2))
    elif a == EDGE + 1:
        source, first, names = right, 0, (near(6), near(5), near(7))
    else:
        source, first, names = field, (a - 1) * SLAB, (g, near(3), near(4))
    if source is field:
        centre = field[g, first : first + SLAB, :].astype(jnp.float32)
    else:
        centre = picked(source, names[0], first, SLAB)
    top = picked(source, names[1], first + SLAB - 16, 16)
    bottom = picked(source, names[2], first, 16)
    return centre, jnp.concatenate([top[8:16], centre, bottom[0:8]], axis=0)


def before_and_behind(cells):
    place = lax.broadcasted_iota(jnp.int32, cells.shape, 1)
    before = jnp.where(place == 0, 0.0, pltpu.roll(cells, 1, 1))
    return before, jnp.where(place == EDGE - 1, 0.0, pltpu.roll(cells, EDGE - 1, 1))


def slab_tiles(cells):
    cells = cells.reshape(EDGE + 2, EDGE, C)
    before, behind = before_and_behind(cells)
    even, odd = [], []
    for shifted in (before, cells, behind):
        even.append(shifted.reshape((EDGE + 2) * EDGE, C).astype(jnp.bfloat16))
        odd.append(shifted[1 : EDGE + 1].reshape(SLAB, C).astype(jnp.bfloat16))
    return [e[0:SLAB] for e in even] + odd + [e[16 : 16 + SLAB] for e in even]


def build_slab(facts, neighbours, field, left, right, a, stack):
    for g in range(field.shape[0]):
        _, cells = padded_cells(facts, neighbours, field, left, right, g, a)
        for t, tile in enumerate(slab_tiles(cells)):
            stack[g, :, t * C : (t + 1) * C] = tile


def build_rows(facts, neighbours, field, left, right, slabs, stack):
    @pl.loop(0, field.shape[0])
    def _(g):
        for a in slabs:
            centre, cells = padded_cells(facts, neighbours, field, left, right, g, a)
            cells = cells.astype(jnp.bfloat16)
            stack[g, a, :, 0:C] = cells[0:SLAB]
            stack[g, a, :, C : 2 * C] = centre.astype(jnp.bfloat16)
            stack[g, a, :, 2 * C :] = cells[16 : 16 + SLAB]


def fill_weights(weights, turned, filled):
    for k1 in range(3):
        for k2 in range(3):
            for k3 in range(3):
                n = 9 * k1 + 3 * k2 + k3
                block = weights[26 - n if turned else n]
                if turned:
                    block = block.astype(jnp.float32).T.astype(jnp.bfloat16)
                for half in range(2):
                    row, column = 3 * (k1 + half) + k2, 2 * k3 + half
                    filled[row * C : (row + 1) * C, column * C : (column + 1) * C] = block
    blank = jnp.zeros((3 * C, C), jnp.bfloat16)
    for k3 in range(3):
        filled[9 * C :, 2 * k3 * C : (2 * k3 + 1) * C] = blank
        filled[: 3 * C, (2 * k3 + 1) * C : (2 * k3 + 2) * C] = blank


def conv_kernel(finish, turned, masked, pairs, n_near, n_far, kinds, facts, neighbours, *rest):
    field, left, right, *rest = rest
    near, rest = rest[:n_near], rest[n_near:]
    done, near = (near[-len(kinds) :], near[: -len(kinds)]) if pairs and not masked else ((), near)
    weights, *rest = rest
    operands, rest = rest[:n_far], rest[n_far:]
    results, rest = rest[: len(kinds)], rest[len(kinds) :]
    edges, rest = (rest[:2], rest[2:]) if kinds[-1] == "vmem" and not done else ((), rest)
    kept, rest = (rest[0], rest[1:]) if masked else (None, rest)
    local, rest = rest[:n_far], rest[n_far:]
    *staged, stack, filled, came, gone = rest
    made, leaving = [], []
    for kind, result in zip(kinds, results):
        made.append(result if kind == "vmem" else staged.pop(0))
        if kind == "hbm":
            leaving.append((made[-1], result))
    copies = [
        pltpu.make_async_copy(there, here, came.at[n])
        for n, (there, here) in enumerate(zip(operands, local))
    ]
    for copy in copies:
        copy.start()
    if masked:
        kept[...] = field[...] * near[0][...]
        field = kept
    computed = pairs or tuple(range(EDGE // 2))
    slabs = sorted({2 * pair + n for pair in computed for n in range(4)})
    build_rows(facts, neighbours, field, left, right, slabs, stack)
    fill_weights(weights, turned, filled)
    for copy in copies:
        copy.wait()
    bricks = field.shape[0] // 2
    factors = [*near, *local]

    def outgoing(pair):
        rows = pl.ds(at(pair * 2 * SLAB), 2 * SLAB)
        return [
            pltpu.make_async_copy(here.at[:, rows, :], there.at[:, rows, :], gone.at[n, pair])
            for n, (here, there) in enumerate(leaving)
        ]

    def step(pair):
        for part in range(2):
            some = slice(part * bricks, (part + 1) * bricks)
            lhs = [stack[some, 2 * pair + n].reshape(bricks * SLAB, 3 * C) for n in range(4)]
            shares = jnp.dot(
                jnp.concatenate(lhs, axis=1), filled[...], preferred_element_type=jnp.float32
            ).reshape(bricks * EDGE, EDGE, 6 * C)
            before, _ = before_and_behind(shares[:, :, : 2 * C])
            _, behind = before_and_behind(shares[:, :, 4 * C :])
            both = (before + shares[:, :, 2 * C : 4 * C] + behind).reshape(bricks * SLAB, 2 * C)
            for half in range(2):
                rows = pl.ds(at((2 * pair + half) * SLAB), SLAB)
                values = both[:, half * C : (half + 1) * C].reshape(bricks, SLAB, C)
                values = finish(
                    values, *[array[some, rows, :].astype(jnp.float32) for array in factors]
                )
                for array, value in zip(made, values):
                    array[some, rows, :] = value.astype(jnp.bfloat16)
        for copy in outgoing(pair):
            copy.start()

    if pairs:
        for pair in pairs:
            step(pair)
        for array, other in zip(made, done):
            for pair in set(range(EDGE // 2)) - set(pairs):
                rows = slice(2 * pair * SLAB, (2 * pair + 2) * SLAB)
                array[:, rows, :] = other[:, rows, :]
    else:

        @pl.loop(0, EDGE // 4)
        def _(n):
            step(2 * n)
            step(2 * n + 1)

    if edges:
        edges[0][...] = made[-1][:, :SLAB, :]
        edges[1][...] = made[-1][:, (EDGE - 1) * SLAB :, :]
    for pair in range(EDGE // 2):
        for copy in outgoing(pair):
            copy.wait()


def at(row):
    return row if isinstance(row, int) else pl.multiple_of(row, SLAB)


def finish_first(values, mask):
    s = jax.nn.sigmoid(values)
    return mask * (s * (1.0 + values * (1.0 - s))), mask * (values * s)


def finish_second(values, mask, cotangent):
    s = jax.nn.sigmoid(values)
    return mask * (values * s), cotangent * mask * (s * (1.0 + values * (1.0 - s)))


def finish_product(values, factor):
    return (factor * values,)


def weight_kernel(scale, counted, facts, neighbours, field, left, right, grads, *rest):
    outs, rest = rest[: -(EDGE + 5)], rest[-(EDGE + 5) :]
    stack, turned, total, blocks = rest[: EDGE + 2], rest[-3], rest[-2], rest[-1]
    bricks = grads.shape[0]

    def turn(a):
        slab = grads[:, a * SLAB : (a + 1) * SLAB, :].reshape(bricks * SLAB, C)
        turned[a] = slab.astype(jnp.float32).T.astype(jnp.bfloat16)

    build_slab(facts, neighbours, field, left, right, 0, stack[0])
    turn(0)
    for a in range(EDGE + 2):
        if a < EDGE + 1:
            build_slab(facts, neighbours, field, left, right, a + 1, stack[a + 1])
        if a < EDGE - 1:
            turn(a + 1)
        first, last = max(0, a - EDGE + 1), min(3, a + 1)
        lhs = [turned[a - k1] for k1 in range(first, last)]
        product = jnp.dot(
            lhs[0] if len(lhs) == 1 else jnp.concatenate(lhs, axis=0),
            stack[a][...].reshape(bricks * SLAB, TAPS),
            preferred_element_type=jnp.float32,
        )
        for n, k1 in enumerate(range(first, last)):
            rows, part = slice(k1 * C, (k1 + 1) * C), product[n * C : (n + 1) * C]
            total[rows, :] = part if a == k1 else total[rows, :] + part
    for n in range(27):
        k1, t = n // 9, n % 9
        block = total[k1 * C : (k1 + 1) * C, t * C : (t + 1) * C].T * scale
        blocks[n * C : (n + 1) * C, :] = block.astype(jnp.bfloat16)
    strays = 0
    for g in range(bricks if counted else 0):
        for column in range(len(DIRECTIONS)):
            lost = (neighbours[g, column] >= 0) & (entry(facts, neighbours, g, column) < 0)
            strays = strays + jnp.where(lost, 1, 0)
    strays = jnp.full((C, C), jnp.minimum(strays, 1), jnp.int32)
    blocks[27 * C :, :] = strays.astype(jnp.float32).astype(jnp.bfloat16)
    n = 1
    for out in outs:
        for piece in range(out.shape[0]):
            first = pl.multiple_of(facts[n], 16)
            out[piece] = blocks[pl.ds(first, out.shape[1]), :]
            n += 1


def join_kernel(places, *rest):
    *pieces, result, blocks, arrived = rest
    for n, piece in enumerate(pieces):
        first = pl.multiple_of(places[n], 16)
        blocks[pl.ds(first, piece.shape[0]), :] = piece[...].astype(jnp.float32)
    copy = pltpu.make_async_copy(blocks.at[pl.ds(0, 27 * C)], result, arrived)
    copy.start()
    copy.wait()


def cost(flops, arrays):
    return pl.CostEstimate(
        flops=flops,
        bytes_accessed=sum(math.prod(a.shape) * a.dtype.itemsize for a in arrays),
        transcendentals=0,
    )


def run_conv(
    finish, turned, masked, facts, neighbours, field, left, right, weights, near, far, kinds, pairs=()
):
    bricks, voxels, _ = field.shape
    rows = jax.ShapeDtypeStruct((bricks, voxels, C), jnp.bfloat16)
    edge = jax.ShapeDtypeStruct((bricks, SLAB, C), jnp.bfloat16)
    operands = [*far]
    spaces = {"vmem": pltpu.VMEM, "hbm": pltpu.HBM}
    outs = [(rows, spaces[kind]) for kind in kinds]
    ends = kinds[-1] == "vmem" and (masked or not pairs)
    outs += [(edge, pltpu.VMEM)] * (2 * ends) + [(rows, pltpu.VMEM)] * masked
    n_hbm = kinds.count("hbm")
    return pl.pallas_call(
        functools.partial(conv_kernel, finish, turned, masked, pairs, len(near), len(far), kinds),
        in_specs=[
            *[pl.BlockSpec(memory_space=pltpu.SMEM)] * 2,
            *[pl.BlockSpec(memory_space=pltpu.VMEM)] * (4 + len(near)),
            *[pl.BlockSpec(memory_space=pltpu.HBM) for _ in operands],
        ],
        out_specs=[pl.BlockSpec(memory_space=space) for _, space in outs],
        out_shape=[shape for shape, _ in outs],
        scratch_shapes=[
            *[pltpu.VMEM(a.shape, a.dtype) for a in operands],
            *[pltpu.VMEM(rows.shape, rows.dtype)] * n_hbm,
            pltpu.VMEM((bricks, EDGE + 2, SLAB, 3 * C), jnp.bfloat16),
            pltpu.VMEM((12 * C, 6 * C), jnp.bfloat16),
            pltpu.SemaphoreType.DMA((max(len(operands), 1),)),
            pltpu.SemaphoreType.DMA((max(n_hbm, 1), EDGE // 2)),
        ],
        compiler_params=pltpu.CompilerParams(vmem_limit_bytes=VMEM_LIMIT),
        cost_estimate=cost(
            (9 * len(pairs) or 36) * 2 * bricks * voxels * C * C, [field, *near, weights, *operands] + [shape for shape, _ in outs]
        ),
    )(facts, neighbours, field, left, right, *near, weights, *operands)


def run_weight(facts, neighbours, field, left, right, grads, scale, shapes, counted):
    bricks, voxels, _ = field.shape
    outs = [jax.ShapeDtypeStruct((*shape, C), jnp.bfloat16) for shape in shapes]
    return pl.pallas_call(
        functools.partial(weight_kernel, scale, counted),
        in_specs=[
            *[pl.BlockSpec(memory_space=pltpu.SMEM)] * 2,
            *[pl.BlockSpec(memory_space=pltpu.VMEM)] * 4,
        ],
        out_specs=[pl.BlockSpec(memory_space=pltpu.VMEM) for _ in outs],
        out_shape=outs,
        scratch_shapes=[
            *[pltpu.VMEM((bricks, SLAB, TAPS), jnp.bfloat16)] * (EDGE + 2),
            pltpu.VMEM((EDGE, C, bricks * SLAB), jnp.bfloat16),
            pltpu.VMEM((3 * C, TAPS), jnp.float32),
            pltpu.VMEM((28 * C, C), jnp.bfloat16),
        ],
        compiler_params=pltpu.CompilerParams(vmem_limit_bytes=VMEM_LIMIT),
        cost_estimate=cost(2 * 27 * bricks * voxels * C * C, [field, left, right, grads, *outs]),
    )(facts, neighbours, field, left, right, grads)


def run_join(places, pieces):
    out = jax.ShapeDtypeStruct((27 * C, C), jnp.float32)
    return pl.pallas_call(
        join_kernel,
        in_specs=[
            pl.BlockSpec(memory_space=pltpu.SMEM),
            *[pl.BlockSpec(memory_space=pltpu.VMEM) for _ in pieces],
        ],
        out_specs=pl.BlockSpec(memory_space=pltpu.HBM),
        out_shape=out,
        scratch_shapes=[pltpu.VMEM((28 * C, C), jnp.float32), pltpu.SemaphoreType.DMA],
        cost_estimate=cost(0, [out, *pieces]),
    )(places, *pieces).reshape(27, C, C)


def beside(low, high):
    count = lax.axis_size("space")
    left = lax.ppermute(high, "space", [(i, i + 1) for i in range(count - 1)])
    right = lax.ppermute(low, "space", [(i + 1, i) for i in range(count - 1)])
    return left, right


def across(values, mask):
    count = lax.axis_size("space")
    return lax.ppermute(values, "space", [(i, i ^ mask) for i in range(count)])


def swapped(half):
    return across(half, 1)


def among(parts):
    count = lax.axis_size("space")
    groups = [[i for i in range(count) if i % 2 == b] for b in range(2)]
    return lax.all_to_all(parts, "space", 0, 0, axis_index_groups=groups, tiled=True)


def handed(part):
    members = lax.axis_size("space") // 2
    masks = [*range(members // 2, members), *range(1, members // 2)]
    came = {m: across(part, 2 * m) for m in masks}
    return [part, *[came[m] for m in range(1, members)]]


def pair_sum(sent, kept):
    total = kept.astype(jnp.float32) + swapped(sent).astype(jnp.float32)
    return total.astype(jnp.bfloat16)


def in_parts(half):
    return half.reshape(lax.axis_size("space") // 2, -1, C)


def part_total(parts):
    return jnp.sum(parts.astype(jnp.float32), axis=0).astype(jnp.bfloat16)


def gathered(part):
    members = lax.axis_size("space") // 2
    return among(jnp.broadcast_to(part[None], (members,) + part.shape)).reshape(14, C, C)


def joined(half):
    other = swapped(half)
    even = lax.axis_index("space") % 2 == 0
    first = jnp.where(even, half, other)
    second = jnp.where(even, other, half)
    blocks = jnp.concatenate([first, second[:13]], axis=0).astype(jnp.float32)
    return blocks, second[13, 0, 0].astype(jnp.float32)


def column_body(feats, mask, neighbours, weight_one, weight_two, cotangent):
    bricks, voxels, channels = feats.shape
    my_index = lax.axis_index("space")
    low, high = (
        feats[:, rows] * mask[:, rows, None].astype(jnp.bfloat16)
        for rows in (slice(0, SLAB), slice(voxels - SLAB, voxels))
    )
    in_left, in_right = beside(low, high)
    spread_mask = jnp.broadcast_to(mask.astype(jnp.bfloat16)[:, :, None], feats.shape)
    scale = 1.0 / math.sqrt(voxels * bricks)

    members = lax.axis_size("space") // 2
    bit, row = my_index % 2, my_index // 2
    rows = 28 * C // (2 * members)
    order = [*range(members // 2, members), *range(members // 2)]
    own = [(bit * members + (row ^ m)) * rows for m in range(members)]
    others = [((1 - bit) * members + (row ^ m)) * rows for m in range(members)]
    starts = [(i % 2 * members + i // 2) * rows for i in range(2 * members)]
    all_facts = jnp.stack([my_index, *starts])
    part_facts = jnp.stack([my_index, *[others[m] for m in order], *[own[m] for m in order]])
    places = jnp.stack([*own, *others])
    together = lax.optimization_barrier
    in_left, in_right, spread_mask, all_facts = together(
        (in_left, in_right, spread_mask, all_facts)
    )

    slope, hidden, low, high, inputs = run_conv(
        finish_first, False, True, all_facts, neighbours, feats, in_left, in_right, weight_one,
        [spread_mask], [], ("vmem", "vmem"), (0, EDGE // 2 - 1),
    )
    h_left, h_right = beside(low, high)
    slope, hidden = run_conv(
        finish_first, False, False, all_facts, neighbours, inputs, in_left, in_right, weight_one,
        [spread_mask, slope, hidden], [], ("vmem", "vmem"), tuple(range(1, EDGE // 2 - 1)),
    )
    output, grad_second, low, high = run_conv(
        finish_second, False, False, all_facts, neighbours, hidden, h_left, h_right, weight_two,
        [spread_mask, cotangent], [], ("hbm", "vmem"),
    )
    s_left, s_right = beside(low, high)
    (pieces_two,) = run_weight(
        all_facts, neighbours, hidden, h_left, h_right, grad_second, scale,
        [(2 * members, rows)], True,
    )
    pieces_two, s_left, s_right = together((pieces_two, s_left, s_right))
    parts_two = lax.all_to_all(pieces_two, "space", 0, 0, tiled=True)
    grad_first, low, high = run_conv(
        finish_product, True, False, all_facts, neighbours, grad_second, s_left, s_right, weight_two,
        [slope], [], ("vmem",),
    )
    far = members - members // 2
    sent_far, sent_near, kept = run_weight(
        part_facts, neighbours, inputs, in_left, in_right, grad_first, scale,
        [(far, rows), (members // 2, rows), (members, rows)], False,
    )
    parts_two, _ = together((parts_two, kept))
    part_two = part_total(parts_two)
    sent_far, sent_near, low, high = together((sent_far, sent_near, low, high))
    received = {
        m: piece[n]
        for piece, masks in ((swapped(sent_far), order[:far]), (swapped(sent_near), order[far:]))
        for n, m in enumerate(masks)
    }
    f_left, f_right = beside(low, high)

    def summed(m):
        return kept[order.index(m)].astype(jnp.float32) + received[m].astype(jnp.float32)

    masks = [m for m in order if m]
    halves = [summed(m).astype(jnp.bfloat16) for m in masks]
    *halves, f_left, f_right, late_weight = together((*halves, f_left, f_right, weight_one))
    arrived = [across(half, 2 * m) for half, m in zip(halves, masks)]
    (grad_input,) = run_conv(
        finish_product, True, False, all_facts, neighbours, grad_first, f_left, f_right,
        late_weight, [spread_mask], [], ("hbm",),
    )
    grad_input, part_two = together((grad_input, part_two))
    half_two = gathered(part_two)
    *arrived, grad_input = together((*arrived, grad_input))
    part = summed(0)
    for half in arrived:
        part = part + half.astype(jnp.float32)
    part = part.astype(jnp.bfloat16)
    same = handed(part)
    other = [swapped(piece) for piece in same]
    grad_w2, strays = joined(half_two)
    *other, grad_w2, strays = together((*other, grad_w2, strays))
    grad_w1 = run_join(places, [*same, *other])
    return strays, (output, grad_input, grad_w1, grad_w2)


def body(*arguments):
    strays, results = column_body(*arguments)

    def again(state):
        return jnp.zeros_like(state[0]), general_body(*arguments)

    return lax.while_loop(lambda state: state[0] > 0.5, again, (strays, results))[1]


def extended(field, source_index):
    bricks = field.shape[0]
    left, right = beside(field, field)
    blank = jnp.zeros((1, *field.shape[1:]), field.dtype)
    sources = jnp.concatenate([left, field, right, blank], axis=0).reshape(-1, EDGE * C)
    cell = jnp.arange(EDGE + 2)
    side = jnp.where(cell == 0, 0, jnp.where(cell == EDGE + 1, 2, 1))
    direction = 3 * side[:, None] + side[None, :]
    own = bricks + jnp.arange(bricks)[:, None]
    named = jnp.concatenate([source_index[:, :4], own, source_index[:, 4:]], axis=1)
    place = (cell - 1) % EDGE
    columns = named[:, direction] * SLAB + place[:, None] * EDGE + place[None, :]
    padded = jnp.take(sources, columns, axis=0).reshape(bricks, EDGE + 2, EDGE + 2, EDGE, C)
    return jnp.pad(padded, ((0, 0), (0, 0), (0, 0), (1, 1), (0, 0)))


def shifted(padded, k):
    bricks = padded.shape[0]
    corner = (0, k // 9, k // 3 % 3, k % 3, 0)
    return lax.dynamic_slice(padded, corner, (bricks, EDGE, EDGE, EDGE, C)).reshape(-1, C)


def general_conv(padded, weight, turned):
    def add(k, total):
        block = lax.dynamic_index_in_dim(weight, k, keepdims=False)
        cells = shifted(padded, 26 - k if turned else k)
        return total + jnp.dot(
            cells, block.T if turned else block, preferred_element_type=jnp.float32
        )

    rows = padded.shape[0] * EDGE**3
    return lax.fori_loop(0, 27, add, jnp.zeros((rows, C), jnp.float32))


def general_grad(padded, grads, scale):
    def one(k):
        contract = (((0,), (0,)), ((), ()))
        return lax.dot_general(
            shifted(padded, k), grads, contract, preferred_element_type=jnp.float32
        )

    term = (lax.map(one, jnp.arange(27)) * scale).astype(jnp.bfloat16)
    halves = jnp.pad(term, ((0, 1), (0, 0), (0, 0))).reshape(2, 14, C, C)
    even = lax.axis_index("space") % 2 == 0
    sent = jnp.where(even, halves[1], halves[0])
    kept = jnp.where(even, halves[0], halves[1])
    return joined(gathered(part_total(among(in_parts(pair_sum(sent, kept))))))[0]


def silu_slope(values):
    s = jax.nn.sigmoid(values)
    return s * (1.0 + values * (1.0 - s))


def general_body(feats, mask, neighbours, weight_one, weight_two, cotangent):
    bricks, voxels, _ = feats.shape
    first_brick = (lax.axis_index("space") - 1) * bricks
    source_index = jnp.where(neighbours >= 0, neighbours - first_brick, 3 * bricks)
    occupied = mask.reshape(-1, 1).astype(jnp.float32)
    scale = 1.0 / math.sqrt(voxels * bricks)

    def rounded(values):
        return values.astype(jnp.bfloat16)

    def extend(values):
        return extended(values.reshape(bricks, voxels, C), source_index)

    padded_in = extend(feats * mask[:, :, None].astype(jnp.bfloat16))
    first_pre = general_conv(padded_in, weight_one, False)
    padded_hidden = extend(rounded(occupied * jax.nn.silu(first_pre)))
    second_pre = general_conv(padded_hidden, weight_two, False)
    output = rounded(occupied * jax.nn.silu(second_pre))
    received = cotangent.reshape(-1, C).astype(jnp.float32)
    grad_second = rounded(received * occupied * silu_slope(second_pre))
    back_second = general_conv(extend(grad_second), weight_two, True)
    grad_first = rounded(occupied * silu_slope(first_pre) * back_second)
    grad_input = rounded(occupied * general_conv(extend(grad_first), weight_one, True))
    return (
        output.reshape(feats.shape),
        grad_input.reshape(feats.shape),
        general_grad(padded_in, grad_first, scale),
        general_grad(padded_hidden, grad_second, scale),
    )


def solution(mesh):
    in_specs = (
        P(("scene", "space"), None, None),
        P(("scene", "space"), None),
        P(("scene", "space"), None),
        P(),
        P(),
        P(("scene", "space"), None, None),
    )
    out_specs = (
        P(("scene", "space"), None, None),
        P(("scene", "space"), None, None),
        P("scene", None, None),
        P("scene", None, None),
    )
    return jax.shard_map(body, mesh=mesh, in_specs=in_specs, out_specs=out_specs, check_vma=False)
```

```python
import functools
import math

import jax
import jax.numpy as jnp
from jax import lax
from jax.experimental import pallas as pl
from jax.experimental.pallas import tpu as pltpu
from jax.sharding import PartitionSpec as P

EDGE = 8
TILE = 1
WIDE = 8
SLAB = EDGE * EDGE
C = 128
TAPS = 9 * C
VMEM_LIMIT = 36 * 1024 * 1024

DIRECTIONS = ((-1, -1), (-1, 0), (-1, 1), (0, -1), (0, 1), (1, -1), (1, 0), (1, 1))


def entry(facts, neighbours, brick, column):
    named = neighbours[brick, column]
    local = named - (facts[0] + DIRECTIONS[column][0]) * (TILE * WIDE)
    inside = (named >= 0) & (local >= 0) & (local < neighbours.shape[0])
    return jnp.where(inside, local, -1)


def picked(source, index, first, rows):
    found = source[jnp.maximum(index, 0), first : first + rows, :].astype(jnp.float32)
    return jnp.where(index >= 0, found, 0.0)


def padded_cells(facts, neighbours, field, left, right, g, a):
    near = functools.partial(entry, facts, neighbours, g)
    if a == 0:
        source, first, names = left, 0, (near(1), near(0), near(2))
    elif a == EDGE + 1:
        source, first, names = right, 0, (near(6), near(5), near(7))
    else:
        source, first, names = field, (a - 1) * SLAB, (g, near(3), near(4))
    if source is field:
        centre = field[g, first : first + SLAB, :].astype(jnp.float32)
    else:
        centre = picked(source, names[0], first, SLAB)
    top = picked(source, names[1], first + SLAB - 16, 16)
    bottom = picked(source, names[2], first, 16)
    return centre, jnp.concatenate([top[8:16], centre, bottom[0:8]], axis=0)


def before_and_behind(cells):
    place = lax.broadcasted_iota(jnp.int32, cells.shape, 1)
    before = jnp.where(place == 0, 0.0, pltpu.roll(cells, 1, 1))
    return before, jnp.where(place == EDGE - 1, 0.0, pltpu.roll(cells, EDGE - 1, 1))


def slab_tiles(cells):
    cells = cells.reshape(EDGE + 2, EDGE, C)
    before, behind = before_and_behind(cells)
    even, odd = [], []
    for shifted in (before, cells, behind):
        even.append(shifted.reshape((EDGE + 2) * EDGE, C).astype(jnp.bfloat16))
        odd.append(shifted[1 : EDGE + 1].reshape(SLAB, C).astype(jnp.bfloat16))
    return [e[0:SLAB] for e in even] + odd + [e[16 : 16 + SLAB] for e in even]


def build_slab(facts, neighbours, field, left, right, a, stack):
    for g in range(field.shape[0]):
        _, cells = padded_cells(facts, neighbours, field, left, right, g, a)
        for t, tile in enumerate(slab_tiles(cells)):
            stack[g, :, t * C : (t + 1) * C] = tile


def build_rows(facts, neighbours, field, left, right, slabs, stack):
    @pl.loop(0, field.shape[0])
    def _(g):
        for a in slabs:
            centre, cells = padded_cells(facts, neighbours, field, left, right, g, a)
            cells = cells.astype(jnp.bfloat16)
            stack[g, a, :, 0:C] = cells[0:SLAB]
            stack[g, a, :, C : 2 * C] = centre.astype(jnp.bfloat16)
            stack[g, a, :, 2 * C :] = cells[16 : 16 + SLAB]


def fill_weights(weights, turned, filled):
    for k1 in range(3):
        for k2 in range(3):
            for k3 in range(3):
                n = 9 * k1 + 3 * k2 + k3
                block = weights[26 - n if turned else n]
                if turned:
                    block = block.astype(jnp.float32).T.astype(jnp.bfloat16)
                for half in range(2):
                    row, column = 3 * (k1 + half) + k2, 2 * k3 + half
                    filled[row * C : (row + 1) * C, column * C : (column + 1) * C] = block
    blank = jnp.zeros((3 * C, C), jnp.bfloat16)
    for k3 in range(3):
        filled[9 * C :, 2 * k3 * C : (2 * k3 + 1) * C] = blank
        filled[: 3 * C, (2 * k3 + 1) * C : (2 * k3 + 2) * C] = blank


def conv_kernel(finish, turned, masked, pairs, n_near, n_far, kinds, facts, neighbours, *rest):
    field, left, right, *rest = rest
    near, rest = rest[:n_near], rest[n_near:]
    done, near = (near[-len(kinds) :], near[: -len(kinds)]) if pairs and not masked else ((), near)
    operands, rest = rest[: 1 + n_far], rest[1 + n_far :]
    results, rest = rest[: len(kinds)], rest[len(kinds) :]
    edges, rest = (rest[:2], rest[2:]) if kinds[-1] == "vmem" and not done else ((), rest)
    kept, rest = (rest[0], rest[1:]) if masked else (None, rest)
    local, rest = rest[: 1 + n_far], rest[1 + n_far :]
    *staged, stack, filled, came, gone = rest
    made, leaving = [], []
    for kind, result in zip(kinds, results):
        made.append(result if kind == "vmem" else staged.pop(0))
        if kind == "hbm":
            leaving.append((made[-1], result))
    copies = [
        pltpu.make_async_copy(there, here, came.at[n])
        for n, (there, here) in enumerate(zip(operands, local))
    ]
    for copy in copies:
        copy.start()
    if masked:
        kept[...] = field[...] * near[0][...]
        field = kept
    computed = pairs or tuple(range(EDGE // 2))
    slabs = sorted({2 * pair + n for pair in computed for n in range(4)})
    build_rows(facts, neighbours, field, left, right, slabs, stack)
    copies[0].wait()
    fill_weights(local[0], turned, filled)
    for copy in copies[1:]:
        copy.wait()
    bricks = field.shape[0] // 2
    factors = [*near, *local[1:]]

    def outgoing(pair):
        rows = pl.ds(at(pair * 2 * SLAB), 2 * SLAB)
        return [
            pltpu.make_async_copy(here.at[:, rows, :], there.at[:, rows, :], gone.at[n, pair])
            for n, (here, there) in enumerate(leaving)
        ]

    def step(pair):
        for part in range(2):
            some = slice(part * bricks, (part + 1) * bricks)
            lhs = [stack[some, 2 * pair + n].reshape(bricks * SLAB, 3 * C) for n in range(4)]
            shares = jnp.dot(
                jnp.concatenate(lhs, axis=1), filled[...], preferred_element_type=jnp.float32
            ).reshape(bricks * EDGE, EDGE, 6 * C)
            before, _ = before_and_behind(shares[:, :, : 2 * C])
            _, behind = before_and_behind(shares[:, :, 4 * C :])
            both = (before + shares[:, :, 2 * C : 4 * C] + behind).reshape(bricks * SLAB, 2 * C)
            for half in range(2):
                rows = pl.ds(at((2 * pair + half) * SLAB), SLAB)
                values = both[:, half * C : (half + 1) * C].reshape(bricks, SLAB, C)
                values = finish(
                    values, *[array[some, rows, :].astype(jnp.float32) for array in factors]
                )
                for array, value in zip(made, values):
                    array[some, rows, :] = value.astype(jnp.bfloat16)
        for copy in outgoing(pair):
            copy.start()

    if pairs:
        for pair in pairs:
            step(pair)
        for array, other in zip(made, done):
            for pair in set(range(EDGE // 2)) - set(pairs):
                rows = slice(2 * pair * SLAB, (2 * pair + 2) * SLAB)
                array[:, rows, :] = other[:, rows, :]
    else:

        @pl.loop(0, EDGE // 4)
        def _(n):
            step(2 * n)
            step(2 * n + 1)

    if edges:
        edges[0][...] = made[-1][:, :SLAB, :]
        edges[1][...] = made[-1][:, (EDGE - 1) * SLAB :, :]
    for pair in range(EDGE // 2):
        for copy in outgoing(pair):
            copy.wait()


def at(row):
    return row if isinstance(row, int) else pl.multiple_of(row, SLAB)


def finish_first(values, mask):
    s = jax.nn.sigmoid(values)
    return mask * (s * (1.0 + values * (1.0 - s))), mask * (values * s)


def finish_second(values, mask, cotangent):
    s = jax.nn.sigmoid(values)
    return mask * (values * s), cotangent * mask * (s * (1.0 + values * (1.0 - s)))


def finish_product(values, factor):
    return (factor * values,)


def weight_kernel(scale, counted, facts, neighbours, field, left, right, grads, *rest):
    outs, rest = rest[: -(EDGE + 5)], rest[-(EDGE + 5) :]
    stack, turned, total, blocks = rest[: EDGE + 2], rest[-3], rest[-2], rest[-1]
    bricks = grads.shape[0]

    def turn(a):
        slab = grads[:, a * SLAB : (a + 1) * SLAB, :].reshape(bricks * SLAB, C)
        turned[a] = slab.astype(jnp.float32).T.astype(jnp.bfloat16)

    build_slab(facts, neighbours, field, left, right, 0, stack[0])
    turn(0)
    for a in range(EDGE + 2):
        if a < EDGE + 1:
            build_slab(facts, neighbours, field, left, right, a + 1, stack[a + 1])
        if a < EDGE - 1:
            turn(a + 1)
        first, last = max(0, a - EDGE + 1), min(3, a + 1)
        lhs = [turned[a - k1] for k1 in range(first, last)]
        product = jnp.dot(
            lhs[0] if len(lhs) == 1 else jnp.concatenate(lhs, axis=0),
            stack[a][...].reshape(bricks * SLAB, TAPS),
            preferred_element_type=jnp.float32,
        )
        for n, k1 in enumerate(range(first, last)):
            rows, part = slice(k1 * C, (k1 + 1) * C), product[n * C : (n + 1) * C]
            total[rows, :] = part if a == k1 else total[rows, :] + part
    for n in range(27):
        k1, t = n // 9, n % 9
        block = total[k1 * C : (k1 + 1) * C, t * C : (t + 1) * C].T * scale
        blocks[n * C : (n + 1) * C, :] = block.astype(jnp.bfloat16)
    strays = 0
    for g in range(bricks if counted else 0):
        for column in range(len(DIRECTIONS)):
            lost = (neighbours[g, column] >= 0) & (entry(facts, neighbours, g, column) < 0)
            strays = strays + jnp.where(lost, 1, 0)
    strays = jnp.full((C, C), jnp.minimum(strays, 1), jnp.int32)
    blocks[27 * C :, :] = strays.astype(jnp.float32).astype(jnp.bfloat16)
    n = 1
    for out in outs:
        for piece in range(out.shape[0]):
            first = pl.multiple_of(facts[n], 16)
            out[piece] = blocks[pl.ds(first, out.shape[1]), :]
            n += 1


def join_kernel(places, *rest):
    *pieces, result, blocks, arrived = rest
    for n, piece in enumerate(pieces):
        first = pl.multiple_of(places[n], 16)
        blocks[pl.ds(first, piece.shape[0]), :] = piece[...].astype(jnp.float32)
    copy = pltpu.make_async_copy(blocks.at[pl.ds(0, 27 * C)], result, arrived)
    copy.start()
    copy.wait()


def cost(flops, arrays):
    return pl.CostEstimate(
        flops=flops,
        bytes_accessed=sum(math.prod(a.shape) * a.dtype.itemsize for a in arrays),
        transcendentals=0,
    )


def run_conv(
    finish, turned, masked, facts, neighbours, field, left, right, weights, near, far, kinds, pairs=()
):
    bricks, voxels, _ = field.shape
    rows = jax.ShapeDtypeStruct((bricks, voxels, C), jnp.bfloat16)
    edge = jax.ShapeDtypeStruct((bricks, SLAB, C), jnp.bfloat16)
    operands = [weights, *far]
    spaces = {"vmem": pltpu.VMEM, "hbm": pltpu.HBM}
    outs = [(rows, spaces[kind]) for kind in kinds]
    ends = kinds[-1] == "vmem" and (masked or not pairs)
    outs += [(edge, pltpu.VMEM)] * (2 * ends) + [(rows, pltpu.VMEM)] * masked
    n_hbm = kinds.count("hbm")
    return pl.pallas_call(
        functools.partial(conv_kernel, finish, turned, masked, pairs, len(near), len(far), kinds),
        in_specs=[
            *[pl.BlockSpec(memory_space=pltpu.SMEM)] * 2,
            *[pl.BlockSpec(memory_space=pltpu.VMEM)] * (3 + len(near)),
            *[pl.BlockSpec(memory_space=pltpu.HBM) for _ in operands],
        ],
        out_specs=[pl.BlockSpec(memory_space=space) for _, space in outs],
        out_shape=[shape for shape, _ in outs],
        scratch_shapes=[
            *[pltpu.VMEM(a.shape, a.dtype) for a in operands],
            *[pltpu.VMEM(rows.shape, rows.dtype)] * n_hbm,
            pltpu.VMEM((bricks, EDGE + 2, SLAB, 3 * C), jnp.bfloat16),
            pltpu.VMEM((12 * C, 6 * C), jnp.bfloat16),
            pltpu.SemaphoreType.DMA((len(operands),)),
            pltpu.SemaphoreType.DMA((max(n_hbm, 1), EDGE // 2)),
        ],
        compiler_params=pltpu.CompilerParams(vmem_limit_bytes=VMEM_LIMIT),
        cost_estimate=cost(
            (9 * len(pairs) or 36) * 2 * bricks * voxels * C * C, [field, *near, *operands] + [shape for shape, _ in outs]
        ),
    )(facts, neighbours, field, left, right, *near, *operands)


def run_weight(facts, neighbours, field, left, right, grads, scale, shapes, counted):
    bricks, voxels, _ = field.shape
    outs = [jax.ShapeDtypeStruct((*shape, C), jnp.bfloat16) for shape in shapes]
    return pl.pallas_call(
        functools.partial(weight_kernel, scale, counted),
        in_specs=[
            *[pl.BlockSpec(memory_space=pltpu.SMEM)] * 2,
            *[pl.BlockSpec(memory_space=pltpu.VMEM)] * 4,
        ],
        out_specs=[pl.BlockSpec(memory_space=pltpu.VMEM) for _ in outs],
        out_shape=outs,
        scratch_shapes=[
            *[pltpu.VMEM((bricks, SLAB, TAPS), jnp.bfloat16)] * (EDGE + 2),
            pltpu.VMEM((EDGE, C, bricks * SLAB), jnp.bfloat16),
            pltpu.VMEM((3 * C, TAPS), jnp.float32),
            pltpu.VMEM((28 * C, C), jnp.bfloat16),
        ],
        compiler_params=pltpu.CompilerParams(vmem_limit_bytes=VMEM_LIMIT),
        cost_estimate=cost(2 * 27 * bricks * voxels * C * C, [field, left, right, grads, *outs]),
    )(facts, neighbours, field, left, right, grads)


def run_join(places, pieces):
    out = jax.ShapeDtypeStruct((27 * C, C), jnp.float32)
    return pl.pallas_call(
        join_kernel,
        in_specs=[
            pl.BlockSpec(memory_space=pltpu.SMEM),
            *[pl.BlockSpec(memory_space=pltpu.VMEM) for _ in pieces],
        ],
        out_specs=pl.BlockSpec(memory_space=pltpu.HBM),
        out_shape=out,
        scratch_shapes=[pltpu.VMEM((28 * C, C), jnp.float32), pltpu.SemaphoreType.DMA],
        cost_estimate=cost(0, [out, *pieces]),
    )(places, *pieces).reshape(27, C, C)


def beside(low, high):
    count = lax.axis_size("space")
    left = lax.ppermute(high, "space", [(i, i + 1) for i in range(count - 1)])
    right = lax.ppermute(low, "space", [(i + 1, i) for i in range(count - 1)])
    return left, right


def across(values, mask):
    count = lax.axis_size("space")
    return lax.ppermute(values, "space", [(i, i ^ mask) for i in range(count)])


def swapped(half):
    return across(half, 1)


def among(parts):
    count = lax.axis_size("space")
    groups = [[i for i in range(count) if i % 2 == b] for b in range(2)]
    return lax.all_to_all(parts, "space", 0, 0, axis_index_groups=groups, tiled=True)


def handed(part):
    members = lax.axis_size("space") // 2
    masks = [*range(members // 2, members), *range(1, members // 2)]
    came = {m: across(part, 2 * m) for m in masks}
    return [part, *[came[m] for m in range(1, members)]]


def pair_sum(sent, kept):
    total = kept.astype(jnp.float32) + swapped(sent).astype(jnp.float32)
    return total.astype(jnp.bfloat16)


def in_parts(half):
    return half.reshape(lax.axis_size("space") // 2, -1, C)


def part_total(parts):
    return jnp.sum(parts.astype(jnp.float32), axis=0).astype(jnp.bfloat16)


def gathered(part):
    members = lax.axis_size("space") // 2
    return among(jnp.broadcast_to(part[None], (members,) + part.shape)).reshape(14, C, C)


def joined(half):
    other = swapped(half)
    even = lax.axis_index("space") % 2 == 0
    first = jnp.where(even, half, other)
    second = jnp.where(even, other, half)
    blocks = jnp.concatenate([first, second[:13]], axis=0).astype(jnp.float32)
    return blocks, second[13, 0, 0].astype(jnp.float32)


def column_body(feats, mask, neighbours, weight_one, weight_two, cotangent):
    bricks, voxels, channels = feats.shape
    my_index = lax.axis_index("space")
    low, high = (
        feats[:, rows] * mask[:, rows, None].astype(jnp.bfloat16)
        for rows in (slice(0, SLAB), slice(voxels - SLAB, voxels))
    )
    in_left, in_right = beside(low, high)
    spread_mask = jnp.broadcast_to(mask.astype(jnp.bfloat16)[:, :, None], feats.shape)
    scale = 1.0 / math.sqrt(voxels * bricks)

    members = lax.axis_size("space") // 2
    bit, row = my_index % 2, my_index // 2
    rows = 28 * C // (2 * members)
    order = [*range(members // 2, members), *range(members // 2)]
    own = [(bit * members + (row ^ m)) * rows for m in range(members)]
    others = [((1 - bit) * members + (row ^ m)) * rows for m in range(members)]
    starts = [(i % 2 * members + i // 2) * rows for i in range(2 * members)]
    all_facts = jnp.stack([my_index, *starts])
    part_facts = jnp.stack([my_index, *[others[m] for m in order], *[own[m] for m in order]])
    places = jnp.stack([*own, *others])
    together = lax.optimization_barrier
    in_left, in_right, spread_mask, all_facts = together(
        (in_left, in_right, spread_mask, all_facts)
    )

    slope, hidden, low, high, inputs = run_conv(
        finish_first, False, True, all_facts, neighbours, feats, in_left, in_right, weight_one,
        [spread_mask], [], ("vmem", "vmem"), (0, EDGE // 2 - 1),
    )
    h_left, h_right = beside(low, high)
    slope, hidden = run_conv(
        finish_first, False, False, all_facts, neighbours, inputs, in_left, in_right, weight_one,
        [spread_mask, slope, hidden], [], ("vmem", "vmem"), tuple(range(1, EDGE // 2 - 1)),
    )
    output, grad_second, low, high = run_conv(
        finish_second, False, False, all_facts, neighbours, hidden, h_left, h_right, weight_two,
        [spread_mask], [cotangent], ("hbm", "vmem"),
    )
    s_left, s_right = beside(low, high)
    (pieces_two,) = run_weight(
        all_facts, neighbours, hidden, h_left, h_right, grad_second, scale,
        [(2 * members, rows)], True,
    )
    pieces_two, s_left, s_right = together((pieces_two, s_left, s_right))
    parts_two = lax.all_to_all(pieces_two, "space", 0, 0, tiled=True)
    grad_first, low, high = run_conv(
        finish_product, True, False, all_facts, neighbours, grad_second, s_left, s_right, weight_two,
        [slope], [], ("vmem",),
    )
    far = members - members // 2
    sent_far, sent_near, kept = run_weight(
        part_facts, neighbours, inputs, in_left, in_right, grad_first, scale,
        [(far, rows), (members // 2, rows), (members, rows)], False,
    )
    parts_two, _ = together((parts_two, kept))
    part_two = part_total(parts_two)
    sent_far, sent_near, low, high = together((sent_far, sent_near, low, high))
    came_far, came_near = swapped(sent_far), swapped(sent_near)
    f_left, f_right = beside(low, high)
    came_far, part_two = together((came_far, part_two))
    half_two = gathered(part_two)
    received = {
        m: piece[n]
        for piece, masks in ((came_far, order[:far]), (came_near, order[far:]))
        for n, m in enumerate(masks)
    }

    def summed(m):
        return kept[order.index(m)].astype(jnp.float32) + received[m].astype(jnp.float32)

    masks = [m for m in order if m]
    halves = [summed(m).astype(jnp.bfloat16) for m in masks]
    *halves, f_left, f_right, late_weight = together((*halves, f_left, f_right, weight_one))
    arrived = [across(half, 2 * m) for half, m in zip(halves, masks)]
    (grad_input,) = run_conv(
        finish_product, True, False, all_facts, neighbours, grad_first, f_left, f_right,
        late_weight, [spread_mask], [], ("hbm",),
    )
    _, half_two = together((grad_input, half_two))
    *arrived, grad_input = together((*arrived, grad_input))
    part = summed(0)
    for half in arrived:
        part = part + half.astype(jnp.float32)
    part = part.astype(jnp.bfloat16)
    same = handed(part)
    other = [swapped(piece) for piece in same]
    grad_w2, strays = joined(half_two)
    *other, grad_w2, strays = together((*other, grad_w2, strays))
    grad_w1 = run_join(places, [*same, *other])
    return strays, (output, grad_input, grad_w1, grad_w2)


def body(*arguments):
    strays, results = column_body(*arguments)

    def again(state):
        return jnp.zeros_like(state[0]), general_body(*arguments)

    return lax.while_loop(lambda state: state[0] > 0.5, again, (strays, results))[1]


def extended(field, source_index):
    bricks = field.shape[0]
    left, right = beside(field, field)
    blank = jnp.zeros((1, *field.shape[1:]), field.dtype)
    sources = jnp.concatenate([left, field, right, blank], axis=0).reshape(-1, EDGE * C)
    cell = jnp.arange(EDGE + 2)
    side = jnp.where(cell == 0, 0, jnp.where(cell == EDGE + 1, 2, 1))
    direction = 3 * side[:, None] + side[None, :]
    own = bricks + jnp.arange(bricks)[:, None]
    named = jnp.concatenate([source_index[:, :4], own, source_index[:, 4:]], axis=1)
    place = (cell - 1) % EDGE
    columns = named[:, direction] * SLAB + place[:, None] * EDGE + place[None, :]
    padded = jnp.take(sources, columns, axis=0).reshape(bricks, EDGE + 2, EDGE + 2, EDGE, C)
    return jnp.pad(padded, ((0, 0), (0, 0), (0, 0), (1, 1), (0, 0)))


def shifted(padded, k):
    bricks = padded.shape[0]
    corner = (0, k // 9, k // 3 % 3, k % 3, 0)
    return lax.dynamic_slice(padded, corner, (bricks, EDGE, EDGE, EDGE, C)).reshape(-1, C)


def general_conv(padded, weight, turned):
    def add(k, total):
        block = lax.dynamic_index_in_dim(weight, k, keepdims=False)
        cells = shifted(padded, 26 - k if turned else k)
        return total + jnp.dot(
            cells, block.T if turned else block, preferred_element_type=jnp.float32
        )

    rows = padded.shape[0] * EDGE**3
    return lax.fori_loop(0, 27, add, jnp.zeros((rows, C), jnp.float32))


def general_grad(padded, grads, scale):
    def one(k):
        contract = (((0,), (0,)), ((), ()))
        return lax.dot_general(
            shifted(padded, k), grads, contract, preferred_element_type=jnp.float32
        )

    term = (lax.map(one, jnp.arange(27)) * scale).astype(jnp.bfloat16)
    halves = jnp.pad(term, ((0, 1), (0, 0), (0, 0))).reshape(2, 14, C, C)
    even = lax.axis_index("space") % 2 == 0
    sent = jnp.where(even, halves[1], halves[0])
    kept = jnp.where(even, halves[0], halves[1])
    return joined(gathered(part_total(among(in_parts(pair_sum(sent, kept))))))[0]


def silu_slope(values):
    s = jax.nn.sigmoid(values)
    return s * (1.0 + values * (1.0 - s))


def general_body(feats, mask, neighbours, weight_one, weight_two, cotangent):
    bricks, voxels, _ = feats.shape
    first_brick = (lax.axis_index("space") - 1) * bricks
    source_index = jnp.where(neighbours >= 0, neighbours - first_brick, 3 * bricks)
    occupied = mask.reshape(-1, 1).astype(jnp.float32)
    scale = 1.0 / math.sqrt(voxels * bricks)

    def rounded(values):
        return values.astype(jnp.bfloat16)

    def extend(values):
        return extended(values.reshape(bricks, voxels, C), source_index)

    padded_in = extend(feats * mask[:, :, None].astype(jnp.bfloat16))
    first_pre = general_conv(padded_in, weight_one, False)
    padded_hidden = extend(rounded(occupied * jax.nn.silu(first_pre)))
    second_pre = general_conv(padded_hidden, weight_two, False)
    output = rounded(occupied * jax.nn.silu(second_pre))
    received = cotangent.reshape(-1, C).astype(jnp.float32)
    grad_second = rounded(received * occupied * silu_slope(second_pre))
    back_second = general_conv(extend(grad_second), weight_two, True)
    grad_first = rounded(occupied * silu_slope(first_pre) * back_second)
    grad_input = rounded(occupied * general_conv(extend(grad_first), weight_one, True))
    return (
        output.reshape(feats.shape),
        grad_input.reshape(feats.shape),
        general_grad(padded_in, grad_first, scale),
        general_grad(padded_hidden, grad_second, scale),
    )


def solution(mesh):
    in_specs = (
        P(("scene", "space"), None, None),
        P(("scene", "space"), None),
        P(("scene", "space"), None),
        P(),
        P(),
        P(("scene", "space"), None, None),
    )
    out_specs = (
        P(("scene", "space"), None, None),
        P(("scene", "space"), None, None),
        P("scene", None, None),
        P("scene", None, None),
    )
    return jax.shard_map(body, mesh=mesh, in_specs=in_specs, out_specs=out_specs, check_vma=False)
```

```python
import functools
import math

import jax
import jax.numpy as jnp
from jax import lax
from jax.experimental import pallas as pl
from jax.experimental.pallas import tpu as pltpu
from jax.sharding import PartitionSpec as P

EDGE = 8
TILE = 1
WIDE = 8
SLAB = EDGE * EDGE
C = 128
TAPS = 9 * C
VMEM_LIMIT = 36 * 1024 * 1024

DIRECTIONS = ((-1, -1), (-1, 0), (-1, 1), (0, -1), (0, 1), (1, -1), (1, 0), (1, 1))


def entry(facts, neighbours, brick, column):
    named = neighbours[brick, column]
    local = named - (facts[0] + DIRECTIONS[column][0]) * (TILE * WIDE)
    inside = (named >= 0) & (local >= 0) & (local < neighbours.shape[0])
    return jnp.where(inside, local, -1)


def picked(source, index, first, rows):
    found = source[jnp.maximum(index, 0), first : first + rows, :].astype(jnp.float32)
    return jnp.where(index >= 0, found, 0.0)


def padded_cells(facts, neighbours, field, left, right, g, a):
    near = functools.partial(entry, facts, neighbours, g)
    if a == 0:
        source, first, names = left, 0, (near(1), near(0), near(2))
    elif a == EDGE + 1:
        source, first, names = right, 0, (near(6), near(5), near(7))
    else:
        source, first, names = field, (a - 1) * SLAB, (g, near(3), near(4))
    if source is field:
        centre = field[g, first : first + SLAB, :].astype(jnp.float32)
    else:
        centre = picked(source, names[0], first, SLAB)
    top = picked(source, names[1], first + SLAB - 16, 16)
    bottom = picked(source, names[2], first, 16)
    return centre, jnp.concatenate([top[8:16], centre, bottom[0:8]], axis=0)


def before_and_behind(cells):
    place = lax.broadcasted_iota(jnp.int32, cells.shape, 1)
    before = jnp.where(place == 0, 0.0, pltpu.roll(cells, 1, 1))
    return before, jnp.where(place == EDGE - 1, 0.0, pltpu.roll(cells, EDGE - 1, 1))


def slab_tiles(cells):
    cells = cells.reshape(EDGE + 2, EDGE, C)
    before, behind = before_and_behind(cells)
    even, odd = [], []
    for shifted in (before, cells, behind):
        even.append(shifted.reshape((EDGE + 2) * EDGE, C).astype(jnp.bfloat16))
        odd.append(shifted[1 : EDGE + 1].reshape(SLAB, C).astype(jnp.bfloat16))
    return [e[0:SLAB] for e in even] + odd + [e[16 : 16 + SLAB] for e in even]


def build_slab(facts, neighbours, field, left, right, a, stack):
    for g in range(field.shape[0]):
        _, cells = padded_cells(facts, neighbours, field, left, right, g, a)
        for t, tile in enumerate(slab_tiles(cells)):
            stack[g, :, t * C : (t + 1) * C] = tile


def build_rows(facts, neighbours, field, left, right, slabs, stack):
    @pl.loop(0, field.shape[0])
    def _(g):
        for a in slabs:
            centre, cells = padded_cells(facts, neighbours, field, left, right, g, a)
            cells = cells.astype(jnp.bfloat16)
            stack[g, a, :, 0:C] = cells[0:SLAB]
            stack[g, a, :, C : 2 * C] = centre.astype(jnp.bfloat16)
            stack[g, a, :, 2 * C :] = cells[16 : 16 + SLAB]


def fill_weights(weights, turned, filled):
    for k1 in range(3):
        for k2 in range(3):
            for k3 in range(3):
                n = 9 * k1 + 3 * k2 + k3
                block = weights[26 - n if turned else n]
                if turned:
                    block = block.astype(jnp.float32).T.astype(jnp.bfloat16)
                for half in range(2):
                    row, column = 3 * (k1 + half) + k2, 2 * k3 + half
                    filled[row * C : (row + 1) * C, column * C : (column + 1) * C] = block
    blank = jnp.zeros((3 * C, C), jnp.bfloat16)
    for k3 in range(3):
        filled[9 * C :, 2 * k3 * C : (2 * k3 + 1) * C] = blank
        filled[: 3 * C, (2 * k3 + 1) * C : (2 * k3 + 2) * C] = blank


def conv_kernel(finish, turned, masked, pairs, n_near, n_far, kinds, facts, neighbours, *rest):
    field, left, right, *rest = rest
    near, rest = rest[:n_near], rest[n_near:]
    done, near = (near[-len(kinds) :], near[: -len(kinds)]) if pairs and not masked else ((), near)
    operands, rest = rest[: 1 + n_far], rest[1 + n_far :]
    results, rest = rest[: len(kinds)], rest[len(kinds) :]
    edges, rest = (rest[:2], rest[2:]) if kinds[-1] == "vmem" and not done else ((), rest)
    kept, rest = (rest[0], rest[1:]) if masked else (None, rest)
    local, rest = rest[: 1 + n_far], rest[1 + n_far :]
    *staged, stack, filled, came, gone = rest
    made, leaving = [], []
    for kind, result in zip(kinds, results):
        made.append(result if kind == "vmem" else staged.pop(0))
        if kind == "hbm":
            leaving.append((made[-1], result))
    copies = [
        pltpu.make_async_copy(there, here, came.at[n])
        for n, (there, here) in enumerate(zip(operands, local))
    ]
    for copy in copies:
        copy.start()
    if masked:
        kept[...] = field[...] * near[0][...]
        field = kept
    computed = pairs or tuple(range(EDGE // 2))
    slabs = sorted({2 * pair + n for pair in computed for n in range(4)})
    build_rows(facts, neighbours, field, left, right, slabs, stack)
    copies[0].wait()
    fill_weights(local[0], turned, filled)
    for copy in copies[1:]:
        copy.wait()
    bricks = field.shape[0] // 2
    factors = [*near, *local[1:]]

    def outgoing(pair):
        rows = pl.ds(at(pair * 2 * SLAB), 2 * SLAB)
        return [
            pltpu.make_async_copy(here.at[:, rows, :], there.at[:, rows, :], gone.at[n, pair])
            for n, (here, there) in enumerate(leaving)
        ]

    def step(pair):
        for part in range(2):
            some = slice(part * bricks, (part + 1) * bricks)
            lhs = [stack[some, 2 * pair + n].reshape(bricks * SLAB, 3 * C) for n in range(4)]
            shares = jnp.dot(
                jnp.concatenate(lhs, axis=1), filled[...], preferred_element_type=jnp.float32
            ).reshape(bricks * EDGE, EDGE, 6 * C)
            before, _ = before_and_behind(shares[:, :, : 2 * C])
            _, behind = before_and_behind(shares[:, :, 4 * C :])
            both = (before + shares[:, :, 2 * C : 4 * C] + behind).reshape(bricks * SLAB, 2 * C)
            for half in range(2):
                rows = pl.ds(at((2 * pair + half) * SLAB), SLAB)
                values = both[:, half * C : (half + 1) * C].reshape(bricks, SLAB, C)
                values = finish(
                    values, *[array[some, rows, :].astype(jnp.float32) for array in factors]
                )
                for array, value in zip(made, values):
                    array[some, rows, :] = value.astype(jnp.bfloat16)
        for copy in outgoing(pair):
            copy.start()

    if pairs:
        for pair in pairs:
            step(pair)
        for array, other in zip(made, done):
            for pair in set(range(EDGE // 2)) - set(pairs):
                rows = slice(2 * pair * SLAB, (2 * pair + 2) * SLAB)
                array[:, rows, :] = other[:, rows, :]
    else:

        @pl.loop(0, EDGE // 4)
        def _(n):
            step(2 * n)
            step(2 * n + 1)

    if edges:
        edges[0][...] = made[-1][:, :SLAB, :]
        edges[1][...] = made[-1][:, (EDGE - 1) * SLAB :, :]
    for pair in range(EDGE // 2):
        for copy in outgoing(pair):
            copy.wait()


def at(row):
    return row if isinstance(row, int) else pl.multiple_of(row, SLAB)


def finish_first(values, mask):
    s = jax.nn.sigmoid(values)
    return mask * (s * (1.0 + values * (1.0 - s))), mask * (values * s)


def finish_second(values, mask, cotangent):
    s = jax.nn.sigmoid(values)
    return mask * (values * s), cotangent * mask * (s * (1.0 + values * (1.0 - s)))


def finish_product(values, factor):
    return (factor * values,)


def weight_kernel(scale, counted, facts, neighbours, field, left, right, grads, *rest):
    outs, rest = rest[: -(EDGE + 5)], rest[-(EDGE + 5) :]
    stack, turned, total, blocks = rest[: EDGE + 2], rest[-3], rest[-2], rest[-1]
    bricks = grads.shape[0]

    def turn(a):
        slab = grads[:, a * SLAB : (a + 1) * SLAB, :].reshape(bricks * SLAB, C)
        turned[a] = slab.astype(jnp.float32).T.astype(jnp.bfloat16)

    build_slab(facts, neighbours, field, left, right, 0, stack[0])
    turn(0)
    for a in range(EDGE + 2):
        if a < EDGE + 1:
            build_slab(facts, neighbours, field, left, right, a + 1, stack[a + 1])
        if a < EDGE - 1:
            turn(a + 1)
        first, last = max(0, a - EDGE + 1), min(3, a + 1)
        lhs = [turned[a - k1] for k1 in range(first, last)]
        product = jnp.dot(
            lhs[0] if len(lhs) == 1 else jnp.concatenate(lhs, axis=0),
            stack[a][...].reshape(bricks * SLAB, TAPS),
            preferred_element_type=jnp.float32,
        )
        for n, k1 in enumerate(range(first, last)):
            rows, part = slice(k1 * C, (k1 + 1) * C), product[n * C : (n + 1) * C]
            total[rows, :] = part if a == k1 else total[rows, :] + part
    for n in range(27):
        k1, t = n // 9, n % 9
        block = total[k1 * C : (k1 + 1) * C, t * C : (t + 1) * C].T * scale
        blocks[n * C : (n + 1) * C, :] = block.astype(jnp.bfloat16)
    strays = 0
    for g in range(bricks if counted else 0):
        for column in range(len(DIRECTIONS)):
            lost = (neighbours[g, column] >= 0) & (entry(facts, neighbours, g, column) < 0)
            strays = strays + jnp.where(lost, 1, 0)
    strays = jnp.full((C, C), jnp.minimum(strays, 1), jnp.int32)
    blocks[27 * C :, :] = strays.astype(jnp.float32).astype(jnp.bfloat16)
    n = 1
    for out in outs:
        for piece in range(out.shape[0]):
            first = pl.multiple_of(facts[n], 16)
            out[piece] = blocks[pl.ds(first, out.shape[1]), :]
            n += 1


def join_kernel(places, *rest):
    *pieces, result, blocks, arrived = rest
    for n, piece in enumerate(pieces):
        first = pl.multiple_of(places[n], 16)
        blocks[pl.ds(first, piece.shape[0]), :] = piece[...].astype(jnp.float32)
    copy = pltpu.make_async_copy(blocks.at[pl.ds(0, 27 * C)], result, arrived)
    copy.start()
    copy.wait()


def cost(flops, arrays):
    return pl.CostEstimate(
        flops=flops,
        bytes_accessed=sum(math.prod(a.shape) * a.dtype.itemsize for a in arrays),
        transcendentals=0,
    )


def run_conv(
    finish, turned, masked, facts, neighbours, field, left, right, weights, near, far, kinds, pairs=()
):
    bricks, voxels, _ = field.shape
    rows = jax.ShapeDtypeStruct((bricks, voxels, C), jnp.bfloat16)
    edge = jax.ShapeDtypeStruct((bricks, SLAB, C), jnp.bfloat16)
    operands = [weights, *far]
    spaces = {"vmem": pltpu.VMEM, "hbm": pltpu.HBM}
    outs = [(rows, spaces[kind]) for kind in kinds]
    ends = kinds[-1] == "vmem" and (masked or not pairs)
    outs += [(edge, pltpu.VMEM)] * (2 * ends) + [(rows, pltpu.VMEM)] * masked
    n_hbm = kinds.count("hbm")
    return pl.pallas_call(
        functools.partial(conv_kernel, finish, turned, masked, pairs, len(near), len(far), kinds),
        in_specs=[
            *[pl.BlockSpec(memory_space=pltpu.SMEM)] * 2,
            *[pl.BlockSpec(memory_space=pltpu.VMEM)] * (3 + len(near)),
            *[pl.BlockSpec(memory_space=pltpu.HBM) for _ in operands],
        ],
        out_specs=[pl.BlockSpec(memory_space=space) for _, space in outs],
        out_shape=[shape for shape, _ in outs],
        scratch_shapes=[
            *[pltpu.VMEM(a.shape, a.dtype) for a in operands],
            *[pltpu.VMEM(rows.shape, rows.dtype)] * n_hbm,
            pltpu.VMEM((bricks, EDGE + 2, SLAB, 3 * C), jnp.bfloat16),
            pltpu.VMEM((12 * C, 6 * C), jnp.bfloat16),
            pltpu.SemaphoreType.DMA((len(operands),)),
            pltpu.SemaphoreType.DMA((max(n_hbm, 1), EDGE // 2)),
        ],
        compiler_params=pltpu.CompilerParams(vmem_limit_bytes=VMEM_LIMIT),
        cost_estimate=cost(
            (9 * len(pairs) or 36) * 2 * bricks * voxels * C * C, [field, *near, *operands] + [shape for shape, _ in outs]
        ),
    )(facts, neighbours, field, left, right, *near, *operands)


def run_weight(facts, neighbours, field, left, right, grads, scale, shapes, counted):
    bricks, voxels, _ = field.shape
    outs = [jax.ShapeDtypeStruct((*shape, C), jnp.bfloat16) for shape in shapes]
    return pl.pallas_call(
        functools.partial(weight_kernel, scale, counted),
        in_specs=[
            *[pl.BlockSpec(memory_space=pltpu.SMEM)] * 2,
            *[pl.BlockSpec(memory_space=pltpu.VMEM)] * 4,
        ],
        out_specs=[pl.BlockSpec(memory_space=pltpu.VMEM) for _ in outs],
        out_shape=outs,
        scratch_shapes=[
            *[pltpu.VMEM((bricks, SLAB, TAPS), jnp.bfloat16)] * (EDGE + 2),
            pltpu.VMEM((EDGE, C, bricks * SLAB), jnp.bfloat16),
            pltpu.VMEM((3 * C, TAPS), jnp.float32),
            pltpu.VMEM((28 * C, C), jnp.bfloat16),
        ],
        compiler_params=pltpu.CompilerParams(vmem_limit_bytes=VMEM_LIMIT),
        cost_estimate=cost(2 * 27 * bricks * voxels * C * C, [field, left, right, grads, *outs]),
    )(facts, neighbours, field, left, right, grads)


def run_join(places, pieces):
    out = jax.ShapeDtypeStruct((27 * C, C), jnp.float32)
    return pl.pallas_call(
        join_kernel,
        in_specs=[
            pl.BlockSpec(memory_space=pltpu.SMEM),
            *[pl.BlockSpec(memory_space=pltpu.VMEM) for _ in pieces],
        ],
        out_specs=pl.BlockSpec(memory_space=pltpu.HBM),
        out_shape=out,
        scratch_shapes=[pltpu.VMEM((28 * C, C), jnp.float32), pltpu.SemaphoreType.DMA],
        cost_estimate=cost(0, [out, *pieces]),
    )(places, *pieces).reshape(27, C, C)


def beside(low, high):
    count = lax.axis_size("space")
    left = lax.ppermute(high, "space", [(i, i + 1) for i in range(count - 1)])
    right = lax.ppermute(low, "space", [(i + 1, i) for i in range(count - 1)])
    return left, right


def across(values, mask):
    count = lax.axis_size("space")
    return lax.ppermute(values, "space", [(i, i ^ mask) for i in range(count)])


def swapped(half):
    return across(half, 1)


def among(parts):
    count = lax.axis_size("space")
    groups = [[i for i in range(count) if i % 2 == b] for b in range(2)]
    return lax.all_to_all(parts, "space", 0, 0, axis_index_groups=groups, tiled=True)


def handed(part):
    members = lax.axis_size("space") // 2
    masks = [*range(members // 2, members), *range(1, members // 2)]
    came = {m: across(part, 2 * m) for m in masks}
    return [part, *[came[m] for m in range(1, members)]]


def pair_sum(sent, kept):
    total = kept.astype(jnp.float32) + swapped(sent).astype(jnp.float32)
    return total.astype(jnp.bfloat16)


def in_parts(half):
    return half.reshape(lax.axis_size("space") // 2, -1, C)


def part_total(parts):
    return jnp.sum(parts.astype(jnp.float32), axis=0).astype(jnp.bfloat16)


def gathered(part):
    members = lax.axis_size("space") // 2
    return among(jnp.broadcast_to(part[None], (members,) + part.shape)).reshape(14, C, C)


def joined(half):
    other = swapped(half)
    even = lax.axis_index("space") % 2 == 0
    first = jnp.where(even, half, other)
    second = jnp.where(even, other, half)
    blocks = jnp.concatenate([first, second[:13]], axis=0).astype(jnp.float32)
    return blocks, second[13, 0, 0].astype(jnp.float32)


def column_body(feats, mask, neighbours, weight_one, weight_two, cotangent):
    bricks, voxels, channels = feats.shape
    my_index = lax.axis_index("space")
    low, high = (
        feats[:, rows] * mask[:, rows, None].astype(jnp.bfloat16)
        for rows in (slice(0, SLAB), slice(voxels - SLAB, voxels))
    )
    in_left, in_right = beside(low, high)
    spread_mask = jnp.broadcast_to(mask.astype(jnp.bfloat16)[:, :, None], feats.shape)
    scale = 1.0 / math.sqrt(voxels * bricks)

    members = lax.axis_size("space") // 2
    bit, row = my_index % 2, my_index // 2
    rows = 28 * C // (2 * members)
    order = [*range(members // 2, members), *range(members // 2)]
    own = [(bit * members + (row ^ m)) * rows for m in range(members)]
    others = [((1 - bit) * members + (row ^ m)) * rows for m in range(members)]
    starts = [(i % 2 * members + i // 2) * rows for i in range(2 * members)]
    all_facts = jnp.stack([my_index, *starts])
    part_facts = jnp.stack([my_index, *[others[m] for m in order], *[own[m] for m in order]])
    places = jnp.stack([*own, *others])
    together = lax.optimization_barrier
    in_left, in_right, spread_mask, all_facts, places = together(
        (in_left, in_right, spread_mask, all_facts, places)
    )

    slope, hidden, low, high, inputs = run_conv(
        finish_first, False, True, all_facts, neighbours, feats, in_left, in_right, weight_one,
        [spread_mask], [], ("vmem", "vmem"), (0, EDGE // 2 - 1),
    )
    h_left, h_right = beside(low, high)
    slope, hidden = run_conv(
        finish_first, False, False, all_facts, neighbours, inputs, in_left, in_right, weight_one,
        [spread_mask, slope, hidden], [], ("vmem", "vmem"), tuple(range(1, EDGE // 2 - 1)),
    )
    output, grad_second, low, high = run_conv(
        finish_second, False, False, all_facts, neighbours, hidden, h_left, h_right, weight_two,
        [spread_mask], [cotangent], ("hbm", "vmem"),
    )
    s_left, s_right = beside(low, high)
    (pieces_two,) = run_weight(
        all_facts, neighbours, hidden, h_left, h_right, grad_second, scale,
        [(2 * members, rows)], True,
    )
    pieces_two, s_left, s_right = together((pieces_two, s_left, s_right))
    parts_two = lax.all_to_all(pieces_two, "space", 0, 0, tiled=True)
    grad_first, low, high = run_conv(
        finish_product, True, False, all_facts, neighbours, grad_second, s_left, s_right, weight_two,
        [slope], [], ("vmem",),
    )
    far = members - members // 2
    sent_far, sent_near, kept = run_weight(
        part_facts, neighbours, inputs, in_left, in_right, grad_first, scale,
        [(far, rows), (members // 2, rows), (members, rows)], False,
    )
    parts_two, _ = together((parts_two, kept))
    part_two = part_total(parts_two)
    sent_far, sent_near, low, high = together((sent_far, sent_near, low, high))
    came_far, came_near = swapped(sent_far), swapped(sent_near)
    f_left, f_right = beside(low, high)
    came_far, part_two = together((came_far, part_two))
    half_two = gathered(part_two)
    received = {
        m: piece[n]
        for piece, masks in ((came_far, order[:far]), (came_near, order[far:]))
        for n, m in enumerate(masks)
    }

    def summed(m):
        return kept[order.index(m)].astype(jnp.float32) + received[m].astype(jnp.float32)

    masks = [m for m in order if m]
    halves = [summed(m).astype(jnp.bfloat16) for m in masks]
    *halves, f_left, f_right, late_weight = together((*halves, f_left, f_right, weight_one))
    arrived = [across(half, 2 * m) for half, m in zip(halves, masks)]
    (grad_input,) = run_conv(
        finish_product, True, False, all_facts, neighbours, grad_first, f_left, f_right,
        late_weight, [spread_mask], [], ("hbm",),
    )
    _, half_two = together((grad_input, half_two))
    *arrived, grad_input = together((*arrived, grad_input))
    part = summed(0)
    for half in arrived:
        part = part + half.astype(jnp.float32)
    part = part.astype(jnp.bfloat16)
    same = handed(part)
    grad_w2, strays = joined(half_two)
    same[1], grad_w2, strays = together((same[1], grad_w2, strays))
    other = [swapped(piece) for piece in same]
    grad_w1 = run_join(places, [*same, *other])
    return strays, (output, grad_input, grad_w1, grad_w2)


def body(*arguments):
    strays, results = column_body(*arguments)

    def again(state):
        return jnp.zeros_like(state[0]), general_body(*arguments)

    return lax.while_loop(lambda state: state[0] > 0.5, again, (strays, results))[1]


def extended(field, source_index):
    bricks = field.shape[0]
    left, right = beside(field, field)
    blank = jnp.zeros((1, *field.shape[1:]), field.dtype)
    sources = jnp.concatenate([left, field, right, blank], axis=0).reshape(-1, EDGE * C)
    cell = jnp.arange(EDGE + 2)
    side = jnp.where(cell == 0, 0, jnp.where(cell == EDGE + 1, 2, 1))
    direction = 3 * side[:, None] + side[None, :]
    own = bricks + jnp.arange(bricks)[:, None]
    named = jnp.concatenate([source_index[:, :4], own, source_index[:, 4:]], axis=1)
    place = (cell - 1) % EDGE
    columns = named[:, direction] * SLAB + place[:, None] * EDGE + place[None, :]
    padded = jnp.take(sources, columns, axis=0).reshape(bricks, EDGE + 2, EDGE + 2, EDGE, C)
    return jnp.pad(padded, ((0, 0), (0, 0), (0, 0), (1, 1), (0, 0)))


def shifted(padded, k):
    bricks = padded.shape[0]
    corner = (0, k // 9, k // 3 % 3, k % 3, 0)
    return lax.dynamic_slice(padded, corner, (bricks, EDGE, EDGE, EDGE, C)).reshape(-1, C)


def general_conv(padded, weight, turned):
    def add(k, total):
        block = lax.dynamic_index_in_dim(weight, k, keepdims=False)
        cells = shifted(padded, 26 - k if turned else k)
        return total + jnp.dot(
            cells, block.T if turned else block, preferred_element_type=jnp.float32
        )

    rows = padded.shape[0] * EDGE**3
    return lax.fori_loop(0, 27, add, jnp.zeros((rows, C), jnp.float32))


def general_grad(padded, grads, scale):
    def one(k):
        contract = (((0,), (0,)), ((), ()))
        return lax.dot_general(
            shifted(padded, k), grads, contract, preferred_element_type=jnp.float32
        )

    term = (lax.map(one, jnp.arange(27)) * scale).astype(jnp.bfloat16)
    halves = jnp.pad(term, ((0, 1), (0, 0), (0, 0))).reshape(2, 14, C, C)
    even = lax.axis_index("space") % 2 == 0
    sent = jnp.where(even, halves[1], halves[0])
    kept = jnp.where(even, halves[0], halves[1])
    return joined(gathered(part_total(among(in_parts(pair_sum(sent, kept))))))[0]


def silu_slope(values):
    s = jax.nn.sigmoid(values)
    return s * (1.0 + values * (1.0 - s))


def general_body(feats, mask, neighbours, weight_one, weight_two, cotangent):
    bricks, voxels, _ = feats.shape
    first_brick = (lax.axis_index("space") - 1) * bricks
    source_index = jnp.where(neighbours >= 0, neighbours - first_brick, 3 * bricks)
    occupied = mask.reshape(-1, 1).astype(jnp.float32)
    scale = 1.0 / math.sqrt(voxels * bricks)

    def rounded(values):
        return values.astype(jnp.bfloat16)

    def extend(values):
        return extended(values.reshape(bricks, voxels, C), source_index)

    padded_in = extend(feats * mask[:, :, None].astype(jnp.bfloat16))
    first_pre = general_conv(padded_in, weight_one, False)
    padded_hidden = extend(rounded(occupied * jax.nn.silu(first_pre)))
    second_pre = general_conv(padded_hidden, weight_two, False)
    output = rounded(occupied * jax.nn.silu(second_pre))
    received = cotangent.reshape(-1, C).astype(jnp.float32)
    grad_second = rounded(received * occupied * silu_slope(second_pre))
    back_second = general_conv(extend(grad_second), weight_two, True)
    grad_first = rounded(occupied * silu_slope(first_pre) * back_second)
    grad_input = rounded(occupied * general_conv(extend(grad_first), weight_one, True))
    return (
        output.reshape(feats.shape),
        grad_input.reshape(feats.shape),
        general_grad(padded_in, grad_first, scale),
        general_grad(padded_hidden, grad_second, scale),
    )


def solution(mesh):
    in_specs = (
        P(("scene", "space"), None, None),
        P(("scene", "space"), None),
        P(("scene", "space"), None),
        P(),
        P(),
        P(("scene", "space"), None, None),
    )
    out_specs = (
        P(("scene", "space"), None, None),
        P(("scene", "space"), None, None),
        P("scene", None, None),
        P("scene", None, None),
    )
    return jax.shard_map(body, mesh=mesh, in_specs=in_specs, out_specs=out_specs, check_vma=False)
```

```python
import functools
import math

import jax
import jax.numpy as jnp
from jax import lax
from jax.experimental import pallas as pl
from jax.experimental.pallas import tpu as pltpu
from jax.sharding import PartitionSpec as P

EDGE = 8
TILE = 1
WIDE = 8
SLAB = EDGE * EDGE
C = 128
TAPS = 9 * C
VMEM_LIMIT = 46 * 1024 * 1024

DIRECTIONS = ((-1, -1), (-1, 0), (-1, 1), (0, -1), (0, 1), (1, -1), (1, 0), (1, 1))


def entry(facts, neighbours, brick, column):
    named = neighbours[brick, column]
    local = named - (facts[0] + DIRECTIONS[column][0]) * (TILE * WIDE)
    inside = (named >= 0) & (local >= 0) & (local < neighbours.shape[0])
    return jnp.where(inside, local, -1)


def picked(source, index, first, rows):
    found = source[jnp.maximum(index, 0), first : first + rows, :].astype(jnp.float32)
    return jnp.where(index >= 0, found, 0.0)


def padded_cells(facts, neighbours, field, left, right, g, a):
    near = functools.partial(entry, facts, neighbours, g)
    if a == 0:
        source, first, names = left, 0, (near(1), near(0), near(2))
    elif a == EDGE + 1:
        source, first, names = right, 0, (near(6), near(5), near(7))
    else:
        source, first, names = field, (a - 1) * SLAB, (g, near(3), near(4))
    if source is field:
        centre = field[g, first : first + SLAB, :].astype(jnp.float32)
    else:
        centre = picked(source, names[0], first, SLAB)
    top = picked(source, names[1], first + SLAB - 16, 16)
    bottom = picked(source, names[2], first, 16)
    return centre, jnp.concatenate([top[8:16], centre, bottom[0:8]], axis=0)


def before_and_behind(cells):
    place = lax.broadcasted_iota(jnp.int32, cells.shape, 1)
    before = jnp.where(place == 0, 0.0, pltpu.roll(cells, 1, 1))
    return before, jnp.where(place == EDGE - 1, 0.0, pltpu.roll(cells, EDGE - 1, 1))


def slab_tiles(cells):
    cells = cells.reshape(EDGE + 2, EDGE, C)
    before, behind = before_and_behind(cells)
    even, odd = [], []
    for shifted in (before, cells, behind):
        even.append(shifted.reshape((EDGE + 2) * EDGE, C).astype(jnp.bfloat16))
        odd.append(shifted[1 : EDGE + 1].reshape(SLAB, C).astype(jnp.bfloat16))
    return [e[0:SLAB] for e in even] + odd + [e[16 : 16 + SLAB] for e in even]


def build_slab(facts, neighbours, field, left, right, a, stack):
    for g in range(field.shape[0]):
        _, cells = padded_cells(facts, neighbours, field, left, right, g, a)
        for t, tile in enumerate(slab_tiles(cells)):
            stack[g, :, t * C : (t + 1) * C] = tile


def build_rows(facts, neighbours, field, left, right, slabs, stack):
    @pl.loop(0, field.shape[0])
    def _(g):
        for a in slabs:
            centre, cells = padded_cells(facts, neighbours, field, left, right, g, a)
            cells = cells.astype(jnp.bfloat16)
            stack[g, a, :, 0:C] = cells[0:SLAB]
            stack[g, a, :, C : 2 * C] = centre.astype(jnp.bfloat16)
            stack[g, a, :, 2 * C :] = cells[16 : 16 + SLAB]


def fill_weights(weights, turned, filled):
    for k1 in range(3):
        for k2 in range(3):
            for k3 in range(3):
                n = 9 * k1 + 3 * k2 + k3
                block = weights[26 - n if turned else n]
                if turned:
                    block = block.astype(jnp.float32).T.astype(jnp.bfloat16)
                for half in range(2):
                    row, column = 3 * (k1 + half) + k2, 2 * k3 + half
                    filled[row * C : (row + 1) * C, column * C : (column + 1) * C] = block
    blank = jnp.zeros((3 * C, C), jnp.bfloat16)
    for k3 in range(3):
        filled[9 * C :, 2 * k3 * C : (2 * k3 + 1) * C] = blank
        filled[: 3 * C, (2 * k3 + 1) * C : (2 * k3 + 2) * C] = blank


def conv_kernel(finish, turned, masked, pairs, n_near, n_far, kinds, facts, neighbours, *rest):
    field, left, right, *rest = rest
    near, rest = rest[:n_near], rest[n_near:]
    done, near = (near[-len(kinds) :], near[: -len(kinds)]) if pairs and not masked else ((), near)
    operands, rest = rest[: 1 + n_far], rest[1 + n_far :]
    results, rest = rest[: len(kinds)], rest[len(kinds) :]
    edges, rest = (rest[:2], rest[2:]) if kinds[-1] == "vmem" and not done else ((), rest)
    kept, rest = (rest[0], rest[1:]) if masked else (None, rest)
    local, rest = rest[: 1 + n_far], rest[1 + n_far :]
    *staged, stack, filled, came, gone = rest
    made, leaving = [], []
    for kind, result in zip(kinds, results):
        made.append(result if kind == "vmem" else staged.pop(0))
        if kind == "hbm":
            leaving.append((made[-1], result))
    copies = [
        pltpu.make_async_copy(there, here, came.at[n])
        for n, (there, here) in enumerate(zip(operands, local))
    ]
    for copy in copies:
        copy.start()
    if masked:
        kept[...] = field[...] * near[0][...]
        field = kept
    computed = pairs or tuple(range(EDGE // 2))
    slabs = sorted({2 * pair + n for pair in computed for n in range(4)})
    build_rows(facts, neighbours, field, left, right, slabs, stack)
    copies[0].wait()
    fill_weights(local[0], turned, filled)
    for copy in copies[1:]:
        copy.wait()
    bricks = field.shape[0] // 2
    factors = [*near, *local[1:]]

    def outgoing(pair):
        rows = pl.ds(at(pair * 2 * SLAB), 2 * SLAB)
        return [
            pltpu.make_async_copy(here.at[:, rows, :], there.at[:, rows, :], gone.at[n, pair])
            for n, (here, there) in enumerate(leaving)
        ]

    def step(pair):
        for part in range(2):
            some = slice(part * bricks, (part + 1) * bricks)
            lhs = [stack[some, 2 * pair + n].reshape(bricks * SLAB, 3 * C) for n in range(4)]
            shares = jnp.dot(
                jnp.concatenate(lhs, axis=1), filled[...], preferred_element_type=jnp.float32
            ).reshape(bricks * EDGE, EDGE, 6 * C)
            before, _ = before_and_behind(shares[:, :, : 2 * C])
            _, behind = before_and_behind(shares[:, :, 4 * C :])
            both = (before + shares[:, :, 2 * C : 4 * C] + behind).reshape(bricks * SLAB, 2 * C)
            for half in range(2):
                rows = pl.ds(at((2 * pair + half) * SLAB), SLAB)
                values = both[:, half * C : (half + 1) * C].reshape(bricks, SLAB, C)
                values = finish(
                    values, *[array[some, rows, :].astype(jnp.float32) for array in factors]
                )
                for array, value in zip(made, values):
                    array[some, rows, :] = value.astype(jnp.bfloat16)
        for copy in outgoing(pair):
            copy.start()

    if pairs:
        for pair in pairs:
            step(pair)
        for array, other in zip(made, done):
            for pair in set(range(EDGE // 2)) - set(pairs):
                rows = slice(2 * pair * SLAB, (2 * pair + 2) * SLAB)
                array[:, rows, :] = other[:, rows, :]
    else:

        @pl.loop(0, EDGE // 4)
        def _(n):
            step(2 * n)
            step(2 * n + 1)

    if edges:
        edges[0][...] = made[-1][:, :SLAB, :]
        edges[1][...] = made[-1][:, (EDGE - 1) * SLAB :, :]
    for pair in range(EDGE // 2):
        for copy in outgoing(pair):
            copy.wait()


def at(row):
    return row if isinstance(row, int) else pl.multiple_of(row, SLAB)


def finish_first(values, mask):
    s = jax.nn.sigmoid(values)
    return mask * (s * (1.0 + values * (1.0 - s))), mask * (values * s)


def finish_second(values, mask, cotangent):
    s = jax.nn.sigmoid(values)
    return mask * (values * s), cotangent * mask * (s * (1.0 + values * (1.0 - s)))


def finish_product(values, factor):
    return (factor * values,)


def weight_kernel(scale, counted, facts, neighbours, field, left, right, grads, *rest):
    outs, rest = rest[: -(EDGE + 5)], rest[-(EDGE + 5) :]
    stack, turned, total, blocks = rest[: EDGE + 2], rest[-3], rest[-2], rest[-1]
    bricks = grads.shape[0]

    def turn(a):
        slab = grads[:, a * SLAB : (a + 1) * SLAB, :].reshape(bricks * SLAB, C)
        turned[a] = slab.astype(jnp.float32).T.astype(jnp.bfloat16)

    build_slab(facts, neighbours, field, left, right, 0, stack[0])
    turn(0)
    for a in range(EDGE + 2):
        if a < EDGE + 1:
            build_slab(facts, neighbours, field, left, right, a + 1, stack[a + 1])
        if a < EDGE - 1:
            turn(a + 1)
        first, last = max(0, a - EDGE + 1), min(3, a + 1)
        lhs = [turned[a - k1] for k1 in range(first, last)]
        product = jnp.dot(
            lhs[0] if len(lhs) == 1 else jnp.concatenate(lhs, axis=0),
            stack[a][...].reshape(bricks * SLAB, TAPS),
            preferred_element_type=jnp.float32,
        )
        for n, k1 in enumerate(range(first, last)):
            rows, part = slice(k1 * C, (k1 + 1) * C), product[n * C : (n + 1) * C]
            total[rows, :] = part if a == k1 else total[rows, :] + part
    for n in range(27):
        k1, t = n // 9, n % 9
        block = total[k1 * C : (k1 + 1) * C, t * C : (t + 1) * C].T * scale
        blocks[n * C : (n + 1) * C, :] = block.astype(jnp.bfloat16)
    strays = 0
    for g in range(bricks if counted else 0):
        for column in range(len(DIRECTIONS)):
            lost = (neighbours[g, column] >= 0) & (entry(facts, neighbours, g, column) < 0)
            strays = strays + jnp.where(lost, 1, 0)
    strays = jnp.full((C, C), jnp.minimum(strays, 1), jnp.int32)
    blocks[27 * C :, :] = strays.astype(jnp.float32).astype(jnp.bfloat16)
    n = 1
    for out in outs:
        for piece in range(out.shape[0]):
            first = pl.multiple_of(facts[n], 16)
            out[piece] = blocks[pl.ds(first, out.shape[1]), :]
            n += 1


def join_kernel(places, *rest):
    *pieces, result, blocks, arrived = rest
    for n, piece in enumerate(pieces):
        first = pl.multiple_of(places[n], 16)
        blocks[pl.ds(first, piece.shape[0]), :] = piece[...].astype(jnp.float32)
    copy = pltpu.make_async_copy(blocks.at[pl.ds(0, 27 * C)], result, arrived)
    copy.start()
    copy.wait()


def cost(flops, arrays):
    return pl.CostEstimate(
        flops=flops,
        bytes_accessed=sum(math.prod(a.shape) * a.dtype.itemsize for a in arrays),
        transcendentals=0,
    )


def run_conv(
    finish, turned, masked, facts, neighbours, field, left, right, weights, near, far, kinds, pairs=()
):
    bricks, voxels, _ = field.shape
    rows = jax.ShapeDtypeStruct((bricks, voxels, C), jnp.bfloat16)
    edge = jax.ShapeDtypeStruct((bricks, SLAB, C), jnp.bfloat16)
    operands = [weights, *far]
    spaces = {"vmem": pltpu.VMEM, "hbm": pltpu.HBM}
    outs = [(rows, spaces[kind]) for kind in kinds]
    ends = kinds[-1] == "vmem" and (masked or not pairs)
    outs += [(edge, pltpu.VMEM)] * (2 * ends) + [(rows, pltpu.VMEM)] * masked
    n_hbm = kinds.count("hbm")
    return pl.pallas_call(
        functools.partial(conv_kernel, finish, turned, masked, pairs, len(near), len(far), kinds),
        in_specs=[
            *[pl.BlockSpec(memory_space=pltpu.SMEM)] * 2,
            *[pl.BlockSpec(memory_space=pltpu.VMEM)] * (3 + len(near)),
            *[pl.BlockSpec(memory_space=pltpu.HBM) for _ in operands],
        ],
        out_specs=[pl.BlockSpec(memory_space=space) for _, space in outs],
        out_shape=[shape for shape, _ in outs],
        scratch_shapes=[
            *[pltpu.VMEM(a.shape, a.dtype) for a in operands],
            *[pltpu.VMEM(rows.shape, rows.dtype)] * n_hbm,
            pltpu.VMEM((bricks, EDGE + 2, SLAB, 3 * C), jnp.bfloat16),
            pltpu.VMEM((12 * C, 6 * C), jnp.bfloat16),
            pltpu.SemaphoreType.DMA((len(operands),)),
            pltpu.SemaphoreType.DMA((max(n_hbm, 1), EDGE // 2)),
        ],
        compiler_params=pltpu.CompilerParams(vmem_limit_bytes=VMEM_LIMIT),
        cost_estimate=cost(
            (9 * len(pairs) or 36) * 2 * bricks * voxels * C * C, [field, *near, *operands] + [shape for shape, _ in outs]
        ),
    )(facts, neighbours, field, left, right, *near, *operands)


def run_weight(facts, neighbours, field, left, right, grads, scale, shapes, counted):
    bricks, voxels, _ = field.shape
    outs = [jax.ShapeDtypeStruct((*shape, C), jnp.bfloat16) for shape in shapes]
    return pl.pallas_call(
        functools.partial(weight_kernel, scale, counted),
        in_specs=[
            *[pl.BlockSpec(memory_space=pltpu.SMEM)] * 2,
            *[pl.BlockSpec(memory_space=pltpu.VMEM)] * 4,
        ],
        out_specs=[pl.BlockSpec(memory_space=pltpu.VMEM) for _ in outs],
        out_shape=outs,
        scratch_shapes=[
            *[pltpu.VMEM((bricks, SLAB, TAPS), jnp.bfloat16)] * (EDGE + 2),
            pltpu.VMEM((EDGE, C, bricks * SLAB), jnp.bfloat16),
            pltpu.VMEM((3 * C, TAPS), jnp.float32),
            pltpu.VMEM((28 * C, C), jnp.bfloat16),
        ],
        compiler_params=pltpu.CompilerParams(vmem_limit_bytes=VMEM_LIMIT),
        cost_estimate=cost(2 * 27 * bricks * voxels * C * C, [field, left, right, grads, *outs]),
    )(facts, neighbours, field, left, right, grads)


def run_join(places, pieces):
    out = jax.ShapeDtypeStruct((27 * C, C), jnp.float32)
    return pl.pallas_call(
        join_kernel,
        in_specs=[
            pl.BlockSpec(memory_space=pltpu.SMEM),
            *[pl.BlockSpec(memory_space=pltpu.VMEM) for _ in pieces],
        ],
        out_specs=pl.BlockSpec(memory_space=pltpu.HBM),
        out_shape=out,
        scratch_shapes=[pltpu.VMEM((28 * C, C), jnp.float32), pltpu.SemaphoreType.DMA],
        cost_estimate=cost(0, [out, *pieces]),
    )(places, *pieces).reshape(27, C, C)


def beside(low, high):
    count = lax.axis_size("space")
    left = lax.ppermute(high, "space", [(i, i + 1) for i in range(count - 1)])
    right = lax.ppermute(low, "space", [(i + 1, i) for i in range(count - 1)])
    return left, right


def across(values, mask):
    count = lax.axis_size("space")
    return lax.ppermute(values, "space", [(i, i ^ mask) for i in range(count)])


def swapped(half):
    return across(half, 1)


def among(parts):
    count = lax.axis_size("space")
    groups = [[i for i in range(count) if i % 2 == b] for b in range(2)]
    return lax.all_to_all(parts, "space", 0, 0, axis_index_groups=groups, tiled=True)


def handed(part):
    members = lax.axis_size("space") // 2
    masks = [*range(members // 2, members), *range(1, members // 2)]
    came = {m: across(part, 2 * m) for m in masks}
    return [part, *[came[m] for m in range(1, members)]]


def pair_sum(sent, kept):
    total = kept.astype(jnp.float32) + swapped(sent).astype(jnp.float32)
    return total.astype(jnp.bfloat16)


def in_parts(half):
    return half.reshape(lax.axis_size("space") // 2, -1, C)


def part_total(parts):
    return jnp.sum(parts.astype(jnp.float32), axis=0).astype(jnp.bfloat16)


def gathered(part):
    members = lax.axis_size("space") // 2
    return among(jnp.broadcast_to(part[None], (members,) + part.shape)).reshape(14, C, C)


def joined(half):
    other = swapped(half)
    even = lax.axis_index("space") % 2 == 0
    first = jnp.where(even, half, other)
    second = jnp.where(even, other, half)
    blocks = jnp.concatenate([first, second[:13]], axis=0).astype(jnp.float32)
    return blocks, second[13, 0, 0].astype(jnp.float32)


def column_body(feats, mask, neighbours, weight_one, weight_two, cotangent):
    bricks, voxels, channels = feats.shape
    my_index = lax.axis_index("space")
    low, high = (
        feats[:, rows] * mask[:, rows, None].astype(jnp.bfloat16)
        for rows in (slice(0, SLAB), slice(voxels - SLAB, voxels))
    )
    in_left, in_right = beside(low, high)
    spread_mask = jnp.broadcast_to(mask.astype(jnp.bfloat16)[:, :, None], feats.shape)
    scale = 1.0 / math.sqrt(voxels * bricks)

    members = lax.axis_size("space") // 2
    bit, row = my_index % 2, my_index // 2
    rows = 28 * C // (2 * members)
    order = [*range(members // 2, members), *range(members // 2)]
    own = [(bit * members + (row ^ m)) * rows for m in range(members)]
    others = [((1 - bit) * members + (row ^ m)) * rows for m in range(members)]
    starts = [(i % 2 * members + i // 2) * rows for i in range(2 * members)]
    all_facts = jnp.stack([my_index, *starts])
    part_facts = jnp.stack([my_index, *[others[m] for m in order], *[own[m] for m in order]])
    places = jnp.stack([*own, *others])
    together = lax.optimization_barrier
    in_left, in_right, spread_mask, all_facts, places = together(
        (in_left, in_right, spread_mask, all_facts, places)
    )

    slope, hidden, low, high, inputs = run_conv(
        finish_first, False, True, all_facts, neighbours, feats, in_left, in_right, weight_one,
        [spread_mask], [], ("vmem", "vmem"), (0, EDGE // 2 - 1),
    )
    h_left, h_right = beside(low, high)
    slope, hidden = run_conv(
        finish_first, False, False, all_facts, neighbours, inputs, in_left, in_right, weight_one,
        [spread_mask, slope, hidden], [], ("vmem", "vmem"), tuple(range(1, EDGE // 2 - 1)),
    )
    output, grad_second, low, high = run_conv(
        finish_second, False, False, all_facts, neighbours, hidden, h_left, h_right, weight_two,
        [spread_mask], [cotangent], ("hbm", "vmem"),
    )
    s_left, s_right = beside(low, high)
    (pieces_two,) = run_weight(
        all_facts, neighbours, hidden, h_left, h_right, grad_second, scale,
        [(2 * members, rows)], True,
    )
    pieces_two, s_left, s_right = together((pieces_two, s_left, s_right))
    parts_two = lax.all_to_all(pieces_two, "space", 0, 0, tiled=True)
    grad_first, low, high = run_conv(
        finish_product, True, False, all_facts, neighbours, grad_second, s_left, s_right, weight_two,
        [slope], [], ("vmem",),
    )
    far = members - members // 2
    sent_far, sent_near, kept = run_weight(
        part_facts, neighbours, inputs, in_left, in_right, grad_first, scale,
        [(far, rows), (members // 2, rows), (members, rows)], False,
    )
    parts_two, _ = together((parts_two, kept))
    part_two = part_total(parts_two)
    sent_far, sent_near, low, high = together((sent_far, sent_near, low, high))
    came_far, came_near = swapped(sent_far), swapped(sent_near)
    f_left, f_right = beside(low, high)
    came_far, part_two = together((came_far, part_two))
    half_two = gathered(part_two)
    received = {
        m: piece[n]
        for piece, masks in ((came_far, order[:far]), (came_near, order[far:]))
        for n, m in enumerate(masks)
    }

    def summed(m):
        return kept[order.index(m)].astype(jnp.float32) + received[m].astype(jnp.float32)

    masks = [m for m in order if m]
    halves = [summed(m).astype(jnp.bfloat16) for m in masks]
    *halves, f_left, f_right, late_weight = together((*halves, f_left, f_right, weight_one))
    arrived = [across(half, 2 * m) for half, m in zip(halves, masks)]
    (grad_input,) = run_conv(
        finish_product, True, False, all_facts, neighbours, grad_first, f_left, f_right,
        late_weight, [spread_mask], [], ("hbm",),
    )
    _, half_two = together((grad_input, half_two))
    *arrived, grad_input = together((*arrived, grad_input))
    part = summed(0)
    for half in arrived:
        part = part + half.astype(jnp.float32)
    part = part.astype(jnp.bfloat16)
    same = handed(part)
    other = [swapped(piece) for piece in same]
    grad_w2, strays = joined(half_two)
    *other, grad_w2, strays = together((*other, grad_w2, strays))
    grad_w1 = run_join(places, [*same, *other])
    return strays, (output, grad_input, grad_w1, grad_w2)


def body(*arguments):
    strays, results = column_body(*arguments)

    def again(state):
        return jnp.zeros_like(state[0]), general_body(*arguments)

    return lax.while_loop(lambda state: state[0] > 0.5, again, (strays, results))[1]


def extended(field, source_index):
    bricks = field.shape[0]
    left, right = beside(field, field)
    blank = jnp.zeros((1, *field.shape[1:]), field.dtype)
    sources = jnp.concatenate([left, field, right, blank], axis=0).reshape(-1, EDGE * C)
    cell = jnp.arange(EDGE + 2)
    side = jnp.where(cell == 0, 0, jnp.where(cell == EDGE + 1, 2, 1))
    direction = 3 * side[:, None] + side[None, :]
    own = bricks + jnp.arange(bricks)[:, None]
    named = jnp.concatenate([source_index[:, :4], own, source_index[:, 4:]], axis=1)
    place = (cell - 1) % EDGE
    columns = named[:, direction] * SLAB + place[:, None] * EDGE + place[None, :]
    padded = jnp.take(sources, columns, axis=0).reshape(bricks, EDGE + 2, EDGE + 2, EDGE, C)
    return jnp.pad(padded, ((0, 0), (0, 0), (0, 0), (1, 1), (0, 0)))


def shifted(padded, k):
    bricks = padded.shape[0]
    corner = (0, k // 9, k // 3 % 3, k % 3, 0)
    return lax.dynamic_slice(padded, corner, (bricks, EDGE, EDGE, EDGE, C)).reshape(-1, C)


def general_conv(padded, weight, turned):
    def add(k, total):
        block = lax.dynamic_index_in_dim(weight, k, keepdims=False)
        cells = shifted(padded, 26 - k if turned else k)
        return total + jnp.dot(
            cells, block.T if turned else block, preferred_element_type=jnp.float32
        )

    rows = padded.shape[0] * EDGE**3
    return lax.fori_loop(0, 27, add, jnp.zeros((rows, C), jnp.float32))


def general_grad(padded, grads, scale):
    def one(k):
        contract = (((0,), (0,)), ((), ()))
        return lax.dot_general(
            shifted(padded, k), grads, contract, preferred_element_type=jnp.float32
        )

    term = (lax.map(one, jnp.arange(27)) * scale).astype(jnp.bfloat16)
    halves = jnp.pad(term, ((0, 1), (0, 0), (0, 0))).reshape(2, 14, C, C)
    even = lax.axis_index("space") % 2 == 0
    sent = jnp.where(even, halves[1], halves[0])
    kept = jnp.where(even, halves[0], halves[1])
    return joined(gathered(part_total(among(in_parts(pair_sum(sent, kept))))))[0]


def silu_slope(values):
    s = jax.nn.sigmoid(values)
    return s * (1.0 + values * (1.0 - s))


def general_body(feats, mask, neighbours, weight_one, weight_two, cotangent):
    bricks, voxels, _ = feats.shape
    first_brick = (lax.axis_index("space") - 1) * bricks
    source_index = jnp.where(neighbours >= 0, neighbours - first_brick, 3 * bricks)
    occupied = mask.reshape(-1, 1).astype(jnp.float32)
    scale = 1.0 / math.sqrt(voxels * bricks)

    def rounded(values):
        return values.astype(jnp.bfloat16)

    def extend(values):
        return extended(values.reshape(bricks, voxels, C), source_index)

    padded_in = extend(feats * mask[:, :, None].astype(jnp.bfloat16))
    first_pre = general_conv(padded_in, weight_one, False)
    padded_hidden = extend(rounded(occupied * jax.nn.silu(first_pre)))
    second_pre = general_conv(padded_hidden, weight_two, False)
    output = rounded(occupied * jax.nn.silu(second_pre))
    received = cotangent.reshape(-1, C).astype(jnp.float32)
    grad_second = rounded(received * occupied * silu_slope(second_pre))
    back_second = general_conv(extend(grad_second), weight_two, True)
    grad_first = rounded(occupied * silu_slope(first_pre) * back_second)
    grad_input = rounded(occupied * general_conv(extend(grad_first), weight_one, True))
    return (
        output.reshape(feats.shape),
        grad_input.reshape(feats.shape),
        general_grad(padded_in, grad_first, scale),
        general_grad(padded_hidden, grad_second, scale),
    )


def solution(mesh):
    in_specs = (
        P(("scene", "space"), None, None),
        P(("scene", "space"), None),
        P(("scene", "space"), None),
        P(),
        P(),
        P(("scene", "space"), None, None),
    )
    out_specs = (
        P(("scene", "space"), None, None),
        P(("scene", "space"), None, None),
        P("scene", None, None),
        P("scene", None, None),
    )
    return jax.shard_map(body, mesh=mesh, in_specs=in_specs, out_specs=out_specs, check_vma=False)
```
